32 devices in a mesh: occ: 8 (over z, core), vir: 4 (over y, x).
Axes of the slice: x: 2, y: 2, z: 4, core: 2. Of those that a mesh axis runs over, the one named last changes fastest.
Arguments:
- amplitudes: bfloat16 [16384, 4096], P('occ'), may hold values from -6 to 6
- amp_mask: int32 [8, 8, 4], P('occ'), may hold values 0 or 1
- integrals: bfloat16 [4096, 4096], P('occ', 'vir'), may hold values from -0.09375 to 0.09375
- int_mask: int32 [4, 4], replicated, may hold values 0 or 1
- group_orbital_numbers: int32 [8], replicated, may hold values from 1 to 16, as said below
- occ_energy: float32 [128], replicated, may hold values from -1.5 to -0.25
- vir_energy: float32 [64], replicated, may hold values from 0.25 to 1.5
Outputs:
- update: float32 [16384, 4096], P('occ', 'vir')
The draws below stay inside these ranges and needn't reach their ends.
Inputs may be any that keep to these rules, and one draw needn't show every extreme that they name: `group_orbital_numbers`: some tile holds exactly 16 occupied orbitals.
All inputs are finite; a program needn't handle non-finite values. No bound on the sum of `amp_mask` on one device may be relied on, other than what follows from the above.
Results may differ from the reference program's by a relative error of at most 0.0003.
Values may be sent and summed in bfloat16 or wider, within the bound.
No kernel may reach another device: no remote copies, remote signals or barrier semaphores. Data moves between devices by JAX's collectives and lax.ppermute only.
A program may use at most 384 MiB of HBM per device.

```python
import jax
import jax.numpy as jnp
from jax import lax

VT = 32
NVT = 2
W = 64
ORBITALS_IN_GRP = 16
NUM_OCCUP_BLOCKS = 8
NOCC = 128
PAIRS = 16384


def draw_group_orbital_numbers(key, part):
    key = jax.random.fold_in(key, 11)
    first_key, second_key = jax.random.split(key)
    counts = jax.random.randint(first_key, (NUM_OCCUP_BLOCKS,), 1, ORBITALS_IN_GRP + 1)
    chosen = jax.random.randint(second_key, (), 0, NUM_OCCUP_BLOCKS)
    return jnp.where(jnp.arange(NUM_OCCUP_BLOCKS) == chosen, ORBITALS_IN_GRP, counts).astype(jnp.int32)


def plant(result, rng, low, top_value):
    longest = result.shape.index(max(result.shape))
    spots = []
    for shift in (0, 1):
        where = [jax.random.randint(jax.random.fold_in(rng, axis), (), 0, length) for axis, length in enumerate(result.shape)]
        where[longest] = (where[longest] + shift) % result.shape[longest]
        spots.append(tuple(where))
    return result.at[spots[0]].set(low).at[spots[1]].set(top_value)


def shard_levels(stream_key, extent, cuts, least, top_value):
    loudness = 1.0
    for axis_at, parts in cuts:
        draws = jax.random.uniform(jax.random.fold_in(jax.random.fold_in(stream_key, 6), axis_at), (parts,), jnp.float32, least / len(cuts), top_value / len(cuts))
        loudness = loudness * jnp.repeat(jnp.exp(draws), extent[axis_at] // parts).reshape((-1,) + (1,) * (len(extent) - 1 - axis_at))
    return loudness


def centred(rng, shape, deviation, most, cuts=(), held_as=jnp.bfloat16):
    values = jax.random.normal(rng, shape, jnp.float32) * deviation
    if len(cuts) > 0:
        values = shard_levels(rng, shape, cuts, -0.22, 0.18) * values
    return jnp.clip(values, min=-most, max=most).astype(held_as)


def setup_inputs(seed: int = 0) -> dict:
    key_of = jax.random.split(jax.random.key(seed), 8)
    return {
        "amplitudes": centred(key_of[0], (PAIRS, W * W), 1.0, 6.0, ((0, 8),)),
        "amp_mask": plant((jax.random.randint(key_of[1], (NUM_OCCUP_BLOCKS, NUM_OCCUP_BLOCKS, NVT * NVT), 0, 4) < 3).astype(jnp.int32), jax.random.fold_in(key_of[1], 1), 0, 1),
        "integrals": centred(key_of[2], (W * W, W * W), (W * W) ** -0.5, 0.09375, ((0, 8), (1, 4))),
        "int_mask": plant((jax.random.randint(key_of[3], (NVT * NVT, NVT * NVT), 0, 4) < 3).astype(jnp.int32), jax.random.fold_in(key_of[3], 1), 0, 1),
        "group_orbital_numbers": draw_group_orbital_numbers(jax.random.fold_in(key_of[7], 71), 0),
        "occ_energy": jnp.clip(jax.random.uniform(key_of[5], (NOCC,), jnp.float32, -1.5, -0.25), -1.5, -0.25),
        "vir_energy": jnp.clip(jax.random.uniform(key_of[6], (W,), jnp.float32, 0.25, 1.5), 0.25, 1.5),
    }


def pair_labels(target_positions):
    return (target_positions // W // VT) * NVT + (target_positions % W) // VT


def reference(amplitudes, amp_mask, integrals, int_mask, group_orbital_numbers, occ_energy, vir_energy):
    width_sq = W * W
    labels = pair_labels(jnp.arange(width_sq, dtype=jnp.int32))
    slab_keep = int_mask[labels[:, None], labels[None, :]]
    screened_slab = integrals * slab_keep.astype(integrals.dtype)
    target_positions = jnp.arange(ORBITALS_IN_GRP, dtype=jnp.int32)
    nonzero_flag = target_positions[None, :] < group_orbital_numbers[:, None]
    occ_table = occ_energy.reshape(NUM_OCCUP_BLOCKS, ORBITALS_IN_GRP)

    def one_row(inputs):
        rows, row_mask, left_index_nonzero = inputs
        right_index_kept = row_mask[:, labels]
        doublet_nonzero_list = (left_index_nonzero[None, :, None] & nonzero_flag[:, None, :]).astype(jnp.int32)
        keeping_filter = doublet_nonzero_list.reshape(NUM_OCCUP_BLOCKS, ORBITALS_IN_GRP * ORBITALS_IN_GRP, 1) * right_index_kept[:, None, :]
        screened = rows.reshape(NUM_OCCUP_BLOCKS, ORBITALS_IN_GRP * ORBITALS_IN_GRP, width_sq) * keeping_filter.astype(rows.dtype)
        return jnp.dot(screened.reshape(-1, width_sq), screened_slab, preferred_element_type=jnp.float32)

    ladder = lax.map(one_row, (amplitudes.reshape(NUM_OCCUP_BLOCKS, NUM_OCCUP_BLOCKS * ORBITALS_IN_GRP * ORBITALS_IN_GRP, width_sq), amp_mask, nonzero_flag))
    ladder = ladder.reshape(NUM_OCCUP_BLOCKS, NUM_OCCUP_BLOCKS, ORBITALS_IN_GRP, ORBITALS_IN_GRP, W, W)
    mirror = ladder.transpose(1, 0, 3, 2, 5, 4)
    denominator = (vir_energy[None, None, None, None, :, None] + vir_energy[None, None, None, None, None, :]
                   - occ_table[:, None, :, None, None, None] - occ_table[None, :, None, :, None, None])
    update = (ladder + mirror) / denominator
    return update.reshape(NUM_OCCUP_BLOCKS * NUM_OCCUP_BLOCKS * ORBITALS_IN_GRP * ORBITALS_IN_GRP, width_sq)
```

```python
import functools

import jax
import jax.numpy as jnp
from jax import lax
from jax.experimental import pallas as pl
from jax.experimental.pallas import tpu as pltpu
from jax.sharding import PartitionSpec as P

VT = 32
NVT = 2
W = 64
ORBITALS_IN_GRP = 16
PAIR_SQ = ORBITALS_IN_GRP * ORBITALS_IN_GRP
CODE_ROWS = 16
TOP = 32700.0
STEPS = 8.0
VMEM_LIMIT = 56 * 1024 * 1024


def one_hot_of(target, amount):
    return (target[:, None] == jnp.arange(amount)[None, :]).astype(jnp.bfloat16)


def split(values):
    high = values.astype(jnp.bfloat16)
    return high, (values - high.astype(jnp.float32)).astype(jnp.bfloat16)


def dot(left, right):
    return jnp.dot(left, right, preferred_element_type=jnp.float32)


def scale_of(code):
    return jnp.exp2(code * (1.0 / STEPS))


def ladder_kernel(vir_count, amp_mask, int_mask, place, numbers, rows_ref, slab_ref, swap_ref, perm_ref,
                  ladder_ref, packed_ref, slab_scr):
    tile = pl.program_id(0)
    cols = slab_ref.shape[1]

    @pl.when(tile == 0)
    def _():
        lane = lax.broadcasted_iota(jnp.int32, (1, cols), 1) % W
        second = lane >= VT
        first_pair = place[1] * NVT

        def screen(c, carry):
            for d_tile in range(NVT):
                label = c // VT * NVT + d_tile
                keep = jnp.where(second, int_mask[label, first_pair + 1], int_mask[label, first_pair])
                at = pl.ds(pl.multiple_of(c * W + d_tile * VT, VT), VT)
                slab_scr[at, :] = slab_ref[at, :] * keep.astype(jnp.float32).astype(jnp.bfloat16)
            return carry

        lax.fori_loop(0, W, screen, 0)

    lane = lax.broadcasted_iota(jnp.int32, (1, W * W), 1)
    low = lane < W * VT
    left = lane % W < VT
    keep = jnp.where(
        low,
        jnp.where(left, amp_mask[tile, 0], amp_mask[tile, 1]),
        jnp.where(left, amp_mask[tile, 2], amp_mask[tile, 3]),
    )
    screened = rows_ref[...] * keep.astype(jnp.float32).astype(jnp.bfloat16)
    ladder = dot(screened, slab_scr[...])
    pair = lax.broadcasted_iota(jnp.int32, (PAIR_SQ, 1), 0)
    nonzero = (pair // ORBITALS_IN_GRP < numbers[place[0]]) & (pair % ORBITALS_IN_GRP < numbers[tile])
    ladder = jnp.where(nonzero, ladder, 0.0)
    ladder_ref[...] = ladder
    high, low_part = split(ladder)
    mirror = dot(dot(swap_ref[...], high).astype(jnp.bfloat16), perm_ref[...]) + dot(
        dot(swap_ref[...], low_part).astype(jnp.bfloat16), perm_ref[...]
    )
    most = jnp.maximum(jnp.max(jnp.abs(mirror), axis=0, keepdims=True), 1e-30)
    code = jnp.ceil(jnp.log2(most) * STEPS)
    coded = jnp.round(mirror * (TOP / scale_of(code))).astype(jnp.int32).astype(jnp.int16)
    code_rows = jnp.broadcast_to(code.astype(jnp.int32), (CODE_ROWS, cols)).astype(jnp.int16)
    block = cols // vir_count
    for v in range(vir_count):
        packed_ref[0, v, :PAIR_SQ] = coded[:, v * block : (v + 1) * block]
        packed_ref[0, v, PAIR_SQ:] = code_rows[:, v * block : (v + 1) * block]


def ladder_call(tile_total, vir_count, chunk_cols, *args):
    block = chunk_cols // vir_count
    smem = pl.BlockSpec(memory_space=pltpu.SMEM)
    whole = lambda tile: (0, 0)
    flops = 2 * tile_total * PAIR_SQ * chunk_cols * (W * W + 2 * PAIR_SQ + 2 * chunk_cols)
    bytes_accessed = tile_total * PAIR_SQ * (W * W * 2 + chunk_cols * 6) + W * W * chunk_cols * 2
    return pl.pallas_call(
        functools.partial(ladder_kernel, vir_count),
        grid=(tile_total,),
        in_specs=[
            smem,
            smem,
            smem,
            smem,
            pl.BlockSpec((PAIR_SQ, W * W), lambda tile: (tile, 0)),
            pl.BlockSpec((W * W, chunk_cols), whole),
            pl.BlockSpec((PAIR_SQ, PAIR_SQ), whole),
            pl.BlockSpec((chunk_cols, chunk_cols), whole),
        ],
        out_specs=[
            pl.BlockSpec((PAIR_SQ, chunk_cols), lambda tile: (tile, 0)),
            pl.BlockSpec((1, vir_count, PAIR_SQ + CODE_ROWS, block), lambda tile: (tile, 0, 0, 0)),
        ],
        out_shape=[
            jax.ShapeDtypeStruct((tile_total * PAIR_SQ, chunk_cols), jnp.float32),
            jax.ShapeDtypeStruct((tile_total, vir_count, PAIR_SQ + CODE_ROWS, block), jnp.int16),
        ],
        scratch_shapes=[pltpu.VMEM((W * W, chunk_cols), jnp.bfloat16)],
        compiler_params=pltpu.CompilerParams(vmem_limit_bytes=VMEM_LIMIT),
        cost_estimate=pl.CostEstimate(flops=flops, bytes_accessed=bytes_accessed, transcendentals=0),
        name="ladder",
    )(*args)


def update_kernel(chunks, vir_count, vir_ref, occ_ref, spread_ref, *refs):
    ladders, arrived, update_ref = refs[:chunks], refs[chunks : 2 * chunks], refs[2 * chunks]
    highs, lows = [], []
    for c in range(chunks):
        for v in range(vir_count):
            code = arrived[c][0, v, PAIR_SQ:].astype(jnp.int32).astype(jnp.float32)[:1]
            values = arrived[c][0, v, :PAIR_SQ].astype(jnp.int32).astype(jnp.float32)
            high, low = split(values * (scale_of(code) * (1.0 / TOP)))
            highs.append(high)
            lows.append(low)
    mirror = dot(jnp.concatenate(highs, axis=1), spread_ref[...]) + dot(
        jnp.concatenate(lows, axis=1), spread_ref[...]
    )
    chunk_cols = ladders[0].shape[1]
    for c in range(chunks):
        at = slice(c * chunk_cols, (c + 1) * chunk_cols)
        denominator = vir_ref[:, at] - occ_ref[:, :1]
        update_ref[:, at] = (ladders[c][...] + mirror[:, at]) / denominator


def update_call(tile_total, vir_count, vir_sum, occ_sum, spread, ladders, arrived):
    chunks = len(ladders)
    chunk_cols = ladders[0].shape[1]
    block = chunk_cols // vir_count
    slab_cols = chunks * chunk_cols
    whole = lambda tile: (0, 0)
    rows = tile_total * PAIR_SQ
    return pl.pallas_call(
        functools.partial(update_kernel, chunks, vir_count),
        grid=(tile_total,),
        in_specs=[
            pl.BlockSpec((1, slab_cols), whole),
            pl.BlockSpec((PAIR_SQ, 128), lambda tile: (tile, 0)),
            pl.BlockSpec((slab_cols, slab_cols), whole),
        ]
        + [pl.BlockSpec((PAIR_SQ, chunk_cols), lambda tile: (tile, 0))] * chunks
        + [pl.BlockSpec((1, vir_count, PAIR_SQ + CODE_ROWS, block), lambda tile: (tile, 0, 0, 0))] * chunks,
        out_specs=pl.BlockSpec((PAIR_SQ, slab_cols), lambda tile: (tile, 0)),
        out_shape=jax.ShapeDtypeStruct((rows, slab_cols), jnp.float32),
        compiler_params=pltpu.CompilerParams(vmem_limit_bytes=VMEM_LIMIT),
        cost_estimate=pl.CostEstimate(
            flops=4 * rows * slab_cols * slab_cols, bytes_accessed=rows * slab_cols * 10, transcendentals=0
        ),
        name="update",
    )(vir_sum, occ_sum, spread, *ladders, *arrived)


def body(amplitudes, amp_mask, integrals, int_mask, group_orbital_numbers, occ_energy, vir_energy):
    tile_total = lax.axis_size("occ")
    vir_count = lax.axis_size("vir")
    row_tile = lax.axis_index("occ")
    vir_place = lax.axis_index("vir")
    vir_span = W // vir_count
    slab_cols = vir_span * W
    chunks = 2 if vir_span >= 16 else 1
    chunk_cols = slab_cols // chunks
    chunk_span = vir_span // chunks
    block = chunk_cols // vir_count

    slabs = [
        lax.all_gather(integrals[:, c * chunk_cols : (c + 1) * chunk_cols], "occ", axis=0, tiled=True)
        for c in range(chunks)
    ]

    pair = jnp.arange(PAIR_SQ)
    swap = one_hot_of(pair % ORBITALS_IN_GRP * ORBITALS_IN_GRP + pair // ORBITALS_IN_GRP, PAIR_SQ)
    col = jnp.arange(chunk_cols)
    a, b = col // W, col % W
    perm = one_hot_of(b // vir_span * block + b % vir_span * chunk_span + a, chunk_cols)
    place = jnp.arange(slab_cols)
    chunk, sender = place // chunk_cols, place % chunk_cols // block
    own, other = place % block // chunk_span, place % chunk_span
    spread = one_hot_of(own * W + sender * vir_span + chunk * chunk_span + other, slab_cols)

    where = jnp.stack([row_tile, vir_place * vir_span // VT]).astype(jnp.int32)
    occ_table = occ_energy.reshape(tile_total, ORBITALS_IN_GRP)
    own_energy = lax.dynamic_slice_in_dim(occ_table, row_tile, 1, 0)[0]
    occ_sum = jnp.broadcast_to(
        (own_energy[None, :, None] + occ_table[:, None, :]).reshape(-1, 1), (tile_total * PAIR_SQ, 128)
    )
    vir_own = lax.dynamic_slice_in_dim(vir_energy, vir_place * vir_span, vir_span, 0)
    vir_sum = (vir_own[:, None] + vir_energy[None, :]).reshape(1, -1)

    ladders, arrived = [], []
    for c in range(chunks):
        ladder, packed = ladder_call(
            tile_total, vir_count, chunk_cols, amp_mask[0], int_mask, where, group_orbital_numbers,
            amplitudes, slabs[c], swap, perm,
        )
        rows = PAIR_SQ + CODE_ROWS
        moved = lax.all_to_all(
            packed.reshape(tile_total * vir_count, rows, block), ("occ", "vir"), split_axis=0, concat_axis=0, tiled=True
        )
        ladders.append(ladder)
        arrived.append(moved.reshape(tile_total, vir_count, rows, block))
    return update_call(tile_total, vir_count, vir_sum, occ_sum, spread, ladders, arrived)


def solution(mesh):
    in_specs = (P("occ", None), P("occ", None, None), P("occ", "vir"), P(), P(), P(), P())
    out_specs = P("occ", "vir")
    return jax.shard_map(body, mesh=mesh, in_specs=in_specs, out_specs=out_specs, check_vma=False)
```

```python
import functools

import jax
import jax.numpy as jnp
from jax import lax
from jax.experimental import pallas as pl
from jax.experimental.pallas import tpu as pltpu
from jax.sharding import PartitionSpec as P

VT = 32
NVT = 2
W = 64
ORBITALS_IN_GRP = 16
PAIR_SQ = ORBITALS_IN_GRP * ORBITALS_IN_GRP
PIECES = 2
PIECE_SPAN = ORBITALS_IN_GRP // PIECES
PIECE_ROWS = PIECE_SPAN * ORBITALS_IN_GRP
TILES_AT_ONCE = 2
TOP = 32700.0
STEPS = 8.0
VMEM_LIMIT = 56 * 1024 * 1024


def one_hot_of(target, amount):
    return (target[:, None] == jnp.arange(amount)[None, :]).astype(jnp.bfloat16)


def split(values):
    high = values.astype(jnp.bfloat16)
    return high, (values - high.astype(jnp.float32)).astype(jnp.bfloat16)


def dot(left, right):
    return jnp.dot(left, right, preferred_element_type=jnp.float32)


def scale_of(code):
    return jnp.exp2(code * (1.0 / STEPS))


def screen_kernel(vir_count, int_mask, slab_ref, screened_ref):
    slab_rows, slab_cols = slab_ref.shape
    row_label = lax.axis_index("occ") * slab_rows // W // VT * NVT
    col_label = lax.axis_index("vir") * slab_cols // W // VT * NVT
    right = lax.broadcasted_iota(jnp.int32, (VT, slab_cols), 1) % W >= VT
    keep = []
    for d_tile in range(NVT):
        label = row_label + d_tile
        kept = jnp.where(right, int_mask[label, col_label + 1], int_mask[label, col_label])
        keep.append(kept.astype(jnp.float32).astype(jnp.bfloat16))
    for at in range(0, slab_rows, VT):
        screened_ref[at : at + VT, :] = slab_ref[at : at + VT, :] * keep[at // VT % NVT]


def screen_call(vir_count, int_mask, integrals):
    return pl.pallas_call(
        functools.partial(screen_kernel, vir_count),
        in_specs=[pl.BlockSpec(memory_space=pltpu.SMEM), pl.BlockSpec(memory_space=pltpu.VMEM)],
        out_specs=pl.BlockSpec(memory_space=pltpu.VMEM),
        out_shape=jax.ShapeDtypeStruct(integrals.shape, integrals.dtype),
        name="screen",
    )(int_mask, integrals)


def ladder_kernel(piece, vir_count, amp_mask, numbers, rows_ref, slab_ref, swap_ref, perm_ref,
                  ladder_ref, packed_ref, code_ref):
    tiles = rows_ref.shape[0]
    cols = slab_ref.shape[1]
    first = pl.program_id(1) * tiles
    lane = lax.broadcasted_iota(jnp.int32, (1, W * W), 1)
    low = lane < W * VT
    left = lane % W < VT
    pair = lax.broadcasted_iota(jnp.int32, (PIECE_ROWS, 1), 0)
    own_number = numbers[lax.axis_index("occ")]
    screened, nonzero = [], []
    for n in range(tiles):
        tile = first + n
        keep = jnp.where(
            low,
            jnp.where(left, amp_mask[tile, 0], amp_mask[tile, 1]),
            jnp.where(left, amp_mask[tile, 2], amp_mask[tile, 3]),
        )
        screened.append(rows_ref[n, 0] * keep.astype(jnp.float32).astype(jnp.bfloat16))
        nonzero.append(
            (pair // ORBITALS_IN_GRP + piece * PIECE_SPAN < own_number)
            & (pair % ORBITALS_IN_GRP < numbers[tile])
        )
    ladder = dot(jnp.concatenate(screened, axis=0), slab_ref[...])
    ladder = jnp.where(jnp.concatenate(nonzero, axis=0), ladder, 0.0)
    ladder_ref[...] = ladder.reshape(ladder_ref.shape)
    high, low_part = split(ladder)
    mirror = dot(dot(swap_ref[...], high).astype(jnp.bfloat16), perm_ref[...]) + dot(
        dot(swap_ref[...], low_part).astype(jnp.bfloat16), perm_ref[...]
    )
    block = cols // vir_count
    for n in range(tiles):
        part = mirror[n * PIECE_ROWS : (n + 1) * PIECE_ROWS]
        most = jnp.maximum(jnp.max(jnp.abs(part), axis=0, keepdims=True), 1e-30)
        code = jnp.ceil(jnp.log2(most) * STEPS)
        code_ref[0, n : n + 1, :] = code
        coded = jnp.round(part * (TOP / scale_of(code))).astype(jnp.int32).astype(jnp.int16)
        for v in range(vir_count):
            packed_ref[n, v] = coded[:, v * block : (v + 1) * block]


def ladder_call(piece, tile_total, vir_count, cut, amp_mask, numbers, amplitudes, slab, swap, perm):
    slab_cols = slab.shape[1]
    chunk = slab_cols // cut
    block = chunk // vir_count
    tiles = TILES_AT_ONCE
    smem = pl.BlockSpec(memory_space=pltpu.SMEM)
    whole = lambda c, t: (0, 0)
    rows = tile_total * PIECE_ROWS
    flops = 2 * rows * slab_cols * (W * W + 2 * tiles * PIECE_ROWS + 2 * chunk)
    bytes_accessed = rows * (W * W * 2 * cut + slab_cols * 6) + W * W * slab_cols * 2
    return pl.pallas_call(
        functools.partial(ladder_kernel, piece, vir_count),
        grid=(cut, tile_total // tiles),
        in_specs=[
            smem,
            smem,
            pl.BlockSpec((tiles, 1, PIECE_ROWS, W * W), lambda c, t: (t, piece, 0, 0)),
            pl.BlockSpec((W * W, chunk), lambda c, t: (0, c)),
            pl.BlockSpec(swap.shape, whole),
            pl.BlockSpec(perm.shape, whole),
        ],
        out_specs=[
            pl.BlockSpec((tiles, PIECE_ROWS, chunk), lambda c, t: (t, 0, c)),
            pl.BlockSpec((tiles, vir_count, PIECE_ROWS, block), lambda c, t: (t, 0, 0, c)),
            pl.BlockSpec((1, tiles, chunk), lambda c, t: (t, 0, c)),
        ],
        out_shape=[
            jax.ShapeDtypeStruct((tile_total, PIECE_ROWS, slab_cols), jnp.float32),
            jax.ShapeDtypeStruct((tile_total, vir_count, PIECE_ROWS, cut * block), jnp.int16),
            jax.ShapeDtypeStruct((tile_total // tiles, tiles, slab_cols), jnp.float32),
        ],
        compiler_params=pltpu.CompilerParams(vmem_limit_bytes=VMEM_LIMIT),
        cost_estimate=pl.CostEstimate(flops=flops, bytes_accessed=bytes_accessed, transcendentals=0),
        name="ladder",
    )(amp_mask, numbers, amplitudes, slab, swap, perm)


def update_kernel(vir_count, code_ref, vir_ref, occ_ref, spread_ref, arrived_ref, *refs):
    ladders, update_ref = refs[:PIECES], refs[-1]
    highs, lows = [], []
    for v in range(vir_count):
        values = arrived_ref[0, v].astype(jnp.int32).astype(jnp.float32)
        high, low = split(values * (scale_of(code_ref[0, v : v + 1, :]) * (1.0 / TOP)))
        highs.append(high)
        lows.append(low)
    mirror = dot(jnp.concatenate(highs, axis=1), spread_ref[...]) + dot(
        jnp.concatenate(lows, axis=1), spread_ref[...]
    )
    slab_cols = mirror.shape[1]
    ladder = jnp.concatenate([ref[...].reshape(-1, slab_cols) for ref in ladders], axis=0)
    denominator = vir_ref[...] - occ_ref[...].reshape(PIECE_ROWS, -1)[:, :1]
    update_ref[...] = ((ladder + mirror) / denominator).reshape(update_ref.shape)


def update_call(piece, tile_total, vir_count, code, vir_sum, occ_sum, spread, arrived, ladders, earlier):
    slab_cols = spread.shape[1]
    rows = tile_total * PIECE_ROWS
    of_piece = lambda span, lanes: pl.BlockSpec(
        (1, span, 1, PIECE_SPAN, lanes), lambda tile: (tile, 0, piece, 0, 0)
    )
    args = [code, vir_sum, occ_sum, spread, arrived, *ladders]
    in_specs = [
        pl.BlockSpec((1,) + code.shape[1:], lambda tile: (tile, 0, 0)),
        pl.BlockSpec((1, slab_cols), lambda tile: (0, 0)),
        of_piece(ORBITALS_IN_GRP, 128),
        pl.BlockSpec(spread.shape, lambda tile: (0, 0)),
        pl.BlockSpec((1,) + arrived.shape[1:], lambda tile: (tile, 0, 0, 0)),
    ] + [of_piece(PIECE_SPAN, slab_cols)] * PIECES
    aliases = {}
    if earlier is not None:
        aliases = {len(args): 0}
        args.append(earlier)
        in_specs.append(pl.BlockSpec(memory_space=pl.ANY))
    return pl.pallas_call(
        functools.partial(update_kernel, vir_count),
        grid=(tile_total,),
        in_specs=in_specs,
        out_specs=of_piece(ORBITALS_IN_GRP, slab_cols),
        out_shape=jax.ShapeDtypeStruct((tile_total, ORBITALS_IN_GRP, PIECES, PIECE_SPAN, slab_cols), jnp.float32),
        input_output_aliases=aliases,
        compiler_params=pltpu.CompilerParams(vmem_limit_bytes=VMEM_LIMIT),
        cost_estimate=pl.CostEstimate(
            flops=4 * rows * slab_cols * slab_cols, bytes_accessed=rows * slab_cols * 10, transcendentals=0
        ),
        name="update",
    )(*args)


def body(amplitudes, amp_mask, integrals, int_mask, group_orbital_numbers, occ_energy, vir_energy):
    tile_total = lax.axis_size("occ")
    vir_count = lax.axis_size("vir")
    row_tile = lax.axis_index("occ")
    vir_place = lax.axis_index("vir")
    vir_span = W // vir_count
    slab_cols = vir_span * W
    cut = 2 if vir_span >= 16 else 1
    chunk = slab_cols // cut
    chunk_span = vir_span // cut
    block = chunk // vir_count

    slab = lax.all_gather(screen_call(vir_count, int_mask, integrals), "occ", axis=0, tiled=True)

    rows = jnp.arange(TILES_AT_ONCE * PIECE_ROWS)
    in_tile = rows % PIECE_ROWS
    swap = one_hot_of(
        rows // PIECE_ROWS * PIECE_ROWS + in_tile % PIECE_SPAN * ORBITALS_IN_GRP + in_tile // PIECE_SPAN, rows.size
    )
    col = jnp.arange(chunk)
    a, b = col // W, col % W
    perm = one_hot_of(b // vir_span * block + b % vir_span * chunk_span + a, chunk)
    place = jnp.arange(slab_cols)
    sender, part = place // (cut * block), place // block % cut
    own, other = place % block // chunk_span, place % chunk_span
    spread = one_hot_of(own * W + sender * vir_span + part * chunk_span + other, slab_cols)

    occ_table = occ_energy.reshape(tile_total, ORBITALS_IN_GRP)
    own_energy = lax.dynamic_slice_in_dim(occ_table, row_tile, 1, 0)[0]
    occ_sum = jnp.broadcast_to(
        (own_energy[None, :, None] + occ_table[:, None, :]).reshape(
            tile_total, ORBITALS_IN_GRP, PIECES, PIECE_SPAN, 1
        ),
        (tile_total, ORBITALS_IN_GRP, PIECES, PIECE_SPAN, 128),
    )
    vir_own = lax.dynamic_slice_in_dim(vir_energy, vir_place * vir_span, vir_span, 0)
    vir_sum = (vir_own[:, None] + vir_energy[None, :]).reshape(1, -1)

    by_piece = amplitudes.reshape(tile_total, PIECES, PIECE_ROWS, W * W)
    ladders, arrived, codes = [], [], []
    for piece in range(PIECES):
        ladder, packed, code = ladder_call(
            piece, tile_total, vir_count, cut, amp_mask[0], group_orbital_numbers, by_piece, slab, swap, perm
        )
        moved = lax.all_to_all(
            packed.reshape(tile_total * vir_count, PIECE_ROWS, cut * block),
            ("occ", "vir"), split_axis=0, concat_axis=0, tiled=True,
        )
        all_codes = lax.all_gather(code, ("occ", "vir"), axis=0, tiled=False)
        all_codes = all_codes.reshape(tile_total, vir_count, tile_total, cut, vir_count, block)
        own_codes = lax.dynamic_slice(
            all_codes, (0, 0, row_tile, 0, vir_place, 0), (tile_total, vir_count, 1, cut, 1, block)
        )
        ladders.append(ladder.reshape(tile_total, PIECE_SPAN, PIECES, PIECE_SPAN, slab_cols))
        arrived.append(moved.reshape(tile_total, vir_count, PIECE_ROWS, cut * block))
        codes.append(own_codes.reshape(tile_total, vir_count, cut * block))
    update = None
    for piece in range(PIECES):
        update = update_call(
            piece, tile_total, vir_count, codes[piece], vir_sum, occ_sum, spread, arrived[piece], ladders, update
        )
    return update.reshape(tile_total * PAIR_SQ, slab_cols)


def solution(mesh):
    in_specs = (P("occ", None), P("occ", None, None), P("occ", "vir"), P(), P(), P(), P())
    out_specs = P("occ", "vir")
    return jax.shard_map(body, mesh=mesh, in_specs=in_specs, out_specs=out_specs, check_vma=False)
```

```python
import functools

import jax
import jax.numpy as jnp
from jax import lax
from jax.experimental import pallas as pl
from jax.experimental.pallas import tpu as pltpu
from jax.sharding import PartitionSpec as P

VT = 32
NVT = 2
W = 64
ORBITALS_IN_GRP = 16
PAIR_SQ = ORBITALS_IN_GRP * ORBITALS_IN_GRP
CODE_ROWS = 16
AT_ONCE = 2
TOP = 32700.0
STEPS = 8.0
VMEM_LIMIT = 56 * 1024 * 1024


def one_hot_of(target, amount):
    return (target[:, None] == jnp.arange(amount)[None, :]).astype(jnp.bfloat16)


def split(values):
    high = values.astype(jnp.bfloat16)
    return high, (values - high.astype(jnp.float32)).astype(jnp.bfloat16)


def dot(left, right):
    return jnp.dot(left, right, preferred_element_type=jnp.float32)


def scale_of(code):
    return jnp.exp2(code * (1.0 / STEPS))


def screen_kernel(int_mask, slab_ref, screened_ref):
    slab_rows, slab_cols = slab_ref.shape
    row_label = lax.axis_index("occ") * slab_rows // W // VT * NVT
    col_label = lax.axis_index("vir") * slab_cols // W // VT * NVT
    right = lax.broadcasted_iota(jnp.int32, (VT, slab_cols), 1) % W >= VT
    keep = []
    for d_tile in range(NVT):
        label = row_label + d_tile
        kept = jnp.where(right, int_mask[label, col_label + 1], int_mask[label, col_label])
        keep.append(kept.astype(jnp.float32).astype(jnp.bfloat16))
    for at in range(0, slab_rows, VT):
        screened_ref[at : at + VT, :] = slab_ref[at : at + VT, :] * keep[at // VT % NVT]


def screen_call(int_mask, integrals):
    return pl.pallas_call(
        screen_kernel,
        in_specs=[pl.BlockSpec(memory_space=pltpu.SMEM), pl.BlockSpec(memory_space=pltpu.VMEM)],
        out_specs=pl.BlockSpec(memory_space=pltpu.VMEM),
        out_shape=jax.ShapeDtypeStruct(integrals.shape, integrals.dtype),
        name="screen",
    )(int_mask, integrals)


def ladder_kernel(distances, vir_count, cut, own, amp_mask, numbers, *refs):
    count = len(distances)
    rows_refs, (slab_ref, swap_ref, perm_ref, ladder_ref), packed_refs = (
        refs[:count], refs[count : count + 4], refs[count + 4 :]
    )
    part = pl.program_id(0)
    cols = slab_ref.shape[1]
    block = cols // vir_count
    lane = lax.broadcasted_iota(jnp.int32, (1, W * W), 1)
    low = lane < W * VT
    left = lane % W < VT
    pair = lax.broadcasted_iota(jnp.int32, (PAIR_SQ, 1), 0)
    screened = []
    for n in range(count):
        tile = own[0] ^ distances[n]
        keep = jnp.where(
            low,
            jnp.where(left, amp_mask[tile, 0], amp_mask[tile, 1]),
            jnp.where(left, amp_mask[tile, 2], amp_mask[tile, 3]),
        )
        screened.append(rows_refs[n][...] * keep.astype(jnp.float32).astype(jnp.bfloat16))
    product = dot(jnp.concatenate(screened, axis=0), slab_ref[...])
    code_row = lax.broadcasted_iota(jnp.int32, (CODE_ROWS, block), 0) == part
    for n in range(count):
        tile = own[0] ^ distances[n]
        nonzero = (pair // ORBITALS_IN_GRP < numbers[own[0]]) & (pair % ORBITALS_IN_GRP < numbers[tile])
        ladder = jnp.where(nonzero, product[n * PAIR_SQ : (n + 1) * PAIR_SQ], 0.0)
        ladder_ref[n] = ladder
        high, low_part = split(ladder)
        mirror = dot(dot(swap_ref[...], high).astype(jnp.bfloat16), perm_ref[...]) + dot(
            dot(swap_ref[...], low_part).astype(jnp.bfloat16), perm_ref[...]
        )
        most = jnp.maximum(jnp.max(jnp.abs(mirror), axis=0, keepdims=True), 1e-30)
        code = jnp.ceil(jnp.log2(most) * STEPS)
        coded = jnp.round(mirror * (TOP / scale_of(code))).astype(jnp.int32).astype(jnp.int16)
        code_int = code.astype(jnp.int32)
        for v in range(vir_count):
            at = slice(v * block, (v + 1) * block)
            packed = packed_refs[n * vir_count + v]
            packed[pl.ds(pl.multiple_of(part * PAIR_SQ, PAIR_SQ), PAIR_SQ), :] = coded[:, at]
            before = packed[cut * PAIR_SQ :, :].astype(jnp.int32)
            packed[cut * PAIR_SQ :, :] = jnp.where(
                code_row, jnp.broadcast_to(code_int[:, at], (CODE_ROWS, block)), before
            ).astype(jnp.int16)


def ladder_call(distances, vir_count, cut, own, amp_mask, numbers, amplitudes, slab, swap, perm):
    slab_cols = slab.shape[1]
    chunk = slab_cols // cut
    block = chunk // vir_count
    count = len(distances)
    smem = pl.BlockSpec(memory_space=pltpu.SMEM)
    whole = lambda c, own: (0, 0)
    rows = count * PAIR_SQ
    packed_shape = (cut * PAIR_SQ + CODE_ROWS, block)
    flops = 2 * rows * slab_cols * (W * W + 2 * PAIR_SQ + 2 * chunk)
    bytes_accessed = rows * (W * W * 2 + slab_cols * 6) + W * W * slab_cols * 2
    return pl.pallas_call(
        functools.partial(ladder_kernel, distances, vir_count, cut),
        grid_spec=pltpu.PrefetchScalarGridSpec(
            num_scalar_prefetch=1,
            grid=(cut,),
            in_specs=[smem, smem]
            + [pl.BlockSpec((PAIR_SQ, W * W), lambda c, own, d=d: (own[0] ^ d, 0)) for d in distances]
            + [
                pl.BlockSpec((W * W, chunk), lambda c, own: (0, c)),
                pl.BlockSpec(swap.shape, whole),
                pl.BlockSpec(perm.shape, whole),
            ],
            out_specs=[pl.BlockSpec((count, PAIR_SQ, chunk), lambda c, own: (0, 0, c))]
            + [pl.BlockSpec(packed_shape, whole)] * (count * vir_count),
        ),
        out_shape=[jax.ShapeDtypeStruct((count, PAIR_SQ, slab_cols), jnp.float32)]
        + [jax.ShapeDtypeStruct(packed_shape, jnp.int16)] * (count * vir_count),
        compiler_params=pltpu.CompilerParams(vmem_limit_bytes=VMEM_LIMIT),
        cost_estimate=pl.CostEstimate(flops=flops, bytes_accessed=bytes_accessed, transcendentals=0),
        name="ladder",
    )(own, amp_mask, numbers, *[amplitudes] * count, slab, swap, perm)


def update_kernel(vir_count, cut, own, vir_ref, occ_ref, spread_ref, ladder_ref, *refs):
    arrived, update_ref = refs[:vir_count], refs[-1]
    highs, lows = [], []
    for ref in arrived:
        codes = ref[cut * PAIR_SQ :, :].astype(jnp.int32).astype(jnp.float32)
        for c in range(cut):
            values = ref[c * PAIR_SQ : (c + 1) * PAIR_SQ, :].astype(jnp.int32).astype(jnp.float32)
            high, low = split(values * (scale_of(codes[c : c + 1]) * (1.0 / TOP)))
            highs.append(high)
            lows.append(low)
    mirror = dot(jnp.concatenate(highs, axis=1), spread_ref[...]) + dot(
        jnp.concatenate(lows, axis=1), spread_ref[...]
    )
    update_ref[...] = (ladder_ref[0] + mirror) / (vir_ref[...] - occ_ref[:, :1])


def update_call(tile_total, distance, n, cut, own, vir_sum, occ_sum, spread, ladder, arrived, earlier):
    slab_cols = spread.shape[1]
    args = [vir_sum, occ_sum, spread, ladder, *arrived]
    in_specs = [
        pl.BlockSpec((1, slab_cols), lambda g, own: (0, 0)),
        pl.BlockSpec((PAIR_SQ, 128), lambda g, own: (own[0] ^ distance, 0)),
        pl.BlockSpec(spread.shape, lambda g, own: (0, 0)),
        pl.BlockSpec((1, PAIR_SQ, slab_cols), lambda g, own: (n, 0, 0)),
    ] + [pl.BlockSpec(arrived[0].shape, lambda g, own: (0, 0))] * len(arrived)
    aliases = {}
    if earlier is not None:
        aliases = {len(args) + 1: 0}
        args.append(earlier)
        in_specs.append(pl.BlockSpec(memory_space=pl.ANY))
    return pl.pallas_call(
        functools.partial(update_kernel, len(arrived), cut),
        grid_spec=pltpu.PrefetchScalarGridSpec(
            num_scalar_prefetch=1,
            grid=(1,),
            in_specs=in_specs,
            out_specs=pl.BlockSpec((PAIR_SQ, slab_cols), lambda g, own: (own[0] ^ distance, 0)),
        ),
        out_shape=jax.ShapeDtypeStruct((tile_total * PAIR_SQ, slab_cols), jnp.float32),
        input_output_aliases=aliases,
        compiler_params=pltpu.CompilerParams(vmem_limit_bytes=VMEM_LIMIT),
        cost_estimate=pl.CostEstimate(
            flops=4 * PAIR_SQ * slab_cols * slab_cols, bytes_accessed=PAIR_SQ * slab_cols * 10, transcendentals=0
        ),
        name="update",
    )(own, *args)


def body(amplitudes, amp_mask, integrals, int_mask, group_orbital_numbers, occ_energy, vir_energy):
    tile_total = lax.axis_size("occ")
    vir_count = lax.axis_size("vir")
    row_tile = lax.axis_index("occ")
    vir_place = lax.axis_index("vir")
    vir_span = W // vir_count
    slab_cols = vir_span * W
    cut = 2 if vir_span >= 16 else 1
    chunk = slab_cols // cut
    chunk_span = vir_span // cut
    block = chunk // vir_count

    slab = lax.all_gather(screen_call(int_mask, integrals), "occ", axis=0, tiled=True)

    own = row_tile.astype(jnp.int32).reshape(1)
    rows = jnp.arange(PAIR_SQ)
    swap = one_hot_of(rows % ORBITALS_IN_GRP * ORBITALS_IN_GRP + rows // ORBITALS_IN_GRP, PAIR_SQ)
    col = jnp.arange(chunk)
    a, b = col // W, col % W
    perm = one_hot_of((b // vir_span ^ vir_place) * block + b % vir_span * chunk_span + a, chunk)
    place = jnp.arange(slab_cols)
    sender, part = place // (cut * block) ^ vir_place, place // block % cut
    here, there = place % block // chunk_span, place % chunk_span
    spread = one_hot_of(here * W + sender * vir_span + part * chunk_span + there, slab_cols)

    occ_table = occ_energy.reshape(tile_total, ORBITALS_IN_GRP)
    own_energy = lax.dynamic_slice_in_dim(occ_table, row_tile, 1, 0)[0]
    occ_sum = jnp.broadcast_to(
        (own_energy[None, :, None] + occ_table[:, None, :]).reshape(-1, 1), (tile_total * PAIR_SQ, 128)
    )
    vir_own = lax.dynamic_slice_in_dim(vir_energy, vir_place * vir_span, vir_span, 0)
    vir_sum = (vir_own[:, None] + vir_energy[None, :]).reshape(1, -1)

    devices = tile_total * vir_count
    first = tile_total // 2
    order = list(range(first, tile_total)) + list(range(2, first)) + [0, 1]
    parts = []
    for at in range(0, tile_total, AT_ONCE):
        distances = order[at : at + AT_ONCE]
        ladder, *packed = ladder_call(
            distances, vir_count, cut, own, amp_mask[0], group_orbital_numbers, amplitudes, slab, swap, perm
        )
        for n, distance in enumerate(distances):
            arrived = []
            for v in range(vir_count):
                shift = distance * vir_count + v
                block_sent = packed[n * vir_count + v]
                if shift > 0:
                    block_sent = lax.ppermute(block_sent, ("occ", "vir"), [(s, s ^ shift) for s in range(devices)])
                arrived.append(block_sent)
            parts.append((distance, n, ladder, arrived))
    update = None
    for distance, n, ladder, arrived in parts[first:] + parts[:first]:
        update = update_call(
            tile_total, distance, n, cut, own, vir_sum, occ_sum, spread, ladder, arrived, update
        )
    return update


def solution(mesh):
    in_specs = (P("occ", None), P("occ", None, None), P("occ", "vir"), P(), P(), P(), P())
    out_specs = P("occ", "vir")
    return jax.shard_map(body, mesh=mesh, in_specs=in_specs, out_specs=out_specs, check_vma=False)
```

```python
import functools

import jax
import jax.numpy as jnp
from jax import lax
from jax.experimental import pallas as pl
from jax.experimental.pallas import tpu as pltpu
from jax.sharding import PartitionSpec as P

VT = 32
NVT = 2
W = 64
ORBITALS_IN_GRP = 16
PAIR_SQ = ORBITALS_IN_GRP * ORBITALS_IN_GRP
CORES = 2
CODE_ROWS = 16
TOP = 32700.0
STEPS = 8.0
VMEM_LIMIT = 56 * 1024 * 1024


def one_hot_of(target, amount):
    return (target[:, None] == jnp.arange(amount)[None, :]).astype(jnp.bfloat16)


def split(values):
    high = values.astype(jnp.bfloat16)
    return high, (values - high.astype(jnp.float32)).astype(jnp.bfloat16)


def dot(left, right):
    return jnp.dot(left, right, preferred_element_type=jnp.float32)


def scale_of(code):
    return jnp.exp2(code * (1.0 / STEPS))


def screen_kernel(int_mask, slab_ref, *screened_refs):
    slab_rows, slab_cols = slab_ref.shape
    chunk = slab_cols // len(screened_refs)
    row_label = lax.axis_index("occ") * slab_rows // W // VT * NVT
    col_label = lax.axis_index("vir") * slab_cols // W // VT * NVT
    right = lax.broadcasted_iota(jnp.int32, (VT, chunk), 1) % W >= VT
    keep = []
    for d_tile in range(NVT):
        label = row_label + d_tile
        kept = jnp.where(right, int_mask[label, col_label + 1], int_mask[label, col_label])
        keep.append(kept.astype(jnp.float32).astype(jnp.bfloat16))
    for c, screened_ref in enumerate(screened_refs):
        for at in range(0, slab_rows, VT):
            screened_ref[at : at + VT, :] = (
                slab_ref[at : at + VT, c * chunk : (c + 1) * chunk] * keep[at // VT % NVT]
            )


def screen_call(chunks, int_mask, integrals):
    slab_rows, slab_cols = integrals.shape
    vmem = pl.BlockSpec(memory_space=pltpu.VMEM)
    return pl.pallas_call(
        screen_kernel,
        in_specs=[pl.BlockSpec(memory_space=pltpu.SMEM), vmem],
        out_specs=[vmem] * chunks,
        out_shape=[jax.ShapeDtypeStruct((slab_rows, slab_cols // chunks), integrals.dtype)] * chunks,
        name="screen",
    )(int_mask, integrals)


def line_gather(part, tile_total):
    chips = tile_total // CORES
    partner = lambda array: lax.ppermute(array, "occ", [(t, t ^ 1) for t in range(tile_total)])
    pieces = [(0, 0, False, part), (0, 0, True, partner(part))]
    travel = {1: part, -1: part}
    for step in range(1, chips):
        for sign in (1, -1):
            pairs = []
            for t in range(tile_total):
                chip = t // CORES
                if 0 <= chip + sign * step < chips:
                    pairs.append((t + sign * CORES, t))
            travel[sign] = lax.ppermute(travel[sign], "occ", pairs)
        for sign in (1, -1):
            holders = [t for t in range(tile_total) if 0 <= t // CORES + sign * step < chips]
            across = lax.ppermute(travel[sign], "occ", [(t, t ^ 1) for t in holders])
            pieces.append((sign, step, False, travel[sign]))
            pieces.append((sign, step, True, across))
    return pieces, travel


def fill_slab(layout, slab_rows, refs, slab_scr, sems):
    tile = lax.axis_index("occ")
    chips = lax.axis_size("occ") // CORES
    chip, core = tile // CORES, tile % CORES

    def each(act):
        for n, (sign, step, other) in enumerate(layout):
            at_chip = chip + sign * step

            @pl.when((at_chip >= 0) & (at_chip < chips))
            def _():
                place = at_chip * CORES + (1 - core if other else core)
                at = pl.ds(pl.multiple_of(place * slab_rows, slab_rows), slab_rows)
                act(pltpu.make_async_copy(refs[n], slab_scr.at[at, :], sems.at[n]))

    each(lambda copy: copy.start())
    each(lambda copy: copy.wait())


def ladder_kernel(vir_count, layout, amp_mask, numbers, rows_ref, swap_ref, perm_ref, *refs):
    pieces, (ladder_ref, packed_ref) = refs[: len(layout)], refs[len(layout) : len(layout) + 2]
    tile = pl.program_id(0)
    cols = perm_ref.shape[1]
    if len(layout) > 1:
        slab_ref, sems = refs[len(layout) + 2 :]

        @pl.when(tile == 0)
        def _():
            fill_slab(layout, pieces[0].shape[0], pieces, slab_ref, sems)
    else:
        slab_ref = pieces[0]

    lane = lax.broadcasted_iota(jnp.int32, (1, W * W), 1)
    low = lane < W * VT
    left = lane % W < VT
    keep = jnp.where(
        low,
        jnp.where(left, amp_mask[tile, 0], amp_mask[tile, 1]),
        jnp.where(left, amp_mask[tile, 2], amp_mask[tile, 3]),
    )
    screened = rows_ref[...] * keep.astype(jnp.float32).astype(jnp.bfloat16)
    ladder = dot(screened, slab_ref[...])
    pair = lax.broadcasted_iota(jnp.int32, (PAIR_SQ, 1), 0)
    own_number = numbers[lax.axis_index("occ")]
    nonzero = (pair // ORBITALS_IN_GRP < own_number) & (pair % ORBITALS_IN_GRP < numbers[tile])
    ladder = jnp.where(nonzero, ladder, 0.0)
    ladder_ref[...] = ladder
    high, low_part = split(ladder)
    mirror = dot(dot(swap_ref[...], high).astype(jnp.bfloat16), perm_ref[...]) + dot(
        dot(swap_ref[...], low_part).astype(jnp.bfloat16), perm_ref[...]
    )
    most = jnp.maximum(jnp.max(jnp.abs(mirror), axis=0, keepdims=True), 1e-30)
    code = jnp.ceil(jnp.log2(most) * STEPS)
    coded = jnp.round(mirror * (TOP / scale_of(code))).astype(jnp.int32).astype(jnp.int16)
    code_rows = jnp.broadcast_to(code.astype(jnp.int32), (CODE_ROWS, cols)).astype(jnp.int16)
    block = cols // vir_count
    for v in range(vir_count):
        packed_ref[0, v, :PAIR_SQ] = coded[:, v * block : (v + 1) * block]
        packed_ref[0, v, PAIR_SQ:] = code_rows[:, v * block : (v + 1) * block]


def ladder_call(tile_total, vir_count, layout, amp_mask, numbers, amplitudes, swap, perm, slab_parts):
    cols = perm.shape[1]
    block = cols // vir_count
    smem = pl.BlockSpec(memory_space=pltpu.SMEM)
    whole = lambda tile: (0, 0)
    rows = tile_total * PAIR_SQ
    if len(layout) > 1:
        slab_specs = [pl.BlockSpec(memory_space=pl.ANY)] * len(layout)
        scratch = [pltpu.VMEM((W * W, cols), jnp.bfloat16), pltpu.SemaphoreType.DMA((len(layout),))]
    else:
        slab_specs = [pl.BlockSpec((W * W, cols), whole)]
        scratch = []
    return pl.pallas_call(
        functools.partial(ladder_kernel, vir_count, layout),
        grid=(tile_total,),
        in_specs=[
            smem,
            smem,
            pl.BlockSpec((PAIR_SQ, W * W), lambda tile: (tile, 0)),
            pl.BlockSpec(swap.shape, whole),
            pl.BlockSpec(perm.shape, whole),
        ]
        + slab_specs,
        out_specs=[
            pl.BlockSpec((PAIR_SQ, cols), lambda tile: (tile, 0)),
            pl.BlockSpec((1, vir_count, PAIR_SQ + CODE_ROWS, block), lambda tile: (tile, 0, 0, 0)),
        ],
        out_shape=[
            jax.ShapeDtypeStruct((rows, cols), jnp.float32),
            jax.ShapeDtypeStruct((tile_total, vir_count, PAIR_SQ + CODE_ROWS, block), jnp.int16),
        ],
        scratch_shapes=scratch,
        compiler_params=pltpu.CompilerParams(vmem_limit_bytes=VMEM_LIMIT),
        cost_estimate=pl.CostEstimate(
            flops=2 * rows * cols * (W * W + 2 * PAIR_SQ + 2 * cols),
            bytes_accessed=rows * (W * W * 2 + cols * 6) + W * W * cols * 2,
            transcendentals=0,
        ),
        name="ladder",
    )(amp_mask, numbers, amplitudes, swap, perm, *slab_parts)


def mirror_of(vir_count, arrived_ref, spread_ref):
    highs, lows = [], []
    for v in range(vir_count):
        code = arrived_ref[0, v, PAIR_SQ:].astype(jnp.int32).astype(jnp.float32)[:1]
        values = arrived_ref[0, v, :PAIR_SQ].astype(jnp.int32).astype(jnp.float32)
        high, low = split(values * (scale_of(code) * (1.0 / TOP)))
        highs.append(high)
        lows.append(low)
    return dot(jnp.concatenate(highs, axis=1), spread_ref[...]) + dot(jnp.concatenate(lows, axis=1), spread_ref[...])


def add_kernel(vir_count, spread_ref, arrived_ref, *refs):
    ladders, total_ref = refs[:-1], refs[-1]
    mirror = mirror_of(vir_count, arrived_ref, spread_ref)
    cols = ladders[0].shape[1]
    for c, ladder_ref in enumerate(ladders):
        at = slice(c * cols, (c + 1) * cols)
        total_ref[:, at] = ladder_ref[...] + mirror[:, at]


def update_kernel(vir_count, spread_ref, arrived_ref, vir_ref, occ_ref, *refs):
    totals, update_ref = refs[:-1], refs[-1]
    mirror = mirror_of(vir_count, arrived_ref, spread_ref)
    cols = totals[0].shape[1]
    for c, total_ref in enumerate(totals):
        at = slice(c * cols, (c + 1) * cols)
        denominator = vir_ref[:, at] - occ_ref[:, :1]
        update_ref[:, at] = (total_ref[...] + mirror[:, at]) / denominator


def mirror_call(kernel, name, tile_total, spread, arrived, energies, totals):
    slab_cols = spread.shape[1]
    rows = tile_total * PAIR_SQ
    by_tile = lambda tile: (tile, 0)
    energy_specs = [pl.BlockSpec((1, slab_cols), lambda tile: (0, 0)), pl.BlockSpec((PAIR_SQ, 128), by_tile)]
    return pl.pallas_call(
        functools.partial(kernel, arrived.shape[1]),
        grid=(tile_total,),
        in_specs=[
            pl.BlockSpec(spread.shape, lambda tile: (0, 0)),
            pl.BlockSpec((1,) + arrived.shape[1:], lambda tile: (tile, 0, 0, 0)),
        ]
        + energy_specs[: len(energies)]
        + [pl.BlockSpec((PAIR_SQ, total.shape[1]), by_tile) for total in totals],
        out_specs=pl.BlockSpec((PAIR_SQ, slab_cols), by_tile),
        out_shape=jax.ShapeDtypeStruct((rows, slab_cols), jnp.float32),
        compiler_params=pltpu.CompilerParams(vmem_limit_bytes=VMEM_LIMIT),
        cost_estimate=pl.CostEstimate(
            flops=4 * rows * spread.shape[0] * slab_cols, bytes_accessed=rows * slab_cols * 9, transcendentals=0
        ),
        name=name,
    )(spread, arrived, *energies, *totals)


def body(amplitudes, amp_mask, integrals, int_mask, group_orbital_numbers, occ_energy, vir_energy):
    tile_total = lax.axis_size("occ")
    vir_count = lax.axis_size("vir")
    row_tile = lax.axis_index("occ")
    vir_place = lax.axis_index("vir")
    vir_span = W // vir_count
    slab_cols = vir_span * W
    chunks = 2 if vir_span >= 16 else 1
    chunk_cols = slab_cols // chunks
    chunk_span = vir_span // chunks
    block = chunk_cols // vir_count

    screened = screen_call(chunks, int_mask, integrals)
    pieces, last = line_gather(screened[0], tile_total)
    slabs = [([piece[:3] for piece in pieces], [piece[3] for piece in pieces])]
    if chunks > 1:
        later, _, _ = lax.optimization_barrier((screened[1], last[1], last[-1]))
        slabs.append(([(0, 0, False)], [lax.all_gather(later, "occ", axis=0, tiled=True)]))

    pair = jnp.arange(PAIR_SQ)
    swap = one_hot_of(pair % ORBITALS_IN_GRP * ORBITALS_IN_GRP + pair // ORBITALS_IN_GRP, PAIR_SQ)
    col = jnp.arange(chunk_cols)
    a, b = col // W, col % W
    perm = one_hot_of(b // vir_span * block + b % vir_span * chunk_span + a, chunk_cols)
    place = jnp.arange(chunk_cols)
    sender, here, there = place // block, place % block // chunk_span, place % chunk_span
    to_column = here * W + sender * vir_span + there

    occ_table = occ_energy.reshape(tile_total, ORBITALS_IN_GRP)
    own_energy = lax.dynamic_slice_in_dim(occ_table, row_tile, 1, 0)[0]
    occ_sum = jnp.broadcast_to(
        (own_energy[None, :, None] + occ_table[:, None, :]).reshape(-1, 1), (tile_total * PAIR_SQ, 128)
    )
    vir_own = lax.dynamic_slice_in_dim(vir_energy, vir_place * vir_span, vir_span, 0)
    vir_sum = (vir_own[:, None] + vir_energy[None, :]).reshape(1, -1)

    ladders, arrived = [], []
    for layout, slab_parts in slabs:
        ladder, packed = ladder_call(
            tile_total, vir_count, layout, amp_mask[0], group_orbital_numbers, amplitudes, swap, perm, slab_parts
        )
        rows = PAIR_SQ + CODE_ROWS
        moved = lax.all_to_all(
            packed.reshape(tile_total * vir_count, rows, block), ("occ", "vir"), split_axis=0, concat_axis=0, tiled=True
        )
        ladders.append(ladder)
        arrived.append(moved.reshape(tile_total, vir_count, rows, block))
    spreads = [one_hot_of(to_column + c * chunk_span, slab_cols) for c in range(chunks)]
    totals = ladders
    for c in range(chunks - 1):
        totals = [mirror_call(add_kernel, "add", tile_total, spreads[c], arrived[c], [], totals)]
    return mirror_call(
        update_kernel, "update", tile_total, spreads[-1], arrived[-1], [vir_sum, occ_sum], totals
    )


def solution(mesh):
    in_specs = (P("occ", None), P("occ", None, None), P("occ", "vir"), P(), P(), P(), P())
    out_specs = P("occ", "vir")
    return jax.shard_map(body, mesh=mesh, in_specs=in_specs, out_specs=out_specs, check_vma=False)
```

```python
import functools

import jax
import jax.numpy as jnp
from jax import lax
from jax.experimental import pallas as pl
from jax.experimental.pallas import tpu as pltpu
from jax.sharding import PartitionSpec as P

VT = 32
NVT = 2
W = 64
ORBITALS_IN_GRP = 16
PAIR_SQ = ORBITALS_IN_GRP * ORBITALS_IN_GRP
CORES = 2
CODE_ROWS = 16
TOP = 32700.0
STEPS = 8.0
VMEM_LIMIT = 56 * 1024 * 1024


def one_hot_of(target, amount):
    return (target[:, None] == jnp.arange(amount)[None, :]).astype(jnp.bfloat16)


def split(values):
    high = values.astype(jnp.bfloat16)
    return high, (values - high.astype(jnp.float32)).astype(jnp.bfloat16)


def dot(left, right):
    return jnp.dot(left, right, preferred_element_type=jnp.float32)


def scale_of(code):
    return jnp.exp2(code * (1.0 / STEPS))


def screen_kernel(int_mask, slab_ref, *screened_refs):
    slab_rows, slab_cols = slab_ref.shape
    chunk = slab_cols // len(screened_refs)
    row_label = lax.axis_index("occ") * slab_rows // W // VT * NVT
    col_label = lax.axis_index("vir") * slab_cols // W // VT * NVT
    right = lax.broadcasted_iota(jnp.int32, (VT, chunk), 1) % W >= VT
    keep = []
    for d_tile in range(NVT):
        label = row_label + d_tile
        kept = jnp.where(right, int_mask[label, col_label + 1], int_mask[label, col_label])
        keep.append(kept.astype(jnp.float32).astype(jnp.bfloat16))
    for c, screened_ref in enumerate(screened_refs):
        for at in range(0, slab_rows, VT):
            screened_ref[at : at + VT, :] = (
                slab_ref[at : at + VT, c * chunk : (c + 1) * chunk] * keep[at // VT % NVT]
            )


def screen_call(chunks, int_mask, integrals):
    slab_rows, slab_cols = integrals.shape
    vmem = pl.BlockSpec(memory_space=pltpu.VMEM)
    return pl.pallas_call(
        screen_kernel,
        in_specs=[pl.BlockSpec(memory_space=pltpu.SMEM), vmem],
        out_specs=[vmem] * chunks,
        out_shape=[jax.ShapeDtypeStruct((slab_rows, slab_cols // chunks), integrals.dtype)] * chunks,
        name="screen",
    )(int_mask, integrals)


def line_gather(part, tile_total):
    chips = tile_total // CORES
    partner = lambda array: lax.ppermute(array, "occ", [(t, t ^ 1) for t in range(tile_total)])
    across = partner(part)
    pieces = [(0, 0, False, part), (0, 0, True, across)]
    travel = {1: part, -1: part}
    crossed = [across]
    reached = []
    for step in range(1, chips):
        for sign in (1, -1):
            pairs = []
            for t in range(tile_total):
                chip = t // CORES
                if 0 <= chip + sign * step < chips:
                    pairs.append((t + sign * CORES, t))
            travel[sign] = lax.ppermute(travel[sign], "occ", pairs)
        reached.append(tuple(travel.values()))
        latest = []
        for sign in (1, -1):
            holders = [t for t in range(tile_total) if 0 <= t // CORES + sign * step < chips]
            across = lax.ppermute(travel[sign], "occ", [(t, t ^ 1) for t in holders])
            pieces.append((sign, step, False, travel[sign]))
            pieces.append((sign, step, True, across))
            latest.append(across)
        travel[1], travel[-1], *_ = lax.optimization_barrier((travel[1], travel[-1], *crossed))
        crossed = latest
    return pieces, reached


def fill_slab(layout, slab_rows, refs, slab_scr, sems):
    tile = lax.axis_index("occ")
    chips = lax.axis_size("occ") // CORES
    chip, core = tile // CORES, tile % CORES

    def each(act):
        for n, (sign, step, other) in enumerate(layout):
            at_chip = chip + sign * step

            @pl.when((at_chip >= 0) & (at_chip < chips))
            def _():
                place = at_chip * CORES + (1 - core if other else core)
                at = pl.ds(pl.multiple_of(place * slab_rows, slab_rows), slab_rows)
                act(pltpu.make_async_copy(refs[n], slab_scr.at[at, :], sems.at[n]))

    each(lambda copy: copy.start())
    each(lambda copy: copy.wait())


def ladder_kernel(vir_count, layout, amp_mask, numbers, rows_ref, perm_ref, *refs):
    pieces, (ladder_ref, packed_ref) = refs[: len(layout)], refs[len(layout) : len(layout) + 2]
    tile = pl.program_id(0)
    cols = perm_ref.shape[1]
    if len(layout) > 1:
        slab_ref, sems = refs[len(layout) + 2 :]

        @pl.when(tile == 0)
        def _():
            fill_slab(layout, pieces[0].shape[0], pieces, slab_ref, sems)
    else:
        slab_ref = pieces[0]

    lane = lax.broadcasted_iota(jnp.int32, (1, W * W), 1)
    low = lane < W * VT
    left = lane % W < VT
    keep = jnp.where(
        low,
        jnp.where(left, amp_mask[tile, 0], amp_mask[tile, 1]),
        jnp.where(left, amp_mask[tile, 2], amp_mask[tile, 3]),
    )
    screened = rows_ref[...] * keep.astype(jnp.float32).astype(jnp.bfloat16)
    ladder = dot(screened, slab_ref[...])
    pair = lax.broadcasted_iota(jnp.int32, (PAIR_SQ, 1), 0)
    own_number = numbers[lax.axis_index("occ")]
    nonzero = (pair // ORBITALS_IN_GRP < own_number) & (pair % ORBITALS_IN_GRP < numbers[tile])
    ladder = jnp.where(nonzero, ladder, 0.0)
    ladder_ref[...] = ladder
    by_place = ladder.reshape(ORBITALS_IN_GRP, ORBITALS_IN_GRP, cols)
    high, low_part = split(jnp.swapaxes(by_place, 0, 1).reshape(PAIR_SQ, cols))
    mirror = dot(high, perm_ref[...]) + dot(low_part, perm_ref[...])
    most = jnp.maximum(jnp.max(jnp.abs(mirror), axis=0, keepdims=True), 1e-30)
    code = jnp.ceil(jnp.log2(most) * STEPS)
    coded = jnp.round(mirror * (TOP / scale_of(code))).astype(jnp.int32).astype(jnp.int16)
    code_rows = jnp.broadcast_to(code.astype(jnp.int32), (CODE_ROWS, cols)).astype(jnp.int16)
    block = cols // vir_count
    for v in range(vir_count):
        packed_ref[0, v, :PAIR_SQ] = coded[:, v * block : (v + 1) * block]
        packed_ref[0, v, PAIR_SQ:] = code_rows[:, v * block : (v + 1) * block]


def ladder_call(tile_total, vir_count, layout, amp_mask, numbers, amplitudes, perm, slab_parts):
    cols = perm.shape[1]
    block = cols // vir_count
    smem = pl.BlockSpec(memory_space=pltpu.SMEM)
    whole = lambda tile: (0, 0)
    rows = tile_total * PAIR_SQ
    if len(layout) > 1:
        slab_specs = [pl.BlockSpec(memory_space=pl.ANY)] * len(layout)
        scratch = [pltpu.VMEM((W * W, cols), jnp.bfloat16), pltpu.SemaphoreType.DMA((len(layout),))]
    else:
        slab_specs = [pl.BlockSpec((W * W, cols), whole)]
        scratch = []
    return pl.pallas_call(
        functools.partial(ladder_kernel, vir_count, layout),
        grid=(tile_total,),
        in_specs=[
            smem,
            smem,
            pl.BlockSpec((PAIR_SQ, W * W), lambda tile: (tile, 0)),
            pl.BlockSpec(perm.shape, whole),
        ]
        + slab_specs,
        out_specs=[
            pl.BlockSpec((PAIR_SQ, cols), lambda tile: (tile, 0)),
            pl.BlockSpec((1, vir_count, PAIR_SQ + CODE_ROWS, block), lambda tile: (tile, 0, 0, 0)),
        ],
        out_shape=[
            jax.ShapeDtypeStruct((rows, cols), jnp.float32),
            jax.ShapeDtypeStruct((tile_total, vir_count, PAIR_SQ + CODE_ROWS, block), jnp.int16),
        ],
        scratch_shapes=scratch,
        compiler_params=pltpu.CompilerParams(vmem_limit_bytes=VMEM_LIMIT),
        cost_estimate=pl.CostEstimate(
            flops=2 * rows * cols * (W * W + 2 * cols),
            bytes_accessed=rows * (W * W * 2 + cols * 6) + W * W * cols * 2,
            transcendentals=0,
        ),
        name="ladder",
    )(amp_mask, numbers, amplitudes, perm, *slab_parts)


def decoded(vir_count, arrived_ref):
    highs, lows = [], []
    for v in range(vir_count):
        code = arrived_ref[0, v, PAIR_SQ:].astype(jnp.int32).astype(jnp.float32)[:1]
        values = arrived_ref[0, v, :PAIR_SQ].astype(jnp.int32).astype(jnp.float32)
        high, low = split(values * (scale_of(code) * (1.0 / TOP)))
        highs.append(high)
        lows.append(low)
    return highs, lows


def mirror_halves(vir_count, halves, spread_ref, arrived_ref, totals):
    parts = decoded(vir_count, arrived_ref)
    lanes = parts[0][0].shape[1] // halves
    cols = spread_ref.shape[1]
    for h in range(halves):
        high, low = [
            jnp.concatenate([block[:, h * lanes : (h + 1) * lanes] for block in blocks], axis=1) for blocks in parts
        ]
        mirror = dot(high, spread_ref[...]) + dot(low, spread_ref[...])
        at = slice(h * cols, (h + 1) * cols)
        total = totals[h][...] if len(totals) == halves else totals[0][:, at]
        yield at, total + mirror


def add_kernel(vir_count, halves, spread_ref, arrived_ref, *refs):
    for at, total in mirror_halves(vir_count, halves, spread_ref, arrived_ref, refs[:-1]):
        refs[-1][:, at] = total


def update_kernel(vir_count, halves, spread_ref, arrived_ref, vir_ref, occ_ref, *refs):
    for at, total in mirror_halves(vir_count, halves, spread_ref, arrived_ref, refs[:-1]):
        refs[-1][:, at] = total / (vir_ref[:, at] - occ_ref[:, :1])


def mirror_call(kernel, name, tile_total, halves, spread, arrived, energies, totals):
    slab_cols = spread.shape[1] * halves
    rows = tile_total * PAIR_SQ
    by_tile = lambda tile: (tile, 0)
    energy_specs = [pl.BlockSpec((1, slab_cols), lambda tile: (0, 0)), pl.BlockSpec((PAIR_SQ, 128), by_tile)]
    return pl.pallas_call(
        functools.partial(kernel, arrived.shape[1], halves),
        grid=(tile_total,),
        in_specs=[
            pl.BlockSpec(spread.shape, lambda tile: (0, 0)),
            pl.BlockSpec((1,) + arrived.shape[1:], lambda tile: (tile, 0, 0, 0)),
        ]
        + energy_specs[: len(energies)]
        + [pl.BlockSpec((PAIR_SQ, total.shape[1]), by_tile) for total in totals],
        out_specs=pl.BlockSpec((PAIR_SQ, slab_cols), by_tile),
        out_shape=jax.ShapeDtypeStruct((rows, slab_cols), jnp.float32),
        compiler_params=pltpu.CompilerParams(vmem_limit_bytes=VMEM_LIMIT),
        cost_estimate=pl.CostEstimate(
            flops=4 * rows * spread.shape[0] * slab_cols, bytes_accessed=rows * slab_cols * 9, transcendentals=0
        ),
        name=name,
    )(spread, arrived, *energies, *totals)


def body(amplitudes, amp_mask, integrals, int_mask, group_orbital_numbers, occ_energy, vir_energy):
    tile_total = lax.axis_size("occ")
    vir_count = lax.axis_size("vir")
    row_tile = lax.axis_index("occ")
    vir_place = lax.axis_index("vir")
    vir_span = W // vir_count
    slab_cols = vir_span * W
    chunks = 2 if vir_span >= 16 else 1
    chunk_cols = slab_cols // chunks
    chunk_span = vir_span // chunks
    block = chunk_cols // vir_count

    screened = screen_call(chunks, int_mask, integrals)
    pieces, reached = line_gather(screened[0], tile_total)
    slabs = [([piece[:3] for piece in pieces], [piece[3] for piece in pieces])]
    if chunks > 1:
        later, *_ = lax.optimization_barrier((screened[1], *reached[-2]) if len(reached) > 1 else (screened[1],))
        slabs.append(([(0, 0, False)], [lax.all_gather(later, "occ", axis=0, tiled=True)]))

    col = jnp.arange(chunk_cols)
    a, b = col // W, col % W
    perm = one_hot_of(b // vir_span * block + b % vir_span * chunk_span + a, chunk_cols)
    halves = chunks
    lanes = block // halves
    place = jnp.arange(vir_count * lanes)
    sender, here, there = place // lanes, place % lanes // chunk_span, place % chunk_span
    to_column = here * W + sender * vir_span + there

    occ_table = occ_energy.reshape(tile_total, ORBITALS_IN_GRP)
    own_energy = lax.dynamic_slice_in_dim(occ_table, row_tile, 1, 0)[0]
    occ_sum = jnp.broadcast_to(
        (own_energy[None, :, None] + occ_table[:, None, :]).reshape(-1, 1), (tile_total * PAIR_SQ, 128)
    )
    vir_own = lax.dynamic_slice_in_dim(vir_energy, vir_place * vir_span, vir_span, 0)
    vir_sum = (vir_own[:, None] + vir_energy[None, :]).reshape(1, -1)

    ladders, arrived = [], []
    for layout, slab_parts in slabs:
        ladder, packed = ladder_call(
            tile_total, vir_count, layout, amp_mask[0], group_orbital_numbers, amplitudes, perm, slab_parts
        )
        rows = PAIR_SQ + CODE_ROWS
        moved = lax.all_to_all(
            packed.reshape(tile_total * vir_count, rows, block), ("occ", "vir"), split_axis=0, concat_axis=0, tiled=True
        )
        ladders.append(ladder)
        arrived.append(moved.reshape(tile_total, vir_count, rows, block))
    spreads = [one_hot_of(to_column + c * chunk_span, slab_cols // halves) for c in range(chunks)]
    totals = ladders
    for c in range(chunks - 1):
        totals = [mirror_call(add_kernel, "add", tile_total, halves, spreads[c], arrived[c], [], totals)]
    return mirror_call(
        update_kernel, "update", tile_total, halves, spreads[-1], arrived[-1], [vir_sum, occ_sum], totals
    )


def solution(mesh):
    in_specs = (P("occ", None), P("occ", None, None), P("occ", "vir"), P(), P(), P(), P())
    out_specs = P("occ", "vir")
    return jax.shard_map(body, mesh=mesh, in_specs=in_specs, out_specs=out_specs, check_vma=False)
```

```python
import functools

import jax
import jax.numpy as jnp
from jax import lax
from jax.experimental import pallas as pl
from jax.experimental.pallas import tpu as pltpu
from jax.sharding import PartitionSpec as P

VT = 32
NVT = 2
W = 64
ORBITALS_IN_GRP = 16
PAIR_SQ = ORBITALS_IN_GRP * ORBITALS_IN_GRP
CORES = 2
CODE_ROWS = 16
TOP = 32700.0
STEPS = 8.0
VMEM_LIMIT = 56 * 1024 * 1024


def one_hot_of(target, amount):
    return (target[:, None] == jnp.arange(amount)[None, :]).astype(jnp.bfloat16)


def split(values):
    high = values.astype(jnp.bfloat16)
    return high, (values - high.astype(jnp.float32)).astype(jnp.bfloat16)


def dot(left, right):
    return jnp.dot(left, right, preferred_element_type=jnp.float32)


def scale_of(code):
    return jnp.exp2(code * (1.0 / STEPS))


def screen_kernel(chunk, part, int_mask, slab_ref, screened_ref):
    slab_rows, slab_cols = slab_ref.shape
    cols = screened_ref.shape[1]
    span = slab_cols // W
    row_label = lax.axis_index("occ") * slab_rows // W // VT * NVT
    col_label = lax.axis_index("vir") * slab_cols // W // VT * NVT
    natural = lax.broadcasted_iota(jnp.int32, (slab_cols, 1), 0)
    a, b = natural // W, natural % W
    target = b // span * (part * span) + (a // part * part + b % part) * part + a % part
    target = jnp.where(b % span // part == chunk, target, -1)
    place = lax.broadcasted_iota(jnp.int32, (slab_cols, cols), 1)
    moved = dot(slab_ref[...], (place == target).astype(jnp.float32).astype(jnp.bfloat16)).astype(jnp.bfloat16)
    to = lax.broadcasted_iota(jnp.int32, (VT, cols), 1)
    owner, of_part = to // (part * span), to // part % part
    right = owner * span + chunk * part + of_part >= VT
    for d_tile in range(NVT):
        label = row_label + d_tile
        kept = jnp.where(right, int_mask[label, col_label + 1], int_mask[label, col_label])
        kept = kept.astype(jnp.float32).astype(jnp.bfloat16)
        for at in range(d_tile * VT, slab_rows, NVT * VT):
            screened_ref[at : at + VT, :] = moved[at : at + VT, :] * kept


def screen_call(chunk, chunks, int_mask, integrals):
    slab_rows, slab_cols = integrals.shape
    vmem = pl.BlockSpec(memory_space=pltpu.VMEM)
    return pl.pallas_call(
        functools.partial(screen_kernel, chunk, slab_cols // W // chunks),
        in_specs=[pl.BlockSpec(memory_space=pltpu.SMEM), vmem],
        out_specs=vmem,
        out_shape=jax.ShapeDtypeStruct((slab_rows, slab_cols // chunks), integrals.dtype),
        compiler_params=pltpu.CompilerParams(vmem_limit_bytes=VMEM_LIMIT),
        name="screen",
    )(int_mask, integrals)


def line_step(travel, step, tile_total):
    chips = tile_total // CORES
    arrived = {}
    for sign in (1, -1):
        pairs = [(t + sign * CORES, t) for t in range(tile_total) if 0 <= t // CORES + sign * step < chips]
        arrived[sign] = lax.ppermute(travel[sign], "occ", pairs)
    return arrived


def across(travel, step, tile_total):
    chips = tile_total // CORES
    pieces = []
    for sign in (1, -1) if step else (1,):
        pairs = [(t, t ^ 1) for t in range(tile_total) if 0 <= t // CORES + sign * step < chips]
        pieces.append((sign, step, False, travel[sign]))
        pieces.append((sign, step, True, lax.ppermute(travel[sign], "occ", pairs)))
    return pieces


def fill_slab(layout, refs, slab_scr, sems):
    tile = lax.axis_index("occ")
    chips = lax.axis_size("occ") // CORES
    chip, core = tile // CORES, tile % CORES
    slab_rows = refs[0].shape[0]

    def each(act):
        for n, (sign, step, other) in enumerate(layout):
            at_chip = chip + sign * step

            @pl.when((at_chip >= 0) & (at_chip < chips))
            def _():
                place = at_chip * CORES + (1 - core if other else core)
                at = pl.ds(pl.multiple_of(place * slab_rows, slab_rows), slab_rows)
                act(pltpu.make_async_copy(refs[n], slab_scr.at[at, :], sems.at[n]))

    each(lambda copy: copy.start())
    each(lambda copy: copy.wait())


def ladder_kernel(first, vir_count, chunks, layout, amp_mask, numbers, rows_ref, *refs):
    pieces, refs = refs[: len(layout)], refs[len(layout) :]
    if first:
        refs = refs[2:]
    ladder_ref, packed_ref, refs = refs[0], refs[1], refs[2:]
    tile = pl.program_id(0) + first
    if len(layout) > 1:
        slab_ref, sems = refs

        @pl.when(pl.program_id(0) == 0)
        def _():
            fill_slab(layout, pieces, slab_ref, sems)
    else:
        slab_ref = pieces[0]
    cols = slab_ref.shape[1]
    lane = lax.broadcasted_iota(jnp.int32, (1, W * W), 1)
    low = lane < W * VT
    left = lane % W < VT
    keep = jnp.where(
        low,
        jnp.where(left, amp_mask[tile, 0], amp_mask[tile, 1]),
        jnp.where(left, amp_mask[tile, 2], amp_mask[tile, 3]),
    )
    screened = rows_ref[...] * keep.astype(jnp.float32).astype(jnp.bfloat16)
    ladder = dot(screened, slab_ref[...])
    pair = lax.broadcasted_iota(jnp.int32, (PAIR_SQ, 1), 0)
    own_number = numbers[lax.axis_index("occ")]
    nonzero = (pair // ORBITALS_IN_GRP < own_number) & (pair % ORBITALS_IN_GRP < numbers[tile])
    ladder = jnp.where(nonzero, ladder, 0.0)
    block = cols // vir_count
    lanes = block // chunks
    for h in range(chunks):
        ladder_ref[h] = jnp.concatenate(
            [ladder[:, v * block + h * lanes : v * block + (h + 1) * lanes] for v in range(vir_count)], axis=1
        )
    by_place = ladder.reshape(ORBITALS_IN_GRP, ORBITALS_IN_GRP, cols)
    mirror = jnp.swapaxes(by_place, 0, 1).reshape(PAIR_SQ, cols)
    most = jnp.maximum(jnp.max(jnp.abs(ladder), axis=0, keepdims=True), 1e-30)
    code = jnp.ceil(jnp.log2(most) * STEPS)
    coded = jnp.round(mirror * (TOP / scale_of(code))).astype(jnp.int32).astype(jnp.int16)
    code_rows = jnp.broadcast_to(code.astype(jnp.int32), (CODE_ROWS, cols)).astype(jnp.int16)
    for v in range(vir_count):
        packed_ref[0, v, :PAIR_SQ] = coded[:, v * block : (v + 1) * block]
        packed_ref[0, v, PAIR_SQ:] = code_rows[:, v * block : (v + 1) * block]


def ladder_call(tiles, tile_total, vir_count, chunks, layout, amp_mask, numbers, amplitudes, slab_parts, earlier):
    first, last = tiles
    cols = slab_parts[0].shape[1]
    block = cols // vir_count
    smem = pl.BlockSpec(memory_space=pltpu.SMEM)
    somewhere = pl.BlockSpec(memory_space=pl.ANY)
    rows = (last - first) * PAIR_SQ
    if len(layout) > 1:
        slab_specs = [somewhere] * len(layout)
        scratch = [pltpu.VMEM((W * W, cols), jnp.bfloat16), pltpu.SemaphoreType.DMA((len(layout),))]
    else:
        slab_specs = [pl.BlockSpec((W * W, cols), lambda tile: (0, 0))]
        scratch = []
    args = [amp_mask, numbers, amplitudes, *slab_parts]
    aliases = {len(args): 0, len(args) + 1: 1} if first else {}
    return pl.pallas_call(
        functools.partial(ladder_kernel, first, vir_count, chunks, layout),
        grid=(last - first,),
        in_specs=[smem, smem, pl.BlockSpec((PAIR_SQ, W * W), lambda tile: (tile + first, 0))]
        + slab_specs
        + [somewhere] * len(aliases),
        out_specs=[
            pl.BlockSpec((chunks, PAIR_SQ, cols // chunks), lambda tile: (0, tile + first, 0)),
            pl.BlockSpec((1, vir_count, PAIR_SQ + CODE_ROWS, block), lambda tile: (tile + first, 0, 0, 0)),
        ],
        out_shape=[
            jax.ShapeDtypeStruct((chunks, tile_total * PAIR_SQ, cols // chunks), jnp.float32),
            jax.ShapeDtypeStruct((tile_total, vir_count, PAIR_SQ + CODE_ROWS, block), jnp.int16),
        ],
        scratch_shapes=scratch,
        input_output_aliases=aliases,
        compiler_params=pltpu.CompilerParams(vmem_limit_bytes=VMEM_LIMIT),
        cost_estimate=pl.CostEstimate(
            flops=2 * rows * cols * W * W,
            bytes_accessed=rows * (W * W * 2 + cols * 6) + W * W * cols * 2,
            transcendentals=0,
        ),
        name="ladder",
    )(*args, *(earlier if first else []))


def update_kernel(chunks, vir_count, arrived_ref, spread_ref, vir_ref, occ_ref, *refs):
    ladders, update_ref = refs[:chunks], refs[-1]
    highs, lows = [], []

    def take(values):
        high, low = split(values)
        highs.append(high)
        lows.append(low)

    for v in range(vir_count):
        code = arrived_ref[0, v, PAIR_SQ:].astype(jnp.int32).astype(jnp.float32)[:1]
        values = arrived_ref[0, v, :PAIR_SQ].astype(jnp.int32).astype(jnp.float32)
        take(values * (scale_of(code) * (1.0 / TOP)))
    for ladder_ref in ladders:
        take(ladder_ref[0])
    total = dot(jnp.concatenate(highs, axis=1), spread_ref[...]) + dot(jnp.concatenate(lows, axis=1), spread_ref[...])
    update_ref[...] = total / (vir_ref[...] - occ_ref[:, :1])


def update_call(chunk, tile_total, arrived, spread, vir_sum, occ_sum, ladders, earlier):
    chunks = len(ladders)
    cols = spread.shape[1]
    rows = tile_total * PAIR_SQ
    args = [arrived, spread, vir_sum, occ_sum, *ladders]
    in_specs = [
        pl.BlockSpec((1,) + arrived.shape[1:], lambda tile: (tile, 0, 0, 0)),
        pl.BlockSpec(spread.shape, lambda tile: (0, 0)),
        pl.BlockSpec((1, cols), lambda tile: (0, chunk)),
        pl.BlockSpec((PAIR_SQ, 128), lambda tile: (tile, 0)),
    ] + [pl.BlockSpec((1, PAIR_SQ, ladder.shape[2]), lambda tile: (chunk, tile, 0)) for ladder in ladders]
    aliases = {}
    if earlier is not None:
        aliases = {len(args): 0}
        args.append(earlier)
        in_specs.append(pl.BlockSpec(memory_space=pl.ANY))
    return pl.pallas_call(
        functools.partial(update_kernel, chunks, arrived.shape[1]),
        grid=(tile_total,),
        in_specs=in_specs,
        out_specs=pl.BlockSpec((PAIR_SQ, cols), lambda tile: (tile, chunk)),
        out_shape=jax.ShapeDtypeStruct((rows, chunks * cols), jnp.float32),
        input_output_aliases=aliases,
        compiler_params=pltpu.CompilerParams(vmem_limit_bytes=VMEM_LIMIT),
        cost_estimate=pl.CostEstimate(
            flops=4 * rows * spread.shape[0] * cols, bytes_accessed=rows * cols * 10, transcendentals=0
        ),
        name="update",
    )(*args)


def body(amplitudes, amp_mask, integrals, int_mask, group_orbital_numbers, occ_energy, vir_energy):
    tile_total = lax.axis_size("occ")
    vir_count = lax.axis_size("vir")
    row_tile = lax.axis_index("occ")
    vir_place = lax.axis_index("vir")
    span = W // vir_count
    slab_cols = span * W
    chunks = 2 if span >= 16 else 1
    part = span // chunks
    block = part * span
    rows = PAIR_SQ + CODE_ROWS
    barrier = lax.optimization_barrier

    def ladder_of(tiles, layout, slab_parts, earlier=None):
        return ladder_call(
            tiles, tile_total, vir_count, chunks, layout, amp_mask[0], group_orbital_numbers, amplitudes,
            slab_parts, earlier,
        )

    def exchanged(packed):
        moved = lax.all_to_all(
            packed.reshape(tile_total * vir_count, rows, block), ("occ", "vir"), split_axis=0, concat_axis=0, tiled=True
        )
        return moved.reshape(tile_total, vir_count, rows, block)

    if chunks > 1:
        ring_part = screen_call(1, chunks, int_mask, integrals)
        ring_part, integrals = barrier((ring_part, integrals))
        travel = {1: ring_part, -1: ring_part}
        pieces = across(travel, 0, tile_total)
        steps = tile_total // CORES - 1
        for step in range(1, steps):
            travel = line_step(travel, step, tile_total)
            pieces += across(travel, step, tile_total)
    slab = lax.all_gather(screen_call(0, chunks, int_mask, integrals), "occ", axis=0, tiled=True)
    whole = [(0, 0, False)]
    half = tile_total // 2
    results = list(ladder_of((0, half), whole, [slab]))
    if chunks > 1 and steps > 0:
        travel[1], travel[-1], results[1] = barrier((travel[1], travel[-1], results[1]))
        travel = line_step(travel, steps, tile_total)
        pieces += across(travel, steps, tile_total)
    results = [ladder_of((half, tile_total), whole, [slab], results)]
    arrived = [exchanged(results[0][1])]
    if chunks > 1:
        results.append(ladder_of((0, tile_total), [piece[:3] for piece in pieces], [piece[3] for piece in pieces]))
        arrived.append(exchanged(results[1][1]))
    ladders = [result[0] for result in results]

    place = jnp.arange(vir_count * block)
    owner, there_part = place // block, place // (part * part) % chunks
    here, there = place // part % part, place % part
    mirror_to = here * W + owner * span + there_part * part + there
    place = jnp.arange(vir_count * part * part)
    owner, b, a = place // (part * part), place // part % part, place % part
    direct_to = [a * W + owner * span + c * part + b for c in range(chunks)]
    spread = one_hot_of(jnp.concatenate([mirror_to, *direct_to]), part * W)

    occ_table = occ_energy.reshape(tile_total, ORBITALS_IN_GRP)
    own_energy = lax.dynamic_slice_in_dim(occ_table, row_tile, 1, 0)[0]
    occ_sum = jnp.broadcast_to(
        (own_energy[None, :, None] + occ_table[:, None, :]).reshape(-1, 1), (tile_total * PAIR_SQ, 128)
    )
    vir_own = lax.dynamic_slice_in_dim(vir_energy, vir_place * span, span, 0)
    vir_sum = (vir_own[:, None] + vir_energy[None, :]).reshape(1, -1)
    update = None
    for chunk in range(chunks):
        update = update_call(chunk, tile_total, arrived[chunk], spread, vir_sum, occ_sum, ladders, update)
    return update


def solution(mesh):
    in_specs = (P("occ", None), P("occ", None, None), P("occ", "vir"), P(), P(), P(), P())
    out_specs = P("occ", "vir")
    return jax.shard_map(body, mesh=mesh, in_specs=in_specs, out_specs=out_specs, check_vma=False)
```

```python
import functools

import jax
import jax.numpy as jnp
from jax import lax
from jax.experimental import pallas as pl
from jax.experimental.pallas import tpu as pltpu
from jax.sharding import PartitionSpec as P

VT = 32
NVT = 2
W = 64
ORBITALS_IN_GRP = 16
PAIR_SQ = ORBITALS_IN_GRP * ORBITALS_IN_GRP
CORES = 2
CODE_ROWS = 16
AT_ONCE = 2
TOP = 32700.0
STEPS = 8.0
VMEM_LIMIT = 56 * 1024 * 1024


def one_hot_of(target, amount):
    return (target[:, None] == jnp.arange(amount)[None, :]).astype(jnp.bfloat16)


def split(values):
    high = values.astype(jnp.bfloat16)
    return high, (values - high.astype(jnp.float32)).astype(jnp.bfloat16)


def dot(left, right):
    return jnp.dot(left, right, preferred_element_type=jnp.float32)


def scale_of(code):
    return jnp.exp2(code * (1.0 / STEPS))


def screen_kernel(chunk, part, int_mask, slab_ref, screened_ref):
    slab_rows, slab_cols = slab_ref.shape
    cols = screened_ref.shape[1]
    span = slab_cols // W
    row_label = lax.axis_index("occ") * slab_rows // W // VT * NVT
    col_label = lax.axis_index("vir") * slab_cols // W // VT * NVT
    natural = lax.broadcasted_iota(jnp.int32, (slab_cols, 1), 0)
    a, b = natural // W, natural % W
    target = b // span * (part * span) + (a // part * part + b % part) * part + a % part
    target = jnp.where(b % span // part == chunk, target, -1)
    place = lax.broadcasted_iota(jnp.int32, (slab_cols, cols), 1)
    moved = dot(slab_ref[...], (place == target).astype(jnp.float32).astype(jnp.bfloat16)).astype(jnp.bfloat16)
    to = lax.broadcasted_iota(jnp.int32, (VT, cols), 1)
    owner, of_part = to // (part * span), to // part % part
    right = owner * span + chunk * part + of_part >= VT
    for d_tile in range(NVT):
        label = row_label + d_tile
        kept = jnp.where(right, int_mask[label, col_label + 1], int_mask[label, col_label])
        kept = kept.astype(jnp.float32).astype(jnp.bfloat16)
        for at in range(d_tile * VT, slab_rows, NVT * VT):
            screened_ref[at : at + VT, :] = moved[at : at + VT, :] * kept


def screen_call(chunk, chunks, int_mask, integrals):
    slab_rows, slab_cols = integrals.shape
    vmem = pl.BlockSpec(memory_space=pltpu.VMEM)
    return pl.pallas_call(
        functools.partial(screen_kernel, chunk, slab_cols // W // chunks),
        in_specs=[pl.BlockSpec(memory_space=pltpu.SMEM), vmem],
        out_specs=vmem,
        out_shape=jax.ShapeDtypeStruct((slab_rows, slab_cols // chunks), integrals.dtype),
        compiler_params=pltpu.CompilerParams(vmem_limit_bytes=VMEM_LIMIT),
        name="screen",
    )(int_mask, integrals)


def line_step(travel, step, tile_total):
    chips = tile_total // CORES
    arrived = {}
    for sign in (1, -1):
        pairs = [(t + sign * CORES, t) for t in range(tile_total) if 0 <= t // CORES + sign * step < chips]
        arrived[sign] = lax.ppermute(travel[sign], "occ", pairs)
    return arrived


def across(travel, step, tile_total):
    chips = tile_total // CORES
    pieces = []
    for sign in (1, -1) if step else (1,):
        pairs = [(t, t ^ 1) for t in range(tile_total) if 0 <= t // CORES + sign * step < chips]
        pieces.append((sign, step, False, travel[sign]))
        pieces.append((sign, step, True, lax.ppermute(travel[sign], "occ", pairs)))
    return pieces


def fill_slab(layout, refs, slab_scr, sems):
    tile = lax.axis_index("occ")
    chips = lax.axis_size("occ") // CORES
    chip, core = tile // CORES, tile % CORES
    slab_rows = refs[0].shape[0]

    def each(act):
        for n, (sign, step, other) in enumerate(layout):
            at_chip = chip + sign * step

            @pl.when((at_chip >= 0) & (at_chip < chips))
            def _():
                place = at_chip * CORES + (1 - core if other else core)
                at = pl.ds(pl.multiple_of(place * slab_rows, slab_rows), slab_rows)
                act(pltpu.make_async_copy(refs[n], slab_scr.at[at, :], sems.at[n]))

    each(lambda copy: copy.start())
    each(lambda copy: copy.wait())


def ladder_kernel(tile_total, vir_count, chunks, layout, amp_mask, numbers, rows_ref, *refs):
    pieces, refs = refs[: len(layout)], refs[len(layout) :]
    ladder_ref, packed_ref, product, refs = refs[0], refs[1], refs[2], refs[3:]
    step = pl.program_id(0)
    if len(layout) > 1:
        slab_ref, sems = refs

        @pl.when(step == 0)
        def _():
            fill_slab(layout, pieces, slab_ref, sems)
    else:
        slab_ref = pieces[0]
    cols = slab_ref.shape[1]

    tile = jnp.maximum(step - 1, 0)
    pair = lax.broadcasted_iota(jnp.int32, (PAIR_SQ, 1), 0)
    own_number = numbers[lax.axis_index("occ")]
    nonzero = (pair // ORBITALS_IN_GRP < own_number) & (pair % ORBITALS_IN_GRP < numbers[tile])
    ladder = jnp.where(nonzero, product[...], 0.0)
    block = cols // vir_count
    lanes = block // chunks
    for h in range(chunks):
        ladder_ref[h] = jnp.concatenate(
            [ladder[:, v * block + h * lanes : v * block + (h + 1) * lanes] for v in range(vir_count)], axis=1
        )
    by_place = ladder.reshape(ORBITALS_IN_GRP, ORBITALS_IN_GRP, cols)
    mirror = jnp.swapaxes(by_place, 0, 1).reshape(PAIR_SQ, cols)
    most = jnp.maximum(jnp.max(jnp.abs(ladder), axis=0, keepdims=True), 1e-30)
    code = jnp.ceil(jnp.log2(most) * STEPS)
    coded = jnp.round(mirror * (TOP / scale_of(code))).astype(jnp.int32).astype(jnp.int16)
    code_rows = jnp.broadcast_to(code.astype(jnp.int32), (CODE_ROWS, cols)).astype(jnp.int16)
    for v in range(vir_count):
        packed_ref[0, v, :PAIR_SQ] = coded[:, v * block : (v + 1) * block]
        packed_ref[0, v, PAIR_SQ:] = code_rows[:, v * block : (v + 1) * block]

    tile = jnp.minimum(step, tile_total - 1)
    lane = lax.broadcasted_iota(jnp.int32, (1, W * W), 1)
    low = lane < W * VT
    left = lane % W < VT
    keep = jnp.where(
        low,
        jnp.where(left, amp_mask[tile, 0], amp_mask[tile, 1]),
        jnp.where(left, amp_mask[tile, 2], amp_mask[tile, 3]),
    )
    screened = rows_ref[...] * keep.astype(jnp.float32).astype(jnp.bfloat16)
    product[...] = dot(screened, slab_ref[...])


def ladder_call(tile_total, vir_count, chunks, layout, amp_mask, numbers, amplitudes, slab_parts):
    cols = slab_parts[0].shape[1]
    block = cols // vir_count
    smem = pl.BlockSpec(memory_space=pltpu.SMEM)
    rows = tile_total * PAIR_SQ
    scratch = [pltpu.VMEM((PAIR_SQ, cols), jnp.float32)]
    if len(layout) > 1:
        slab_specs = [pl.BlockSpec(memory_space=pl.ANY)] * len(layout)
        scratch += [pltpu.VMEM((W * W, cols), jnp.bfloat16), pltpu.SemaphoreType.DMA((len(layout),))]
    else:
        slab_specs = [pl.BlockSpec((W * W, cols), lambda step: (0, 0))]
    return pl.pallas_call(
        functools.partial(ladder_kernel, tile_total, vir_count, chunks, layout),
        grid=(tile_total + 1,),
        in_specs=[smem, smem, pl.BlockSpec((PAIR_SQ, W * W), lambda step: (jnp.minimum(step, tile_total - 1), 0))]
        + slab_specs,
        out_specs=[
            pl.BlockSpec((chunks, PAIR_SQ, cols // chunks), lambda step: (0, jnp.maximum(step - 1, 0), 0)),
            pl.BlockSpec(
                (1, vir_count, PAIR_SQ + CODE_ROWS, block), lambda step: (jnp.maximum(step - 1, 0), 0, 0, 0)
            ),
        ],
        out_shape=[
            jax.ShapeDtypeStruct((chunks, rows, cols // chunks), jnp.float32),
            jax.ShapeDtypeStruct((tile_total, vir_count, PAIR_SQ + CODE_ROWS, block), jnp.int16),
        ],
        scratch_shapes=scratch,
        compiler_params=pltpu.CompilerParams(vmem_limit_bytes=VMEM_LIMIT),
        cost_estimate=pl.CostEstimate(
            flops=2 * rows * cols * W * W,
            bytes_accessed=rows * (W * W * 2 + cols * 6) + W * W * cols * 2,
            transcendentals=0,
        ),
        name="ladder",
    )(amp_mask, numbers, amplitudes, *slab_parts)


def moved_columns(values, spread_ref):
    both = dot(jnp.concatenate(split(values), axis=0), spread_ref[...])
    return both[: values.shape[0]] + both[values.shape[0] :]


def direct_kernel(spread_ref, *refs):
    refs[-1][...] = moved_columns(jnp.concatenate([ref[0] for ref in refs[:-1]], axis=1), spread_ref)


def direct_call(chunk, spread, ladders):
    rows = ladders[0].shape[1]
    step_rows = AT_ONCE * PAIR_SQ
    return pl.pallas_call(
        direct_kernel,
        grid=(rows // step_rows,),
        in_specs=[pl.BlockSpec(spread.shape, lambda step: (0, 0))]
        + [pl.BlockSpec((1, step_rows, ladder.shape[2]), lambda step: (chunk, step, 0)) for ladder in ladders],
        out_specs=pl.BlockSpec((step_rows, spread.shape[1]), lambda step: (step, 0)),
        out_shape=jax.ShapeDtypeStruct((rows, spread.shape[1]), jnp.float32),
        compiler_params=pltpu.CompilerParams(vmem_limit_bytes=VMEM_LIMIT),
        cost_estimate=pl.CostEstimate(
            flops=4 * rows * spread.size, bytes_accessed=rows * spread.shape[1] * 8, transcendentals=0
        ),
        name="direct",
    )(spread, *ladders)


def update_kernel(vir_count, arrived_ref, spread_ref, vir_ref, occ_ref, direct_ref, *refs):
    tiles = []
    for n in range(AT_ONCE):
        blocks = []
        for v in range(vir_count):
            code = arrived_ref[n, v, PAIR_SQ:].astype(jnp.int32).astype(jnp.float32)[:1]
            values = arrived_ref[n, v, :PAIR_SQ].astype(jnp.int32).astype(jnp.float32)
            blocks.append(values * (scale_of(code) * (1.0 / TOP)))
        tiles.append(jnp.concatenate(blocks, axis=1))
    mirror = moved_columns(jnp.concatenate(tiles, axis=0), spread_ref)
    refs[-1][...] = (direct_ref[...] + mirror) / (vir_ref[...] - occ_ref[:, :1])


def update_call(chunk, chunks, arrived, spread, vir_sum, occ_sum, direct, earlier):
    cols = spread.shape[1]
    rows = direct.shape[0]
    step_rows = AT_ONCE * PAIR_SQ
    args = [arrived, spread, vir_sum, occ_sum, direct]
    in_specs = [
        pl.BlockSpec((AT_ONCE,) + arrived.shape[1:], lambda step: (step, 0, 0, 0)),
        pl.BlockSpec(spread.shape, lambda step: (0, 0)),
        pl.BlockSpec((1, cols), lambda step: (0, chunk)),
        pl.BlockSpec((step_rows, 128), lambda step: (step, 0)),
        pl.BlockSpec((step_rows, cols), lambda step: (step, 0)),
    ]
    aliases = {}
    if earlier is not None:
        aliases = {len(args): 0}
        args.append(earlier)
        in_specs.append(pl.BlockSpec(memory_space=pl.ANY))
    return pl.pallas_call(
        functools.partial(update_kernel, arrived.shape[1]),
        grid=(rows // step_rows,),
        in_specs=in_specs,
        out_specs=pl.BlockSpec((step_rows, cols), lambda step: (step, chunk)),
        out_shape=jax.ShapeDtypeStruct((rows, chunks * cols), jnp.float32),
        input_output_aliases=aliases,
        compiler_params=pltpu.CompilerParams(vmem_limit_bytes=VMEM_LIMIT),
        cost_estimate=pl.CostEstimate(
            flops=4 * rows * spread.size, bytes_accessed=rows * cols * 10, transcendentals=0
        ),
        name="update",
    )(*args)


def body(amplitudes, amp_mask, integrals, int_mask, group_orbital_numbers, occ_energy, vir_energy):
    tile_total = lax.axis_size("occ")
    vir_count = lax.axis_size("vir")
    row_tile = lax.axis_index("occ")
    vir_place = lax.axis_index("vir")
    span = W // vir_count
    slab_cols = span * W
    chunks = 2 if span >= 16 else 1
    part = span // chunks
    block = part * span
    rows = PAIR_SQ + CODE_ROWS
    barrier = lax.optimization_barrier

    def ladder_of(layout, slab_parts):
        return ladder_call(
            tile_total, vir_count, chunks, layout, amp_mask[0], group_orbital_numbers, amplitudes, slab_parts
        )

    def exchanged(packed):
        moved = lax.all_to_all(
            packed.reshape(tile_total * vir_count, rows, block), ("occ", "vir"), split_axis=0, concat_axis=0, tiled=True
        )
        return moved.reshape(tile_total, vir_count, rows, block)

    slabs = []
    if chunks > 1:
        ring_part, integrals = barrier((screen_call(0, chunks, int_mask, integrals), integrals))
    last = screen_call(chunks - 1, chunks, int_mask, integrals)
    if chunks > 1:
        travel = {1: ring_part, -1: ring_part}
        reached = ()
        pieces = across(travel, 0, tile_total)
        crossed = [piece[3] for piece in pieces] + [last]
        for step in range(1, tile_total // CORES):
            travel = line_step(travel, step, tile_total)
            reached = travel[1], travel[-1]
            exchange = across(travel, step, tile_total)
            pieces += exchange
            travel[1], travel[-1], *_ = barrier((*reached, *crossed))
            crossed = [piece[3] for piece in exchange]
        last, *_ = barrier((last, *reached))
        slabs.append(([piece[:3] for piece in pieces], [piece[3] for piece in pieces]))
    slabs.append(([(0, 0, False)], [lax.all_gather(last, "occ", axis=0, tiled=True)]))
    ladders, arrived = [], []
    for layout, slab_parts in slabs:
        ladder, packed = ladder_of(layout, slab_parts)
        ladders.append(ladder)
        arrived.append(exchanged(packed))

    place = jnp.arange(vir_count * block)
    owner, there_part = place // block, place // (part * part) % chunks
    here, there = place // part % part, place % part
    mirror_spread = one_hot_of(here * W + owner * span + there_part * part + there, part * W)
    place = jnp.arange(vir_count * part * part)
    owner, b, a = place // (part * part), place // part % part, place % part
    direct_spread = one_hot_of(
        jnp.concatenate([a * W + owner * span + c * part + b for c in range(chunks)]), part * W
    )

    occ_table = occ_energy.reshape(tile_total, ORBITALS_IN_GRP)
    own_energy = lax.dynamic_slice_in_dim(occ_table, row_tile, 1, 0)[0]
    occ_sum = jnp.broadcast_to(
        (own_energy[None, :, None] + occ_table[:, None, :]).reshape(-1, 1), (tile_total * PAIR_SQ, 128)
    )
    vir_own = lax.dynamic_slice_in_dim(vir_energy, vir_place * span, span, 0)
    vir_sum = (vir_own[:, None] + vir_energy[None, :]).reshape(1, -1)
    update = None
    for chunk in range(chunks):
        direct = direct_call(chunk, direct_spread, ladders)
        update = update_call(chunk, chunks, arrived[chunk], mirror_spread, vir_sum, occ_sum, direct, update)
    return update


def solution(mesh):
    in_specs = (P("occ", None), P("occ", None, None), P("occ", "vir"), P(), P(), P(), P())
    out_specs = P("occ", "vir")
    return jax.shard_map(body, mesh=mesh, in_specs=in_specs, out_specs=out_specs, check_vma=False)
```

```python
import functools

import jax
import jax.numpy as jnp
from jax import lax
from jax.experimental import pallas as pl
from jax.experimental.pallas import tpu as pltpu
from jax.sharding import PartitionSpec as P

VT = 32
NVT = 2
W = 64
ORBITALS_IN_GRP = 16
PAIR_SQ = ORBITALS_IN_GRP * ORBITALS_IN_GRP
CODE_ROWS = 16
AT_ONCE = 2
SLAB_BITS = 14.0
TOP = 32700.0
STEPS = 8.0
VMEM_LIMIT = 56 * 1024 * 1024


def one_hot_of(target, amount):
    return (target[:, None] == jnp.arange(amount)[None, :]).astype(jnp.bfloat16)


def split(values):
    high = values.astype(jnp.bfloat16)
    return high, (values - high.astype(jnp.float32)).astype(jnp.bfloat16)


def dot(left, right):
    return jnp.dot(left, right, preferred_element_type=jnp.float32)


def scale_of(code):
    return jnp.exp2(code * (1.0 / STEPS))


def screen_kernel(part, int_mask, slab_ref, coded_ref, *later_refs):
    slab_rows, slab_cols = slab_ref.shape
    cols = coded_ref.shape[1]
    span = slab_cols // W
    row_label = lax.axis_index("occ") * slab_rows // W // VT * NVT
    col_label = lax.axis_index("vir") * slab_cols // W // VT * NVT
    natural = lax.broadcasted_iota(jnp.int32, (slab_cols, 1), 0)
    a, b = natural // W, natural % W
    target = b // span * (part * span) + (a // part * part + b % part) * part + a % part
    place = lax.broadcasted_iota(jnp.int32, (slab_cols, cols), 1)
    to = lax.broadcasted_iota(jnp.int32, (1, cols), 1)
    second = lax.broadcasted_iota(jnp.int32, (slab_rows, 1), 0) % W >= VT
    for chunk in range(1 + len(later_refs)):
        right = to // (part * span) * span + chunk * part + to // part % part >= VT
        kept = [
            jnp.where(right, int_mask[label, col_label + 1], int_mask[label, col_label])
            for label in (row_label, row_label + 1)
        ]
        ones = place == jnp.where(b % span // part == chunk, target, -1)
        moved = dot(slab_ref[...], ones.astype(jnp.float32).astype(jnp.bfloat16))
        moved = jnp.where(jnp.where(second, kept[1], kept[0]) > 0, moved, 0.0)
        if chunk:
            later_refs[chunk - 1][...] = moved.astype(jnp.bfloat16)
        else:
            most = jnp.maximum(jnp.max(jnp.abs(moved), axis=0, keepdims=True), 1e-30)
            code = jnp.floor(jnp.log2(most)) + 1.0
            coded = jnp.round(moved * jnp.exp2(SLAB_BITS - code)).astype(jnp.int32)
            coded_ref[:slab_rows, :] = coded.astype(jnp.int16)
            coded_ref[slab_rows:, :] = jnp.broadcast_to(code.astype(jnp.int32), (CODE_ROWS, cols)).astype(jnp.int16)


def screen_call(chunks, int_mask, integrals):
    slab_rows, slab_cols = integrals.shape
    cols = slab_cols // chunks
    vmem = pl.BlockSpec(memory_space=pltpu.VMEM)
    return pl.pallas_call(
        functools.partial(screen_kernel, slab_cols // W // chunks),
        in_specs=[pl.BlockSpec(memory_space=pltpu.SMEM), vmem],
        out_specs=[vmem] * chunks,
        out_shape=[jax.ShapeDtypeStruct((slab_rows + CODE_ROWS, cols), jnp.int16)]
        + [jax.ShapeDtypeStruct((slab_rows, cols), integrals.dtype)] * (chunks - 1),
        compiler_params=pltpu.CompilerParams(vmem_limit_bytes=VMEM_LIMIT),
        name="screen",
    )(int_mask, integrals)


def decode_slab(tile_total, coded_ref, stage, slab_scr, sems):
    slab_rows = slab_scr.shape[0] // tile_total
    coded_rows = slab_rows + CODE_ROWS

    def copy_of(tile):
        at = pl.ds(pl.multiple_of(tile * coded_rows, CODE_ROWS), coded_rows)
        return pltpu.make_async_copy(coded_ref.at[at, :], stage.at[at, :], sems.at[tile])

    for tile in range(tile_total):
        copy_of(tile).start()

    def decode(tile, carry):
        copy_of(tile).wait()
        at = pl.multiple_of(tile * coded_rows, CODE_ROWS)
        code = stage[pl.ds(pl.multiple_of(at + slab_rows, CODE_ROWS), CODE_ROWS), :]
        values = stage[pl.ds(at, slab_rows), :].astype(jnp.int32).astype(jnp.float32)
        scale = jnp.exp2(code.astype(jnp.int32).astype(jnp.float32)[:1] - SLAB_BITS)
        to = pl.ds(pl.multiple_of(tile * slab_rows, slab_rows), slab_rows)
        slab_scr[to, :] = (values * scale).astype(jnp.bfloat16)
        return carry

    lax.fori_loop(0, tile_total, decode, 0)


def ladder_kernel(tile_total, vir_count, chunks, amp_mask, numbers, rows_ref, slab_ref, *refs):
    ladder_ref, packed_ref, product = refs[:3]
    step = pl.program_id(0)
    if len(refs) > 3:
        coded_ref, (stage, slab_ref, sems) = slab_ref, refs[3:]

        @pl.when(step == 0)
        def _():
            decode_slab(tile_total, coded_ref, stage, slab_ref, sems)
    cols = slab_ref.shape[1]

    tile = jnp.maximum(step - 1, 0)
    pair = lax.broadcasted_iota(jnp.int32, (PAIR_SQ, 1), 0)
    own_number = numbers[lax.axis_index("occ")]
    nonzero = (pair // ORBITALS_IN_GRP < own_number) & (pair % ORBITALS_IN_GRP < numbers[tile])
    ladder = jnp.where(nonzero, product[...], 0.0)
    block = cols // vir_count
    lanes = block // chunks
    for h in range(chunks):
        ladder_ref[h] = jnp.concatenate(
            [ladder[:, v * block + h * lanes : v * block + (h + 1) * lanes] for v in range(vir_count)], axis=1
        )
    by_place = ladder.reshape(ORBITALS_IN_GRP, ORBITALS_IN_GRP, cols)
    mirror = jnp.swapaxes(by_place, 0, 1).reshape(PAIR_SQ, cols)
    most = jnp.maximum(jnp.max(jnp.abs(ladder), axis=0, keepdims=True), 1e-30)
    code = jnp.ceil(jnp.log2(most) * STEPS)
    coded = jnp.round(mirror * (TOP / scale_of(code))).astype(jnp.int32).astype(jnp.int16)
    code_rows = jnp.broadcast_to(code.astype(jnp.int32), (CODE_ROWS, cols)).astype(jnp.int16)
    for v in range(vir_count):
        packed_ref[0, v, :PAIR_SQ] = coded[:, v * block : (v + 1) * block]
        packed_ref[0, v, PAIR_SQ:] = code_rows[:, v * block : (v + 1) * block]

    tile = jnp.minimum(step, tile_total - 1)
    lane = lax.broadcasted_iota(jnp.int32, (1, W * W), 1)
    low = lane < W * VT
    left = lane % W < VT
    keep = jnp.where(
        low,
        jnp.where(left, amp_mask[tile, 0], amp_mask[tile, 1]),
        jnp.where(left, amp_mask[tile, 2], amp_mask[tile, 3]),
    )
    screened = rows_ref[...] * keep.astype(jnp.float32).astype(jnp.bfloat16)
    product[...] = dot(screened, slab_ref[...])


def ladder_call(tile_total, vir_count, chunks, amp_mask, numbers, amplitudes, slab):
    cols = slab.shape[1]
    block = cols // vir_count
    smem = pl.BlockSpec(memory_space=pltpu.SMEM)
    rows = tile_total * PAIR_SQ
    scratch = [pltpu.VMEM((PAIR_SQ, cols), jnp.float32)]
    slab_spec = pl.BlockSpec((W * W, cols), lambda step: (0, 0))
    if slab.dtype == jnp.int16:
        slab_spec = pl.BlockSpec(memory_space=pl.ANY)
        scratch += [
            pltpu.VMEM(slab.shape, slab.dtype),
            pltpu.VMEM((W * W, cols), jnp.bfloat16),
            pltpu.SemaphoreType.DMA((tile_total,)),
        ]
    return pl.pallas_call(
        functools.partial(ladder_kernel, tile_total, vir_count, chunks),
        grid=(tile_total + 1,),
        in_specs=[
            smem,
            smem,
            pl.BlockSpec((PAIR_SQ, W * W), lambda step: (jnp.minimum(step, tile_total - 1), 0)),
            slab_spec,
        ],
        out_specs=[
            pl.BlockSpec((chunks, PAIR_SQ, cols // chunks), lambda step: (0, jnp.maximum(step - 1, 0), 0)),
            pl.BlockSpec(
                (1, vir_count, PAIR_SQ + CODE_ROWS, block), lambda step: (jnp.maximum(step - 1, 0), 0, 0, 0)
            ),
        ],
        out_shape=[
            jax.ShapeDtypeStruct((chunks, rows, cols // chunks), jnp.float32),
            jax.ShapeDtypeStruct((tile_total, vir_count, PAIR_SQ + CODE_ROWS, block), jnp.int16),
        ],
        scratch_shapes=scratch,
        compiler_params=pltpu.CompilerParams(vmem_limit_bytes=VMEM_LIMIT),
        cost_estimate=pl.CostEstimate(
            flops=2 * rows * cols * W * W,
            bytes_accessed=rows * (W * W * 2 + cols * 6) + W * W * cols * 2,
            transcendentals=0,
        ),
        name="ladder",
    )(amp_mask, numbers, amplitudes, slab)


def moved_columns(values, spread_ref):
    both = dot(jnp.concatenate(split(values), axis=0), spread_ref[...])
    return both[: values.shape[0]] + both[values.shape[0] :]


def direct_kernel(spread_ref, *refs):
    refs[-1][...] = moved_columns(jnp.concatenate([ref[0] for ref in refs[:-1]], axis=1), spread_ref)


def direct_call(chunk, spread, ladders):
    rows = ladders[0].shape[1]
    step_rows = AT_ONCE * PAIR_SQ
    return pl.pallas_call(
        direct_kernel,
        grid=(rows // step_rows,),
        in_specs=[pl.BlockSpec(spread.shape, lambda step: (0, 0))]
        + [pl.BlockSpec((1, step_rows, ladder.shape[2]), lambda step: (chunk, step, 0)) for ladder in ladders],
        out_specs=pl.BlockSpec((step_rows, spread.shape[1]), lambda step: (step, 0)),
        out_shape=jax.ShapeDtypeStruct((rows, spread.shape[1]), jnp.float32),
        compiler_params=pltpu.CompilerParams(vmem_limit_bytes=VMEM_LIMIT),
        cost_estimate=pl.CostEstimate(
            flops=4 * rows * spread.size, bytes_accessed=rows * spread.shape[1] * 8, transcendentals=0
        ),
        name="direct",
    )(spread, *ladders)


def update_kernel(vir_count, arrived_ref, spread_ref, vir_ref, occ_ref, direct_ref, *refs):
    tiles = []
    for n in range(AT_ONCE):
        blocks = []
        for v in range(vir_count):
            code = arrived_ref[n, v, PAIR_SQ:].astype(jnp.int32).astype(jnp.float32)[:1]
            values = arrived_ref[n, v, :PAIR_SQ].astype(jnp.int32).astype(jnp.float32)
            blocks.append(values * (scale_of(code) * (1.0 / TOP)))
        tiles.append(jnp.concatenate(blocks, axis=1))
    mirror = moved_columns(jnp.concatenate(tiles, axis=0), spread_ref)
    refs[-1][...] = (direct_ref[...] + mirror) / (vir_ref[...] - occ_ref[:, :1])


def update_call(chunk, chunks, arrived, spread, vir_sum, occ_sum, direct, earlier):
    cols = spread.shape[1]
    rows = direct.shape[0]
    step_rows = AT_ONCE * PAIR_SQ
    args = [arrived, spread, vir_sum, occ_sum, direct]
    in_specs = [
        pl.BlockSpec((AT_ONCE,) + arrived.shape[1:], lambda step: (step, 0, 0, 0)),
        pl.BlockSpec(spread.shape, lambda step: (0, 0)),
        pl.BlockSpec((1, cols), lambda step: (0, chunk)),
        pl.BlockSpec((step_rows, 128), lambda step: (step, 0)),
        pl.BlockSpec((step_rows, cols), lambda step: (step, 0)),
    ]
    aliases = {}
    if earlier is not None:
        aliases = {len(args): 0}
        args.append(earlier)
        in_specs.append(pl.BlockSpec(memory_space=pl.ANY))
    return pl.pallas_call(
        functools.partial(update_kernel, arrived.shape[1]),
        grid=(rows // step_rows,),
        in_specs=in_specs,
        out_specs=pl.BlockSpec((step_rows, cols), lambda step: (step, chunk)),
        out_shape=jax.ShapeDtypeStruct((rows, chunks * cols), jnp.float32),
        input_output_aliases=aliases,
        compiler_params=pltpu.CompilerParams(vmem_limit_bytes=VMEM_LIMIT),
        cost_estimate=pl.CostEstimate(
            flops=4 * rows * spread.size, bytes_accessed=rows * cols * 10, transcendentals=0
        ),
        name="update",
    )(*args)


def body(amplitudes, amp_mask, integrals, int_mask, group_orbital_numbers, occ_energy, vir_energy):
    tile_total = lax.axis_size("occ")
    vir_count = lax.axis_size("vir")
    row_tile = lax.axis_index("occ")
    vir_place = lax.axis_index("vir")
    span = W // vir_count
    slab_cols = span * W
    chunks = 2 if span >= 16 else 1
    part = span // chunks
    block = part * span
    rows = PAIR_SQ + CODE_ROWS

    def exchanged(packed):
        moved = lax.all_to_all(
            packed.reshape(tile_total * vir_count, rows, block), ("occ", "vir"), split_axis=0, concat_axis=0, tiled=True
        )
        return moved.reshape(tile_total, vir_count, rows, block)

    coded, *later = screen_call(chunks, int_mask, integrals)
    slabs = [lax.all_gather(coded, "occ", axis=0, tiled=True)]
    for part_later in later:
        part_later, _ = lax.optimization_barrier((part_later, slabs[-1]))
        slabs.append(lax.all_gather(part_later, "occ", axis=0, tiled=True))
    ladders, arrived = [], []
    for slab in slabs:
        ladder, packed = ladder_call(
            tile_total, vir_count, chunks, amp_mask[0], group_orbital_numbers, amplitudes, slab
        )
        ladders.append(ladder)
        arrived.append(exchanged(packed))

    place = jnp.arange(vir_count * block)
    owner, there_part = place // block, place // (part * part) % chunks
    here, there = place // part % part, place % part
    mirror_spread = one_hot_of(here * W + owner * span + there_part * part + there, part * W)
    place = jnp.arange(vir_count * part * part)
    owner, b, a = place // (part * part), place // part % part, place % part
    direct_spread = one_hot_of(
        jnp.concatenate([a * W + owner * span + c * part + b for c in range(chunks)]), part * W
    )

    occ_table = occ_energy.reshape(tile_total, ORBITALS_IN_GRP)
    own_energy = lax.dynamic_slice_in_dim(occ_table, row_tile, 1, 0)[0]
    occ_sum = jnp.broadcast_to(
        (own_energy[None, :, None] + occ_table[:, None, :]).reshape(-1, 1), (tile_total * PAIR_SQ, 128)
    )
    vir_own = lax.dynamic_slice_in_dim(vir_energy, vir_place * span, span, 0)
    vir_sum = (vir_own[:, None] + vir_energy[None, :]).reshape(1, -1)
    update = None
    for chunk in range(chunks):
        direct = direct_call(chunk, direct_spread, ladders)
        update = update_call(chunk, chunks, arrived[chunk], mirror_spread, vir_sum, occ_sum, direct, update)
    return update


def solution(mesh):
    in_specs = (P("occ", None), P("occ", None, None), P("occ", "vir"), P(), P(), P(), P())
    out_specs = P("occ", "vir")
    return jax.shard_map(body, mesh=mesh, in_specs=in_specs, out_specs=out_specs, check_vma=False)
```

```python
import functools

import jax
import jax.numpy as jnp
from jax import lax
from jax.experimental import pallas as pl
from jax.experimental.pallas import tpu as pltpu
from jax.sharding import PartitionSpec as P

VT = 32
NVT = 2
W = 64
ORBITALS_IN_GRP = 16
PAIR_SQ = ORBITALS_IN_GRP * ORBITALS_IN_GRP
CODE_ROWS = 16
EXCHANGE_CODE_ROWS = 8
AT_ONCE = 2
SLAB_BITS = 14.0
TOP = 32700.0
STEPS = 8.0
VMEM_LIMIT = 56 * 1024 * 1024


def one_hot_of(target, amount):
    return (target[:, None] == jnp.arange(amount)[None, :]).astype(jnp.bfloat16)


def split(values):
    high = values.astype(jnp.bfloat16)
    return high, (values - high.astype(jnp.float32)).astype(jnp.bfloat16)


def dot(left, right):
    return jnp.dot(left, right, preferred_element_type=jnp.float32)


def scale_of(code):
    return jnp.exp2(code * (1.0 / STEPS))


def screen_kernel(part, int_mask, slab_ref, coded_ref, *later_refs):
    slab_rows, slab_cols = slab_ref.shape
    cols = coded_ref.shape[1]
    span = slab_cols // W
    row_label = lax.axis_index("occ") * slab_rows // W // VT * NVT
    col_label = lax.axis_index("vir") * slab_cols // W // VT * NVT
    natural = lax.broadcasted_iota(jnp.int32, (slab_cols, 1), 0)
    a, b = natural // W, natural % W
    target = b // span * (part * span) + (a // part * part + b % part) * part + a % part
    place = lax.broadcasted_iota(jnp.int32, (slab_cols, cols), 1)
    to = lax.broadcasted_iota(jnp.int32, (1, cols), 1)
    second = lax.broadcasted_iota(jnp.int32, (slab_rows, 1), 0) % W >= VT
    for chunk in range(1 + len(later_refs)):
        right = to // (part * span) * span + chunk * part + to // part % part >= VT
        kept = [
            jnp.where(right, int_mask[label, col_label + 1], int_mask[label, col_label])
            for label in (row_label, row_label + 1)
        ]
        ones = place == jnp.where(b % span // part == chunk, target, -1)
        moved = dot(slab_ref[...], ones.astype(jnp.float32).astype(jnp.bfloat16))
        moved = jnp.where(jnp.where(second, kept[1], kept[0]) > 0, moved, 0.0)
        if chunk:
            later_refs[chunk - 1][...] = moved.astype(jnp.bfloat16)
        else:
            most = jnp.maximum(jnp.max(jnp.abs(moved), axis=0, keepdims=True), 1e-30)
            code = jnp.floor(jnp.log2(most)) + 1.0
            coded = jnp.round(moved * jnp.exp2(SLAB_BITS - code)).astype(jnp.int32)
            coded_ref[:slab_rows, :] = coded.astype(jnp.int16)
            coded_ref[slab_rows:, :] = jnp.broadcast_to(code.astype(jnp.int32), (CODE_ROWS, cols)).astype(jnp.int16)


def screen_call(chunks, int_mask, integrals):
    slab_rows, slab_cols = integrals.shape
    cols = slab_cols // chunks
    vmem = pl.BlockSpec(memory_space=pltpu.VMEM)
    return pl.pallas_call(
        functools.partial(screen_kernel, slab_cols // W // chunks),
        in_specs=[pl.BlockSpec(memory_space=pltpu.SMEM), vmem],
        out_specs=[vmem] * chunks,
        out_shape=[jax.ShapeDtypeStruct((slab_rows + CODE_ROWS, cols), jnp.int16)]
        + [jax.ShapeDtypeStruct((slab_rows, cols), integrals.dtype)] * (chunks - 1),
        compiler_params=pltpu.CompilerParams(vmem_limit_bytes=VMEM_LIMIT),
        name="screen",
    )(int_mask, integrals)


def decode_slab(tile_total, coded_ref, stage, slab_scr, sems):
    slab_rows = slab_scr.shape[0] // tile_total
    coded_rows = slab_rows + CODE_ROWS

    def copy_of(tile):
        at = pl.ds(pl.multiple_of(tile * coded_rows, CODE_ROWS), coded_rows)
        return pltpu.make_async_copy(coded_ref.at[at, :], stage.at[at, :], sems.at[tile])

    for tile in range(tile_total):
        copy_of(tile).start()

    def decode(tile, carry):
        copy_of(tile).wait()
        at = pl.multiple_of(tile * coded_rows, CODE_ROWS)
        code = stage[pl.ds(pl.multiple_of(at + slab_rows, CODE_ROWS), CODE_ROWS), :]
        values = stage[pl.ds(at, slab_rows), :].astype(jnp.int32).astype(jnp.float32)
        scale = jnp.exp2(code.astype(jnp.int32).astype(jnp.float32)[:1] - SLAB_BITS)
        to = pl.ds(pl.multiple_of(tile * slab_rows, slab_rows), slab_rows)
        slab_scr[to, :] = (values * scale).astype(jnp.bfloat16)
        return carry

    lax.fori_loop(0, tile_total, decode, 0)


def ladder_kernel(tile_total, vir_count, chunks, amp_mask, numbers, rows_ref, slab_ref, *refs):
    ladder_ref, packed_ref, product = refs[:3]
    step = pl.program_id(0)
    if len(refs) > 3:
        coded_ref, (stage, slab_ref, sems) = slab_ref, refs[3:]

        @pl.when(step == 0)
        def _():
            decode_slab(tile_total, coded_ref, stage, slab_ref, sems)
    cols = slab_ref.shape[1]

    tile = jnp.maximum(step - 1, 0)
    pair = lax.broadcasted_iota(jnp.int32, (PAIR_SQ, 1), 0)
    own_number = numbers[lax.axis_index("occ")]
    nonzero = (pair // ORBITALS_IN_GRP < own_number) & (pair % ORBITALS_IN_GRP < numbers[tile])
    ladder = jnp.where(nonzero, product[...], 0.0)
    block = cols // vir_count
    lanes = block // chunks
    for h in range(chunks):
        ladder_ref[h] = jnp.concatenate(
            [ladder[:, v * block + h * lanes : v * block + (h + 1) * lanes] for v in range(vir_count)], axis=1
        )
    by_place = ladder.reshape(ORBITALS_IN_GRP, ORBITALS_IN_GRP, cols)
    mirror = jnp.swapaxes(by_place, 0, 1).reshape(PAIR_SQ, cols)
    most = jnp.maximum(jnp.max(jnp.abs(ladder), axis=0, keepdims=True), 1e-30)
    code = jnp.ceil(jnp.log2(most) * STEPS)
    coded = jnp.round(mirror * (TOP / scale_of(code))).astype(jnp.int32).astype(jnp.int16)
    code_rows = jnp.broadcast_to(code.astype(jnp.int32), (EXCHANGE_CODE_ROWS, cols)).astype(jnp.int16)
    for v in range(vir_count):
        packed_ref[0, v, :PAIR_SQ] = coded[:, v * block : (v + 1) * block]
        packed_ref[0, v, PAIR_SQ:] = code_rows[:, v * block : (v + 1) * block]

    tile = jnp.minimum(step, tile_total - 1)
    lane = lax.broadcasted_iota(jnp.int32, (1, W * W), 1)
    low = lane < W * VT
    left = lane % W < VT
    keep = jnp.where(
        low,
        jnp.where(left, amp_mask[tile, 0], amp_mask[tile, 1]),
        jnp.where(left, amp_mask[tile, 2], amp_mask[tile, 3]),
    )
    screened = rows_ref[...] * keep.astype(jnp.float32).astype(jnp.bfloat16)
    product[...] = dot(screened, slab_ref[...])


def ladder_call(tile_total, vir_count, chunks, amp_mask, numbers, amplitudes, slab):
    cols = slab.shape[1]
    block = cols // vir_count
    smem = pl.BlockSpec(memory_space=pltpu.SMEM)
    rows = tile_total * PAIR_SQ
    scratch = [pltpu.VMEM((PAIR_SQ, cols), jnp.float32)]
    slab_spec = pl.BlockSpec((W * W, cols), lambda step: (0, 0))
    if slab.dtype == jnp.int16:
        slab_spec = pl.BlockSpec(memory_space=pl.ANY)
        scratch += [
            pltpu.VMEM(slab.shape, slab.dtype),
            pltpu.VMEM((W * W, cols), jnp.bfloat16),
            pltpu.SemaphoreType.DMA((tile_total,)),
        ]
    return pl.pallas_call(
        functools.partial(ladder_kernel, tile_total, vir_count, chunks),
        grid=(tile_total + 1,),
        in_specs=[
            smem,
            smem,
            pl.BlockSpec((PAIR_SQ, W * W), lambda step: (jnp.minimum(step, tile_total - 1), 0)),
            slab_spec,
        ],
        out_specs=[
            pl.BlockSpec((chunks, PAIR_SQ, cols // chunks), lambda step: (0, jnp.maximum(step - 1, 0), 0)),
            pl.BlockSpec(
                (1, vir_count, PAIR_SQ + EXCHANGE_CODE_ROWS, block), lambda step: (jnp.maximum(step - 1, 0), 0, 0, 0)
            ),
        ],
        out_shape=[
            jax.ShapeDtypeStruct((chunks, rows, cols // chunks), jnp.float32),
            jax.ShapeDtypeStruct((tile_total, vir_count, PAIR_SQ + EXCHANGE_CODE_ROWS, block), jnp.int16),
        ],
        scratch_shapes=scratch,
        compiler_params=pltpu.CompilerParams(vmem_limit_bytes=VMEM_LIMIT),
        cost_estimate=pl.CostEstimate(
            flops=2 * rows * cols * W * W,
            bytes_accessed=rows * (W * W * 2 + cols * 6) + W * W * cols * 2,
            transcendentals=0,
        ),
        name="ladder",
    )(amp_mask, numbers, amplitudes, slab)


def moved_columns(values, spread_ref):
    both = dot(jnp.concatenate(split(values), axis=0), spread_ref[...])
    return both[: values.shape[0]] + both[values.shape[0] :]


def direct_kernel(spread_ref, *refs):
    refs[-1][...] = moved_columns(jnp.concatenate([ref[0] for ref in refs[:-1]], axis=1), spread_ref)


def direct_call(chunk, spread, ladders):
    rows = ladders[0].shape[1]
    step_rows = AT_ONCE * PAIR_SQ
    return pl.pallas_call(
        direct_kernel,
        grid=(rows // step_rows,),
        in_specs=[pl.BlockSpec(spread.shape, lambda step: (0, 0))]
        + [pl.BlockSpec((1, step_rows, ladder.shape[2]), lambda step: (chunk, step, 0)) for ladder in ladders],
        out_specs=pl.BlockSpec((step_rows, spread.shape[1]), lambda step: (step, 0)),
        out_shape=jax.ShapeDtypeStruct((rows, spread.shape[1]), jnp.float32),
        compiler_params=pltpu.CompilerParams(vmem_limit_bytes=VMEM_LIMIT),
        cost_estimate=pl.CostEstimate(
            flops=4 * rows * spread.size, bytes_accessed=rows * spread.shape[1] * 8, transcendentals=0
        ),
        name="direct",
    )(spread, *ladders)


def update_kernel(vir_count, arrived_ref, spread_ref, vir_ref, occ_ref, direct_ref, *refs):
    tiles = []
    for n in range(AT_ONCE):
        blocks = []
        for v in range(vir_count):
            code = arrived_ref[n, v, PAIR_SQ:].astype(jnp.int32).astype(jnp.float32)[:1]
            values = arrived_ref[n, v, :PAIR_SQ].astype(jnp.int32).astype(jnp.float32)
            blocks.append(values * (scale_of(code) * (1.0 / TOP)))
        tiles.append(jnp.concatenate(blocks, axis=1))
    mirror = moved_columns(jnp.concatenate(tiles, axis=0), spread_ref)
    refs[-1][...] = (direct_ref[...] + mirror) / (vir_ref[...] - occ_ref[:, :1])


def update_call(chunk, chunks, arrived, spread, vir_sum, occ_sum, direct, earlier):
    cols = spread.shape[1]
    rows = direct.shape[0]
    step_rows = AT_ONCE * PAIR_SQ
    args = [arrived, spread, vir_sum, occ_sum, direct]
    in_specs = [
        pl.BlockSpec((AT_ONCE,) + arrived.shape[1:], lambda step: (step, 0, 0, 0)),
        pl.BlockSpec(spread.shape, lambda step: (0, 0)),
        pl.BlockSpec((1, cols), lambda step: (0, chunk)),
        pl.BlockSpec((step_rows, 128), lambda step: (step, 0)),
        pl.BlockSpec((step_rows, cols), lambda step: (step, 0)),
    ]
    aliases = {}
    if earlier is not None:
        aliases = {len(args): 0}
        args.append(earlier)
        in_specs.append(pl.BlockSpec(memory_space=pl.ANY))
    return pl.pallas_call(
        functools.partial(update_kernel, arrived.shape[1]),
        grid=(rows // step_rows,),
        in_specs=in_specs,
        out_specs=pl.BlockSpec((step_rows, cols), lambda step: (step, chunk)),
        out_shape=jax.ShapeDtypeStruct((rows, chunks * cols), jnp.float32),
        input_output_aliases=aliases,
        compiler_params=pltpu.CompilerParams(vmem_limit_bytes=VMEM_LIMIT),
        cost_estimate=pl.CostEstimate(
            flops=4 * rows * spread.size, bytes_accessed=rows * cols * 10, transcendentals=0
        ),
        name="update",
    )(*args)


def body(amplitudes, amp_mask, integrals, int_mask, group_orbital_numbers, occ_energy, vir_energy):
    tile_total = lax.axis_size("occ")
    vir_count = lax.axis_size("vir")
    row_tile = lax.axis_index("occ")
    vir_place = lax.axis_index("vir")
    span = W // vir_count
    slab_cols = span * W
    chunks = 2 if span >= 16 else 1
    part = span // chunks
    block = part * span
    rows = PAIR_SQ + EXCHANGE_CODE_ROWS

    def exchanged(packed):
        moved = lax.all_to_all(
            packed.reshape(tile_total * vir_count, rows, block), ("occ", "vir"), split_axis=0, concat_axis=0, tiled=True
        )
        return moved.reshape(tile_total, vir_count, rows, block)

    coded, *later = screen_call(chunks, int_mask, integrals)
    slabs = [lax.all_gather(coded, "occ", axis=0, tiled=True)]
    for part_later in later:
        part_later, _ = lax.optimization_barrier((part_later, slabs[-1]))
        slabs.append(lax.all_gather(part_later, "occ", axis=0, tiled=True))
    ladders, arrived = [], []
    for slab in slabs:
        ladder, packed = ladder_call(
            tile_total, vir_count, chunks, amp_mask[0], group_orbital_numbers, amplitudes, slab
        )
        packed, _ = lax.optimization_barrier((packed, slabs[-1]))
        ladders.append(ladder)
        arrived.append(exchanged(packed))

    place = jnp.arange(vir_count * block)
    owner, there_part = place // block, place // (part * part) % chunks
    here, there = place // part % part, place % part
    mirror_spread = one_hot_of(here * W + owner * span + there_part * part + there, part * W)
    place = jnp.arange(vir_count * part * part)
    owner, b, a = place // (part * part), place // part % part, place % part
    direct_spread = one_hot_of(
        jnp.concatenate([a * W + owner * span + c * part + b for c in range(chunks)]), part * W
    )

    occ_table = occ_energy.reshape(tile_total, ORBITALS_IN_GRP)
    own_energy = lax.dynamic_slice_in_dim(occ_table, row_tile, 1, 0)[0]
    occ_sum = jnp.broadcast_to(
        (own_energy[None, :, None] + occ_table[:, None, :]).reshape(-1, 1), (tile_total * PAIR_SQ, 128)
    )
    vir_own = lax.dynamic_slice_in_dim(vir_energy, vir_place * span, span, 0)
    vir_sum = (vir_own[:, None] + vir_energy[None, :]).reshape(1, -1)
    update = None
    for chunk in range(chunks):
        direct = direct_call(chunk, direct_spread, ladders)
        update = update_call(chunk, chunks, arrived[chunk], mirror_spread, vir_sum, occ_sum, direct, update)
    return update


def solution(mesh):
    in_specs = (P("occ", None), P("occ", None, None), P("occ", "vir"), P(), P(), P(), P())
    out_specs = P("occ", "vir")
    return jax.shard_map(body, mesh=mesh, in_specs=in_specs, out_specs=out_specs, check_vma=False)
```

```python
import functools

import jax
import jax.numpy as jnp
from jax import lax
from jax.experimental import pallas as pl
from jax.experimental.pallas import tpu as pltpu
from jax.sharding import PartitionSpec as P

VT = 32
NVT = 2
W = 64
ORBITALS_IN_GRP = 16
PAIR_SQ = ORBITALS_IN_GRP * ORBITALS_IN_GRP
CODE_ROWS = 16
EXCHANGE_CODE_ROWS = 8
CODED_PARTS = 2
AT_ONCE = 2
SLAB_BITS = 14.0
TOP = 32700.0
STEPS = 8.0
VMEM_LIMIT = 56 * 1024 * 1024


def one_hot_of(target, amount):
    return (target[:, None] == jnp.arange(amount)[None, :]).astype(jnp.bfloat16)


def split(values):
    high = values.astype(jnp.bfloat16)
    return high, (values - high.astype(jnp.float32)).astype(jnp.bfloat16)


def dot(left, right):
    return jnp.dot(left, right, preferred_element_type=jnp.float32)


def scale_of(code):
    return jnp.exp2(code * (1.0 / STEPS))


def screen_kernel(part, int_mask, slab_ref, *refs):
    coded_refs, later_refs = refs[:CODED_PARTS], refs[CODED_PARTS:]
    slab_rows, slab_cols = slab_ref.shape
    coded_cols = coded_refs[0].shape[1]
    cols = coded_cols * CODED_PARTS
    span = slab_cols // W
    row_label = lax.axis_index("occ") * slab_rows // W // VT * NVT
    col_label = lax.axis_index("vir") * slab_cols // W // VT * NVT
    natural = lax.broadcasted_iota(jnp.int32, (slab_cols, 1), 0)
    a, b = natural // W, natural % W
    target = b // span * (part * span) + (a // part * part + b % part) * part + a % part
    place = lax.broadcasted_iota(jnp.int32, (slab_cols, cols), 1)
    to = lax.broadcasted_iota(jnp.int32, (1, cols), 1)
    second = lax.broadcasted_iota(jnp.int32, (slab_rows, 1), 0) % W >= VT
    for chunk in range(1 + len(later_refs)):
        right = to // (part * span) * span + chunk * part + to // part % part >= VT
        kept = [
            jnp.where(right, int_mask[label, col_label + 1], int_mask[label, col_label])
            for label in (row_label, row_label + 1)
        ]
        ones = place == jnp.where(b % span // part == chunk, target, -1)
        moved = dot(slab_ref[...], ones.astype(jnp.float32).astype(jnp.bfloat16))
        moved = jnp.where(jnp.where(second, kept[1], kept[0]) > 0, moved, 0.0)
        if chunk:
            later_refs[chunk - 1][...] = moved.astype(jnp.bfloat16)
        else:
            most = jnp.maximum(jnp.max(jnp.abs(moved), axis=0, keepdims=True), 1e-30)
            code = jnp.floor(jnp.log2(most)) + 1.0
            coded = jnp.round(moved * jnp.exp2(SLAB_BITS - code)).astype(jnp.int32).astype(jnp.int16)
            code_rows = jnp.broadcast_to(code.astype(jnp.int32), (CODE_ROWS, cols)).astype(jnp.int16)
            for n, coded_ref in enumerate(coded_refs):
                at = slice(n * coded_cols, (n + 1) * coded_cols)
                coded_ref[:slab_rows, :] = coded[:, at]
                coded_ref[slab_rows:, :] = code_rows[:, at]


def screen_call(chunks, int_mask, integrals):
    slab_rows, slab_cols = integrals.shape
    cols = slab_cols // chunks
    vmem = pl.BlockSpec(memory_space=pltpu.VMEM)
    return pl.pallas_call(
        functools.partial(screen_kernel, slab_cols // W // chunks),
        in_specs=[pl.BlockSpec(memory_space=pltpu.SMEM), vmem],
        out_specs=[vmem] * (CODED_PARTS + chunks - 1),
        out_shape=[jax.ShapeDtypeStruct((slab_rows + CODE_ROWS, cols // CODED_PARTS), jnp.int16)] * CODED_PARTS
        + [jax.ShapeDtypeStruct((slab_rows, cols), integrals.dtype)] * (chunks - 1),
        compiler_params=pltpu.CompilerParams(vmem_limit_bytes=VMEM_LIMIT),
        name="screen",
    )(int_mask, integrals)


def decode_slab(tile_total, coded_refs, stage, slab_scr, sems):
    slab_rows = slab_scr.shape[0] // tile_total
    coded_rows, cols = slab_rows + CODE_ROWS, coded_refs[0].shape[1]

    def copy_of(part, tile):
        at = pl.ds(pl.multiple_of(tile * coded_rows, CODE_ROWS), coded_rows)
        return pltpu.make_async_copy(coded_refs[part].at[at, :], stage.at[part, at, :], sems.at[part, tile])

    for tile in range(tile_total):
        for part in range(CODED_PARTS):
            copy_of(part, tile).start()

    def decode(tile, carry):
        at = pl.multiple_of(tile * coded_rows, CODE_ROWS)
        to = pl.ds(pl.multiple_of(tile * slab_rows, slab_rows), slab_rows)
        for part in range(CODED_PARTS):
            copy_of(part, tile).wait()
            code = stage[part, pl.ds(pl.multiple_of(at + slab_rows, CODE_ROWS), CODE_ROWS), :]
            values = stage[part, pl.ds(at, slab_rows), :].astype(jnp.int32).astype(jnp.float32)
            scale = jnp.exp2(code.astype(jnp.int32).astype(jnp.float32)[:1] - SLAB_BITS)
            slab_scr[to, part * cols : (part + 1) * cols] = (values * scale).astype(jnp.bfloat16)
        return carry

    lax.fori_loop(0, tile_total, decode, 0)


def ladder_kernel(tile_total, vir_count, chunks, coded, amp_mask, numbers, rows_ref, *refs):
    slab_refs, refs = (refs[:CODED_PARTS], refs[CODED_PARTS:]) if coded else (refs[:1], refs[1:])
    ladder_ref, packed_ref, product = refs[:3]
    step = pl.program_id(0)
    slab_ref = slab_refs[0]
    if coded:
        stage, slab_ref, sems = refs[3:]

        @pl.when(step == 0)
        def _():
            decode_slab(tile_total, slab_refs, stage, slab_ref, sems)
    cols = slab_ref.shape[1]

    tile = jnp.maximum(step - 1, 0)
    pair = lax.broadcasted_iota(jnp.int32, (PAIR_SQ, 1), 0)
    own_number = numbers[lax.axis_index("occ")]
    nonzero = (pair // ORBITALS_IN_GRP < own_number) & (pair % ORBITALS_IN_GRP < numbers[tile])
    ladder = jnp.where(nonzero, product[...], 0.0)
    block = cols // vir_count
    lanes = block // chunks
    for h in range(chunks):
        ladder_ref[h] = jnp.concatenate(
            [ladder[:, v * block + h * lanes : v * block + (h + 1) * lanes] for v in range(vir_count)], axis=1
        )
    by_place = ladder.reshape(ORBITALS_IN_GRP, ORBITALS_IN_GRP, cols)
    mirror = jnp.swapaxes(by_place, 0, 1).reshape(PAIR_SQ, cols)
    most = jnp.maximum(jnp.max(jnp.abs(ladder), axis=0, keepdims=True), 1e-30)
    code = jnp.ceil(jnp.log2(most) * STEPS)
    coded = jnp.round(mirror * (TOP / scale_of(code))).astype(jnp.int32).astype(jnp.int16)
    code_rows = jnp.broadcast_to(code.astype(jnp.int32), (EXCHANGE_CODE_ROWS, cols)).astype(jnp.int16)
    for v in range(vir_count):
        packed_ref[0, v, :PAIR_SQ] = coded[:, v * block : (v + 1) * block]
        packed_ref[0, v, PAIR_SQ:] = code_rows[:, v * block : (v + 1) * block]

    tile = jnp.minimum(step, tile_total - 1)
    lane = lax.broadcasted_iota(jnp.int32, (1, W * W), 1)
    low = lane < W * VT
    left = lane % W < VT
    keep = jnp.where(
        low,
        jnp.where(left, amp_mask[tile, 0], amp_mask[tile, 1]),
        jnp.where(left, amp_mask[tile, 2], amp_mask[tile, 3]),
    )
    screened = rows_ref[...] * keep.astype(jnp.float32).astype(jnp.bfloat16)
    product[...] = dot(screened, slab_ref[...])


def ladder_call(tile_total, vir_count, chunks, amp_mask, numbers, amplitudes, slab):
    coded = len(slab) > 1
    cols = sum(part.shape[1] for part in slab)
    block = cols // vir_count
    smem = pl.BlockSpec(memory_space=pltpu.SMEM)
    rows = tile_total * PAIR_SQ
    scratch = [pltpu.VMEM((PAIR_SQ, cols), jnp.float32)]
    slab_specs = [pl.BlockSpec((W * W, cols), lambda step: (0, 0))]
    if coded:
        slab_specs = [pl.BlockSpec(memory_space=pl.ANY)] * CODED_PARTS
        scratch += [
            pltpu.VMEM((CODED_PARTS,) + slab[0].shape, slab[0].dtype),
            pltpu.VMEM((W * W, cols), jnp.bfloat16),
            pltpu.SemaphoreType.DMA((CODED_PARTS, tile_total)),
        ]
    return pl.pallas_call(
        functools.partial(ladder_kernel, tile_total, vir_count, chunks, coded),
        grid=(tile_total + 1,),
        in_specs=[
            smem,
            smem,
            pl.BlockSpec((PAIR_SQ, W * W), lambda step: (jnp.minimum(step, tile_total - 1), 0)),
            *slab_specs,
        ],
        out_specs=[
            pl.BlockSpec((chunks, PAIR_SQ, cols // chunks), lambda step: (0, jnp.maximum(step - 1, 0), 0)),
            pl.BlockSpec(
                (1, vir_count, PAIR_SQ + EXCHANGE_CODE_ROWS, block), lambda step: (jnp.maximum(step - 1, 0), 0, 0, 0)
            ),
        ],
        out_shape=[
            jax.ShapeDtypeStruct((chunks, rows, cols // chunks), jnp.float32),
            jax.ShapeDtypeStruct((tile_total, vir_count, PAIR_SQ + EXCHANGE_CODE_ROWS, block), jnp.int16),
        ],
        scratch_shapes=scratch,
        compiler_params=pltpu.CompilerParams(vmem_limit_bytes=VMEM_LIMIT),
        cost_estimate=pl.CostEstimate(
            flops=2 * rows * cols * W * W,
            bytes_accessed=rows * (W * W * 2 + cols * 6) + W * W * cols * 2,
            transcendentals=0,
        ),
        name="ladder",
    )(amp_mask, numbers, amplitudes, *slab)


def moved_columns(values, spread_ref):
    both = dot(jnp.concatenate(split(values), axis=0), spread_ref[...])
    return both[: values.shape[0]] + both[values.shape[0] :]


def direct_kernel(spread_ref, *refs):
    refs[-1][...] = moved_columns(jnp.concatenate([ref[0] for ref in refs[:-1]], axis=1), spread_ref)


def direct_call(chunk, spread, ladders):
    rows = ladders[0].shape[1]
    step_rows = AT_ONCE * PAIR_SQ
    return pl.pallas_call(
        direct_kernel,
        grid=(rows // step_rows,),
        in_specs=[pl.BlockSpec(spread.shape, lambda step: (0, 0))]
        + [pl.BlockSpec((1, step_rows, ladder.shape[2]), lambda step: (chunk, step, 0)) for ladder in ladders],
        out_specs=pl.BlockSpec((step_rows, spread.shape[1]), lambda step: (step, 0)),
        out_shape=jax.ShapeDtypeStruct((rows, spread.shape[1]), jnp.float32),
        compiler_params=pltpu.CompilerParams(vmem_limit_bytes=VMEM_LIMIT),
        cost_estimate=pl.CostEstimate(
            flops=4 * rows * spread.size, bytes_accessed=rows * spread.shape[1] * 8, transcendentals=0
        ),
        name="direct",
    )(spread, *ladders)


def update_kernel(vir_count, arrived_ref, spread_ref, vir_ref, occ_ref, direct_ref, *refs):
    tiles = []
    for n in range(AT_ONCE):
        blocks = []
        for v in range(vir_count):
            code = arrived_ref[n, v, PAIR_SQ:].astype(jnp.int32).astype(jnp.float32)[:1]
            values = arrived_ref[n, v, :PAIR_SQ].astype(jnp.int32).astype(jnp.float32)
            blocks.append(values * (scale_of(code) * (1.0 / TOP)))
        tiles.append(jnp.concatenate(blocks, axis=1))
    mirror = moved_columns(jnp.concatenate(tiles, axis=0), spread_ref)
    refs[-1][...] = (direct_ref[...] + mirror) / (vir_ref[...] - occ_ref[:, :1])


def update_call(chunk, chunks, arrived, spread, vir_sum, occ_sum, direct, earlier):
    cols = spread.shape[1]
    rows = direct.shape[0]
    step_rows = AT_ONCE * PAIR_SQ
    args = [arrived, spread, vir_sum, occ_sum, direct]
    in_specs = [
        pl.BlockSpec((AT_ONCE,) + arrived.shape[1:], lambda step: (step, 0, 0, 0)),
        pl.BlockSpec(spread.shape, lambda step: (0, 0)),
        pl.BlockSpec((1, cols), lambda step: (0, chunk)),
        pl.BlockSpec((step_rows, 128), lambda step: (step, 0)),
        pl.BlockSpec((step_rows, cols), lambda step: (step, 0)),
    ]
    aliases = {}
    if earlier is not None:
        aliases = {len(args): 0}
        args.append(earlier)
        in_specs.append(pl.BlockSpec(memory_space=pl.ANY))
    return pl.pallas_call(
        functools.partial(update_kernel, arrived.shape[1]),
        grid=(rows // step_rows,),
        in_specs=in_specs,
        out_specs=pl.BlockSpec((step_rows, cols), lambda step: (step, chunk)),
        out_shape=jax.ShapeDtypeStruct((rows, chunks * cols), jnp.float32),
        input_output_aliases=aliases,
        compiler_params=pltpu.CompilerParams(vmem_limit_bytes=VMEM_LIMIT),
        cost_estimate=pl.CostEstimate(
            flops=4 * rows * spread.size, bytes_accessed=rows * cols * 10, transcendentals=0
        ),
        name="update",
    )(*args)


def body(amplitudes, amp_mask, integrals, int_mask, group_orbital_numbers, occ_energy, vir_energy):
    tile_total = lax.axis_size("occ")
    vir_count = lax.axis_size("vir")
    row_tile = lax.axis_index("occ")
    vir_place = lax.axis_index("vir")
    span = W // vir_count
    slab_cols = span * W
    chunks = 2 if span >= 16 else 1
    width = span // chunks
    block = width * span
    rows = PAIR_SQ + EXCHANGE_CODE_ROWS

    def exchanged(packed):
        moved = lax.all_to_all(
            packed.reshape(tile_total * vir_count, rows, block), ("occ", "vir"), split_axis=0, concat_axis=0, tiled=True
        )
        return moved.reshape(tile_total, vir_count, rows, block)

    parts = screen_call(chunks, int_mask, integrals)
    coded, later = parts[:CODED_PARTS], parts[CODED_PARTS:]
    first = lax.all_gather(coded[0], "occ", axis=0, tiled=True)
    *coded, first = lax.optimization_barrier((*coded[1:], first))
    slabs = [[first] + [lax.all_gather(part, "occ", axis=0, tiled=True) for part in coded]]
    for part in later:
        part, _ = lax.optimization_barrier((part, first))
        slabs.append([lax.all_gather(part, "occ", axis=0, tiled=True)])
    ladders, arrived = [], []
    for slab in slabs:
        ladder, packed = ladder_call(
            tile_total, vir_count, chunks, amp_mask[0], group_orbital_numbers, amplitudes, slab
        )
        ladders.append(ladder)
        arrived.append(exchanged(packed))

    place = jnp.arange(vir_count * block)
    owner, there_part = place // block, place // (width * width) % chunks
    here, there = place // width % width, place % width
    mirror_spread = one_hot_of(here * W + owner * span + there_part * width + there, width * W)
    place = jnp.arange(vir_count * width * width)
    owner, b, a = place // (width * width), place // width % width, place % width
    direct_spread = one_hot_of(
        jnp.concatenate([a * W + owner * span + c * width + b for c in range(chunks)]), width * W
    )

    occ_table = occ_energy.reshape(tile_total, ORBITALS_IN_GRP)
    own_energy = lax.dynamic_slice_in_dim(occ_table, row_tile, 1, 0)[0]
    occ_sum = jnp.broadcast_to(
        (own_energy[None, :, None] + occ_table[:, None, :]).reshape(-1, 1), (tile_total * PAIR_SQ, 128)
    )
    vir_own = lax.dynamic_slice_in_dim(vir_energy, vir_place * span, span, 0)
    vir_sum = (vir_own[:, None] + vir_energy[None, :]).reshape(1, -1)
    update = None
    for chunk in range(chunks):
        direct = direct_call(chunk, direct_spread, ladders)
        update = update_call(chunk, chunks, arrived[chunk], mirror_spread, vir_sum, occ_sum, direct, update)
    return update


def solution(mesh):
    in_specs = (P("occ", None), P("occ", None, None), P("occ", "vir"), P(), P(), P(), P())
    out_specs = P("occ", "vir")
    return jax.shard_map(body, mesh=mesh, in_specs=in_specs, out_specs=out_specs, check_vma=False)
```

```python
import functools

import jax
import jax.numpy as jnp
from jax import lax
from jax.experimental import pallas as pl
from jax.experimental.pallas import tpu as pltpu
from jax.sharding import PartitionSpec as P

VT = 32
NVT = 2
W = 64
ORBITALS_IN_GRP = 16
PAIR_SQ = ORBITALS_IN_GRP * ORBITALS_IN_GRP
CODE_ROWS = 16
EXCHANGE_CODE_ROWS = 8
CODED_PARTS = 1
PIECES = 4
AT_ONCE = 2
SLAB_BITS = 14.0
TOP = 32700.0
STEPS = 8.0
VMEM_LIMIT = 56 * 1024 * 1024


def one_hot_of(target, amount):
    return (target[:, None] == jnp.arange(amount)[None, :]).astype(jnp.bfloat16)


def split(values):
    high = values.astype(jnp.bfloat16)
    return high, (values - high.astype(jnp.float32)).astype(jnp.bfloat16)


def dot(left, right):
    return jnp.dot(left, right, preferred_element_type=jnp.float32)


def scale_of(code):
    return jnp.exp2(code * (1.0 / STEPS))


def screen_kernel(part, int_mask, slab_ref, *refs):
    coded_refs, later_refs = refs[:CODED_PARTS], refs[CODED_PARTS:]
    slab_rows, slab_cols = slab_ref.shape
    coded_cols = coded_refs[0].shape[1]
    cols = coded_cols * CODED_PARTS
    span = slab_cols // W
    row_label = lax.axis_index("occ") * slab_rows // W // VT * NVT
    col_label = lax.axis_index("vir") * slab_cols // W // VT * NVT
    natural = lax.broadcasted_iota(jnp.int32, (slab_cols, 1), 0)
    a, b = natural // W, natural % W
    target = b // span * (part * span) + (a // part * part + b % part) * part + a % part
    place = lax.broadcasted_iota(jnp.int32, (slab_cols, cols), 1)
    to = lax.broadcasted_iota(jnp.int32, (1, cols), 1)
    second = lax.broadcasted_iota(jnp.int32, (slab_rows, 1), 0) % W >= VT
    for chunk in range(1 + len(later_refs)):
        right = to // (part * span) * span + chunk * part + to // part % part >= VT
        kept = [
            jnp.where(right, int_mask[label, col_label + 1], int_mask[label, col_label])
            for label in (row_label, row_label + 1)
        ]
        ones = place == jnp.where(b % span // part == chunk, target, -1)
        moved = dot(slab_ref[...], ones.astype(jnp.float32).astype(jnp.bfloat16))
        moved = jnp.where(jnp.where(second, kept[1], kept[0]) > 0, moved, 0.0)
        if chunk:
            later_refs[chunk - 1][...] = moved.astype(jnp.bfloat16)
        else:
            most = jnp.maximum(jnp.max(jnp.abs(moved), axis=0, keepdims=True), 1e-30)
            code = jnp.floor(jnp.log2(most)) + 1.0
            coded = jnp.round(moved * jnp.exp2(SLAB_BITS - code)).astype(jnp.int32).astype(jnp.int16)
            code_rows = jnp.broadcast_to(code.astype(jnp.int32), (CODE_ROWS, cols)).astype(jnp.int16)
            for n, coded_ref in enumerate(coded_refs):
                at = slice(n * coded_cols, (n + 1) * coded_cols)
                coded_ref[:slab_rows, :] = coded[:, at]
                coded_ref[slab_rows:, :] = code_rows[:, at]


def screen_call(chunks, int_mask, integrals):
    slab_rows, slab_cols = integrals.shape
    cols = slab_cols // chunks
    vmem = pl.BlockSpec(memory_space=pltpu.VMEM)
    return pl.pallas_call(
        functools.partial(screen_kernel, slab_cols // W // chunks),
        in_specs=[pl.BlockSpec(memory_space=pltpu.SMEM), vmem],
        out_specs=[vmem] * (CODED_PARTS + chunks - 1),
        out_shape=[jax.ShapeDtypeStruct((slab_rows + CODE_ROWS, cols // CODED_PARTS), jnp.int16)] * CODED_PARTS
        + [jax.ShapeDtypeStruct((slab_rows, cols), integrals.dtype)] * (chunks - 1),
        compiler_params=pltpu.CompilerParams(vmem_limit_bytes=VMEM_LIMIT),
        name="screen",
    )(int_mask, integrals)


def decode_slab(tile_total, coded_refs, stage, slab_scr, sems):
    slab_rows = slab_scr.shape[0] // tile_total
    coded_rows, cols = slab_rows + CODE_ROWS, coded_refs[0].shape[1]

    def copy_of(part, tile):
        at = pl.ds(pl.multiple_of(tile * coded_rows, CODE_ROWS), coded_rows)
        return pltpu.make_async_copy(coded_refs[part].at[at, :], stage.at[part, at, :], sems.at[part, tile])

    for tile in range(tile_total):
        for part in range(CODED_PARTS):
            copy_of(part, tile).start()

    def decode(tile, carry):
        at = pl.multiple_of(tile * coded_rows, CODE_ROWS)
        to = pl.ds(pl.multiple_of(tile * slab_rows, slab_rows), slab_rows)
        for part in range(CODED_PARTS):
            copy_of(part, tile).wait()
            code = stage[part, pl.ds(pl.multiple_of(at + slab_rows, CODE_ROWS), CODE_ROWS), :]
            values = stage[part, pl.ds(at, slab_rows), :].astype(jnp.int32).astype(jnp.float32)
            scale = jnp.exp2(code.astype(jnp.int32).astype(jnp.float32)[:1] - SLAB_BITS)
            slab_scr[to, part * cols : (part + 1) * cols] = (values * scale).astype(jnp.bfloat16)
        return carry

    lax.fori_loop(0, tile_total, decode, 0)


def ladder_kernel(tile_total, vir_count, chunks, coded, amp_mask, numbers, *refs):
    rows_refs, refs = refs[:PIECES], refs[PIECES:]
    slab_refs, refs = (refs[:CODED_PARTS], refs[CODED_PARTS:]) if coded else (refs[:1], refs[1:])
    ladder_ref, packed_ref, product = refs[:3]
    step = pl.program_id(0)
    slab_ref = slab_refs[0]
    if coded:
        stage, slab_ref, sems = refs[3:]

        @pl.when(step == 0)
        def _():
            decode_slab(tile_total, slab_refs, stage, slab_ref, sems)
    cols = slab_ref.shape[1]

    tile = jnp.maximum(step - 1, 0)
    pair = lax.broadcasted_iota(jnp.int32, (PAIR_SQ, 1), 0)
    own_number = numbers[lax.axis_index("occ")]
    nonzero = (pair // ORBITALS_IN_GRP < own_number) & (pair % ORBITALS_IN_GRP < numbers[tile])
    ladder = jnp.where(nonzero, product[...], 0.0)
    block = cols // vir_count
    lanes = block // chunks
    for h in range(chunks):
        ladder_ref[h] = jnp.concatenate(
            [ladder[:, v * block + h * lanes : v * block + (h + 1) * lanes] for v in range(vir_count)], axis=1
        )
    by_place = ladder.reshape(ORBITALS_IN_GRP, ORBITALS_IN_GRP, cols)
    mirror = jnp.swapaxes(by_place, 0, 1).reshape(PAIR_SQ, cols)
    most = jnp.maximum(jnp.max(jnp.abs(ladder), axis=0, keepdims=True), 1e-30)
    code = jnp.ceil(jnp.log2(most) * STEPS)
    coded = jnp.round(mirror * (TOP / scale_of(code))).astype(jnp.int32).astype(jnp.int16)
    code_rows = jnp.broadcast_to(code.astype(jnp.int32), (EXCHANGE_CODE_ROWS, cols)).astype(jnp.int16)
    for v in range(vir_count):
        packed_ref[0, v, :PAIR_SQ] = coded[:, v * block : (v + 1) * block]
        packed_ref[0, v, PAIR_SQ:] = code_rows[:, v * block : (v + 1) * block]

    tile = jnp.minimum(step, tile_total - 1)
    lane = lax.broadcasted_iota(jnp.int32, (1, W * W), 1)
    low = lane < W * VT
    left = lane % W < VT
    keep = jnp.where(
        low,
        jnp.where(left, amp_mask[tile, 0], amp_mask[tile, 1]),
        jnp.where(left, amp_mask[tile, 2], amp_mask[tile, 3]),
    )
    keep = keep.astype(jnp.float32).astype(jnp.bfloat16)
    screened = jnp.concatenate([rows_ref[...] * keep for rows_ref in rows_refs], axis=0)
    product[...] = dot(screened, slab_ref[...])


def ladder_call(tile_total, vir_count, chunks, amp_mask, numbers, amplitudes, slab):
    coded = slab[0].dtype == jnp.int16
    cols = sum(part.shape[1] for part in slab)
    block = cols // vir_count
    smem = pl.BlockSpec(memory_space=pltpu.SMEM)
    rows = tile_total * PAIR_SQ
    scratch = [pltpu.VMEM((PAIR_SQ, cols), jnp.float32)]
    slab_specs = [pl.BlockSpec((W * W, cols), lambda step: (0, 0))]
    if coded:
        slab_specs = [pl.BlockSpec(memory_space=pl.ANY)] * CODED_PARTS
        scratch += [
            pltpu.VMEM((CODED_PARTS,) + slab[0].shape, slab[0].dtype),
            pltpu.VMEM((W * W, cols), jnp.bfloat16),
            pltpu.SemaphoreType.DMA((CODED_PARTS, tile_total)),
        ]
    return pl.pallas_call(
        functools.partial(ladder_kernel, tile_total, vir_count, chunks, coded),
        grid=(tile_total + 1,),
        in_specs=[
            smem,
            smem,
            *[
                pl.BlockSpec(
                    (PAIR_SQ // PIECES, W * W),
                    lambda step, n=n: (jnp.minimum(step, tile_total - 1) * PIECES + n, 0),
                )
                for n in range(PIECES)
            ],
            *slab_specs,
        ],
        out_specs=[
            pl.BlockSpec((chunks, PAIR_SQ, cols // chunks), lambda step: (0, jnp.maximum(step - 1, 0), 0)),
            pl.BlockSpec(
                (1, vir_count, PAIR_SQ + EXCHANGE_CODE_ROWS, block), lambda step: (jnp.maximum(step - 1, 0), 0, 0, 0)
            ),
        ],
        out_shape=[
            jax.ShapeDtypeStruct((chunks, rows, cols // chunks), jnp.float32),
            jax.ShapeDtypeStruct((tile_total, vir_count, PAIR_SQ + EXCHANGE_CODE_ROWS, block), jnp.int16),
        ],
        scratch_shapes=scratch,
        compiler_params=pltpu.CompilerParams(vmem_limit_bytes=VMEM_LIMIT),
        cost_estimate=pl.CostEstimate(
            flops=2 * rows * cols * W * W,
            bytes_accessed=rows * (W * W * 2 + cols * 6) + W * W * cols * 2,
            transcendentals=0,
        ),
        name="ladder",
    )(amp_mask, numbers, *[amplitudes] * PIECES, *slab)


def moved_columns(values, spread_ref):
    both = dot(jnp.concatenate(split(values), axis=0), spread_ref[...])
    return both[: values.shape[0]] + both[values.shape[0] :]


def direct_kernel(spread_ref, *refs):
    refs[-1][...] = moved_columns(jnp.concatenate([ref[0] for ref in refs[:-1]], axis=1), spread_ref)


def direct_call(chunk, spread, ladders):
    rows = ladders[0].shape[1]
    step_rows = AT_ONCE * PAIR_SQ
    return pl.pallas_call(
        direct_kernel,
        grid=(rows // step_rows,),
        in_specs=[pl.BlockSpec(spread.shape, lambda step: (0, 0))]
        + [pl.BlockSpec((1, step_rows, ladder.shape[2]), lambda step: (chunk, step, 0)) for ladder in ladders],
        out_specs=pl.BlockSpec((step_rows, spread.shape[1]), lambda step: (step, 0)),
        out_shape=jax.ShapeDtypeStruct((rows, spread.shape[1]), jnp.float32),
        compiler_params=pltpu.CompilerParams(vmem_limit_bytes=VMEM_LIMIT),
        cost_estimate=pl.CostEstimate(
            flops=4 * rows * spread.size, bytes_accessed=rows * spread.shape[1] * 8, transcendentals=0
        ),
        name="direct",
    )(spread, *ladders)


def update_kernel(vir_count, spread_ref, vir_ref, occ_ref, *refs):
    arrived_refs, refs = refs[:vir_count], refs[vir_count:]
    direct_refs = refs[:AT_ONCE]
    tiles = []
    for n in range(AT_ONCE):
        blocks = []
        for v in range(vir_count):
            code = arrived_refs[v][n, 0, PAIR_SQ:].astype(jnp.int32).astype(jnp.float32)[:1]
            values = arrived_refs[v][n, 0, :PAIR_SQ].astype(jnp.int32).astype(jnp.float32)
            blocks.append(values * (scale_of(code) * (1.0 / TOP)))
        tiles.append(jnp.concatenate(blocks, axis=1))
    mirror = moved_columns(jnp.concatenate(tiles, axis=0), spread_ref)
    for n, direct_ref in enumerate(direct_refs):
        at = slice(n * PAIR_SQ, (n + 1) * PAIR_SQ)
        refs[-1][at, :] = (direct_ref[...] + mirror[at]) / (vir_ref[...] - occ_ref[at, :1])


def update_call(chunk, chunks, arrived, spread, vir_sum, occ_sum, direct, earlier):
    cols = spread.shape[1]
    rows = direct.shape[0]
    step_rows = AT_ONCE * PAIR_SQ
    vir_count = arrived.shape[1]
    args = [spread, vir_sum, occ_sum] + [arrived] * vir_count + [direct] * AT_ONCE
    in_specs = [
        pl.BlockSpec(spread.shape, lambda step: (0, 0)),
        pl.BlockSpec((1, cols), lambda step: (0, chunk)),
        pl.BlockSpec((step_rows, 128), lambda step: (step, 0)),
    ]
    in_specs += [
        pl.BlockSpec((AT_ONCE, 1) + arrived.shape[2:], lambda step, v=v: (step, v, 0, 0)) for v in range(vir_count)
    ]
    in_specs += [pl.BlockSpec((PAIR_SQ, cols), lambda step, n=n: (step * AT_ONCE + n, 0)) for n in range(AT_ONCE)]
    aliases = {}
    if earlier is not None:
        aliases = {len(args): 0}
        args.append(earlier)
        in_specs.append(pl.BlockSpec(memory_space=pl.ANY))
    return pl.pallas_call(
        functools.partial(update_kernel, vir_count),
        grid=(rows // step_rows,),
        in_specs=in_specs,
        out_specs=pl.BlockSpec((step_rows, cols), lambda step: (step, chunk)),
        out_shape=jax.ShapeDtypeStruct((rows, chunks * cols), jnp.float32),
        input_output_aliases=aliases,
        compiler_params=pltpu.CompilerParams(vmem_limit_bytes=VMEM_LIMIT),
        cost_estimate=pl.CostEstimate(
            flops=4 * rows * spread.size, bytes_accessed=rows * cols * 10, transcendentals=0
        ),
        name="update",
    )(*args)


def body(amplitudes, amp_mask, integrals, int_mask, group_orbital_numbers, occ_energy, vir_energy):
    tile_total = lax.axis_size("occ")
    vir_count = lax.axis_size("vir")
    row_tile = lax.axis_index("occ")
    vir_place = lax.axis_index("vir")
    span = W // vir_count
    slab_cols = span * W
    chunks = 2 if span >= 16 else 1
    width = span // chunks
    block = width * span
    rows = PAIR_SQ + EXCHANGE_CODE_ROWS

    def exchanged(packed):
        moved = lax.all_to_all(
            packed.reshape(tile_total * vir_count, rows, block), ("occ", "vir"), split_axis=0, concat_axis=0, tiled=True
        )
        return moved.reshape(tile_total, vir_count, rows, block)

    parts = screen_call(chunks, int_mask, integrals)
    coded, later = parts[:CODED_PARTS], parts[CODED_PARTS:]
    first = lax.all_gather(coded[0], "occ", axis=0, tiled=True)
    *coded, first = lax.optimization_barrier((*coded[1:], first))
    slabs = [[first] + [lax.all_gather(part, "occ", axis=0, tiled=True) for part in coded]]
    for part in later:
        part, _ = lax.optimization_barrier((part, first))
        slabs.append([lax.all_gather(part, "occ", axis=0, tiled=True)])
    ladders, arrived = [], []
    for slab in slabs:
        ladder, packed = ladder_call(
            tile_total, vir_count, chunks, amp_mask[0], group_orbital_numbers, amplitudes, slab
        )
        ladders.append(ladder)
        arrived.append(exchanged(packed))

    place = jnp.arange(vir_count * block)
    owner, there_part = place // block, place // (width * width) % chunks
    here, there = place // width % width, place % width
    mirror_spread = one_hot_of(here * W + owner * span + there_part * width + there, width * W)
    place = jnp.arange(vir_count * width * width)
    owner, b, a = place // (width * width), place // width % width, place % width
    direct_spread = one_hot_of(
        jnp.concatenate([a * W + owner * span + c * width + b for c in range(chunks)]), width * W
    )

    occ_table = occ_energy.reshape(tile_total, ORBITALS_IN_GRP)
    own_energy = lax.dynamic_slice_in_dim(occ_table, row_tile, 1, 0)[0]
    occ_sum = jnp.broadcast_to(
        (own_energy[None, :, None] + occ_table[:, None, :]).reshape(-1, 1), (tile_total * PAIR_SQ, 128)
    )
    vir_own = lax.dynamic_slice_in_dim(vir_energy, vir_place * span, span, 0)
    vir_sum = (vir_own[:, None] + vir_energy[None, :]).reshape(1, -1)
    update = None
    for chunk in range(chunks):
        direct = direct_call(chunk, direct_spread, ladders)
        update = update_call(chunk, chunks, arrived[chunk], mirror_spread, vir_sum, occ_sum, direct, update)
    return update


def solution(mesh):
    in_specs = (P("occ", None), P("occ", None, None), P("occ", "vir"), P(), P(), P(), P())
    out_specs = P("occ", "vir")
    return jax.shard_map(body, mesh=mesh, in_specs=in_specs, out_specs=out_specs, check_vma=False)
```

```python
import functools

import jax
import jax.numpy as jnp
from jax import lax
from jax.experimental import pallas as pl
from jax.experimental.pallas import tpu as pltpu
from jax.sharding import PartitionSpec as P

VT = 32
NVT = 2
W = 64
ORBITALS_IN_GRP = 16
PAIR_SQ = ORBITALS_IN_GRP * ORBITALS_IN_GRP
CODE_ROWS = 16
EXCHANGE_CODE_ROWS = 8
CODED_PARTS = 1
AT_ONCE = 2
SLAB_BITS = 14.0
TOP = 32700.0
STEPS = 8.0
VMEM_LIMIT = 56 * 1024 * 1024


def one_hot_of(target, amount):
    return (target[:, None] == jnp.arange(amount)[None, :]).astype(jnp.bfloat16)


def split(values):
    high = values.astype(jnp.bfloat16)
    return high, (values - high.astype(jnp.float32)).astype(jnp.bfloat16)


def dot(left, right):
    return jnp.dot(left, right, preferred_element_type=jnp.float32)


def scale_of(code):
    return jnp.exp2(code * (1.0 / STEPS))


def screen_kernel(part, int_mask, slab_ref, *refs):
    coded_refs, later_refs = refs[:CODED_PARTS], refs[CODED_PARTS:]
    slab_rows, slab_cols = slab_ref.shape
    coded_cols = coded_refs[0].shape[1]
    cols = coded_cols * CODED_PARTS
    span = slab_cols // W
    row_label = lax.axis_index("occ") * slab_rows // W // VT * NVT
    col_label = lax.axis_index("vir") * slab_cols // W // VT * NVT
    natural = lax.broadcasted_iota(jnp.int32, (slab_cols, 1), 0)
    a, b = natural // W, natural % W
    target = b // span * (part * span) + (a // part * part + b % part) * part + a % part
    place = lax.broadcasted_iota(jnp.int32, (slab_cols, cols), 1)
    to = lax.broadcasted_iota(jnp.int32, (1, cols), 1)
    second = lax.broadcasted_iota(jnp.int32, (slab_rows, 1), 0) % W >= VT
    for chunk in range(1 + len(later_refs)):
        right = to // (part * span) * span + chunk * part + to // part % part >= VT
        kept = [
            jnp.where(right, int_mask[label, col_label + 1], int_mask[label, col_label])
            for label in (row_label, row_label + 1)
        ]
        ones = place == jnp.where(b % span // part == chunk, target, -1)
        moved = dot(slab_ref[...], ones.astype(jnp.float32).astype(jnp.bfloat16))
        moved = jnp.where(jnp.where(second, kept[1], kept[0]) > 0, moved, 0.0)
        if chunk:
            later_refs[chunk - 1][...] = moved.astype(jnp.bfloat16)
        else:
            most = jnp.maximum(jnp.max(jnp.abs(moved), axis=0, keepdims=True), 1e-30)
            code = jnp.floor(jnp.log2(most)) + 1.0
            coded = jnp.round(moved * jnp.exp2(SLAB_BITS - code)).astype(jnp.int32).astype(jnp.int16)
            code_rows = jnp.broadcast_to(code.astype(jnp.int32), (CODE_ROWS, cols)).astype(jnp.int16)
            for n, coded_ref in enumerate(coded_refs):
                at = slice(n * coded_cols, (n + 1) * coded_cols)
                coded_ref[:slab_rows, :] = coded[:, at]
                coded_ref[slab_rows:, :] = code_rows[:, at]


def screen_call(chunks, int_mask, integrals):
    slab_rows, slab_cols = integrals.shape
    cols = slab_cols // chunks
    vmem = pl.BlockSpec(memory_space=pltpu.VMEM)
    return pl.pallas_call(
        functools.partial(screen_kernel, slab_cols // W // chunks),
        in_specs=[pl.BlockSpec(memory_space=pltpu.SMEM), vmem],
        out_specs=[vmem] * (CODED_PARTS + chunks - 1),
        out_shape=[jax.ShapeDtypeStruct((slab_rows + CODE_ROWS, cols // CODED_PARTS), jnp.int16)] * CODED_PARTS
        + [jax.ShapeDtypeStruct((slab_rows, cols), integrals.dtype)] * (chunks - 1),
        compiler_params=pltpu.CompilerParams(vmem_limit_bytes=VMEM_LIMIT),
        name="screen",
    )(int_mask, integrals)


def decode_slab(tile_total, coded_refs, stage, slab_scr, sems):
    slab_rows = slab_scr.shape[0] // tile_total
    coded_rows, cols = slab_rows + CODE_ROWS, coded_refs[0].shape[1]

    def copy_of(part, tile):
        at = pl.ds(pl.multiple_of(tile * coded_rows, CODE_ROWS), coded_rows)
        return pltpu.make_async_copy(coded_refs[part].at[at, :], stage.at[part, at, :], sems.at[part, tile])

    for tile in range(tile_total):
        for part in range(CODED_PARTS):
            copy_of(part, tile).start()

    def decode(tile, carry):
        at = pl.multiple_of(tile * coded_rows, CODE_ROWS)
        to = pl.ds(pl.multiple_of(tile * slab_rows, slab_rows), slab_rows)
        for part in range(CODED_PARTS):
            copy_of(part, tile).wait()
            code = stage[part, pl.ds(pl.multiple_of(at + slab_rows, CODE_ROWS), CODE_ROWS), :]
            values = stage[part, pl.ds(at, slab_rows), :].astype(jnp.int32).astype(jnp.float32)
            scale = jnp.exp2(code.astype(jnp.int32).astype(jnp.float32)[:1] - SLAB_BITS)
            slab_scr[to, part * cols : (part + 1) * cols] = (values * scale).astype(jnp.bfloat16)
        return carry

    lax.fori_loop(0, tile_total, decode, 0)


def ladder_kernel(tile_total, vir_count, chunks, tiles, dot_cols, coded, amp_mask, numbers, rows_ref, *refs):
    slab_refs, refs = (refs[:CODED_PARTS], refs[CODED_PARTS:]) if coded else (refs[:1], refs[1:])
    ladder_ref, packed_ref, product = refs[:3]
    step = pl.program_id(0)
    slab_ref = slab_refs[0]
    if coded:
        stage, slab_ref, sems = refs[3:]

        @pl.when(step == 0)
        def _():
            decode_slab(tile_total, slab_refs, stage, slab_ref, sems)
    cols = slab_ref.shape[1]
    block = cols // vir_count
    lanes = block // chunks

    pair = lax.broadcasted_iota(jnp.int32, (PAIR_SQ, 1), 0)
    own_number = numbers[lax.axis_index("occ")]
    for n in range(tiles):
        tile = jnp.maximum(step - 1, 0) * tiles + n
        rows = slice(n * PAIR_SQ, (n + 1) * PAIR_SQ)
        nonzero = (pair // ORBITALS_IN_GRP < own_number) & (pair % ORBITALS_IN_GRP < numbers[tile])
        ladder = jnp.where(nonzero, product[rows, :], 0.0)
        for h in range(chunks):
            ladder_ref[h, rows, :] = jnp.concatenate(
                [ladder[:, v * block + h * lanes : v * block + (h + 1) * lanes] for v in range(vir_count)], axis=1
            )
        by_place = ladder.reshape(ORBITALS_IN_GRP, ORBITALS_IN_GRP, cols)
        mirror = jnp.swapaxes(by_place, 0, 1).reshape(PAIR_SQ, cols)
        most = jnp.maximum(jnp.max(jnp.abs(ladder), axis=0, keepdims=True), 1e-30)
        code = jnp.ceil(jnp.log2(most) * STEPS)
        coded_rows = jnp.round(mirror * (TOP / scale_of(code))).astype(jnp.int32).astype(jnp.int16)
        code_rows = jnp.broadcast_to(code.astype(jnp.int32), (EXCHANGE_CODE_ROWS, cols)).astype(jnp.int16)
        for v in range(vir_count):
            packed_ref[n, v, :PAIR_SQ] = coded_rows[:, v * block : (v + 1) * block]
            packed_ref[n, v, PAIR_SQ:] = code_rows[:, v * block : (v + 1) * block]

    lane = lax.broadcasted_iota(jnp.int32, (1, W * W), 1)
    low = lane < W * VT
    left = lane % W < VT
    screened = []
    for n in range(tiles):
        tile = jnp.minimum(step * tiles + n, tile_total - 1)
        keep = jnp.where(
            low,
            jnp.where(left, amp_mask[tile, 0], amp_mask[tile, 1]),
            jnp.where(left, amp_mask[tile, 2], amp_mask[tile, 3]),
        )
        keep = keep.astype(jnp.float32).astype(jnp.bfloat16)
        screened.append(rows_ref[n * PAIR_SQ : (n + 1) * PAIR_SQ, :] * keep)
    screened = jnp.concatenate(screened, axis=0)
    for at in range(0, cols, dot_cols):
        product[:, at : at + dot_cols] = dot(screened, slab_ref[:, at : at + dot_cols])


def ladder_call(tile_total, vir_count, chunks, tiles, dot_cols, amp_mask, numbers, amplitudes, slab):
    coded = slab[0].dtype == jnp.int16
    cols = sum(part.shape[1] for part in slab)
    block = cols // vir_count
    smem = pl.BlockSpec(memory_space=pltpu.SMEM)
    rows = tile_total * PAIR_SQ
    steps = tile_total // tiles
    scratch = [pltpu.VMEM((tiles * PAIR_SQ, cols), jnp.float32)]
    slab_specs = [pl.BlockSpec((W * W, cols), lambda step: (0, 0))]
    if coded:
        slab_specs = [pl.BlockSpec(memory_space=pl.ANY)] * CODED_PARTS
        scratch += [
            pltpu.VMEM((CODED_PARTS,) + slab[0].shape, slab[0].dtype),
            pltpu.VMEM((W * W, cols), jnp.bfloat16),
            pltpu.SemaphoreType.DMA((CODED_PARTS, tile_total)),
        ]
    before = lambda step: jnp.maximum(step - 1, 0)
    packed_block = (vir_count, PAIR_SQ + EXCHANGE_CODE_ROWS, block)
    return pl.pallas_call(
        functools.partial(ladder_kernel, tile_total, vir_count, chunks, tiles, min(dot_cols, cols), coded),
        grid=(steps + 1,),
        in_specs=[
            smem,
            smem,
            pl.BlockSpec((tiles * PAIR_SQ, W * W), lambda step: (jnp.minimum(step, steps - 1), 0)),
            *slab_specs,
        ],
        out_specs=[
            pl.BlockSpec((chunks, tiles * PAIR_SQ, cols // chunks), lambda step: (0, before(step), 0)),
            pl.BlockSpec((tiles,) + packed_block, lambda step: (before(step), 0, 0, 0)),
        ],
        out_shape=[
            jax.ShapeDtypeStruct((chunks, rows, cols // chunks), jnp.float32),
            jax.ShapeDtypeStruct((tile_total,) + packed_block, jnp.int16),
        ],
        scratch_shapes=scratch,
        compiler_params=pltpu.CompilerParams(vmem_limit_bytes=VMEM_LIMIT),
        cost_estimate=pl.CostEstimate(
            flops=2 * rows * cols * W * W,
            bytes_accessed=rows * (W * W * 2 + cols * 6) + W * W * cols * 2,
            transcendentals=0,
        ),
        name="ladder",
    )(amp_mask, numbers, amplitudes, *slab)


def moved_columns(values, spread_ref):
    both = dot(jnp.concatenate(split(values), axis=0), spread_ref[...])
    return both[: values.shape[0]] + both[values.shape[0] :]


def direct_kernel(spread_ref, *refs):
    refs[-1][...] = moved_columns(jnp.concatenate([ref[0] for ref in refs[:-1]], axis=1), spread_ref)


def direct_call(chunk, spread, ladders):
    rows = ladders[0].shape[1]
    step_rows = AT_ONCE * PAIR_SQ
    return pl.pallas_call(
        direct_kernel,
        grid=(rows // step_rows,),
        in_specs=[pl.BlockSpec(spread.shape, lambda step: (0, 0))]
        + [pl.BlockSpec((1, step_rows, ladder.shape[2]), lambda step: (chunk, step, 0)) for ladder in ladders],
        out_specs=pl.BlockSpec((step_rows, spread.shape[1]), lambda step: (step, 0)),
        out_shape=jax.ShapeDtypeStruct((rows, spread.shape[1]), jnp.float32),
        compiler_params=pltpu.CompilerParams(vmem_limit_bytes=VMEM_LIMIT),
        cost_estimate=pl.CostEstimate(
            flops=4 * rows * spread.size, bytes_accessed=rows * spread.shape[1] * 8, transcendentals=0
        ),
        name="direct",
    )(spread, *ladders)


def update_kernel(vir_count, at_once, spread_ref, vir_ref, occ_ref, *refs):
    arrived_refs, refs = refs[:vir_count], refs[vir_count:]
    direct_refs = refs[:at_once]
    tiles = []
    for n in range(at_once):
        blocks = []
        for v in range(vir_count):
            code = arrived_refs[v][n, 0, PAIR_SQ:].astype(jnp.int32).astype(jnp.float32)[:1]
            values = arrived_refs[v][n, 0, :PAIR_SQ].astype(jnp.int32).astype(jnp.float32)
            blocks.append(values * (scale_of(code) * (1.0 / TOP)))
        tiles.append(jnp.concatenate(blocks, axis=1))
    mirror = moved_columns(jnp.concatenate(tiles, axis=0), spread_ref)
    for n, direct_ref in enumerate(direct_refs):
        at = slice(n * PAIR_SQ, (n + 1) * PAIR_SQ)
        refs[-1][at, :] = (direct_ref[...] + mirror[at]) / (vir_ref[...] - occ_ref[at, :1])


def update_call(chunk, chunks, at_once, arrived, spread, vir_sum, occ_sum, direct, earlier):
    cols = spread.shape[1]
    rows = direct.shape[0]
    step_rows = at_once * PAIR_SQ
    vir_count = arrived.shape[1]
    args = [spread, vir_sum, occ_sum] + [arrived] * vir_count + [direct] * at_once
    in_specs = [
        pl.BlockSpec(spread.shape, lambda step: (0, 0)),
        pl.BlockSpec((1, cols), lambda step: (0, chunk)),
        pl.BlockSpec((step_rows, 128), lambda step: (step, 0)),
    ]
    in_specs += [
        pl.BlockSpec((at_once, 1) + arrived.shape[2:], lambda step, v=v: (step, v, 0, 0)) for v in range(vir_count)
    ]
    in_specs += [pl.BlockSpec((PAIR_SQ, cols), lambda step, n=n: (step * at_once + n, 0)) for n in range(at_once)]
    aliases = {}
    if earlier is not None:
        aliases = {len(args): 0}
        args.append(earlier)
        in_specs.append(pl.BlockSpec(memory_space=pl.ANY))
    return pl.pallas_call(
        functools.partial(update_kernel, vir_count, at_once),
        grid=(rows // step_rows,),
        in_specs=in_specs,
        out_specs=pl.BlockSpec((step_rows, cols), lambda step: (step, chunk)),
        out_shape=jax.ShapeDtypeStruct((rows, chunks * cols), jnp.float32),
        input_output_aliases=aliases,
        compiler_params=pltpu.CompilerParams(vmem_limit_bytes=VMEM_LIMIT),
        cost_estimate=pl.CostEstimate(
            flops=4 * rows * spread.size, bytes_accessed=rows * cols * 10, transcendentals=0
        ),
        name="update",
    )(*args)


def body(amplitudes, amp_mask, integrals, int_mask, group_orbital_numbers, occ_energy, vir_energy):
    tile_total = lax.axis_size("occ")
    vir_count = lax.axis_size("vir")
    row_tile = lax.axis_index("occ")
    vir_place = lax.axis_index("vir")
    span = W // vir_count
    slab_cols = span * W
    chunks = 2 if span >= 16 else 1
    width = span // chunks
    block = width * span
    rows = PAIR_SQ + EXCHANGE_CODE_ROWS

    def exchanged(packed):
        moved = lax.all_to_all(
            packed.reshape(tile_total * vir_count, rows, block), ("occ", "vir"), split_axis=0, concat_axis=0, tiled=True
        )
        return moved.reshape(tile_total, vir_count, rows, block)

    parts = screen_call(chunks, int_mask, integrals)
    coded, later = parts[:CODED_PARTS], parts[CODED_PARTS:]
    first = lax.all_gather(coded[0], "occ", axis=0, tiled=True)
    *coded, first = lax.optimization_barrier((*coded[1:], first))
    slabs = [[first] + [lax.all_gather(part, "occ", axis=0, tiled=True) for part in coded]]
    for part in later:
        part, _ = lax.optimization_barrier((part, first))
        slabs.append([lax.all_gather(part, "occ", axis=0, tiled=True)])
    ladders, arrived = [], []
    for slab in slabs:
        tiles, dot_cols = (2, 512) if ladders else (1, 256)
        ladder, packed = ladder_call(
            tile_total, vir_count, chunks, tiles, dot_cols, amp_mask[0], group_orbital_numbers, amplitudes, slab
        )
        ladders.append(ladder)
        arrived.append(exchanged(packed))

    place = jnp.arange(vir_count * block)
    owner, there_part = place // block, place // (width * width) % chunks
    here, there = place // width % width, place % width
    mirror_spread = one_hot_of(here * W + owner * span + there_part * width + there, width * W)
    place = jnp.arange(vir_count * width * width)
    owner, b, a = place // (width * width), place // width % width, place % width
    direct_spread = one_hot_of(
        jnp.concatenate([a * W + owner * span + c * width + b for c in range(chunks)]), width * W
    )

    occ_table = occ_energy.reshape(tile_total, ORBITALS_IN_GRP)
    own_energy = lax.dynamic_slice_in_dim(occ_table, row_tile, 1, 0)[0]
    occ_sum = jnp.broadcast_to(
        (own_energy[None, :, None] + occ_table[:, None, :]).reshape(-1, 1), (tile_total * PAIR_SQ, 128)
    )
    vir_own = lax.dynamic_slice_in_dim(vir_energy, vir_place * span, span, 0)
    vir_sum = (vir_own[:, None] + vir_energy[None, :]).reshape(1, -1)
    update = None
    for chunk in range(chunks):
        direct = direct_call(chunk, direct_spread, ladders)
        update = update_call(chunk, chunks, 4 if chunk else 1, arrived[chunk], mirror_spread, vir_sum, occ_sum, direct, update)
    return update


def solution(mesh):
    in_specs = (P("occ", None), P("occ", None, None), P("occ", "vir"), P(), P(), P(), P())
    out_specs = P("occ", "vir")
    return jax.shard_map(body, mesh=mesh, in_specs=in_specs, out_specs=out_specs, check_vma=False)
```

```python
import functools

import jax
import jax.numpy as jnp
from jax import lax
from jax.experimental import pallas as pl
from jax.experimental.pallas import tpu as pltpu
from jax.sharding import PartitionSpec as P

VT = 32
NVT = 2
W = 64
ORBITALS_IN_GRP = 16
PAIR_SQ = ORBITALS_IN_GRP * ORBITALS_IN_GRP
CODE_ROWS = 16
EXCHANGE_CODE_ROWS = 8
CODED_PARTS = 1
AT_ONCE = 4
SLAB_BITS = 14.0
TOP = 32700.0
STEPS = 8.0
VMEM_LIMIT = 56 * 1024 * 1024
LADDER_VMEM_LIMIT = 30 * 1024 * 1024


def one_hot_of(target, amount):
    return (target[:, None] == jnp.arange(amount)[None, :]).astype(jnp.bfloat16)


def split(values):
    high = values.astype(jnp.bfloat16)
    return high, (values - high.astype(jnp.float32)).astype(jnp.bfloat16)


def dot(left, right):
    return jnp.dot(left, right, preferred_element_type=jnp.float32)


def scale_of(code):
    return jnp.exp2(code * (1.0 / STEPS))


def screen_kernel(part, int_mask, slab_ref, *refs):
    coded_refs, later_refs = refs[:CODED_PARTS], refs[CODED_PARTS:]
    slab_rows, slab_cols = slab_ref.shape
    coded_cols = coded_refs[0].shape[1]
    cols = coded_cols * CODED_PARTS
    span = slab_cols // W
    row_label = lax.axis_index("occ") * slab_rows // W // VT * NVT
    col_label = lax.axis_index("vir") * slab_cols // W // VT * NVT
    natural = lax.broadcasted_iota(jnp.int32, (slab_cols, 1), 0)
    a, b = natural // W, natural % W
    target = b // span * (part * span) + (a // part * part + b % part) * part + a % part
    place = lax.broadcasted_iota(jnp.int32, (slab_cols, cols), 1)
    to = lax.broadcasted_iota(jnp.int32, (1, cols), 1)
    second = lax.broadcasted_iota(jnp.int32, (slab_rows, 1), 0) % W >= VT
    for chunk in range(1 + len(later_refs)):
        right = to // (part * span) * span + chunk * part + to // part % part >= VT
        kept = [
            jnp.where(right, int_mask[label, col_label + 1], int_mask[label, col_label])
            for label in (row_label, row_label + 1)
        ]
        ones = place == jnp.where(b % span // part == chunk, target, -1)
        moved = dot(slab_ref[...], ones.astype(jnp.float32).astype(jnp.bfloat16))
        moved = jnp.where(jnp.where(second, kept[1], kept[0]) > 0, moved, 0.0)
        if chunk:
            later_refs[chunk - 1][...] = moved.astype(jnp.bfloat16)
        else:
            most = jnp.maximum(jnp.max(jnp.abs(moved), axis=0, keepdims=True), 1e-30)
            code = jnp.floor(jnp.log2(most)) + 1.0
            coded = jnp.round(moved * jnp.exp2(SLAB_BITS - code)).astype(jnp.int32).astype(jnp.int16)
            code_rows = jnp.broadcast_to(code.astype(jnp.int32), (CODE_ROWS, cols)).astype(jnp.int16)
            for n, coded_ref in enumerate(coded_refs):
                at = slice(n * coded_cols, (n + 1) * coded_cols)
                coded_ref[:slab_rows, :] = coded[:, at]
                coded_ref[slab_rows:, :] = code_rows[:, at]


def screen_call(chunks, int_mask, integrals):
    slab_rows, slab_cols = integrals.shape
    cols = slab_cols // chunks
    vmem = pl.BlockSpec(memory_space=pltpu.VMEM)
    return pl.pallas_call(
        functools.partial(screen_kernel, slab_cols // W // chunks),
        in_specs=[pl.BlockSpec(memory_space=pltpu.SMEM), vmem],
        out_specs=[vmem] * (CODED_PARTS + chunks - 1),
        out_shape=[jax.ShapeDtypeStruct((slab_rows + CODE_ROWS, cols // CODED_PARTS), jnp.int16)] * CODED_PARTS
        + [jax.ShapeDtypeStruct((slab_rows, cols), integrals.dtype)] * (chunks - 1),
        compiler_params=pltpu.CompilerParams(vmem_limit_bytes=VMEM_LIMIT),
        name="screen",
    )(int_mask, integrals)


def decode_slab(tile_total, coded_refs, stage, slab_scr, sems):
    slab_rows = slab_scr.shape[0] // tile_total
    coded_rows, cols = slab_rows + CODE_ROWS, coded_refs[0].shape[1]

    def copy_of(part, tile):
        at = pl.ds(pl.multiple_of(tile * coded_rows, CODE_ROWS), coded_rows)
        return pltpu.make_async_copy(coded_refs[part].at[at, :], stage.at[part, at, :], sems.at[part, tile])

    for tile in range(tile_total):
        for part in range(CODED_PARTS):
            copy_of(part, tile).start()

    def decode(tile, carry):
        at = pl.multiple_of(tile * coded_rows, CODE_ROWS)
        to = pl.ds(pl.multiple_of(tile * slab_rows, slab_rows), slab_rows)
        for part in range(CODED_PARTS):
            copy_of(part, tile).wait()
            code = stage[part, pl.ds(pl.multiple_of(at + slab_rows, CODE_ROWS), CODE_ROWS), :]
            values = stage[part, pl.ds(at, slab_rows), :].astype(jnp.int32).astype(jnp.float32)
            scale = jnp.exp2(code.astype(jnp.int32).astype(jnp.float32)[:1] - SLAB_BITS)
            slab_scr[to, part * cols : (part + 1) * cols] = (values * scale).astype(jnp.bfloat16)
        return carry

    lax.fori_loop(0, tile_total, decode, 0)


def ladder_kernel(tile_total, vir_count, chunks, tiles, dot_cols, coded, amp_mask, numbers, all_rows_ref, *refs):
    slab_refs, refs = (refs[:CODED_PARTS], refs[CODED_PARTS:]) if coded else (refs[:1], refs[1:])
    ladder_ref, packed_ref, product, rows_scr, rows_sems = refs[:5]
    step = pl.program_id(0)
    slab_ref = slab_refs[0]
    if coded:
        stage, slab_ref, sems = refs[5:]
    steps = tile_total // tiles

    def rows_copy(at_step):
        at = pl.ds(pl.multiple_of(at_step * (tiles * PAIR_SQ), PAIR_SQ), tiles * PAIR_SQ)
        slot = lax.rem(at_step, 2)
        return pltpu.make_async_copy(all_rows_ref.at[at, :], rows_scr.at[slot], rows_sems.at[slot])

    @pl.when(step == 0)
    def _():
        rows_copy(0).start()

    @pl.when(step + 1 < steps)
    def _():
        rows_copy(step + 1).start()

    if coded:

        @pl.when(step == 0)
        def _():
            decode_slab(tile_total, slab_refs, stage, slab_ref, sems)

    @pl.when(step < steps)
    def _():
        rows_copy(step).wait()

    cols = slab_ref.shape[1]
    block = cols // vir_count
    lanes = block // chunks
    rows_ref = rows_scr.at[lax.rem(jnp.minimum(step, steps - 1), 2)]

    pair = lax.broadcasted_iota(jnp.int32, (PAIR_SQ, 1), 0)
    own_number = numbers[lax.axis_index("occ")]
    for n in range(tiles):
        tile = jnp.maximum(step - 1, 0) * tiles + n
        rows = slice(n * PAIR_SQ, (n + 1) * PAIR_SQ)
        nonzero = (pair // ORBITALS_IN_GRP < own_number) & (pair % ORBITALS_IN_GRP < numbers[tile])
        ladder = jnp.where(nonzero, product[rows, :], 0.0)
        for h in range(chunks):
            ladder_ref[h, rows, :] = jnp.concatenate(
                [ladder[:, v * block + h * lanes : v * block + (h + 1) * lanes] for v in range(vir_count)], axis=1
            )
        by_place = ladder.reshape(ORBITALS_IN_GRP, ORBITALS_IN_GRP, cols)
        mirror = jnp.swapaxes(by_place, 0, 1).reshape(PAIR_SQ, cols)
        most = jnp.maximum(jnp.max(jnp.abs(ladder), axis=0, keepdims=True), 1e-30)
        code = jnp.ceil(jnp.log2(most) * STEPS)
        coded_rows = jnp.round(mirror * (TOP / scale_of(code))).astype(jnp.int32).astype(jnp.int16)
        code_rows = jnp.broadcast_to(code.astype(jnp.int32), (EXCHANGE_CODE_ROWS, cols)).astype(jnp.int16)
        for v in range(vir_count):
            packed_ref[n, v, :PAIR_SQ] = coded_rows[:, v * block : (v + 1) * block]
            packed_ref[n, v, PAIR_SQ:] = code_rows[:, v * block : (v + 1) * block]

    lane = lax.broadcasted_iota(jnp.int32, (1, W * W), 1)
    low = lane < W * VT
    left = lane % W < VT
    screened = []
    for n in range(tiles):
        tile = jnp.minimum(step * tiles + n, tile_total - 1)
        keep = jnp.where(
            low,
            jnp.where(left, amp_mask[tile, 0], amp_mask[tile, 1]),
            jnp.where(left, amp_mask[tile, 2], amp_mask[tile, 3]),
        )
        keep = keep.astype(jnp.float32).astype(jnp.bfloat16)
        screened.append(rows_ref[n * PAIR_SQ : (n + 1) * PAIR_SQ, :] * keep)
    screened = jnp.concatenate(screened, axis=0)
    for at in range(0, cols, dot_cols):
        product[:, at : at + dot_cols] = dot(screened, slab_ref[:, at : at + dot_cols])


def ladder_call(tile_total, vir_count, chunks, tiles, dot_cols, amp_mask, numbers, amplitudes, slab):
    coded = slab[0].dtype == jnp.int16
    cols = sum(part.shape[1] for part in slab)
    block = cols // vir_count
    smem = pl.BlockSpec(memory_space=pltpu.SMEM)
    rows = tile_total * PAIR_SQ
    steps = tile_total // tiles
    scratch = [
        pltpu.VMEM((tiles * PAIR_SQ, cols), jnp.float32),
        pltpu.VMEM((2, tiles * PAIR_SQ, W * W), jnp.bfloat16),
        pltpu.SemaphoreType.DMA((2,)),
    ]
    slab_specs = [pl.BlockSpec((W * W, cols), lambda step: (0, 0))]
    if coded:
        slab_specs = [pl.BlockSpec(memory_space=pl.ANY)] * CODED_PARTS
        scratch += [
            pltpu.VMEM((CODED_PARTS,) + slab[0].shape, slab[0].dtype),
            pltpu.VMEM((W * W, cols), jnp.bfloat16),
            pltpu.SemaphoreType.DMA((CODED_PARTS, tile_total)),
        ]
    before = lambda step: jnp.maximum(step - 1, 0)
    packed_block = (vir_count, PAIR_SQ + EXCHANGE_CODE_ROWS, block)
    return pl.pallas_call(
        functools.partial(ladder_kernel, tile_total, vir_count, chunks, tiles, min(dot_cols, cols), coded),
        grid=(steps + 1,),
        in_specs=[
            smem,
            smem,
            pl.BlockSpec(memory_space=pl.ANY),
            *slab_specs,
        ],
        out_specs=[
            pl.BlockSpec((chunks, tiles * PAIR_SQ, cols // chunks), lambda step: (0, before(step), 0)),
            pl.BlockSpec((tiles,) + packed_block, lambda step: (before(step), 0, 0, 0)),
        ],
        out_shape=[
            jax.ShapeDtypeStruct((chunks, rows, cols // chunks), jnp.float32),
            jax.ShapeDtypeStruct((tile_total,) + packed_block, jnp.int16),
        ],
        scratch_shapes=scratch,
        compiler_params=pltpu.CompilerParams(vmem_limit_bytes=LADDER_VMEM_LIMIT),
        cost_estimate=pl.CostEstimate(
            flops=2 * rows * cols * W * W,
            bytes_accessed=rows * (W * W * 2 + cols * 6) + W * W * cols * 2,
            transcendentals=0,
        ),
        name="ladder",
    )(amp_mask, numbers, amplitudes, *slab)


def moved_columns(values, spread_ref):
    both = dot(jnp.concatenate(split(values), axis=0), spread_ref[...])
    return both[: values.shape[0]] + both[values.shape[0] :]


def direct_kernel(spread_ref, *refs):
    refs[-1][...] = moved_columns(jnp.concatenate([ref[0] for ref in refs[:-1]], axis=1), spread_ref)


def direct_call(chunk, spread, ladders):
    rows = ladders[0].shape[1]
    step_rows = AT_ONCE * PAIR_SQ
    return pl.pallas_call(
        direct_kernel,
        grid=(rows // step_rows,),
        in_specs=[pl.BlockSpec(spread.shape, lambda step: (0, 0))]
        + [pl.BlockSpec((1, step_rows, ladder.shape[2]), lambda step: (chunk, step, 0)) for ladder in ladders],
        out_specs=pl.BlockSpec((step_rows, spread.shape[1]), lambda step: (step, 0)),
        out_shape=jax.ShapeDtypeStruct((rows, spread.shape[1]), jnp.float32),
        compiler_params=pltpu.CompilerParams(vmem_limit_bytes=VMEM_LIMIT),
        cost_estimate=pl.CostEstimate(
            flops=4 * rows * spread.size, bytes_accessed=rows * spread.shape[1] * 8, transcendentals=0
        ),
        name="direct",
    )(spread, *ladders)


def update_kernel(vir_count, at_once, spread_ref, vir_ref, occ_ref, *refs):
    arrived_refs, refs = refs[:vir_count], refs[vir_count:]
    direct_refs = refs[:at_once]
    tiles = []
    for n in range(at_once):
        blocks = []
        for v in range(vir_count):
            code = arrived_refs[v][n, 0, PAIR_SQ:].astype(jnp.int32).astype(jnp.float32)[:1]
            values = arrived_refs[v][n, 0, :PAIR_SQ].astype(jnp.int32).astype(jnp.float32)
            blocks.append(values * (scale_of(code) * (1.0 / TOP)))
        tiles.append(jnp.concatenate(blocks, axis=1))
    mirror = moved_columns(jnp.concatenate(tiles, axis=0), spread_ref)
    for n, direct_ref in enumerate(direct_refs):
        at = slice(n * PAIR_SQ, (n + 1) * PAIR_SQ)
        refs[-1][at, :] = (direct_ref[...] + mirror[at]) / (vir_ref[...] - occ_ref[at, :1])


def update_call(chunk, chunks, at_once, arrived, spread, vir_sum, occ_sum, direct, earlier):
    cols = spread.shape[1]
    rows = direct.shape[0]
    step_rows = at_once * PAIR_SQ
    vir_count = arrived.shape[1]
    args = [spread, vir_sum, occ_sum] + [arrived] * vir_count + [direct] * at_once
    in_specs = [
        pl.BlockSpec(spread.shape, lambda step: (0, 0)),
        pl.BlockSpec((1, cols), lambda step: (0, chunk)),
        pl.BlockSpec((step_rows, 128), lambda step: (step, 0)),
    ]
    in_specs += [
        pl.BlockSpec((at_once, 1) + arrived.shape[2:], lambda step, v=v: (step, v, 0, 0)) for v in range(vir_count)
    ]
    in_specs += [pl.BlockSpec((PAIR_SQ, cols), lambda step, n=n: (step * at_once + n, 0)) for n in range(at_once)]
    aliases = {}
    if earlier is not None:
        aliases = {len(args): 0}
        args.append(earlier)
        in_specs.append(pl.BlockSpec(memory_space=pl.ANY))
    return pl.pallas_call(
        functools.partial(update_kernel, vir_count, at_once),
        grid=(rows // step_rows,),
        in_specs=in_specs,
        out_specs=pl.BlockSpec((step_rows, cols), lambda step: (step, chunk)),
        out_shape=jax.ShapeDtypeStruct((rows, chunks * cols), jnp.float32),
        input_output_aliases=aliases,
        compiler_params=pltpu.CompilerParams(vmem_limit_bytes=VMEM_LIMIT),
        cost_estimate=pl.CostEstimate(
            flops=4 * rows * spread.size, bytes_accessed=rows * cols * 10, transcendentals=0
        ),
        name="update",
    )(*args)


def body(amplitudes, amp_mask, integrals, int_mask, group_orbital_numbers, occ_energy, vir_energy):
    tile_total = lax.axis_size("occ")
    vir_count = lax.axis_size("vir")
    row_tile = lax.axis_index("occ")
    vir_place = lax.axis_index("vir")
    span = W // vir_count
    slab_cols = span * W
    chunks = 2 if span >= 16 else 1
    width = span // chunks
    block = width * span
    rows = PAIR_SQ + EXCHANGE_CODE_ROWS

    def exchanged(packed):
        moved = lax.all_to_all(
            packed.reshape(tile_total * vir_count, rows, block), ("occ", "vir"), split_axis=0, concat_axis=0, tiled=True
        )
        return moved.reshape(tile_total, vir_count, rows, block)

    parts = screen_call(chunks, int_mask, integrals)
    coded, later = parts[:CODED_PARTS], parts[CODED_PARTS:]
    first = lax.all_gather(coded[0], "occ", axis=0, tiled=True)
    *coded, first = lax.optimization_barrier((*coded[1:], first))
    slabs = [[first] + [lax.all_gather(part, "occ", axis=0, tiled=True) for part in coded]]
    for part in later:
        part, _ = lax.optimization_barrier((part, first))
        slabs.append([lax.all_gather(part, "occ", axis=0, tiled=True)])
    ladders, arrived = [], []
    for slab in slabs:
        tiles, dot_cols = (1, 512)
        ladder, packed = ladder_call(
            tile_total, vir_count, chunks, tiles, dot_cols, amp_mask[0], group_orbital_numbers, amplitudes, slab
        )
        ladders.append(ladder)
        arrived.append(exchanged(packed))

    place = jnp.arange(vir_count * block)
    owner, there_part = place // block, place // (width * width) % chunks
    here, there = place // width % width, place % width
    mirror_spread = one_hot_of(here * W + owner * span + there_part * width + there, width * W)
    place = jnp.arange(vir_count * width * width)
    owner, b, a = place // (width * width), place // width % width, place % width
    direct_spread = one_hot_of(
        jnp.concatenate([a * W + owner * span + c * width + b for c in range(chunks)]), width * W
    )

    occ_table = occ_energy.reshape(tile_total, ORBITALS_IN_GRP)
    own_energy = lax.dynamic_slice_in_dim(occ_table, row_tile, 1, 0)[0]
    occ_sum = jnp.broadcast_to(
        (own_energy[None, :, None] + occ_table[:, None, :]).reshape(-1, 1), (tile_total * PAIR_SQ, 128)
    )
    vir_own = lax.dynamic_slice_in_dim(vir_energy, vir_place * span, span, 0)
    vir_sum = (vir_own[:, None] + vir_energy[None, :]).reshape(1, -1)
    update = None
    for chunk in range(chunks):
        direct = direct_call(chunk, direct_spread, ladders)
        update = update_call(chunk, chunks, 4, arrived[chunk], mirror_spread, vir_sum, occ_sum, direct, update)
    return update


def solution(mesh):
    in_specs = (P("occ", None), P("occ", None, None), P("occ", "vir"), P(), P(), P(), P())
    out_specs = P("occ", "vir")
    return jax.shard_map(body, mesh=mesh, in_specs=in_specs, out_specs=out_specs, check_vma=False)
```

```python
import functools

import jax
import jax.numpy as jnp
from jax import lax
from jax.experimental import pallas as pl
from jax.experimental.pallas import tpu as pltpu
from jax.sharding import PartitionSpec as P

VT = 32
NVT = 2
W = 64
ORBITALS_IN_GRP = 16
PAIR_SQ = ORBITALS_IN_GRP * ORBITALS_IN_GRP
CODE_ROWS = 16
EXCHANGE_CODE_ROWS = 8
AT_ONCE = 4
SLAB_BITS = 14.0
TOP = 32700.0
STEPS = 8.0
VMEM_LIMIT = 56 * 1024 * 1024


def one_hot_of(target, amount):
    return (target[:, None] == jnp.arange(amount)[None, :]).astype(jnp.bfloat16)


def split(values):
    high = values.astype(jnp.bfloat16)
    return high, (values - high.astype(jnp.float32)).astype(jnp.bfloat16)


def dot(left, right):
    return jnp.dot(left, right, preferred_element_type=jnp.float32)


def scale_of(code):
    return jnp.exp2(code * (1.0 / STEPS))


def screen_kernel(part, int_mask, slab_ref, coded_ref, *later_refs):
    slab_rows, slab_cols = slab_ref.shape
    cols = coded_ref.shape[1]
    span = slab_cols // W
    row_label = lax.axis_index("occ") * slab_rows // W // VT * NVT
    col_label = lax.axis_index("vir") * slab_cols // W // VT * NVT
    natural = lax.broadcasted_iota(jnp.int32, (slab_cols, 1), 0)
    a, b = natural // W, natural % W
    target = b // span * (part * span) + (a // part * part + b % part) * part + a % part
    place = lax.broadcasted_iota(jnp.int32, (slab_cols, cols), 1)
    to = lax.broadcasted_iota(jnp.int32, (1, cols), 1)
    second = lax.broadcasted_iota(jnp.int32, (slab_rows, 1), 0) % W >= VT
    for chunk in range(1 + len(later_refs)):
        right = to // (part * span) * span + chunk * part + to // part % part >= VT
        kept = [
            jnp.where(right, int_mask[label, col_label + 1], int_mask[label, col_label])
            for label in (row_label, row_label + 1)
        ]
        ones = place == jnp.where(b % span // part == chunk, target, -1)
        moved = dot(slab_ref[...], ones.astype(jnp.float32).astype(jnp.bfloat16))
        moved = jnp.where(jnp.where(second, kept[1], kept[0]) > 0, moved, 0.0)
        if chunk:
            later_refs[chunk - 1][...] = moved.astype(jnp.bfloat16)
        else:
            most = jnp.maximum(jnp.max(jnp.abs(moved), axis=0, keepdims=True), 1e-30)
            code = jnp.floor(jnp.log2(most)) + 1.0
            coded = jnp.round(moved * jnp.exp2(SLAB_BITS - code)).astype(jnp.int32).astype(jnp.int16)
            code_rows = jnp.broadcast_to(code.astype(jnp.int32), (CODE_ROWS, cols)).astype(jnp.int16)
            coded_ref[:slab_rows, :] = coded
            coded_ref[slab_rows:, :] = code_rows


def screen_call(chunks, int_mask, integrals):
    slab_rows, slab_cols = integrals.shape
    cols = slab_cols // chunks
    vmem = pl.BlockSpec(memory_space=pltpu.VMEM)
    return pl.pallas_call(
        functools.partial(screen_kernel, slab_cols // W // chunks),
        in_specs=[pl.BlockSpec(memory_space=pltpu.SMEM), vmem],
        out_specs=[vmem] * chunks,
        out_shape=[jax.ShapeDtypeStruct((slab_rows + CODE_ROWS, cols), jnp.int16)]
        + [jax.ShapeDtypeStruct((slab_rows, cols), integrals.dtype)] * (chunks - 1),
        compiler_params=pltpu.CompilerParams(vmem_limit_bytes=VMEM_LIMIT),
        name="screen",
    )(int_mask, integrals)


def ladder_kernel(tile_total, vir_count, chunks, coded, amp_mask, numbers, rows_ref, gathered_ref, *refs):
    ladder_ref, packed_ref, product, slab_scr, sems = refs[:5]
    stage = refs[5] if coded else slab_scr
    step = pl.program_id(0)
    cols = slab_scr.shape[1]
    slab_rows = slab_scr.shape[0] // tile_total
    shard_rows = stage.shape[0] // tile_total
    block = cols // vir_count
    lanes = block // chunks

    def masks(tile, at, width):
        lane = lax.broadcasted_iota(jnp.int32, (1, width), 1) + at
        left = lane % W < VT
        keep = jnp.where(
            lane < W * VT,
            jnp.where(left, amp_mask[tile, 0], amp_mask[tile, 1]),
            jnp.where(left, amp_mask[tile, 2], amp_mask[tile, 3]),
        )
        return keep.astype(jnp.float32).astype(jnp.bfloat16)

    def finish():
        tile = step - 1
        pair = lax.broadcasted_iota(jnp.int32, (PAIR_SQ, 1), 0)
        own_number = numbers[lax.axis_index("occ")]
        nonzero = (pair // ORBITALS_IN_GRP < own_number) & (pair % ORBITALS_IN_GRP < numbers[tile])
        ladder = jnp.where(nonzero, product[...], 0.0)
        for h in range(chunks):
            ladder_ref[h] = jnp.concatenate(
                [ladder[:, v * block + h * lanes : v * block + (h + 1) * lanes] for v in range(vir_count)], axis=1
            )
        by_place = ladder.reshape(ORBITALS_IN_GRP, ORBITALS_IN_GRP, cols)
        mirror = jnp.swapaxes(by_place, 0, 1).reshape(PAIR_SQ, cols)
        most = jnp.maximum(jnp.max(jnp.abs(ladder), axis=0, keepdims=True), 1e-30)
        code = jnp.ceil(jnp.log2(most) * STEPS)
        coded_rows = jnp.round(mirror * (TOP / scale_of(code))).astype(jnp.int32).astype(jnp.int16)
        code_rows = jnp.broadcast_to(code.astype(jnp.int32), (EXCHANGE_CODE_ROWS, cols)).astype(jnp.int16)
        for v in range(vir_count):
            packed_ref[0, v, :PAIR_SQ] = coded_rows[:, v * block : (v + 1) * block]
            packed_ref[0, v, PAIR_SQ:] = code_rows[:, v * block : (v + 1) * block]

    @pl.when(step == 0)
    def _():
        def copy_of(shard):
            at = pl.ds(pl.multiple_of(shard * shard_rows, CODE_ROWS), shard_rows)
            return pltpu.make_async_copy(gathered_ref.at[at, :], stage.at[at, :], sems.at[shard])

        for shard in range(tile_total):
            copy_of(shard).start()
        product[...] = jnp.zeros_like(product)

        def use(shard, carry):
            copy_of(shard).wait()
            to = pl.ds(pl.multiple_of(shard * slab_rows, slab_rows), slab_rows)
            if coded:
                at = pl.multiple_of(shard * shard_rows, CODE_ROWS)
                code = stage[pl.ds(pl.multiple_of(at + slab_rows, CODE_ROWS), CODE_ROWS), :]
                values = stage[pl.ds(at, slab_rows), :].astype(jnp.int32).astype(jnp.float32)
                scale = jnp.exp2(code.astype(jnp.int32).astype(jnp.float32)[:1] - SLAB_BITS)
                slab_scr[to, :] = (values * scale).astype(jnp.bfloat16)
            screened = rows_ref[:, to] * masks(0, shard * slab_rows, slab_rows)
            product[...] += dot(screened, slab_scr[to, :])
            return carry

        lax.fori_loop(0, tile_total, use, 0)

    @pl.when((step > 0) & (step < tile_total))
    def _():
        finish()
        product[...] = dot(rows_ref[...] * masks(step, 0, W * W), slab_scr[...])

    @pl.when(step == tile_total)
    def _():
        finish()


def ladder_call(tile_total, vir_count, chunks, amp_mask, numbers, amplitudes, slab):
    coded = slab.dtype == jnp.int16
    cols = slab.shape[1]
    block = cols // vir_count
    smem = pl.BlockSpec(memory_space=pltpu.SMEM)
    rows = tile_total * PAIR_SQ
    before = lambda step: jnp.maximum(step - 1, 0)
    packed_block = (vir_count, PAIR_SQ + EXCHANGE_CODE_ROWS, block)
    return pl.pallas_call(
        functools.partial(ladder_kernel, tile_total, vir_count, chunks, coded),
        grid=(tile_total + 1,),
        in_specs=[
            smem,
            smem,
            pl.BlockSpec((PAIR_SQ, W * W), lambda step: (jnp.minimum(step, tile_total - 1), 0)),
            pl.BlockSpec(memory_space=pl.ANY),
        ],
        out_specs=[
            pl.BlockSpec((chunks, PAIR_SQ, cols // chunks), lambda step: (0, before(step), 0)),
            pl.BlockSpec((1,) + packed_block, lambda step: (before(step), 0, 0, 0)),
        ],
        out_shape=[
            jax.ShapeDtypeStruct((chunks, rows, cols // chunks), jnp.float32),
            jax.ShapeDtypeStruct((tile_total,) + packed_block, jnp.int16),
        ],
        scratch_shapes=[
            pltpu.VMEM((PAIR_SQ, cols), jnp.float32),
            pltpu.VMEM((W * W, cols), jnp.bfloat16),
            pltpu.SemaphoreType.DMA((tile_total,)),
        ]
        + [pltpu.VMEM(slab.shape, slab.dtype)] * coded,
        compiler_params=pltpu.CompilerParams(vmem_limit_bytes=VMEM_LIMIT),
        cost_estimate=pl.CostEstimate(
            flops=2 * rows * cols * W * W,
            bytes_accessed=rows * (W * W * 2 + cols * 6) + W * W * cols * 2,
            transcendentals=0,
        ),
        name="ladder",
    )(amp_mask, numbers, amplitudes, slab)


def moved_columns(values, spread_ref):
    both = dot(jnp.concatenate(split(values), axis=0), spread_ref[...])
    return both[: values.shape[0]] + both[values.shape[0] :]


def direct_kernel(spread_ref, *refs):
    refs[-1][...] = moved_columns(jnp.concatenate([ref[0] for ref in refs[:-1]], axis=1), spread_ref)


def direct_call(chunk, spread, ladders):
    rows = ladders[0].shape[1]
    step_rows = AT_ONCE * PAIR_SQ
    return pl.pallas_call(
        direct_kernel,
        grid=(rows // step_rows,),
        in_specs=[pl.BlockSpec(spread.shape, lambda step: (0, 0))]
        + [pl.BlockSpec((1, step_rows, ladder.shape[2]), lambda step: (chunk, step, 0)) for ladder in ladders],
        out_specs=pl.BlockSpec((step_rows, spread.shape[1]), lambda step: (step, 0)),
        out_shape=jax.ShapeDtypeStruct((rows, spread.shape[1]), jnp.float32),
        compiler_params=pltpu.CompilerParams(vmem_limit_bytes=VMEM_LIMIT),
        cost_estimate=pl.CostEstimate(
            flops=4 * rows * spread.size, bytes_accessed=rows * spread.shape[1] * 8, transcendentals=0
        ),
        name="direct",
    )(spread, *ladders)


def update_kernel(vir_count, at_once, spread_ref, vir_ref, occ_ref, *refs):
    arrived_refs, refs = refs[:vir_count], refs[vir_count:]
    direct_refs = refs[:at_once]
    tiles = []
    for n in range(at_once):
        blocks = []
        for v in range(vir_count):
            code = arrived_refs[v][n, 0, PAIR_SQ:].astype(jnp.int32).astype(jnp.float32)[:1]
            values = arrived_refs[v][n, 0, :PAIR_SQ].astype(jnp.int32).astype(jnp.float32)
            blocks.append(values * (scale_of(code) * (1.0 / TOP)))
        tiles.append(jnp.concatenate(blocks, axis=1))
    mirror = moved_columns(jnp.concatenate(tiles, axis=0), spread_ref)
    for n, direct_ref in enumerate(direct_refs):
        at = slice(n * PAIR_SQ, (n + 1) * PAIR_SQ)
        refs[-1][at, :] = (direct_ref[...] + mirror[at]) / (vir_ref[...] - occ_ref[at, :1])


def update_call(chunk, chunks, at_once, arrived, spread, vir_sum, occ_sum, direct, earlier):
    cols = spread.shape[1]
    rows = direct.shape[0]
    step_rows = at_once * PAIR_SQ
    vir_count = arrived.shape[1]
    args = [spread, vir_sum, occ_sum] + [arrived] * vir_count + [direct] * at_once
    in_specs = [
        pl.BlockSpec(spread.shape, lambda step: (0, 0)),
        pl.BlockSpec((1, cols), lambda step: (0, chunk)),
        pl.BlockSpec((step_rows, 128), lambda step: (step, 0)),
    ]
    in_specs += [
        pl.BlockSpec((at_once, 1) + arrived.shape[2:], lambda step, v=v: (step, v, 0, 0)) for v in range(vir_count)
    ]
    in_specs += [pl.BlockSpec((PAIR_SQ, cols), lambda step, n=n: (step * at_once + n, 0)) for n in range(at_once)]
    aliases = {}
    if earlier is not None:
        aliases = {len(args): 0}
        args.append(earlier)
        in_specs.append(pl.BlockSpec(memory_space=pl.ANY))
    return pl.pallas_call(
        functools.partial(update_kernel, vir_count, at_once),
        grid=(rows // step_rows,),
        in_specs=in_specs,
        out_specs=pl.BlockSpec((step_rows, cols), lambda step: (step, chunk)),
        out_shape=jax.ShapeDtypeStruct((rows, chunks * cols), jnp.float32),
        input_output_aliases=aliases,
        compiler_params=pltpu.CompilerParams(vmem_limit_bytes=VMEM_LIMIT),
        cost_estimate=pl.CostEstimate(
            flops=4 * rows * spread.size, bytes_accessed=rows * cols * 10, transcendentals=0
        ),
        name="update",
    )(*args)


def body(amplitudes, amp_mask, integrals, int_mask, group_orbital_numbers, occ_energy, vir_energy):
    tile_total = lax.axis_size("occ")
    vir_count = lax.axis_size("vir")
    row_tile = lax.axis_index("occ")
    vir_place = lax.axis_index("vir")
    span = W // vir_count
    slab_cols = span * W
    chunks = 2 if span >= 16 else 1
    width = span // chunks
    block = width * span
    rows = PAIR_SQ + EXCHANGE_CODE_ROWS

    def exchanged(packed):
        moved = lax.all_to_all(
            packed.reshape(tile_total * vir_count, rows, block), ("occ", "vir"), split_axis=0, concat_axis=0, tiled=True
        )
        return moved.reshape(tile_total, vir_count, rows, block)

    coded, *later = screen_call(chunks, int_mask, integrals)
    slabs = [lax.all_gather(coded, "occ", axis=0, tiled=True)]
    for part in later:
        part, _ = lax.optimization_barrier((part, slabs[-1]))
        slabs.append(lax.all_gather(part, "occ", axis=0, tiled=True))
    ladders, arrived = [], []
    for slab in slabs:
        ladder, packed = ladder_call(
            tile_total, vir_count, chunks, amp_mask[0], group_orbital_numbers, amplitudes, slab
        )
        ladders.append(ladder)
        arrived.append(exchanged(packed))

    place = jnp.arange(vir_count * block)
    owner, there_part = place // block, place // (width * width) % chunks
    here, there = place // width % width, place % width
    mirror_spread = one_hot_of(here * W + owner * span + there_part * width + there, width * W)
    place = jnp.arange(vir_count * width * width)
    owner, b, a = place // (width * width), place // width % width, place % width
    direct_spread = one_hot_of(
        jnp.concatenate([a * W + owner * span + c * width + b for c in range(chunks)]), width * W
    )

    occ_table = occ_energy.reshape(tile_total, ORBITALS_IN_GRP)
    own_energy = lax.dynamic_slice_in_dim(occ_table, row_tile, 1, 0)[0]
    occ_sum = jnp.broadcast_to(
        (own_energy[None, :, None] + occ_table[:, None, :]).reshape(-1, 1), (tile_total * PAIR_SQ, 128)
    )
    vir_own = lax.dynamic_slice_in_dim(vir_energy, vir_place * span, span, 0)
    vir_sum = (vir_own[:, None] + vir_energy[None, :]).reshape(1, -1)
    update = None
    for chunk in range(chunks):
        direct = direct_call(chunk, direct_spread, ladders)
        update = update_call(chunk, chunks, 4, arrived[chunk], mirror_spread, vir_sum, occ_sum, direct, update)
    return update


def solution(mesh):
    in_specs = (P("occ", None), P("occ", None, None), P("occ", "vir"), P(), P(), P(), P())
    out_specs = P("occ", "vir")
    return jax.shard_map(body, mesh=mesh, in_specs=in_specs, out_specs=out_specs, check_vma=False)
```

```python
import functools

import jax
import jax.numpy as jnp
from jax import lax
from jax.experimental import pallas as pl
from jax.experimental.pallas import tpu as pltpu
from jax.sharding import PartitionSpec as P

VT = 32
NVT = 2
W = 64
ORBITALS_IN_GRP = 16
PAIR_SQ = ORBITALS_IN_GRP * ORBITALS_IN_GRP
CODE_ROWS = 16
EXCHANGE_CODE_ROWS = 8
AT_ONCE = 4
SLAB_BITS = 14.0
TOP = 32700.0
STEPS = 8.0
VMEM_LIMIT = 56 * 1024 * 1024


def one_hot_of(target, amount):
    return (target[:, None] == jnp.arange(amount)[None, :]).astype(jnp.bfloat16)


def split(values):
    high = values.astype(jnp.bfloat16)
    return high, (values - high.astype(jnp.float32)).astype(jnp.bfloat16)


def dot(left, right):
    return jnp.dot(left, right, preferred_element_type=jnp.float32)


def scale_of(code):
    return jnp.exp2(code * (1.0 / STEPS))


def encoded(values):
    most = jnp.maximum(jnp.max(jnp.abs(values), axis=0, keepdims=True), 1e-30)
    code = jnp.ceil(jnp.log2(most) * STEPS)
    coded = jnp.round(values * (TOP / scale_of(code))).astype(jnp.int32).astype(jnp.int16)
    code_rows = jnp.broadcast_to(code.astype(jnp.int32), (EXCHANGE_CODE_ROWS, values.shape[1])).astype(jnp.int16)
    return coded, code_rows


def decoded(coded, code_rows):
    scale = scale_of(code_rows.astype(jnp.int32).astype(jnp.float32)[:1]) * (1.0 / TOP)
    return coded.astype(jnp.int32).astype(jnp.float32) * scale


def swapped(values):
    by_place = values.reshape(ORBITALS_IN_GRP, ORBITALS_IN_GRP, -1)
    return jnp.swapaxes(by_place, 0, 1).reshape(values.shape)


def screen_kernel(part, int_mask, slab_ref, coded_ref, *later_refs):
    slab_rows, slab_cols = slab_ref.shape
    cols = coded_ref.shape[1]
    span = slab_cols // W
    row_label = lax.axis_index("occ") * slab_rows // W // VT * NVT
    col_label = lax.axis_index("vir") * slab_cols // W // VT * NVT
    natural = lax.broadcasted_iota(jnp.int32, (slab_cols, 1), 0)
    a, b = natural // W, natural % W
    target = b // span * (part * span) + (a // part * part + b % part) * part + a % part
    place = lax.broadcasted_iota(jnp.int32, (slab_cols, cols), 1)
    to = lax.broadcasted_iota(jnp.int32, (1, cols), 1)
    second = lax.broadcasted_iota(jnp.int32, (slab_rows, 1), 0) % W >= VT
    for chunk in range(1 + len(later_refs)):
        right = to // (part * span) * span + chunk * part + to // part % part >= VT
        kept = [
            jnp.where(right, int_mask[label, col_label + 1], int_mask[label, col_label])
            for label in (row_label, row_label + 1)
        ]
        ones = place == jnp.where(b % span // part == chunk, target, -1)
        moved = dot(slab_ref[...], ones.astype(jnp.float32).astype(jnp.bfloat16))
        moved = jnp.where(jnp.where(second, kept[1], kept[0]) > 0, moved, 0.0)
        if chunk:
            later_refs[chunk - 1][...] = moved.astype(jnp.bfloat16)
        else:
            most = jnp.maximum(jnp.max(jnp.abs(moved), axis=0, keepdims=True), 1e-30)
            code = jnp.floor(jnp.log2(most)) + 1.0
            coded = jnp.round(moved * jnp.exp2(SLAB_BITS - code)).astype(jnp.int32).astype(jnp.int16)
            code_rows = jnp.broadcast_to(code.astype(jnp.int32), (CODE_ROWS, cols)).astype(jnp.int16)
            coded_ref[:slab_rows, :] = coded
            coded_ref[slab_rows:, :] = code_rows


def screen_call(chunks, int_mask, integrals):
    slab_rows, slab_cols = integrals.shape
    cols = slab_cols // chunks
    vmem = pl.BlockSpec(memory_space=pltpu.VMEM)
    return pl.pallas_call(
        functools.partial(screen_kernel, slab_cols // W // chunks),
        in_specs=[pl.BlockSpec(memory_space=pltpu.SMEM), vmem],
        out_specs=[vmem] * chunks,
        out_shape=[jax.ShapeDtypeStruct((slab_rows + CODE_ROWS, cols), jnp.int16)]
        + [jax.ShapeDtypeStruct((slab_rows, cols), integrals.dtype)] * (chunks - 1),
        compiler_params=pltpu.CompilerParams(vmem_limit_bytes=VMEM_LIMIT),
        name="screen",
    )(int_mask, integrals)


def ladder_kernel(tile_total, vir_count, coded, amp_mask, numbers, rows_ref, gathered_ref, *refs):
    packed_ref, product, slab_scr, sems = refs[:4]
    stage = refs[4] if coded else slab_scr
    step = pl.program_id(0)
    cols = slab_scr.shape[1]
    slab_rows = slab_scr.shape[0] // tile_total
    shard_rows = stage.shape[0] // tile_total
    block = cols // vir_count

    def masks(tile, at, width):
        lane = lax.broadcasted_iota(jnp.int32, (1, width), 1) + at
        left = lane % W < VT
        keep = jnp.where(
            lane < W * VT,
            jnp.where(left, amp_mask[tile, 0], amp_mask[tile, 1]),
            jnp.where(left, amp_mask[tile, 2], amp_mask[tile, 3]),
        )
        return keep.astype(jnp.float32).astype(jnp.bfloat16)

    def finish():
        tile = step - 1
        pair = lax.broadcasted_iota(jnp.int32, (PAIR_SQ, 1), 0)
        own_number = numbers[lax.axis_index("occ")]
        nonzero = (pair // ORBITALS_IN_GRP < own_number) & (pair % ORBITALS_IN_GRP < numbers[tile])
        ladder = jnp.where(nonzero, product[...], 0.0)
        coded_rows, code_rows = encoded(swapped(ladder))
        for v in range(vir_count):
            packed_ref[0, v, :PAIR_SQ] = coded_rows[:, v * block : (v + 1) * block]
            packed_ref[0, v, PAIR_SQ:] = code_rows[:, v * block : (v + 1) * block]

    @pl.when(step == 0)
    def _():
        def copy_of(shard):
            at = pl.ds(pl.multiple_of(shard * shard_rows, CODE_ROWS), shard_rows)
            return pltpu.make_async_copy(gathered_ref.at[at, :], stage.at[at, :], sems.at[shard])

        for shard in range(tile_total):
            copy_of(shard).start()
        product[...] = jnp.zeros_like(product)

        def use(shard, carry):
            copy_of(shard).wait()
            to = pl.ds(pl.multiple_of(shard * slab_rows, slab_rows), slab_rows)
            if coded:
                at = pl.multiple_of(shard * shard_rows, CODE_ROWS)
                code = stage[pl.ds(pl.multiple_of(at + slab_rows, CODE_ROWS), CODE_ROWS), :]
                values = stage[pl.ds(at, slab_rows), :].astype(jnp.int32).astype(jnp.float32)
                scale = jnp.exp2(code.astype(jnp.int32).astype(jnp.float32)[:1] - SLAB_BITS)
                slab_scr[to, :] = (values * scale).astype(jnp.bfloat16)
            screened = rows_ref[:, to] * masks(0, shard * slab_rows, slab_rows)
            product[...] += dot(screened, slab_scr[to, :])
            return carry

        lax.fori_loop(0, tile_total, use, 0)

    @pl.when((step > 0) & (step < tile_total))
    def _():
        finish()
        product[...] = dot(rows_ref[...] * masks(step, 0, W * W), slab_scr[...])

    @pl.when(step == tile_total)
    def _():
        finish()


def ladder_call(tile_total, vir_count, amp_mask, numbers, amplitudes, slab):
    coded = slab.dtype == jnp.int16
    cols = slab.shape[1]
    block = cols // vir_count
    smem = pl.BlockSpec(memory_space=pltpu.SMEM)
    rows = tile_total * PAIR_SQ
    before = lambda step: jnp.maximum(step - 1, 0)
    packed_block = (vir_count, PAIR_SQ + EXCHANGE_CODE_ROWS, block)
    return pl.pallas_call(
        functools.partial(ladder_kernel, tile_total, vir_count, coded),
        grid=(tile_total + 1,),
        in_specs=[
            smem,
            smem,
            pl.BlockSpec((PAIR_SQ, W * W), lambda step: (jnp.minimum(step, tile_total - 1), 0)),
            pl.BlockSpec(memory_space=pl.ANY),
        ],
        out_specs=pl.BlockSpec((1,) + packed_block, lambda step: (before(step), 0, 0, 0)),
        out_shape=jax.ShapeDtypeStruct((tile_total,) + packed_block, jnp.int16),
        scratch_shapes=[
            pltpu.VMEM((PAIR_SQ, cols), jnp.float32),
            pltpu.VMEM((W * W, cols), jnp.bfloat16),
            pltpu.SemaphoreType.DMA((tile_total,)),
        ]
        + [pltpu.VMEM(slab.shape, slab.dtype)] * coded,
        compiler_params=pltpu.CompilerParams(vmem_limit_bytes=VMEM_LIMIT),
        cost_estimate=pl.CostEstimate(
            flops=2 * rows * cols * W * W,
            bytes_accessed=rows * (W * W * 2 + cols * 2) + W * W * cols * 2,
            transcendentals=0,
        ),
        name="ladder",
    )(amp_mask, numbers, amplitudes, slab)


def moved_columns(values, spread_ref):
    both = dot(jnp.concatenate(split(values), axis=0), spread_ref[...])
    return both[: values.shape[0]] + both[values.shape[0] :]


def direct_kernel(chunk, chunks, spread_ref, *refs):
    packed_refs, direct_ref = refs[:-1], refs[-1]
    lanes = packed_refs[0].shape[3] // chunks

    def one_tile(n, carry):
        blocks = []
        for packed_ref in packed_refs:
            for v in range(packed_ref.shape[1]):
                values = decoded(packed_ref[n, v, :PAIR_SQ], packed_ref[n, v, PAIR_SQ:])
                blocks.append(values[:, chunk * lanes : (chunk + 1) * lanes])
        natural = moved_columns(swapped(jnp.concatenate(blocks, axis=1)), spread_ref)
        direct_ref[n, :PAIR_SQ], direct_ref[n, PAIR_SQ:] = encoded(natural)
        return carry

    lax.fori_loop(0, AT_ONCE, one_tile, 0)


def direct_call(chunk, spread, packed):
    tile_total = packed[0].shape[0]
    cols = spread.shape[1]
    block_shape = (PAIR_SQ + EXCHANGE_CODE_ROWS, cols)
    rows = tile_total * PAIR_SQ
    return pl.pallas_call(
        functools.partial(direct_kernel, chunk, len(packed)),
        grid=(tile_total // AT_ONCE,),
        in_specs=[pl.BlockSpec(spread.shape, lambda step: (0, 0))]
        + [pl.BlockSpec((AT_ONCE,) + each.shape[1:], lambda step: (step, 0, 0, 0)) for each in packed],
        out_specs=pl.BlockSpec((AT_ONCE,) + block_shape, lambda step: (step, 0, 0)),
        out_shape=jax.ShapeDtypeStruct((tile_total,) + block_shape, jnp.int16),
        compiler_params=pltpu.CompilerParams(vmem_limit_bytes=VMEM_LIMIT),
        cost_estimate=pl.CostEstimate(flops=4 * rows * spread.size, bytes_accessed=rows * cols * 6, transcendentals=0),
        name="direct",
    )(spread, *packed)


def update_kernel(vir_count, spread_ref, vir_ref, occ_ref, arrived_ref, direct_ref, *refs):
    tiles = []
    for n in range(AT_ONCE):
        blocks = [decoded(arrived_ref[n, v, :PAIR_SQ], arrived_ref[n, v, PAIR_SQ:]) for v in range(vir_count)]
        tiles.append(jnp.concatenate(blocks, axis=1))
    mirror = moved_columns(jnp.concatenate(tiles, axis=0), spread_ref)
    for n in range(AT_ONCE):
        at = slice(n * PAIR_SQ, (n + 1) * PAIR_SQ)
        direct = decoded(direct_ref[n, :PAIR_SQ], direct_ref[n, PAIR_SQ:])
        occ = jnp.transpose(jnp.broadcast_to(occ_ref[n], (128, PAIR_SQ)))[:, :1]
        refs[-1][at, :] = (direct + mirror[at]) / (vir_ref[...] - occ)


def update_call(chunk, chunks, arrived, spread, vir_sum, occ_sum, direct, earlier):
    tile_total, vir_count = arrived.shape[:2]
    cols = spread.shape[1]
    rows = tile_total * PAIR_SQ
    args = [spread, vir_sum, occ_sum, arrived, direct]
    in_specs = [
        pl.BlockSpec(spread.shape, lambda step: (0, 0)),
        pl.BlockSpec((1, cols), lambda step: (0, chunk)),
        pl.BlockSpec((AT_ONCE, 1, PAIR_SQ), lambda step: (step, 0, 0)),
        pl.BlockSpec((AT_ONCE,) + arrived.shape[1:], lambda step: (step, 0, 0, 0)),
        pl.BlockSpec((AT_ONCE,) + direct.shape[1:], lambda step: (step, 0, 0)),
    ]
    aliases = {}
    if earlier is not None:
        aliases = {len(args): 0}
        args.append(earlier)
        in_specs.append(pl.BlockSpec(memory_space=pl.ANY))
    return pl.pallas_call(
        functools.partial(update_kernel, vir_count),
        grid=(tile_total // AT_ONCE,),
        in_specs=in_specs,
        out_specs=pl.BlockSpec((AT_ONCE * PAIR_SQ, cols), lambda step: (step, chunk)),
        out_shape=jax.ShapeDtypeStruct((rows, chunks * cols), jnp.float32),
        input_output_aliases=aliases,
        compiler_params=pltpu.CompilerParams(vmem_limit_bytes=VMEM_LIMIT),
        cost_estimate=pl.CostEstimate(flops=4 * rows * spread.size, bytes_accessed=rows * cols * 8, transcendentals=0),
        name="update",
    )(*args)


def body(amplitudes, amp_mask, integrals, int_mask, group_orbital_numbers, occ_energy, vir_energy):
    tile_total = lax.axis_size("occ")
    vir_count = lax.axis_size("vir")
    row_tile = lax.axis_index("occ")
    vir_place = lax.axis_index("vir")
    span = W // vir_count
    slab_cols = span * W
    chunks = 2 if span >= 16 else 1
    width = span // chunks
    block = width * span
    rows = PAIR_SQ + EXCHANGE_CODE_ROWS

    def exchanged(packed):
        moved = lax.all_to_all(
            packed.reshape(tile_total * vir_count, rows, block), ("occ", "vir"), split_axis=0, concat_axis=0, tiled=True
        )
        return moved.reshape(tile_total, vir_count, rows, block)

    coded, *later = screen_call(chunks, int_mask, integrals)
    slabs = [lax.all_gather(coded, "occ", axis=0, tiled=True)]
    for part in later:
        part, _ = lax.optimization_barrier((part, slabs[-1]))
        slabs.append(lax.all_gather(part, "occ", axis=0, tiled=True))
    own, arrived = [], []
    for slab in slabs:
        packed = ladder_call(
            tile_total, vir_count, amp_mask[0], group_orbital_numbers, amplitudes, slab
        )
        own.append(packed)
        arrived.append(exchanged(packed))

    place = jnp.arange(vir_count * block)
    owner, there_part = place // block, place // (width * width) % chunks
    here, there = place // width % width, place % width
    mirror_spread = one_hot_of(here * W + owner * span + there_part * width + there, width * W)
    place = jnp.arange(vir_count * width * width)
    owner, b, a = place // (width * width), place // width % width, place % width
    direct_spread = one_hot_of(
        jnp.concatenate([a * W + owner * span + c * width + b for c in range(chunks)]), width * W
    )

    occ_table = occ_energy.reshape(tile_total, ORBITALS_IN_GRP)
    own_energy = lax.dynamic_slice_in_dim(occ_table, row_tile, 1, 0)[0]
    occ_sum = (own_energy[None, :, None] + occ_table[:, None, :]).reshape(tile_total, 1, PAIR_SQ)
    vir_own = lax.dynamic_slice_in_dim(vir_energy, vir_place * span, span, 0)
    vir_sum = (vir_own[:, None] + vir_energy[None, :]).reshape(1, -1)
    update = None
    for chunk in range(chunks):
        direct = direct_call(chunk, direct_spread, own)
        update = update_call(chunk, chunks, arrived[chunk], mirror_spread, vir_sum, occ_sum, direct, update)
    return update


def solution(mesh):
    in_specs = (P("occ", None), P("occ", None, None), P("occ", "vir"), P(), P(), P(), P())
    out_specs = P("occ", "vir")
    return jax.shard_map(body, mesh=mesh, in_specs=in_specs, out_specs=out_specs, check_vma=False)
```

```python
import functools

import jax
import jax.numpy as jnp
from jax import lax
from jax.experimental import pallas as pl
from jax.experimental.pallas import tpu as pltpu
from jax.sharding import PartitionSpec as P

VT = 32
NVT = 2
W = 64
ORBITALS_IN_GRP = 16
PAIR_SQ = ORBITALS_IN_GRP * ORBITALS_IN_GRP
CODE_ROWS = 16
EXCHANGE_CODE_ROWS = 8
AT_ONCE = 4
SLAB_BITS = 14.0
TOP = 32700.0
STEPS = 8.0
VMEM_LIMIT = 56 * 1024 * 1024


def one_hot_of(target, amount):
    return (target[:, None] == jnp.arange(amount)[None, :]).astype(jnp.bfloat16)


def split(values):
    high = values.astype(jnp.bfloat16)
    return high, (values - high.astype(jnp.float32)).astype(jnp.bfloat16)


def dot(left, right):
    return jnp.dot(left, right, preferred_element_type=jnp.float32)


def scale_of(code):
    return jnp.exp2(code * (1.0 / STEPS))


def screen_kernel(part, int_mask, slab_ref, coded_ref, *later_refs):
    slab_rows, slab_cols = slab_ref.shape
    cols = coded_ref.shape[1]
    span = slab_cols // W
    row_label = lax.axis_index("occ") * slab_rows // W // VT * NVT
    col_label = lax.axis_index("vir") * slab_cols // W // VT * NVT
    natural = lax.broadcasted_iota(jnp.int32, (slab_cols, 1), 0)
    a, b = natural // W, natural % W
    target = b // span * (part * span) + (a // part * part + b % part) * part + a % part
    place = lax.broadcasted_iota(jnp.int32, (slab_cols, cols), 1)
    to = lax.broadcasted_iota(jnp.int32, (1, cols), 1)
    second = lax.broadcasted_iota(jnp.int32, (slab_rows, 1), 0) % W >= VT
    for chunk in range(1 + len(later_refs)):
        right = to // (part * span) * span + chunk * part + to // part % part >= VT
        kept = [
            jnp.where(right, int_mask[label, col_label + 1], int_mask[label, col_label])
            for label in (row_label, row_label + 1)
        ]
        ones = place == jnp.where(b % span // part == chunk, target, -1)
        moved = dot(slab_ref[...], ones.astype(jnp.float32).astype(jnp.bfloat16))
        moved = jnp.where(jnp.where(second, kept[1], kept[0]) > 0, moved, 0.0)
        if chunk:
            later_refs[chunk - 1][...] = moved.astype(jnp.bfloat16)
        else:
            most = jnp.maximum(jnp.max(jnp.abs(moved), axis=0, keepdims=True), 1e-30)
            code = jnp.floor(jnp.log2(most)) + 1.0
            coded = jnp.round(moved * jnp.exp2(SLAB_BITS - code)).astype(jnp.int32).astype(jnp.int16)
            code_rows = jnp.broadcast_to(code.astype(jnp.int32), (CODE_ROWS, cols)).astype(jnp.int16)
            coded_ref[:slab_rows, :] = coded
            coded_ref[slab_rows:, :] = code_rows


def screen_call(chunks, int_mask, integrals):
    slab_rows, slab_cols = integrals.shape
    cols = slab_cols // chunks
    vmem = pl.BlockSpec(memory_space=pltpu.VMEM)
    return pl.pallas_call(
        functools.partial(screen_kernel, slab_cols // W // chunks),
        in_specs=[pl.BlockSpec(memory_space=pltpu.SMEM), vmem],
        out_specs=[vmem] * chunks,
        out_shape=[jax.ShapeDtypeStruct((slab_rows + CODE_ROWS, cols), jnp.int16)]
        + [jax.ShapeDtypeStruct((slab_rows, cols), integrals.dtype)] * (chunks - 1),
        compiler_params=pltpu.CompilerParams(vmem_limit_bytes=VMEM_LIMIT),
        name="screen",
    )(int_mask, integrals)


def ladder_kernel(tile_total, vir_count, chunks, coded, amp_mask, numbers, rows_ref, gathered_ref, *refs):
    ladder_ref, packed_ref, product = refs[:3]
    slab_ref, stage, sems = refs[3:] if coded else (gathered_ref, None, None)
    step = pl.program_id(0)
    cols = slab_ref.shape[1]
    slab_rows = slab_ref.shape[0] // tile_total
    shard_rows = slab_rows + CODE_ROWS
    block = cols // vir_count
    lanes = block // chunks

    def multiply():
        tile = step
        lane = lax.broadcasted_iota(jnp.int32, (1, W * W), 1)
        left = lane % W < VT
        keep = jnp.where(
            lane < W * VT,
            jnp.where(left, amp_mask[tile, 0], amp_mask[tile, 1]),
            jnp.where(left, amp_mask[tile, 2], amp_mask[tile, 3]),
        )
        keep = keep.astype(jnp.float32).astype(jnp.bfloat16)
        product[...] = dot(rows_ref[...] * keep, slab_ref[...])

    def decode():
        def copy_of(shard):
            at = pl.ds(pl.multiple_of(shard * shard_rows, CODE_ROWS), shard_rows)
            return pltpu.make_async_copy(gathered_ref.at[at, :], stage.at[at, :], sems.at[shard])

        for shard in range(tile_total):
            copy_of(shard).start()

        def use(shard, carry):
            copy_of(shard).wait()
            at = pl.multiple_of(shard * shard_rows, CODE_ROWS)
            code = stage[pl.ds(pl.multiple_of(at + slab_rows, CODE_ROWS), CODE_ROWS), :]
            values = stage[pl.ds(at, slab_rows), :].astype(jnp.int32).astype(jnp.float32)
            scale = jnp.exp2(code.astype(jnp.int32).astype(jnp.float32)[:1] - SLAB_BITS)
            to = pl.ds(pl.multiple_of(shard * slab_rows, slab_rows), slab_rows)
            slab_ref[to, :] = (values * scale).astype(jnp.bfloat16)
            return carry

        lax.fori_loop(0, tile_total, use, 0)

    def finish():
        tile = jnp.maximum(step - 1, 0)
        pair = lax.broadcasted_iota(jnp.int32, (PAIR_SQ, 1), 0)
        own_number = numbers[lax.axis_index("occ")]
        nonzero = (pair // ORBITALS_IN_GRP < own_number) & (pair % ORBITALS_IN_GRP < numbers[tile])
        ladder = jnp.where(nonzero, product[...], 0.0)
        for h in range(chunks):
            ladder_ref[h] = jnp.concatenate(
                [ladder[:, v * block + h * lanes : v * block + (h + 1) * lanes] for v in range(vir_count)], axis=1
            )
        by_place = ladder.reshape(ORBITALS_IN_GRP, ORBITALS_IN_GRP, cols)
        mirror = jnp.swapaxes(by_place, 0, 1).reshape(PAIR_SQ, cols)
        most = jnp.maximum(jnp.max(jnp.abs(ladder), axis=0, keepdims=True), 1e-30)
        code = jnp.ceil(jnp.log2(most) * STEPS)
        coded_rows = jnp.round(mirror * (TOP / scale_of(code))).astype(jnp.int32).astype(jnp.int16)
        code_rows = jnp.broadcast_to(code.astype(jnp.int32), (EXCHANGE_CODE_ROWS, cols)).astype(jnp.int16)
        for v in range(vir_count):
            packed_ref[0, v, :PAIR_SQ] = coded_rows[:, v * block : (v + 1) * block]
            packed_ref[0, v, PAIR_SQ:] = code_rows[:, v * block : (v + 1) * block]

    if coded:

        @pl.when(step == 0)
        def _():
            decode()

    @pl.when(step < tile_total)
    def _():
        finish()
        multiply()

    @pl.when(step == tile_total)
    def _():
        finish()


def ladder_call(tile_total, vir_count, chunks, amp_mask, numbers, amplitudes, slab):
    coded = slab.dtype == jnp.int16
    cols = slab.shape[1]
    block = cols // vir_count
    smem = pl.BlockSpec(memory_space=pltpu.SMEM)
    rows = tile_total * PAIR_SQ
    before = lambda step: jnp.maximum(step - 1, 0)
    packed_block = (vir_count, PAIR_SQ + EXCHANGE_CODE_ROWS, block)
    return pl.pallas_call(
        functools.partial(ladder_kernel, tile_total, vir_count, chunks, coded),
        grid=(tile_total + 1,),
        in_specs=[
            smem,
            smem,
            pl.BlockSpec((PAIR_SQ, W * W), lambda step: (jnp.minimum(step, tile_total - 1), 0)),
            pl.BlockSpec(memory_space=pl.ANY) if coded else pl.BlockSpec((W * W, cols), lambda step: (0, 0)),
        ],
        out_specs=[
            pl.BlockSpec((chunks, PAIR_SQ, cols // chunks), lambda step: (0, before(step), 0)),
            pl.BlockSpec((1,) + packed_block, lambda step: (before(step), 0, 0, 0)),
        ],
        out_shape=[
            jax.ShapeDtypeStruct((chunks, rows, cols // chunks), jnp.float32),
            jax.ShapeDtypeStruct((tile_total,) + packed_block, jnp.int16),
        ],
        scratch_shapes=[pltpu.VMEM((PAIR_SQ, cols), jnp.float32)]
        + [
            pltpu.VMEM((W * W, cols), jnp.bfloat16),
            pltpu.VMEM(slab.shape, slab.dtype),
            pltpu.SemaphoreType.DMA((tile_total,)),
        ]
        * coded,
        compiler_params=pltpu.CompilerParams(vmem_limit_bytes=VMEM_LIMIT),
        cost_estimate=pl.CostEstimate(
            flops=2 * rows * cols * W * W,
            bytes_accessed=rows * (W * W * 2 + cols * 6) + W * W * cols * 2,
            transcendentals=0,
        ),
        name="ladder",
    )(amp_mask, numbers, amplitudes, slab)


def moved_columns(values, spread_ref):
    both = dot(jnp.concatenate(split(values), axis=0), spread_ref[...])
    return both[: values.shape[0]] + both[values.shape[0] :]


def direct_kernel(spread_ref, *refs):
    refs[-1][...] = moved_columns(jnp.concatenate([ref[0] for ref in refs[:-1]], axis=1), spread_ref)


def direct_call(chunk, spread, ladders):
    rows = ladders[0].shape[1]
    step_rows = AT_ONCE * PAIR_SQ
    return pl.pallas_call(
        direct_kernel,
        grid=(rows // step_rows,),
        in_specs=[pl.BlockSpec(spread.shape, lambda step: (0, 0))]
        + [pl.BlockSpec((1, step_rows, ladder.shape[2]), lambda step: (chunk, step, 0)) for ladder in ladders],
        out_specs=pl.BlockSpec((step_rows, spread.shape[1]), lambda step: (step, 0)),
        out_shape=jax.ShapeDtypeStruct((rows, spread.shape[1]), jnp.float32),
        compiler_params=pltpu.CompilerParams(vmem_limit_bytes=VMEM_LIMIT),
        cost_estimate=pl.CostEstimate(
            flops=4 * rows * spread.size, bytes_accessed=rows * spread.shape[1] * 8, transcendentals=0
        ),
        name="direct",
    )(spread, *ladders)


def update_kernel(vir_count, at_once, spread_ref, vir_ref, occ_ref, *refs):
    arrived_refs, refs = refs[:vir_count], refs[vir_count:]
    direct_refs = refs[:at_once]
    tiles = []
    for n in range(at_once):
        blocks = []
        for v in range(vir_count):
            code = arrived_refs[v][n, 0, PAIR_SQ:].astype(jnp.int32).astype(jnp.float32)[:1]
            values = arrived_refs[v][n, 0, :PAIR_SQ].astype(jnp.int32).astype(jnp.float32)
            blocks.append(values * (scale_of(code) * (1.0 / TOP)))
        tiles.append(jnp.concatenate(blocks, axis=1))
    mirror = moved_columns(jnp.concatenate(tiles, axis=0), spread_ref)
    for n, direct_ref in enumerate(direct_refs):
        at = slice(n * PAIR_SQ, (n + 1) * PAIR_SQ)
        occ = jnp.transpose(jnp.broadcast_to(occ_ref[n], (128, PAIR_SQ)))[:, :1]
        refs[-1][at, :] = (direct_ref[...] + mirror[at]) / (vir_ref[...] - occ)


def update_call(chunk, chunks, at_once, arrived, spread, vir_sum, occ_sum, direct, earlier):
    cols = spread.shape[1]
    rows = direct.shape[0]
    step_rows = at_once * PAIR_SQ
    vir_count = arrived.shape[1]
    args = [spread, vir_sum, occ_sum] + [arrived] * vir_count + [direct] * at_once
    in_specs = [
        pl.BlockSpec(spread.shape, lambda step: (0, 0)),
        pl.BlockSpec((1, cols), lambda step: (0, chunk)),
        pl.BlockSpec((at_once, 1, PAIR_SQ), lambda step: (step, 0, 0)),
    ]
    in_specs += [
        pl.BlockSpec((at_once, 1) + arrived.shape[2:], lambda step, v=v: (step, v, 0, 0)) for v in range(vir_count)
    ]
    in_specs += [pl.BlockSpec((PAIR_SQ, cols), lambda step, n=n: (step * at_once + n, 0)) for n in range(at_once)]
    aliases = {}
    if earlier is not None:
        aliases = {len(args): 0}
        args.append(earlier)
        in_specs.append(pl.BlockSpec(memory_space=pl.ANY))
    return pl.pallas_call(
        functools.partial(update_kernel, vir_count, at_once),
        grid=(rows // step_rows,),
        in_specs=in_specs,
        out_specs=pl.BlockSpec((step_rows, cols), lambda step: (step, chunk)),
        out_shape=jax.ShapeDtypeStruct((rows, chunks * cols), jnp.float32),
        input_output_aliases=aliases,
        compiler_params=pltpu.CompilerParams(vmem_limit_bytes=VMEM_LIMIT),
        cost_estimate=pl.CostEstimate(
            flops=4 * rows * spread.size, bytes_accessed=rows * cols * 10, transcendentals=0
        ),
        name="update",
    )(*args)


def body(amplitudes, amp_mask, integrals, int_mask, group_orbital_numbers, occ_energy, vir_energy):
    tile_total = lax.axis_size("occ")
    vir_count = lax.axis_size("vir")
    row_tile = lax.axis_index("occ")
    vir_place = lax.axis_index("vir")
    span = W // vir_count
    slab_cols = span * W
    chunks = 2 if span >= 16 else 1
    width = span // chunks
    block = width * span
    rows = PAIR_SQ + EXCHANGE_CODE_ROWS

    def exchanged(packed):
        moved = lax.all_to_all(
            packed.reshape(tile_total * vir_count, rows, block), ("occ", "vir"), split_axis=0, concat_axis=0, tiled=True
        )
        return moved.reshape(tile_total, vir_count, rows, block)

    coded, *later = screen_call(chunks, int_mask, integrals)
    slabs = [lax.all_gather(coded, "occ", axis=0, tiled=True)]
    for part in later:
        part, _ = lax.optimization_barrier((part, slabs[-1]))
        slabs.append(lax.all_gather(part, "occ", axis=0, tiled=True))
    ladders, arrived = [], []
    for slab in slabs:
        ladder, packed = ladder_call(
            tile_total, vir_count, chunks, amp_mask[0], group_orbital_numbers, amplitudes, slab
        )
        ladders.append(ladder)
        arrived.append(exchanged(packed))

    place = jnp.arange(vir_count * block)
    owner, there_part = place // block, place // (width * width) % chunks
    here, there = place // width % width, place % width
    mirror_spread = one_hot_of(here * W + owner * span + there_part * width + there, width * W)
    place = jnp.arange(vir_count * width * width)
    owner, b, a = place // (width * width), place // width % width, place % width
    direct_spread = one_hot_of(
        jnp.concatenate([a * W + owner * span + c * width + b for c in range(chunks)]), width * W
    )

    occ_table = occ_energy.reshape(tile_total, ORBITALS_IN_GRP)
    own_energy = lax.dynamic_slice_in_dim(occ_table, row_tile, 1, 0)[0]
    occ_sum = (own_energy[None, :, None] + occ_table[:, None, :]).reshape(tile_total, 1, PAIR_SQ)
    vir_own = lax.dynamic_slice_in_dim(vir_energy, vir_place * span, span, 0)
    vir_sum = (vir_own[:, None] + vir_energy[None, :]).reshape(1, -1)
    update = None
    for chunk in range(chunks):
        direct = direct_call(chunk, direct_spread, ladders)
        update = update_call(chunk, chunks, 4, arrived[chunk], mirror_spread, vir_sum, occ_sum, direct, update)
    return update


def solution(mesh):
    in_specs = (P("occ", None), P("occ", None, None), P("occ", "vir"), P(), P(), P(), P())
    out_specs = P("occ", "vir")
    return jax.shard_map(body, mesh=mesh, in_specs=in_specs, out_specs=out_specs, check_vma=False)
```

```python
import functools

import jax
import jax.numpy as jnp
from jax import lax
from jax.experimental import pallas as pl
from jax.experimental.pallas import tpu as pltpu
from jax.sharding import PartitionSpec as P

VT = 32
NVT = 2
W = 64
ORBITALS_IN_GRP = 16
PAIR_SQ = ORBITALS_IN_GRP * ORBITALS_IN_GRP
CODE_ROWS = 16
EXCHANGE_CODE_ROWS = 8
AT_ONCE = 4
SLAB_BITS = 14.0
TOP = 32700.0
STEPS = 8.0
VMEM_LIMIT = 56 * 1024 * 1024


def one_hot_of(target, amount):
    return (target[:, None] == jnp.arange(amount)[None, :]).astype(jnp.bfloat16)


def split(values):
    high = values.astype(jnp.bfloat16)
    return high, (values - high.astype(jnp.float32)).astype(jnp.bfloat16)


def dot(left, right):
    return jnp.dot(left, right, preferred_element_type=jnp.float32)


def scale_of(code):
    return jnp.exp2(code * (1.0 / STEPS))


def screen_kernel(part, int_mask, slab_ref, coded_ref, *later_refs):
    slab_rows, slab_cols = slab_ref.shape
    cols = coded_ref.shape[1]
    span = slab_cols // W
    row_label = lax.axis_index("occ") * slab_rows // W // VT * NVT
    col_label = lax.axis_index("vir") * slab_cols // W // VT * NVT
    natural = lax.broadcasted_iota(jnp.int32, (slab_cols, 1), 0)
    a, b = natural // W, natural % W
    target = b // span * (part * span) + (a // part * part + b % part) * part + a % part
    place = lax.broadcasted_iota(jnp.int32, (slab_cols, cols), 1)
    to = lax.broadcasted_iota(jnp.int32, (1, cols), 1)
    second = lax.broadcasted_iota(jnp.int32, (slab_rows, 1), 0) % W >= VT
    for chunk in range(1 + len(later_refs)):
        right = to // (part * span) * span + chunk * part + to // part % part >= VT
        kept = [
            jnp.where(right, int_mask[label, col_label + 1], int_mask[label, col_label])
            for label in (row_label, row_label + 1)
        ]
        ones = place == jnp.where(b % span // part == chunk, target, -1)
        moved = dot(slab_ref[...], ones.astype(jnp.float32).astype(jnp.bfloat16))
        moved = jnp.where(jnp.where(second, kept[1], kept[0]) > 0, moved, 0.0)
        if chunk:
            later_refs[chunk - 1][...] = moved.astype(jnp.bfloat16)
        else:
            most = jnp.maximum(jnp.max(jnp.abs(moved), axis=0, keepdims=True), 1e-30)
            code = jnp.floor(jnp.log2(most)) + 1.0
            coded = jnp.round(moved * jnp.exp2(SLAB_BITS - code)).astype(jnp.int32).astype(jnp.int16)
            code_rows = jnp.broadcast_to(code.astype(jnp.int32), (CODE_ROWS, cols)).astype(jnp.int16)
            coded_ref[:slab_rows, :] = coded
            coded_ref[slab_rows:, :] = code_rows


def screen_call(chunks, int_mask, integrals):
    slab_rows, slab_cols = integrals.shape
    cols = slab_cols // chunks
    vmem = pl.BlockSpec(memory_space=pltpu.VMEM)
    return pl.pallas_call(
        functools.partial(screen_kernel, slab_cols // W // chunks),
        in_specs=[pl.BlockSpec(memory_space=pltpu.SMEM), vmem],
        out_specs=[vmem] * chunks,
        out_shape=[jax.ShapeDtypeStruct((slab_rows + CODE_ROWS, cols), jnp.int16)]
        + [jax.ShapeDtypeStruct((slab_rows, cols), integrals.dtype)] * (chunks - 1),
        compiler_params=pltpu.CompilerParams(vmem_limit_bytes=VMEM_LIMIT),
        name="screen",
    )(int_mask, integrals)


def ladder_kernel(tile_total, vir_count, chunks, coded, amp_mask, numbers, rows_ref, gathered_ref, *refs):
    ladder_ref, packed_ref, product = refs[:3]
    slab_ref, stage, sems = refs[3:] if coded else (gathered_ref, None, None)
    step = pl.program_id(0)
    cols = slab_ref.shape[1]
    slab_rows = slab_ref.shape[0] // tile_total
    shard_rows = slab_rows + CODE_ROWS
    block = cols // vir_count
    lanes = block // chunks

    def multiply():
        tile = step
        lane = lax.broadcasted_iota(jnp.int32, (1, W * W), 1)
        left = lane % W < VT
        keep = jnp.where(
            lane < W * VT,
            jnp.where(left, amp_mask[tile, 0], amp_mask[tile, 1]),
            jnp.where(left, amp_mask[tile, 2], amp_mask[tile, 3]),
        )
        keep = keep.astype(jnp.float32).astype(jnp.bfloat16)
        product[...] = dot(rows_ref[...] * keep, slab_ref[...])

    def decode():
        def copy_of(shard):
            at = pl.ds(pl.multiple_of(shard * shard_rows, CODE_ROWS), shard_rows)
            return pltpu.make_async_copy(gathered_ref.at[at, :], stage.at[at, :], sems.at[shard])

        for shard in range(tile_total):
            copy_of(shard).start()

        def use(shard, carry):
            copy_of(shard).wait()
            at = pl.multiple_of(shard * shard_rows, CODE_ROWS)
            code = stage[pl.ds(pl.multiple_of(at + slab_rows, CODE_ROWS), CODE_ROWS), :]
            values = stage[pl.ds(at, slab_rows), :].astype(jnp.int32).astype(jnp.float32)
            scale = jnp.exp2(code.astype(jnp.int32).astype(jnp.float32)[:1] - SLAB_BITS)
            to = pl.ds(pl.multiple_of(shard * slab_rows, slab_rows), slab_rows)
            slab_ref[to, :] = (values * scale).astype(jnp.bfloat16)
            return carry

        lax.fori_loop(0, tile_total, use, 0)

    def finish():
        tile = jnp.maximum(step - 1, 0)
        pair = lax.broadcasted_iota(jnp.int32, (PAIR_SQ, 1), 0)
        own_number = numbers[lax.axis_index("occ")]
        nonzero = (pair // ORBITALS_IN_GRP < own_number) & (pair % ORBITALS_IN_GRP < numbers[tile])
        ladder = jnp.where(nonzero, product[...], 0.0)
        for h in range(chunks):
            ladder_ref[h] = jnp.concatenate(
                [ladder[:, v * block + h * lanes : v * block + (h + 1) * lanes] for v in range(vir_count)], axis=1
            )
        by_place = ladder.reshape(ORBITALS_IN_GRP, ORBITALS_IN_GRP, cols)
        mirror = jnp.swapaxes(by_place, 0, 1).reshape(PAIR_SQ, cols)
        most = jnp.maximum(jnp.max(jnp.abs(ladder), axis=0, keepdims=True), 1e-30)
        code = jnp.ceil(jnp.log2(most) * STEPS)
        coded_rows = jnp.round(mirror * (TOP / scale_of(code))).astype(jnp.int32).astype(jnp.int16)
        code_rows = jnp.broadcast_to(code.astype(jnp.int32), (EXCHANGE_CODE_ROWS, cols)).astype(jnp.int16)
        for v in range(vir_count):
            packed_ref[v, 0, :PAIR_SQ] = coded_rows[:, v * block : (v + 1) * block]
            packed_ref[v, 0, PAIR_SQ:] = code_rows[:, v * block : (v + 1) * block]

    if coded:

        @pl.when(step == 0)
        def _():
            decode()

    @pl.when(step < tile_total)
    def _():
        finish()
        multiply()

    @pl.when(step == tile_total)
    def _():
        finish()


def ladder_call(tile_total, vir_count, chunks, amp_mask, numbers, amplitudes, slab):
    coded = slab.dtype == jnp.int16
    cols = slab.shape[1]
    block = cols // vir_count
    smem = pl.BlockSpec(memory_space=pltpu.SMEM)
    rows = tile_total * PAIR_SQ
    before = lambda step: jnp.maximum(step - 1, 0)
    packed_rows = PAIR_SQ + EXCHANGE_CODE_ROWS
    return pl.pallas_call(
        functools.partial(ladder_kernel, tile_total, vir_count, chunks, coded),
        grid=(tile_total + 1,),
        in_specs=[
            smem,
            smem,
            pl.BlockSpec((PAIR_SQ, W * W), lambda step: (jnp.minimum(step, tile_total - 1), 0)),
            pl.BlockSpec(memory_space=pl.ANY) if coded else pl.BlockSpec((W * W, cols), lambda step: (0, 0)),
        ],
        out_specs=[
            pl.BlockSpec((chunks, PAIR_SQ, cols // chunks), lambda step: (0, before(step), 0)),
            pl.BlockSpec((vir_count, 1, packed_rows, block), lambda step: (0, before(step), 0, 0)),
        ],
        out_shape=[
            jax.ShapeDtypeStruct((chunks, rows, cols // chunks), jnp.float32),
            jax.ShapeDtypeStruct((vir_count, tile_total, packed_rows, block), jnp.int16),
        ],
        scratch_shapes=[pltpu.VMEM((PAIR_SQ, cols), jnp.float32)]
        + [
            pltpu.VMEM((W * W, cols), jnp.bfloat16),
            pltpu.VMEM(slab.shape, slab.dtype),
            pltpu.SemaphoreType.DMA((tile_total,)),
        ]
        * coded,
        compiler_params=pltpu.CompilerParams(vmem_limit_bytes=VMEM_LIMIT),
        cost_estimate=pl.CostEstimate(
            flops=2 * rows * cols * W * W,
            bytes_accessed=rows * (W * W * 2 + cols * 6) + W * W * cols * 2,
            transcendentals=0,
        ),
        name="ladder",
    )(amp_mask, numbers, amplitudes, slab)


def moved_columns(values, spread_ref):
    both = dot(jnp.concatenate(split(values), axis=0), spread_ref[...])
    return both[: values.shape[0]] + both[values.shape[0] :]


def direct_kernel(spread_ref, *refs):
    refs[-1][...] = moved_columns(jnp.concatenate([ref[0] for ref in refs[:-1]], axis=1), spread_ref)


def direct_call(chunk, spread, ladders):
    rows = ladders[0].shape[1]
    step_rows = AT_ONCE * PAIR_SQ
    return pl.pallas_call(
        direct_kernel,
        grid=(rows // step_rows,),
        in_specs=[pl.BlockSpec(spread.shape, lambda step: (0, 0))]
        + [pl.BlockSpec((1, step_rows, ladder.shape[2]), lambda step: (chunk, step, 0)) for ladder in ladders],
        out_specs=pl.BlockSpec((step_rows, spread.shape[1]), lambda step: (step, 0)),
        out_shape=jax.ShapeDtypeStruct((rows, spread.shape[1]), jnp.float32),
        compiler_params=pltpu.CompilerParams(vmem_limit_bytes=VMEM_LIMIT),
        cost_estimate=pl.CostEstimate(
            flops=4 * rows * spread.size, bytes_accessed=rows * spread.shape[1] * 8, transcendentals=0
        ),
        name="direct",
    )(spread, *ladders)


def update_kernel(vir_count, at_once, spread_ref, vir_ref, occ_ref, *refs):
    arrived_refs, refs = refs[:vir_count], refs[vir_count:]
    direct_refs = refs[:at_once]
    tiles = []
    for n in range(at_once):
        blocks = []
        for v in range(vir_count):
            code = arrived_refs[v][0, n, PAIR_SQ:].astype(jnp.int32).astype(jnp.float32)[:1]
            values = arrived_refs[v][0, n, :PAIR_SQ].astype(jnp.int32).astype(jnp.float32)
            blocks.append(values * (scale_of(code) * (1.0 / TOP)))
        tiles.append(jnp.concatenate(blocks, axis=1))
    mirror = moved_columns(jnp.concatenate(tiles, axis=0), spread_ref)
    for n, direct_ref in enumerate(direct_refs):
        at = slice(n * PAIR_SQ, (n + 1) * PAIR_SQ)
        occ = jnp.transpose(jnp.broadcast_to(occ_ref[n], (128, PAIR_SQ)))[:, :1]
        refs[-1][at, :] = (direct_ref[...] + mirror[at]) / (vir_ref[...] - occ)


def update_call(chunk, chunks, at_once, arrived, spread, vir_sum, occ_sum, direct, earlier):
    cols = spread.shape[1]
    rows = direct.shape[0]
    step_rows = at_once * PAIR_SQ
    vir_count = arrived.shape[0]
    args = [spread, vir_sum, occ_sum] + [arrived] * vir_count + [direct] * at_once
    in_specs = [
        pl.BlockSpec(spread.shape, lambda step: (0, 0)),
        pl.BlockSpec((1, cols), lambda step: (0, chunk)),
        pl.BlockSpec((at_once, 1, PAIR_SQ), lambda step: (step, 0, 0)),
    ]
    in_specs += [
        pl.BlockSpec((1, at_once) + arrived.shape[2:], lambda step, v=v: (v, step, 0, 0)) for v in range(vir_count)
    ]
    in_specs += [pl.BlockSpec((PAIR_SQ, cols), lambda step, n=n: (step * at_once + n, 0)) for n in range(at_once)]
    aliases = {}
    if earlier is not None:
        aliases = {len(args): 0}
        args.append(earlier)
        in_specs.append(pl.BlockSpec(memory_space=pl.ANY))
    return pl.pallas_call(
        functools.partial(update_kernel, vir_count, at_once),
        grid=(rows // step_rows,),
        in_specs=in_specs,
        out_specs=pl.BlockSpec((step_rows, cols), lambda step: (step, chunk)),
        out_shape=jax.ShapeDtypeStruct((rows, chunks * cols), jnp.float32),
        input_output_aliases=aliases,
        compiler_params=pltpu.CompilerParams(vmem_limit_bytes=VMEM_LIMIT),
        cost_estimate=pl.CostEstimate(
            flops=4 * rows * spread.size, bytes_accessed=rows * cols * 10, transcendentals=0
        ),
        name="update",
    )(*args)


def body(amplitudes, amp_mask, integrals, int_mask, group_orbital_numbers, occ_energy, vir_energy):
    tile_total = lax.axis_size("occ")
    vir_count = lax.axis_size("vir")
    row_tile = lax.axis_index("occ")
    vir_place = lax.axis_index("vir")
    span = W // vir_count
    slab_cols = span * W
    chunks = 2 if span >= 16 else 1
    width = span // chunks
    block = width * span
    rows = PAIR_SQ + EXCHANGE_CODE_ROWS

    def exchanged(packed):
        moved = lax.all_to_all(
            packed.reshape(vir_count * tile_total, rows, block), ("vir", "occ"), split_axis=0, concat_axis=0, tiled=True
        )
        return moved.reshape(vir_count, tile_total, rows, block)

    coded, *later = screen_call(chunks, int_mask, integrals)
    slabs = [lax.all_gather(coded, "occ", axis=0, tiled=True)]
    for part in later:
        part, _ = lax.optimization_barrier((part, slabs[-1]))
        slabs.append(lax.all_gather(part, "occ", axis=0, tiled=True))
    ladders, arrived = [], []
    for slab in slabs:
        ladder, packed = ladder_call(
            tile_total, vir_count, chunks, amp_mask[0], group_orbital_numbers, amplitudes, slab
        )
        ladders.append(ladder)
        arrived.append(exchanged(packed))

    place = jnp.arange(vir_count * block)
    owner, there_part = place // block, place // (width * width) % chunks
    here, there = place // width % width, place % width
    mirror_spread = one_hot_of(here * W + owner * span + there_part * width + there, width * W)
    place = jnp.arange(vir_count * width * width)
    owner, b, a = place // (width * width), place // width % width, place % width
    direct_spread = one_hot_of(
        jnp.concatenate([a * W + owner * span + c * width + b for c in range(chunks)]), width * W
    )

    occ_table = occ_energy.reshape(tile_total, ORBITALS_IN_GRP)
    own_energy = lax.dynamic_slice_in_dim(occ_table, row_tile, 1, 0)[0]
    occ_sum = (own_energy[None, :, None] + occ_table[:, None, :]).reshape(tile_total, 1, PAIR_SQ)
    vir_own = lax.dynamic_slice_in_dim(vir_energy, vir_place * span, span, 0)
    vir_sum = (vir_own[:, None] + vir_energy[None, :]).reshape(1, -1)
    update = None
    for chunk in range(chunks):
        direct = direct_call(chunk, direct_spread, ladders)
        update = update_call(chunk, chunks, 4, arrived[chunk], mirror_spread, vir_sum, occ_sum, direct, update)
    return update


def solution(mesh):
    in_specs = (P("occ", None), P("occ", None, None), P("occ", "vir"), P(), P(), P(), P())
    out_specs = P("occ", "vir")
    return jax.shard_map(body, mesh=mesh, in_specs=in_specs, out_specs=out_specs, check_vma=False)
```

```python
import functools

import jax
import jax.numpy as jnp
from jax import lax
from jax.experimental import pallas as pl
from jax.experimental.pallas import tpu as pltpu
from jax.sharding import PartitionSpec as P

VT = 32
NVT = 2
W = 64
ORBITALS_IN_GRP = 16
PAIR_SQ = ORBITALS_IN_GRP * ORBITALS_IN_GRP
CODE_ROWS = 16
EXCHANGE_CODE_ROWS = 8
AT_ONCE = 4
SLAB_BITS = 14.0
TOP = 32700.0
STEPS = 8.0
VMEM_LIMIT = 56 * 1024 * 1024


def one_hot_of(target, amount):
    return (target[:, None] == jnp.arange(amount)[None, :]).astype(jnp.bfloat16)


def split(values):
    high = values.astype(jnp.bfloat16)
    return high, (values - high.astype(jnp.float32)).astype(jnp.bfloat16)


def dot(left, right):
    return jnp.dot(left, right, preferred_element_type=jnp.float32)


def scale_of(code):
    return jnp.exp2(code * (1.0 / STEPS))


def screen_kernel(part, int_mask, slab_ref, coded_ref, *later_refs):
    slab_rows, slab_cols = slab_ref.shape
    cols = coded_ref.shape[1]
    span = slab_cols // W
    row_label = lax.axis_index("occ") * slab_rows // W // VT * NVT
    col_label = lax.axis_index("vir") * slab_cols // W // VT * NVT
    natural = lax.broadcasted_iota(jnp.int32, (slab_cols, 1), 0)
    a, b = natural // W, natural % W
    target = b // span * (part * span) + (a // part * part + b % part) * part + a % part
    place = lax.broadcasted_iota(jnp.int32, (slab_cols, cols), 1)
    to = lax.broadcasted_iota(jnp.int32, (1, cols), 1)
    second = lax.broadcasted_iota(jnp.int32, (slab_rows, 1), 0) % W >= VT
    for chunk in range(1 + len(later_refs)):
        right = to // (part * span) * span + chunk * part + to // part % part >= VT
        kept = [
            jnp.where(right, int_mask[label, col_label + 1], int_mask[label, col_label])
            for label in (row_label, row_label + 1)
        ]
        ones = place == jnp.where(b % span // part == chunk, target, -1)
        moved = dot(slab_ref[...], ones.astype(jnp.float32).astype(jnp.bfloat16))
        moved = jnp.where(jnp.where(second, kept[1], kept[0]) > 0, moved, 0.0)
        if chunk:
            later_refs[chunk - 1][...] = moved.astype(jnp.bfloat16)
        else:
            most = jnp.maximum(jnp.max(jnp.abs(moved), axis=0, keepdims=True), 1e-30)
            code = jnp.floor(jnp.log2(most)) + 1.0
            coded = jnp.round(moved * jnp.exp2(SLAB_BITS - code)).astype(jnp.int32).astype(jnp.int16)
            code_rows = jnp.broadcast_to(code.astype(jnp.int32), (CODE_ROWS, cols)).astype(jnp.int16)
            coded_ref[:slab_rows, :] = coded
            coded_ref[slab_rows:, :] = code_rows


def screen_call(chunks, int_mask, integrals):
    slab_rows, slab_cols = integrals.shape
    cols = slab_cols // chunks
    vmem = pl.BlockSpec(memory_space=pltpu.VMEM)
    return pl.pallas_call(
        functools.partial(screen_kernel, slab_cols // W // chunks),
        in_specs=[pl.BlockSpec(memory_space=pltpu.SMEM), vmem],
        out_specs=[vmem] * chunks,
        out_shape=[jax.ShapeDtypeStruct((slab_rows + CODE_ROWS, cols), jnp.int16)]
        + [jax.ShapeDtypeStruct((slab_rows, cols), integrals.dtype)] * (chunks - 1),
        compiler_params=pltpu.CompilerParams(vmem_limit_bytes=VMEM_LIMIT),
        name="screen",
    )(int_mask, integrals)


def ladder_kernel(tile_total, vir_count, chunks, coded, amp_mask, numbers, rows_ref, gathered_ref, *refs):
    ladder_ref, packed_ref, product = refs[:3]
    slab_ref, stage, sems = refs[3:] if coded else (gathered_ref, None, None)
    step = pl.program_id(0)
    cols = slab_ref.shape[1]
    slab_rows = slab_ref.shape[0] // tile_total
    shard_rows = slab_rows + CODE_ROWS
    block = cols // vir_count
    lanes = block // chunks

    def multiply():
        tile = step
        lane = lax.broadcasted_iota(jnp.int32, (1, W * W), 1)
        left = lane % W < VT
        keep = jnp.where(
            lane < W * VT,
            jnp.where(left, amp_mask[tile, 0], amp_mask[tile, 1]),
            jnp.where(left, amp_mask[tile, 2], amp_mask[tile, 3]),
        )
        keep = keep.astype(jnp.float32).astype(jnp.bfloat16)
        product[...] = dot(rows_ref[...] * keep, slab_ref[...])

    def decode():
        def copy_of(shard):
            at = pl.ds(pl.multiple_of(shard * shard_rows, CODE_ROWS), shard_rows)
            return pltpu.make_async_copy(gathered_ref.at[at, :], stage.at[at, :], sems.at[shard])

        for shard in range(tile_total):
            copy_of(shard).start()

        def use(shard, carry):
            copy_of(shard).wait()
            at = pl.multiple_of(shard * shard_rows, CODE_ROWS)
            code = stage[pl.ds(pl.multiple_of(at + slab_rows, CODE_ROWS), CODE_ROWS), :]
            values = stage[pl.ds(at, slab_rows), :].astype(jnp.int32).astype(jnp.float32)
            scale = jnp.exp2(code.astype(jnp.int32).astype(jnp.float32)[:1] - SLAB_BITS)
            to = pl.ds(pl.multiple_of(shard * slab_rows, slab_rows), slab_rows)
            slab_ref[to, :] = (values * scale).astype(jnp.bfloat16)
            return carry

        lax.fori_loop(0, tile_total, use, 0)

    def finish():
        tile = jnp.maximum(step - 1, 0)
        pair = lax.broadcasted_iota(jnp.int32, (PAIR_SQ, 1), 0)
        own_number = numbers[lax.axis_index("occ")]
        nonzero = (pair // ORBITALS_IN_GRP < own_number) & (pair % ORBITALS_IN_GRP < numbers[tile])
        ladder = jnp.where(nonzero, product[...], 0.0)
        for h in range(chunks):
            ladder_ref[h] = jnp.concatenate(
                [ladder[:, v * block + h * lanes : v * block + (h + 1) * lanes] for v in range(vir_count)], axis=1
            )
        by_place = ladder.reshape(ORBITALS_IN_GRP, ORBITALS_IN_GRP, cols)
        mirror = jnp.swapaxes(by_place, 0, 1).reshape(PAIR_SQ, cols)
        most = jnp.maximum(jnp.max(jnp.abs(ladder), axis=0, keepdims=True), 1e-30)
        code = jnp.ceil(jnp.log2(most) * STEPS)
        coded_rows = jnp.round(mirror * (TOP / scale_of(code))).astype(jnp.int32).astype(jnp.int16)
        code_rows = jnp.broadcast_to(code.astype(jnp.int32), (EXCHANGE_CODE_ROWS, cols)).astype(jnp.int16)
        for v in range(vir_count):
            packed_ref[0, v, :PAIR_SQ] = coded_rows[:, v * block : (v + 1) * block]
            packed_ref[0, v, PAIR_SQ:] = code_rows[:, v * block : (v + 1) * block]

    if coded:

        @pl.when(step == 0)
        def _():
            decode()

    @pl.when(step < tile_total)
    def _():
        finish()
        multiply()

    @pl.when(step == tile_total)
    def _():
        finish()


def ladder_call(tile_total, vir_count, chunks, amp_mask, numbers, amplitudes, slab):
    coded = slab.dtype == jnp.int16
    cols = slab.shape[1]
    block = cols // vir_count
    smem = pl.BlockSpec(memory_space=pltpu.SMEM)
    rows = tile_total * PAIR_SQ
    before = lambda step: jnp.maximum(step - 1, 0)
    packed_block = (vir_count, PAIR_SQ + EXCHANGE_CODE_ROWS, block)
    return pl.pallas_call(
        functools.partial(ladder_kernel, tile_total, vir_count, chunks, coded),
        grid=(tile_total + 1,),
        in_specs=[
            smem,
            smem,
            pl.BlockSpec((PAIR_SQ, W * W), lambda step: (jnp.minimum(step, tile_total - 1), 0)),
            pl.BlockSpec(memory_space=pl.ANY) if coded else pl.BlockSpec((W * W, cols), lambda step: (0, 0)),
        ],
        out_specs=[
            pl.BlockSpec((chunks, PAIR_SQ, cols // chunks), lambda step: (0, before(step), 0)),
            pl.BlockSpec((1,) + packed_block, lambda step: (before(step), 0, 0, 0)),
        ],
        out_shape=[
            jax.ShapeDtypeStruct((chunks, rows, cols // chunks), jnp.float32),
            jax.ShapeDtypeStruct((tile_total,) + packed_block, jnp.int16),
        ],
        scratch_shapes=[pltpu.VMEM((PAIR_SQ, cols), jnp.float32)]
        + [
            pltpu.VMEM((W * W, cols), jnp.bfloat16),
            pltpu.VMEM(slab.shape, slab.dtype),
            pltpu.SemaphoreType.DMA((tile_total,)),
        ]
        * coded,
        compiler_params=pltpu.CompilerParams(vmem_limit_bytes=VMEM_LIMIT),
        cost_estimate=pl.CostEstimate(
            flops=2 * rows * cols * W * W,
            bytes_accessed=rows * (W * W * 2 + cols * 6) + W * W * cols * 2,
            transcendentals=0,
        ),
        name="ladder",
    )(amp_mask, numbers, amplitudes, slab)


def moved_columns(values, spread_ref):
    both = dot(jnp.concatenate(split(values), axis=0), spread_ref[...])
    return both[: values.shape[0]] + both[values.shape[0] :]


def direct_kernel(spread_ref, *refs):
    refs[-1][...] = moved_columns(jnp.concatenate([ref[0] for ref in refs[:-1]], axis=1), spread_ref)


def direct_call(chunk, spread, ladders):
    rows = ladders[0].shape[1]
    step_rows = AT_ONCE * PAIR_SQ
    return pl.pallas_call(
        direct_kernel,
        grid=(rows // step_rows,),
        in_specs=[pl.BlockSpec(spread.shape, lambda step: (0, 0))]
        + [pl.BlockSpec((1, step_rows, ladder.shape[2]), lambda step: (chunk, step, 0)) for ladder in ladders],
        out_specs=pl.BlockSpec((step_rows, spread.shape[1]), lambda step: (step, 0)),
        out_shape=jax.ShapeDtypeStruct((rows, spread.shape[1]), jnp.float32),
        compiler_params=pltpu.CompilerParams(vmem_limit_bytes=VMEM_LIMIT),
        cost_estimate=pl.CostEstimate(
            flops=4 * rows * spread.size, bytes_accessed=rows * spread.shape[1] * 8, transcendentals=0
        ),
        name="direct",
    )(spread, *ladders)


def update_kernel(vir_count, at_once, spread_ref, vir_ref, occ_ref, *refs):
    arrived_refs, refs = refs[:vir_count], refs[vir_count:]
    direct_refs = refs[:at_once]
    tiles = []
    for n in range(at_once):
        blocks = []
        for v in range(vir_count):
            code = arrived_refs[v][n, 0, PAIR_SQ:].astype(jnp.int32).astype(jnp.float32)[:1]
            values = arrived_refs[v][n, 0, :PAIR_SQ].astype(jnp.int32).astype(jnp.float32)
            blocks.append(values * (scale_of(code) * (1.0 / TOP)))
        tiles.append(jnp.concatenate(blocks, axis=1))
    mirror = moved_columns(jnp.concatenate(tiles, axis=0), spread_ref)
    for n, direct_ref in enumerate(direct_refs):
        at = slice(n * PAIR_SQ, (n + 1) * PAIR_SQ)
        occ = jnp.transpose(jnp.broadcast_to(occ_ref[n], (128, PAIR_SQ)))[:, :1]
        refs[-1][at, :] = (direct_ref[...] + mirror[at]) / (vir_ref[...] - occ)


def update_call(chunk, chunks, at_once, arrived, spread, vir_sum, occ_sum, direct, earlier):
    cols = spread.shape[1]
    rows = direct.shape[0]
    step_rows = at_once * PAIR_SQ
    vir_count = arrived.shape[1]
    args = [spread, vir_sum, occ_sum] + [arrived] * vir_count + [direct] * at_once
    in_specs = [
        pl.BlockSpec(spread.shape, lambda step: (0, 0)),
        pl.BlockSpec((1, cols), lambda step: (0, chunk)),
        pl.BlockSpec((at_once, 1, PAIR_SQ), lambda step: (step, 0, 0)),
    ]
    in_specs += [
        pl.BlockSpec((at_once, 1) + arrived.shape[2:], lambda step, v=v: (step, v, 0, 0)) for v in range(vir_count)
    ]
    in_specs += [pl.BlockSpec((PAIR_SQ, cols), lambda step, n=n: (step * at_once + n, 0)) for n in range(at_once)]
    aliases = {}
    if earlier is not None:
        aliases = {len(args): 0}
        args.append(earlier)
        in_specs.append(pl.BlockSpec(memory_space=pl.ANY))
    return pl.pallas_call(
        functools.partial(update_kernel, vir_count, at_once),
        grid=(rows // step_rows,),
        in_specs=in_specs,
        out_specs=pl.BlockSpec((step_rows, cols), lambda step: (step, chunk)),
        out_shape=jax.ShapeDtypeStruct((rows, chunks * cols), jnp.float32),
        input_output_aliases=aliases,
        compiler_params=pltpu.CompilerParams(vmem_limit_bytes=VMEM_LIMIT),
        cost_estimate=pl.CostEstimate(
            flops=4 * rows * spread.size, bytes_accessed=rows * cols * 10, transcendentals=0
        ),
        name="update",
    )(*args)


def body(amplitudes, amp_mask, integrals, int_mask, group_orbital_numbers, occ_energy, vir_energy):
    tile_total = lax.axis_size("occ")
    vir_count = lax.axis_size("vir")
    row_tile = lax.axis_index("occ")
    vir_place = lax.axis_index("vir")
    span = W // vir_count
    slab_cols = span * W
    chunks = 2 if span >= 16 else 1
    width = span // chunks
    block = width * span
    rows = PAIR_SQ + EXCHANGE_CODE_ROWS

    def exchanged(packed):
        moved = lax.all_to_all(
            packed.reshape(tile_total * vir_count, rows, block), ("occ", "vir"), split_axis=0, concat_axis=0, tiled=True
        )
        return moved.reshape(tile_total, vir_count, rows, block)

    coded, *later = screen_call(chunks, int_mask, integrals)
    slabs = [lax.all_gather(coded, "occ", axis=0, tiled=True)]
    for part in later:
        slabs.append(lax.all_gather(part, "occ", axis=0, tiled=True))
    ladders, arrived = [], []
    for slab in slabs:
        ladder, packed = ladder_call(
            tile_total, vir_count, chunks, amp_mask[0], group_orbital_numbers, amplitudes, slab
        )
        ladders.append(ladder)
        arrived.append(exchanged(packed))

    place = jnp.arange(vir_count * block)
    owner, there_part = place // block, place // (width * width) % chunks
    here, there = place // width % width, place % width
    mirror_spread = one_hot_of(here * W + owner * span + there_part * width + there, width * W)
    place = jnp.arange(vir_count * width * width)
    owner, b, a = place // (width * width), place // width % width, place % width
    direct_spread = one_hot_of(
        jnp.concatenate([a * W + owner * span + c * width + b for c in range(chunks)]), width * W
    )

    occ_table = occ_energy.reshape(tile_total, ORBITALS_IN_GRP)
    own_energy = lax.dynamic_slice_in_dim(occ_table, row_tile, 1, 0)[0]
    occ_sum = (own_energy[None, :, None] + occ_table[:, None, :]).reshape(tile_total, 1, PAIR_SQ)
    vir_own = lax.dynamic_slice_in_dim(vir_energy, vir_place * span, span, 0)
    vir_sum = (vir_own[:, None] + vir_energy[None, :]).reshape(1, -1)
    update = None
    for chunk in range(chunks):
        direct = direct_call(chunk, direct_spread, ladders)
        update = update_call(chunk, chunks, 4, arrived[chunk], mirror_spread, vir_sum, occ_sum, direct, update)
    return update


def solution(mesh):
    in_specs = (P("occ", None), P("occ", None, None), P("occ", "vir"), P(), P(), P(), P())
    out_specs = P("occ", "vir")
    return jax.shard_map(body, mesh=mesh, in_specs=in_specs, out_specs=out_specs, check_vma=False)
```

```python
import functools

import jax
import jax.numpy as jnp
from jax import lax
from jax.experimental import pallas as pl
from jax.experimental.pallas import tpu as pltpu
from jax.sharding import PartitionSpec as P

VT = 32
NVT = 2
W = 64
ORBITALS_IN_GRP = 16
PAIR_SQ = ORBITALS_IN_GRP * ORBITALS_IN_GRP
CODE_ROWS = 16
EXCHANGE_CODE_ROWS = 8
AT_ONCE = 4
SLAB_BITS = 14.0
TOP = 32700.0
STEPS = 8.0
VMEM_LIMIT = 56 * 1024 * 1024


def one_hot_of(target, amount):
    return (target[:, None] == jnp.arange(amount)[None, :]).astype(jnp.bfloat16)


def split(values):
    high = values.astype(jnp.bfloat16)
    return high, (values - high.astype(jnp.float32)).astype(jnp.bfloat16)


def dot(left, right):
    return jnp.dot(left, right, preferred_element_type=jnp.float32)


def scale_of(code):
    return jnp.exp2(code * (1.0 / STEPS))


def screen_kernel(part, int_mask, slab_ref, coded_ref, *later_refs):
    slab_rows, slab_cols = slab_ref.shape
    cols = coded_ref.shape[1]
    span = slab_cols // W
    row_label = lax.axis_index("occ") * slab_rows // W // VT * NVT
    col_label = lax.axis_index("vir") * slab_cols // W // VT * NVT
    natural = lax.broadcasted_iota(jnp.int32, (slab_cols, 1), 0)
    a, b = natural // W, natural % W
    target = b // span * (part * span) + (a // part * part + b % part) * part + a % part
    place = lax.broadcasted_iota(jnp.int32, (slab_cols, cols), 1)
    to = lax.broadcasted_iota(jnp.int32, (1, cols), 1)
    second = lax.broadcasted_iota(jnp.int32, (slab_rows, 1), 0) % W >= VT
    for chunk in range(span // part):
        right = to // (part * span) * span + chunk * part + to // part % part >= VT
        kept = [
            jnp.where(right, int_mask[label, col_label + 1], int_mask[label, col_label])
            for label in (row_label, row_label + 1)
        ]
        ones = place == jnp.where(b % span // part == chunk, target, -1)
        moved = dot(slab_ref[...], ones.astype(jnp.float32).astype(jnp.bfloat16))
        moved = jnp.where(jnp.where(second, kept[1], kept[0]) > 0, moved, 0.0)
        if chunk:
            at = 0
            for later_ref in later_refs:
                later_ref[...] = moved[:, at : at + later_ref.shape[1]].astype(jnp.bfloat16)
                at += later_ref.shape[1]
        else:
            most = jnp.maximum(jnp.max(jnp.abs(moved), axis=0, keepdims=True), 1e-30)
            code = jnp.floor(jnp.log2(most)) + 1.0
            coded = jnp.round(moved * jnp.exp2(SLAB_BITS - code)).astype(jnp.int32).astype(jnp.int16)
            code_rows = jnp.broadcast_to(code.astype(jnp.int32), (CODE_ROWS, cols)).astype(jnp.int16)
            coded_ref[:slab_rows, :] = coded
            coded_ref[slab_rows:, :] = code_rows


def screen_call(chunks, int_mask, integrals):
    slab_rows, slab_cols = integrals.shape
    cols = slab_cols // chunks
    later_cols = [cols // 4, cols - cols // 4] if chunks > 1 else []
    vmem = pl.BlockSpec(memory_space=pltpu.VMEM)
    return pl.pallas_call(
        functools.partial(screen_kernel, slab_cols // W // chunks),
        in_specs=[pl.BlockSpec(memory_space=pltpu.SMEM), vmem],
        out_specs=[vmem] * (1 + len(later_cols)),
        out_shape=[jax.ShapeDtypeStruct((slab_rows + CODE_ROWS, cols), jnp.int16)]
        + [jax.ShapeDtypeStruct((slab_rows, each), integrals.dtype) for each in later_cols],
        compiler_params=pltpu.CompilerParams(vmem_limit_bytes=VMEM_LIMIT),
        name="screen",
    )(int_mask, integrals)


def ladder_kernel(tile_total, vir_count, chunks, coded, parts, amp_mask, numbers, rows_ref, *refs):
    gathered_refs, refs = refs[:parts], refs[parts:]
    ladder_ref, packed_ref, product = refs[:3]
    slab_refs = gathered_refs
    if coded:
        slab_refs, stage, sems = refs[3:4], refs[4], refs[5]
    step = pl.program_id(0)
    cols = product.shape[1]
    slab_rows = slab_refs[0].shape[0] // tile_total
    shard_rows = slab_rows + CODE_ROWS
    block = cols // vir_count
    lanes = block // chunks

    def multiply():
        tile = step
        lane = lax.broadcasted_iota(jnp.int32, (1, W * W), 1)
        left = lane % W < VT
        keep = jnp.where(
            lane < W * VT,
            jnp.where(left, amp_mask[tile, 0], amp_mask[tile, 1]),
            jnp.where(left, amp_mask[tile, 2], amp_mask[tile, 3]),
        )
        keep = keep.astype(jnp.float32).astype(jnp.bfloat16)
        screened = rows_ref[...] * keep
        at = 0
        for slab_ref in slab_refs:
            product[:, at : at + slab_ref.shape[1]] = dot(screened, slab_ref[...])
            at += slab_ref.shape[1]

    def decode():
        def copy_of(shard):
            at = pl.ds(pl.multiple_of(shard * shard_rows, CODE_ROWS), shard_rows)
            return pltpu.make_async_copy(gathered_refs[0].at[at, :], stage.at[at, :], sems.at[shard])

        for shard in range(tile_total):
            copy_of(shard).start()

        def use(shard, carry):
            copy_of(shard).wait()
            at = pl.multiple_of(shard * shard_rows, CODE_ROWS)
            code = stage[pl.ds(pl.multiple_of(at + slab_rows, CODE_ROWS), CODE_ROWS), :]
            values = stage[pl.ds(at, slab_rows), :].astype(jnp.int32).astype(jnp.float32)
            scale = jnp.exp2(code.astype(jnp.int32).astype(jnp.float32)[:1] - SLAB_BITS)
            to = pl.ds(pl.multiple_of(shard * slab_rows, slab_rows), slab_rows)
            slab_refs[0][to, :] = (values * scale).astype(jnp.bfloat16)
            return carry

        lax.fori_loop(0, tile_total, use, 0)

    def finish():
        tile = jnp.maximum(step - 1, 0)
        pair = lax.broadcasted_iota(jnp.int32, (PAIR_SQ, 1), 0)
        own_number = numbers[lax.axis_index("occ")]
        nonzero = (pair // ORBITALS_IN_GRP < own_number) & (pair % ORBITALS_IN_GRP < numbers[tile])
        ladder = jnp.where(nonzero, product[...], 0.0)
        for h in range(chunks):
            ladder_ref[h] = jnp.concatenate(
                [ladder[:, v * block + h * lanes : v * block + (h + 1) * lanes] for v in range(vir_count)], axis=1
            )
        by_place = ladder.reshape(ORBITALS_IN_GRP, ORBITALS_IN_GRP, cols)
        mirror = jnp.swapaxes(by_place, 0, 1).reshape(PAIR_SQ, cols)
        most = jnp.maximum(jnp.max(jnp.abs(ladder), axis=0, keepdims=True), 1e-30)
        code = jnp.ceil(jnp.log2(most) * STEPS)
        coded_rows = jnp.round(mirror * (TOP / scale_of(code))).astype(jnp.int32).astype(jnp.int16)
        code_rows = jnp.broadcast_to(code.astype(jnp.int32), (EXCHANGE_CODE_ROWS, cols)).astype(jnp.int16)
        for v in range(vir_count):
            packed_ref[0, v, :PAIR_SQ] = coded_rows[:, v * block : (v + 1) * block]
            packed_ref[0, v, PAIR_SQ:] = code_rows[:, v * block : (v + 1) * block]

    if coded:

        @pl.when(step == 0)
        def _():
            decode()

    @pl.when(step < tile_total)
    def _():
        finish()
        multiply()

    @pl.when(step == tile_total)
    def _():
        finish()


def ladder_call(tile_total, vir_count, chunks, amp_mask, numbers, amplitudes, slab):
    coded = slab[0].dtype == jnp.int16
    cols = sum(part.shape[1] for part in slab)
    block = cols // vir_count
    smem = pl.BlockSpec(memory_space=pltpu.SMEM)
    rows = tile_total * PAIR_SQ
    before = lambda step: jnp.maximum(step - 1, 0)
    packed_block = (vir_count, PAIR_SQ + EXCHANGE_CODE_ROWS, block)
    return pl.pallas_call(
        functools.partial(ladder_kernel, tile_total, vir_count, chunks, coded, len(slab)),
        grid=(tile_total + 1,),
        in_specs=[
            smem,
            smem,
            pl.BlockSpec((PAIR_SQ, W * W), lambda step: (jnp.minimum(step, tile_total - 1), 0)),
            *[
                pl.BlockSpec(memory_space=pl.ANY) if coded else pl.BlockSpec(part.shape, lambda step: (0, 0))
                for part in slab
            ],
        ],
        out_specs=[
            pl.BlockSpec((chunks, PAIR_SQ, cols // chunks), lambda step: (0, before(step), 0)),
            pl.BlockSpec((1,) + packed_block, lambda step: (before(step), 0, 0, 0)),
        ],
        out_shape=[
            jax.ShapeDtypeStruct((chunks, rows, cols // chunks), jnp.float32),
            jax.ShapeDtypeStruct((tile_total,) + packed_block, jnp.int16),
        ],
        scratch_shapes=[pltpu.VMEM((PAIR_SQ, cols), jnp.float32)]
        + [
            pltpu.VMEM((W * W, cols), jnp.bfloat16),
            pltpu.VMEM(slab[0].shape, slab[0].dtype),
            pltpu.SemaphoreType.DMA((tile_total,)),
        ]
        * coded,
        compiler_params=pltpu.CompilerParams(vmem_limit_bytes=VMEM_LIMIT),
        cost_estimate=pl.CostEstimate(
            flops=2 * rows * cols * W * W,
            bytes_accessed=rows * (W * W * 2 + cols * 6) + W * W * cols * 2,
            transcendentals=0,
        ),
        name="ladder",
    )(amp_mask, numbers, amplitudes, *slab)


def moved_columns(values, spread_ref):
    both = dot(jnp.concatenate(split(values), axis=0), spread_ref[...])
    return both[: values.shape[0]] + both[values.shape[0] :]


def direct_kernel(spread_ref, *refs):
    refs[-1][...] = moved_columns(jnp.concatenate([ref[0] for ref in refs[:-1]], axis=1), spread_ref)


def direct_call(chunk, spread, ladders):
    rows = ladders[0].shape[1]
    step_rows = AT_ONCE * PAIR_SQ
    return pl.pallas_call(
        direct_kernel,
        grid=(rows // step_rows,),
        in_specs=[pl.BlockSpec(spread.shape, lambda step: (0, 0))]
        + [pl.BlockSpec((1, step_rows, ladder.shape[2]), lambda step: (chunk, step, 0)) for ladder in ladders],
        out_specs=pl.BlockSpec((step_rows, spread.shape[1]), lambda step: (step, 0)),
        out_shape=jax.ShapeDtypeStruct((rows, spread.shape[1]), jnp.float32),
        compiler_params=pltpu.CompilerParams(vmem_limit_bytes=VMEM_LIMIT),
        cost_estimate=pl.CostEstimate(
            flops=4 * rows * spread.size, bytes_accessed=rows * spread.shape[1] * 8, transcendentals=0
        ),
        name="direct",
    )(spread, *ladders)


def update_kernel(vir_count, at_once, spread_ref, vir_ref, occ_ref, *refs):
    arrived_refs, refs = refs[:vir_count], refs[vir_count:]
    direct_refs = refs[:at_once]
    tiles = []
    for n in range(at_once):
        blocks = []
        for v in range(vir_count):
            code = arrived_refs[v][n, 0, PAIR_SQ:].astype(jnp.int32).astype(jnp.float32)[:1]
            values = arrived_refs[v][n, 0, :PAIR_SQ].astype(jnp.int32).astype(jnp.float32)
            blocks.append(values * (scale_of(code) * (1.0 / TOP)))
        tiles.append(jnp.concatenate(blocks, axis=1))
    mirror = moved_columns(jnp.concatenate(tiles, axis=0), spread_ref)
    for n, direct_ref in enumerate(direct_refs):
        at = slice(n * PAIR_SQ, (n + 1) * PAIR_SQ)
        occ = jnp.transpose(jnp.broadcast_to(occ_ref[n], (128, PAIR_SQ)))[:, :1]
        refs[-1][at, :] = (direct_ref[...] + mirror[at]) / (vir_ref[...] - occ)


def update_call(chunk, chunks, at_once, arrived, spread, vir_sum, occ_sum, direct, earlier):
    cols = spread.shape[1]
    rows = direct.shape[0]
    step_rows = at_once * PAIR_SQ
    vir_count = arrived.shape[1]
    args = [spread, vir_sum, occ_sum] + [arrived] * vir_count + [direct] * at_once
    in_specs = [
        pl.BlockSpec(spread.shape, lambda step: (0, 0)),
        pl.BlockSpec((1, cols), lambda step: (0, chunk)),
        pl.BlockSpec((at_once, 1, PAIR_SQ), lambda step: (step, 0, 0)),
    ]
    in_specs += [
        pl.BlockSpec((at_once, 1) + arrived.shape[2:], lambda step, v=v: (step, v, 0, 0)) for v in range(vir_count)
    ]
    in_specs += [pl.BlockSpec((PAIR_SQ, cols), lambda step, n=n: (step * at_once + n, 0)) for n in range(at_once)]
    aliases = {}
    if earlier is not None:
        aliases = {len(args): 0}
        args.append(earlier)
        in_specs.append(pl.BlockSpec(memory_space=pl.ANY))
    return pl.pallas_call(
        functools.partial(update_kernel, vir_count, at_once),
        grid=(rows // step_rows,),
        in_specs=in_specs,
        out_specs=pl.BlockSpec((step_rows, cols), lambda step: (step, chunk)),
        out_shape=jax.ShapeDtypeStruct((rows, chunks * cols), jnp.float32),
        input_output_aliases=aliases,
        compiler_params=pltpu.CompilerParams(vmem_limit_bytes=VMEM_LIMIT),
        cost_estimate=pl.CostEstimate(
            flops=4 * rows * spread.size, bytes_accessed=rows * cols * 10, transcendentals=0
        ),
        name="update",
    )(*args)


def body(amplitudes, amp_mask, integrals, int_mask, group_orbital_numbers, occ_energy, vir_energy):
    tile_total = lax.axis_size("occ")
    vir_count = lax.axis_size("vir")
    row_tile = lax.axis_index("occ")
    vir_place = lax.axis_index("vir")
    span = W // vir_count
    slab_cols = span * W
    chunks = 2 if span >= 16 else 1
    width = span // chunks
    block = width * span
    rows = PAIR_SQ + EXCHANGE_CODE_ROWS

    def exchanged(packed):
        moved = lax.all_to_all(
            packed.reshape(tile_total * vir_count, rows, block), ("occ", "vir"), split_axis=0, concat_axis=0, tiled=True
        )
        return moved.reshape(tile_total, vir_count, rows, block)

    coded, *later = screen_call(chunks, int_mask, integrals)
    later = [lax.all_gather(part, "occ", axis=0, tiled=True) for part in later]
    slabs = [[lax.all_gather(coded, "occ", axis=0, tiled=True)]] + [later] * (chunks - 1)
    ladders, arrived = [], []
    for slab in slabs:
        ladder, packed = ladder_call(
            tile_total, vir_count, chunks, amp_mask[0], group_orbital_numbers, amplitudes, slab
        )
        ladders.append(ladder)
        arrived.append(exchanged(packed))

    place = jnp.arange(vir_count * block)
    owner, there_part = place // block, place // (width * width) % chunks
    here, there = place // width % width, place % width
    mirror_spread = one_hot_of(here * W + owner * span + there_part * width + there, width * W)
    place = jnp.arange(vir_count * width * width)
    owner, b, a = place // (width * width), place // width % width, place % width
    direct_spread = one_hot_of(
        jnp.concatenate([a * W + owner * span + c * width + b for c in range(chunks)]), width * W
    )

    occ_table = occ_energy.reshape(tile_total, ORBITALS_IN_GRP)
    own_energy = lax.dynamic_slice_in_dim(occ_table, row_tile, 1, 0)[0]
    occ_sum = (own_energy[None, :, None] + occ_table[:, None, :]).reshape(tile_total, 1, PAIR_SQ)
    vir_own = lax.dynamic_slice_in_dim(vir_energy, vir_place * span, span, 0)
    vir_sum = (vir_own[:, None] + vir_energy[None, :]).reshape(1, -1)
    update = None
    for chunk in range(chunks):
        direct = direct_call(chunk, direct_spread, ladders)
        update = update_call(chunk, chunks, 4, arrived[chunk], mirror_spread, vir_sum, occ_sum, direct, update)
    return update


def solution(mesh):
    in_specs = (P("occ", None), P("occ", None, None), P("occ", "vir"), P(), P(), P(), P())
    out_specs = P("occ", "vir")
    return jax.shard_map(body, mesh=mesh, in_specs=in_specs, out_specs=out_specs, check_vma=False)
```

```python
import functools

import jax
import jax.numpy as jnp
from jax import lax
from jax.experimental import pallas as pl
from jax.experimental.pallas import tpu as pltpu
from jax.sharding import PartitionSpec as P

VT = 32
NVT = 2
W = 64
ORBITALS_IN_GRP = 16
PAIR_SQ = ORBITALS_IN_GRP * ORBITALS_IN_GRP
CODE_ROWS = 16
EXCHANGE_CODE_ROWS = 8
AT_ONCE = 4
CODED_PARTS = 2
SLAB_BITS = 14.0
TOP = 32700.0
STEPS = 8.0
VMEM_LIMIT = 56 * 1024 * 1024


def one_hot_of(target, amount):
    return (target[:, None] == jnp.arange(amount)[None, :]).astype(jnp.bfloat16)


def split(values):
    high = values.astype(jnp.bfloat16)
    return high, (values - high.astype(jnp.float32)).astype(jnp.bfloat16)


def dot(left, right):
    return jnp.dot(left, right, preferred_element_type=jnp.float32)


def scale_of(code):
    return jnp.exp2(code * (1.0 / STEPS))


def screen_kernel(part, int_mask, slab_ref, *refs):
    coded_refs, later_refs = refs[:CODED_PARTS], refs[CODED_PARTS:]
    slab_rows, slab_cols = slab_ref.shape
    cols = sum(ref.shape[1] for ref in coded_refs)
    span = slab_cols // W
    row_label = lax.axis_index("occ") * slab_rows // W // VT * NVT
    col_label = lax.axis_index("vir") * slab_cols // W // VT * NVT
    natural = lax.broadcasted_iota(jnp.int32, (slab_cols, 1), 0)
    a, b = natural // W, natural % W
    target = b // span * (part * span) + (a // part * part + b % part) * part + a % part
    place = lax.broadcasted_iota(jnp.int32, (slab_cols, cols), 1)
    to = lax.broadcasted_iota(jnp.int32, (1, cols), 1)
    second = lax.broadcasted_iota(jnp.int32, (slab_rows, 1), 0) % W >= VT
    for chunk in range(span // part):
        right = to // (part * span) * span + chunk * part + to // part % part >= VT
        kept = [
            jnp.where(right, int_mask[label, col_label + 1], int_mask[label, col_label])
            for label in (row_label, row_label + 1)
        ]
        ones = place == jnp.where(b % span // part == chunk, target, -1)
        moved = dot(slab_ref[...], ones.astype(jnp.float32).astype(jnp.bfloat16))
        moved = jnp.where(jnp.where(second, kept[1], kept[0]) > 0, moved, 0.0)
        if chunk:
            later_refs[chunk - 1][...] = moved.astype(jnp.bfloat16)
        else:
            most = jnp.maximum(jnp.max(jnp.abs(moved), axis=0, keepdims=True), 1e-30)
            code = jnp.floor(jnp.log2(most)) + 1.0
            coded = jnp.round(moved * jnp.exp2(SLAB_BITS - code)).astype(jnp.int32).astype(jnp.int16)
            code_rows = jnp.broadcast_to(code.astype(jnp.int32), (CODE_ROWS, cols)).astype(jnp.int16)
            at = 0
            for coded_ref in coded_refs:
                end = at + coded_ref.shape[1]
                coded_ref[:slab_rows, :] = coded[:, at:end]
                coded_ref[slab_rows:, :] = code_rows[:, at:end]
                at = end


def screen_call(chunks, int_mask, integrals):
    slab_rows, slab_cols = integrals.shape
    cols = slab_cols // chunks
    coded_cols = [cols - cols // 4, cols // 4]
    vmem = pl.BlockSpec(memory_space=pltpu.VMEM)
    return pl.pallas_call(
        functools.partial(screen_kernel, slab_cols // W // chunks),
        in_specs=[pl.BlockSpec(memory_space=pltpu.SMEM), vmem],
        out_specs=[vmem] * (CODED_PARTS + chunks - 1),
        out_shape=[jax.ShapeDtypeStruct((slab_rows + CODE_ROWS, each), jnp.int16) for each in coded_cols]
        + [jax.ShapeDtypeStruct((slab_rows, cols), integrals.dtype)] * (chunks - 1),
        compiler_params=pltpu.CompilerParams(vmem_limit_bytes=VMEM_LIMIT),
        name="screen",
    )(int_mask, integrals)


def ladder_kernel(tile_total, vir_count, chunks, coded, parts, amp_mask, numbers, rows_ref, *refs):
    gathered_refs, refs = refs[:parts], refs[parts:]
    ladder_ref, packed_ref, product = refs[:3]
    slab_refs = gathered_refs
    if coded:
        slab_refs, sems, stages = refs[3:4], refs[4], refs[5:]
    step = pl.program_id(0)
    cols = product.shape[1]
    slab_rows = slab_refs[0].shape[0] // tile_total
    shard_rows = slab_rows + CODE_ROWS
    block = cols // vir_count
    lanes = block // chunks

    def multiply():
        tile = step
        lane = lax.broadcasted_iota(jnp.int32, (1, W * W), 1)
        left = lane % W < VT
        keep = jnp.where(
            lane < W * VT,
            jnp.where(left, amp_mask[tile, 0], amp_mask[tile, 1]),
            jnp.where(left, amp_mask[tile, 2], amp_mask[tile, 3]),
        )
        keep = keep.astype(jnp.float32).astype(jnp.bfloat16)
        screened = rows_ref[...] * keep
        at = 0
        for slab_ref in slab_refs:
            product[:, at : at + slab_ref.shape[1]] = dot(screened, slab_ref[...])
            at += slab_ref.shape[1]

    def decode():
        def copy_of(n, shard):
            at = pl.ds(pl.multiple_of(shard * shard_rows, CODE_ROWS), shard_rows)
            return pltpu.make_async_copy(gathered_refs[n].at[at, :], stages[n].at[at, :], sems.at[n, shard])

        for shard in range(tile_total):
            for n in range(parts):
                copy_of(n, shard).start()

        def use(shard, carry):
            at = pl.multiple_of(shard * shard_rows, CODE_ROWS)
            to = pl.ds(pl.multiple_of(shard * slab_rows, slab_rows), slab_rows)
            col = 0
            for n, stage in enumerate(stages):
                copy_of(n, shard).wait()
                code = stage[pl.ds(pl.multiple_of(at + slab_rows, CODE_ROWS), CODE_ROWS), :]
                values = stage[pl.ds(at, slab_rows), :].astype(jnp.int32).astype(jnp.float32)
                scale = jnp.exp2(code.astype(jnp.int32).astype(jnp.float32)[:1] - SLAB_BITS)
                slab_refs[0][to, col : col + stage.shape[1]] = (values * scale).astype(jnp.bfloat16)
                col += stage.shape[1]
            return carry

        lax.fori_loop(0, tile_total, use, 0)

    def finish():
        tile = jnp.maximum(step - 1, 0)
        pair = lax.broadcasted_iota(jnp.int32, (PAIR_SQ, 1), 0)
        own_number = numbers[lax.axis_index("occ")]
        nonzero = (pair // ORBITALS_IN_GRP < own_number) & (pair % ORBITALS_IN_GRP < numbers[tile])
        ladder = jnp.where(nonzero, product[...], 0.0)
        for h in range(chunks):
            ladder_ref[h] = jnp.concatenate(
                [ladder[:, v * block + h * lanes : v * block + (h + 1) * lanes] for v in range(vir_count)], axis=1
            )
        by_place = ladder.reshape(ORBITALS_IN_GRP, ORBITALS_IN_GRP, cols)
        mirror = jnp.swapaxes(by_place, 0, 1).reshape(PAIR_SQ, cols)
        most = jnp.maximum(jnp.max(jnp.abs(ladder), axis=0, keepdims=True), 1e-30)
        code = jnp.ceil(jnp.log2(most) * STEPS)
        coded_rows = jnp.round(mirror * (TOP / scale_of(code))).astype(jnp.int32).astype(jnp.int16)
        code_rows = jnp.broadcast_to(code.astype(jnp.int32), (EXCHANGE_CODE_ROWS, cols)).astype(jnp.int16)
        for v in range(vir_count):
            packed_ref[0, v, :PAIR_SQ] = coded_rows[:, v * block : (v + 1) * block]
            packed_ref[0, v, PAIR_SQ:] = code_rows[:, v * block : (v + 1) * block]

    if coded:

        @pl.when(step == 0)
        def _():
            decode()

    @pl.when(step < tile_total)
    def _():
        finish()
        multiply()

    @pl.when(step == tile_total)
    def _():
        finish()


def ladder_call(tile_total, vir_count, chunks, amp_mask, numbers, amplitudes, slab):
    coded = slab[0].dtype == jnp.int16
    cols = sum(part.shape[1] for part in slab)
    block = cols // vir_count
    smem = pl.BlockSpec(memory_space=pltpu.SMEM)
    rows = tile_total * PAIR_SQ
    before = lambda step: jnp.maximum(step - 1, 0)
    packed_block = (vir_count, PAIR_SQ + EXCHANGE_CODE_ROWS, block)
    return pl.pallas_call(
        functools.partial(ladder_kernel, tile_total, vir_count, chunks, coded, len(slab)),
        grid=(tile_total + 1,),
        in_specs=[
            smem,
            smem,
            pl.BlockSpec((PAIR_SQ, W * W), lambda step: (jnp.minimum(step, tile_total - 1), 0)),
            *[
                pl.BlockSpec(memory_space=pl.ANY) if coded else pl.BlockSpec(part.shape, lambda step: (0, 0))
                for part in slab
            ],
        ],
        out_specs=[
            pl.BlockSpec((chunks, PAIR_SQ, cols // chunks), lambda step: (0, before(step), 0)),
            pl.BlockSpec((1,) + packed_block, lambda step: (before(step), 0, 0, 0)),
        ],
        out_shape=[
            jax.ShapeDtypeStruct((chunks, rows, cols // chunks), jnp.float32),
            jax.ShapeDtypeStruct((tile_total,) + packed_block, jnp.int16),
        ],
        scratch_shapes=[pltpu.VMEM((PAIR_SQ, cols), jnp.float32)]
        + [
            pltpu.VMEM((W * W, cols), jnp.bfloat16),
            pltpu.SemaphoreType.DMA((len(slab), tile_total)),
            *[pltpu.VMEM(part.shape, part.dtype) for part in slab],
        ]
        * coded,
        compiler_params=pltpu.CompilerParams(vmem_limit_bytes=VMEM_LIMIT),
        cost_estimate=pl.CostEstimate(
            flops=2 * rows * cols * W * W,
            bytes_accessed=rows * (W * W * 2 + cols * 6) + W * W * cols * 2,
            transcendentals=0,
        ),
        name="ladder",
    )(amp_mask, numbers, amplitudes, *slab)


def moved_columns(values, spread_ref):
    both = dot(jnp.concatenate(split(values), axis=0), spread_ref[...])
    return both[: values.shape[0]] + both[values.shape[0] :]


def direct_kernel(spread_ref, *refs):
    refs[-1][...] = moved_columns(jnp.concatenate([ref[0] for ref in refs[:-1]], axis=1), spread_ref)


def direct_call(chunk, spread, ladders):
    rows = ladders[0].shape[1]
    step_rows = AT_ONCE * PAIR_SQ
    return pl.pallas_call(
        direct_kernel,
        grid=(rows // step_rows,),
        in_specs=[pl.BlockSpec(spread.shape, lambda step: (0, 0))]
        + [pl.BlockSpec((1, step_rows, ladder.shape[2]), lambda step: (chunk, step, 0)) for ladder in ladders],
        out_specs=pl.BlockSpec((step_rows, spread.shape[1]), lambda step: (step, 0)),
        out_shape=jax.ShapeDtypeStruct((rows, spread.shape[1]), jnp.float32),
        compiler_params=pltpu.CompilerParams(vmem_limit_bytes=VMEM_LIMIT),
        cost_estimate=pl.CostEstimate(
            flops=4 * rows * spread.size, bytes_accessed=rows * spread.shape[1] * 8, transcendentals=0
        ),
        name="direct",
    )(spread, *ladders)


def update_kernel(vir_count, at_once, spread_ref, vir_ref, occ_ref, *refs):
    arrived_refs, refs = refs[:vir_count], refs[vir_count:]
    direct_refs = refs[:at_once]
    tiles = []
    for n in range(at_once):
        blocks = []
        for v in range(vir_count):
            code = arrived_refs[v][n, 0, PAIR_SQ:].astype(jnp.int32).astype(jnp.float32)[:1]
            values = arrived_refs[v][n, 0, :PAIR_SQ].astype(jnp.int32).astype(jnp.float32)
            blocks.append(values * (scale_of(code) * (1.0 / TOP)))
        tiles.append(jnp.concatenate(blocks, axis=1))
    mirror = moved_columns(jnp.concatenate(tiles, axis=0), spread_ref)
    for n, direct_ref in enumerate(direct_refs):
        at = slice(n * PAIR_SQ, (n + 1) * PAIR_SQ)
        occ = jnp.transpose(jnp.broadcast_to(occ_ref[n], (128, PAIR_SQ)))[:, :1]
        refs[-1][at, :] = (direct_ref[...] + mirror[at]) / (vir_ref[...] - occ)


def update_call(chunk, chunks, at_once, arrived, spread, vir_sum, occ_sum, direct, earlier):
    cols = spread.shape[1]
    rows = direct.shape[0]
    step_rows = at_once * PAIR_SQ
    vir_count = arrived.shape[1]
    args = [spread, vir_sum, occ_sum] + [arrived] * vir_count + [direct] * at_once
    in_specs = [
        pl.BlockSpec(spread.shape, lambda step: (0, 0)),
        pl.BlockSpec((1, cols), lambda step: (0, chunk)),
        pl.BlockSpec((at_once, 1, PAIR_SQ), lambda step: (step, 0, 0)),
    ]
    in_specs += [
        pl.BlockSpec((at_once, 1) + arrived.shape[2:], lambda step, v=v: (step, v, 0, 0)) for v in range(vir_count)
    ]
    in_specs += [pl.BlockSpec((PAIR_SQ, cols), lambda step, n=n: (step * at_once + n, 0)) for n in range(at_once)]
    aliases = {}
    if earlier is not None:
        aliases = {len(args): 0}
        args.append(earlier)
        in_specs.append(pl.BlockSpec(memory_space=pl.ANY))
    return pl.pallas_call(
        functools.partial(update_kernel, vir_count, at_once),
        grid=(rows // step_rows,),
        in_specs=in_specs,
        out_specs=pl.BlockSpec((step_rows, cols), lambda step: (step, chunk)),
        out_shape=jax.ShapeDtypeStruct((rows, chunks * cols), jnp.float32),
        input_output_aliases=aliases,
        compiler_params=pltpu.CompilerParams(vmem_limit_bytes=VMEM_LIMIT),
        cost_estimate=pl.CostEstimate(
            flops=4 * rows * spread.size, bytes_accessed=rows * cols * 10, transcendentals=0
        ),
        name="update",
    )(*args)


def body(amplitudes, amp_mask, integrals, int_mask, group_orbital_numbers, occ_energy, vir_energy):
    tile_total = lax.axis_size("occ")
    vir_count = lax.axis_size("vir")
    row_tile = lax.axis_index("occ")
    vir_place = lax.axis_index("vir")
    span = W // vir_count
    slab_cols = span * W
    chunks = 2 if span >= 16 else 1
    width = span // chunks
    block = width * span
    rows = PAIR_SQ + EXCHANGE_CODE_ROWS

    def exchanged(packed):
        moved = lax.all_to_all(
            packed.reshape(tile_total * vir_count, rows, block), ("occ", "vir"), split_axis=0, concat_axis=0, tiled=True
        )
        return moved.reshape(tile_total, vir_count, rows, block)

    screened = screen_call(chunks, int_mask, integrals)
    first = lax.all_gather(screened[0], "occ", axis=0, tiled=True)
    *screened, first = lax.optimization_barrier((*screened[1:], first))
    rest = [lax.all_gather(part, "occ", axis=0, tiled=True) for part in screened]
    slabs = [[first, rest[0]]] + [[part] for part in rest[1:]]
    ladders, arrived = [], []
    for slab in slabs:
        ladder, packed = ladder_call(
            tile_total, vir_count, chunks, amp_mask[0], group_orbital_numbers, amplitudes, slab
        )
        ladders.append(ladder)
        arrived.append(exchanged(packed))

    place = jnp.arange(vir_count * block)
    owner, there_part = place // block, place // (width * width) % chunks
    here, there = place // width % width, place % width
    mirror_spread = one_hot_of(here * W + owner * span + there_part * width + there, width * W)
    place = jnp.arange(vir_count * width * width)
    owner, b, a = place // (width * width), place // width % width, place % width
    direct_spread = one_hot_of(
        jnp.concatenate([a * W + owner * span + c * width + b for c in range(chunks)]), width * W
    )

    occ_table = occ_energy.reshape(tile_total, ORBITALS_IN_GRP)
    own_energy = lax.dynamic_slice_in_dim(occ_table, row_tile, 1, 0)[0]
    occ_sum = (own_energy[None, :, None] + occ_table[:, None, :]).reshape(tile_total, 1, PAIR_SQ)
    vir_own = lax.dynamic_slice_in_dim(vir_energy, vir_place * span, span, 0)
    vir_sum = (vir_own[:, None] + vir_energy[None, :]).reshape(1, -1)
    update = None
    for chunk in range(chunks):
        direct = direct_call(chunk, direct_spread, ladders)
        update = update_call(chunk, chunks, 4, arrived[chunk], mirror_spread, vir_sum, occ_sum, direct, update)
    return update


def solution(mesh):
    in_specs = (P("occ", None), P("occ", None, None), P("occ", "vir"), P(), P(), P(), P())
    out_specs = P("occ", "vir")
    return jax.shard_map(body, mesh=mesh, in_specs=in_specs, out_specs=out_specs, check_vma=False)
```

```python
import functools

import jax
import jax.numpy as jnp
from jax import lax
from jax.experimental import pallas as pl
from jax.experimental.pallas import tpu as pltpu
from jax.sharding import PartitionSpec as P

VT = 32
NVT = 2
W = 64
ORBITALS_IN_GRP = 16
PAIR_SQ = ORBITALS_IN_GRP * ORBITALS_IN_GRP
CODE_ROWS = 16
EXCHANGE_CODE_ROWS = 8
AT_ONCE = 4
CODED_PARTS = 2
SLAB_BITS = 14.0
TOP = 32700.0
STEPS = 8.0
VMEM_LIMIT = 56 * 1024 * 1024


def one_hot_of(target, amount):
    return (target[:, None] == jnp.arange(amount)[None, :]).astype(jnp.bfloat16)


def split(values):
    high = values.astype(jnp.bfloat16)
    return high, (values - high.astype(jnp.float32)).astype(jnp.bfloat16)


def dot(left, right):
    return jnp.dot(left, right, preferred_element_type=jnp.float32)


def scale_of(code):
    return jnp.exp2(code * (1.0 / STEPS))


def screen_kernel(part, int_mask, slab_ref, *refs):
    coded_refs, later_refs = refs[:CODED_PARTS], refs[CODED_PARTS:]
    slab_rows, slab_cols = slab_ref.shape
    cols = coded_refs[0].shape[1]
    span = slab_cols // W
    row_label = lax.axis_index("occ") * slab_rows // W // VT * NVT
    col_label = lax.axis_index("vir") * slab_cols // W // VT * NVT
    natural = lax.broadcasted_iota(jnp.int32, (slab_cols, 1), 0)
    a, b = natural // W, natural % W
    target = b // span * (part * span) + (a // part * part + b % part) * part + a % part
    place = lax.broadcasted_iota(jnp.int32, (slab_cols, cols), 1)
    to = lax.broadcasted_iota(jnp.int32, (1, cols), 1)
    second = lax.broadcasted_iota(jnp.int32, (slab_rows, 1), 0) % W >= VT
    for chunk in range(span // part):
        right = to // (part * span) * span + chunk * part + to // part % part >= VT
        kept = [
            jnp.where(right, int_mask[label, col_label + 1], int_mask[label, col_label])
            for label in (row_label, row_label + 1)
        ]
        ones = place == jnp.where(b % span // part == chunk, target, -1)
        moved = dot(slab_ref[...], ones.astype(jnp.float32).astype(jnp.bfloat16))
        moved = jnp.where(jnp.where(second, kept[1], kept[0]) > 0, moved, 0.0)
        if chunk:
            later_refs[chunk - 1][...] = moved.astype(jnp.bfloat16)
        else:
            most = jnp.maximum(jnp.max(jnp.abs(moved), axis=0, keepdims=True), 1e-30)
            code = jnp.floor(jnp.log2(most)) + 1.0
            coded = jnp.round(moved * jnp.exp2(SLAB_BITS - code)).astype(jnp.int32).astype(jnp.int16)
            code_rows = jnp.broadcast_to(code.astype(jnp.int32), (CODE_ROWS, cols)).astype(jnp.int16)
            at = 0
            for coded_ref in coded_refs:
                rows = coded_ref.shape[0] - CODE_ROWS
                coded_ref[:rows, :] = coded[at : at + rows]
                coded_ref[rows:, :] = code_rows
                at += rows


def screen_call(chunks, int_mask, integrals):
    slab_rows, slab_cols = integrals.shape
    cols = slab_cols // chunks
    coded_rows = [slab_rows - slab_rows // 8, slab_rows // 8]
    vmem = pl.BlockSpec(memory_space=pltpu.VMEM)
    return pl.pallas_call(
        functools.partial(screen_kernel, slab_cols // W // chunks),
        in_specs=[pl.BlockSpec(memory_space=pltpu.SMEM), vmem],
        out_specs=[vmem] * (CODED_PARTS + chunks - 1),
        out_shape=[jax.ShapeDtypeStruct((each + CODE_ROWS, cols), jnp.int16) for each in coded_rows]
        + [jax.ShapeDtypeStruct((slab_rows, cols), integrals.dtype)] * (chunks - 1),
        compiler_params=pltpu.CompilerParams(vmem_limit_bytes=VMEM_LIMIT),
        name="screen",
    )(int_mask, integrals)


def ladder_kernel(tile_total, vir_count, chunks, coded, parts, amp_mask, numbers, rows_ref, *refs):
    gathered_refs, refs = refs[:parts], refs[parts:]
    ladder_ref, packed_ref, product = refs[:3]
    slab_refs = gathered_refs
    if coded:
        slab_refs, sems, stages = refs[3:4], refs[4], refs[5:]
    step = pl.program_id(0)
    cols = product.shape[1]
    slab_rows = slab_refs[0].shape[0] // tile_total
    block = cols // vir_count
    lanes = block // chunks

    def multiply():
        tile = step
        lane = lax.broadcasted_iota(jnp.int32, (1, W * W), 1)
        left = lane % W < VT
        keep = jnp.where(
            lane < W * VT,
            jnp.where(left, amp_mask[tile, 0], amp_mask[tile, 1]),
            jnp.where(left, amp_mask[tile, 2], amp_mask[tile, 3]),
        )
        keep = keep.astype(jnp.float32).astype(jnp.bfloat16)
        screened = rows_ref[...] * keep
        at = 0
        for slab_ref in slab_refs:
            product[:, at : at + slab_ref.shape[1]] = dot(screened, slab_ref[...])
            at += slab_ref.shape[1]

    def decode():
        shard_rows = [stage.shape[0] // tile_total for stage in stages]

        def copy_of(n, shard):
            at = pl.ds(pl.multiple_of(shard * shard_rows[n], CODE_ROWS), shard_rows[n])
            return pltpu.make_async_copy(gathered_refs[n].at[at, :], stages[n].at[at, :], sems.at[n, shard])

        for shard in range(tile_total):
            for n in range(parts):
                copy_of(n, shard).start()

        def use(shard, carry):
            first = 0
            for n, stage in enumerate(stages):
                copy_of(n, shard).wait()
                rows = shard_rows[n] - CODE_ROWS
                at = pl.multiple_of(shard * shard_rows[n], CODE_ROWS)
                code = stage[pl.ds(pl.multiple_of(at + rows, CODE_ROWS), CODE_ROWS), :]
                values = stage[pl.ds(at, rows), :].astype(jnp.int32).astype(jnp.float32)
                scale = jnp.exp2(code.astype(jnp.int32).astype(jnp.float32)[:1] - SLAB_BITS)
                to = pl.ds(pl.multiple_of(shard * slab_rows + first, CODE_ROWS), rows)
                slab_refs[0][to, :] = (values * scale).astype(jnp.bfloat16)
                first += rows
            return carry

        lax.fori_loop(0, tile_total, use, 0)

    def finish():
        tile = jnp.maximum(step - 1, 0)
        pair = lax.broadcasted_iota(jnp.int32, (PAIR_SQ, 1), 0)
        own_number = numbers[lax.axis_index("occ")]
        nonzero = (pair // ORBITALS_IN_GRP < own_number) & (pair % ORBITALS_IN_GRP < numbers[tile])
        ladder = jnp.where(nonzero, product[...], 0.0)
        for h in range(chunks):
            ladder_ref[h] = jnp.concatenate(
                [ladder[:, v * block + h * lanes : v * block + (h + 1) * lanes] for v in range(vir_count)], axis=1
            )
        by_place = ladder.reshape(ORBITALS_IN_GRP, ORBITALS_IN_GRP, cols)
        mirror = jnp.swapaxes(by_place, 0, 1).reshape(PAIR_SQ, cols)
        most = jnp.maximum(jnp.max(jnp.abs(ladder), axis=0, keepdims=True), 1e-30)
        code = jnp.ceil(jnp.log2(most) * STEPS)
        coded_rows = jnp.round(mirror * (TOP / scale_of(code))).astype(jnp.int32).astype(jnp.int16)
        code_rows = jnp.broadcast_to(code.astype(jnp.int32), (EXCHANGE_CODE_ROWS, cols)).astype(jnp.int16)
        for v in range(vir_count):
            packed_ref[0, v, :PAIR_SQ] = coded_rows[:, v * block : (v + 1) * block]
            packed_ref[0, v, PAIR_SQ:] = code_rows[:, v * block : (v + 1) * block]

    if coded:

        @pl.when(step == 0)
        def _():
            decode()

    @pl.when(step < tile_total)
    def _():
        finish()
        multiply()

    @pl.when(step == tile_total)
    def _():
        finish()


def ladder_call(tile_total, vir_count, chunks, amp_mask, numbers, amplitudes, slab):
    coded = slab[0].dtype == jnp.int16
    cols = slab[0].shape[1]
    block = cols // vir_count
    smem = pl.BlockSpec(memory_space=pltpu.SMEM)
    rows = tile_total * PAIR_SQ
    before = lambda step: jnp.maximum(step - 1, 0)
    packed_block = (vir_count, PAIR_SQ + EXCHANGE_CODE_ROWS, block)
    return pl.pallas_call(
        functools.partial(ladder_kernel, tile_total, vir_count, chunks, coded, len(slab)),
        grid=(tile_total + 1,),
        in_specs=[
            smem,
            smem,
            pl.BlockSpec((PAIR_SQ, W * W), lambda step: (jnp.minimum(step, tile_total - 1), 0)),
            *[
                pl.BlockSpec(memory_space=pl.ANY) if coded else pl.BlockSpec(part.shape, lambda step: (0, 0))
                for part in slab
            ],
        ],
        out_specs=[
            pl.BlockSpec((chunks, PAIR_SQ, cols // chunks), lambda step: (0, before(step), 0)),
            pl.BlockSpec((1,) + packed_block, lambda step: (before(step), 0, 0, 0)),
        ],
        out_shape=[
            jax.ShapeDtypeStruct((chunks, rows, cols // chunks), jnp.float32),
            jax.ShapeDtypeStruct((tile_total,) + packed_block, jnp.int16),
        ],
        scratch_shapes=[pltpu.VMEM((PAIR_SQ, cols), jnp.float32)]
        + [
            pltpu.VMEM((W * W, cols), jnp.bfloat16),
            pltpu.SemaphoreType.DMA((len(slab), tile_total)),
            *[pltpu.VMEM(part.shape, part.dtype) for part in slab],
        ]
        * coded,
        compiler_params=pltpu.CompilerParams(vmem_limit_bytes=VMEM_LIMIT),
        cost_estimate=pl.CostEstimate(
            flops=2 * rows * cols * W * W,
            bytes_accessed=rows * (W * W * 2 + cols * 6) + W * W * cols * 2,
            transcendentals=0,
        ),
        name="ladder",
    )(amp_mask, numbers, amplitudes, *slab)


def moved_columns(values, spread_ref):
    both = dot(jnp.concatenate(split(values), axis=0), spread_ref[...])
    return both[: values.shape[0]] + both[values.shape[0] :]


def direct_kernel(spread_ref, *refs):
    refs[-1][...] = moved_columns(jnp.concatenate([ref[0] for ref in refs[:-1]], axis=1), spread_ref)


def direct_call(chunk, spread, ladders):
    rows = ladders[0].shape[1]
    step_rows = AT_ONCE * PAIR_SQ
    return pl.pallas_call(
        direct_kernel,
        grid=(rows // step_rows,),
        in_specs=[pl.BlockSpec(spread.shape, lambda step: (0, 0))]
        + [pl.BlockSpec((1, step_rows, ladder.shape[2]), lambda step: (chunk, step, 0)) for ladder in ladders],
        out_specs=pl.BlockSpec((step_rows, spread.shape[1]), lambda step: (step, 0)),
        out_shape=jax.ShapeDtypeStruct((rows, spread.shape[1]), jnp.float32),
        compiler_params=pltpu.CompilerParams(vmem_limit_bytes=VMEM_LIMIT),
        cost_estimate=pl.CostEstimate(
            flops=4 * rows * spread.size, bytes_accessed=rows * spread.shape[1] * 8, transcendentals=0
        ),
        name="direct",
    )(spread, *ladders)


def update_kernel(vir_count, at_once, spread_ref, vir_ref, occ_ref, *refs):
    arrived_refs, refs = refs[:vir_count], refs[vir_count:]
    direct_refs = refs[:at_once]
    tiles = []
    for n in range(at_once):
        blocks = []
        for v in range(vir_count):
            code = arrived_refs[v][n, 0, PAIR_SQ:].astype(jnp.int32).astype(jnp.float32)[:1]
            values = arrived_refs[v][n, 0, :PAIR_SQ].astype(jnp.int32).astype(jnp.float32)
            blocks.append(values * (scale_of(code) * (1.0 / TOP)))
        tiles.append(jnp.concatenate(blocks, axis=1))
    mirror = moved_columns(jnp.concatenate(tiles, axis=0), spread_ref)
    for n, direct_ref in enumerate(direct_refs):
        at = slice(n * PAIR_SQ, (n + 1) * PAIR_SQ)
        occ = jnp.transpose(jnp.broadcast_to(occ_ref[n], (128, PAIR_SQ)))[:, :1]
        refs[-1][at, :] = (direct_ref[...] + mirror[at]) / (vir_ref[...] - occ)


def update_call(chunk, chunks, at_once, arrived, spread, vir_sum, occ_sum, direct, earlier):
    cols = spread.shape[1]
    rows = direct.shape[0]
    step_rows = at_once * PAIR_SQ
    vir_count = arrived.shape[1]
    args = [spread, vir_sum, occ_sum] + [arrived] * vir_count + [direct] * at_once
    in_specs = [
        pl.BlockSpec(spread.shape, lambda step: (0, 0)),
        pl.BlockSpec((1, cols), lambda step: (0, chunk)),
        pl.BlockSpec((at_once, 1, PAIR_SQ), lambda step: (step, 0, 0)),
    ]
    in_specs += [
        pl.BlockSpec((at_once, 1) + arrived.shape[2:], lambda step, v=v: (step, v, 0, 0)) for v in range(vir_count)
    ]
    in_specs += [pl.BlockSpec((PAIR_SQ, cols), lambda step, n=n: (step * at_once + n, 0)) for n in range(at_once)]
    aliases = {}
    if earlier is not None:
        aliases = {len(args): 0}
        args.append(earlier)
        in_specs.append(pl.BlockSpec(memory_space=pl.ANY))
    return pl.pallas_call(
        functools.partial(update_kernel, vir_count, at_once),
        grid=(rows // step_rows,),
        in_specs=in_specs,
        out_specs=pl.BlockSpec((step_rows, cols), lambda step: (step, chunk)),
        out_shape=jax.ShapeDtypeStruct((rows, chunks * cols), jnp.float32),
        input_output_aliases=aliases,
        compiler_params=pltpu.CompilerParams(vmem_limit_bytes=VMEM_LIMIT),
        cost_estimate=pl.CostEstimate(
            flops=4 * rows * spread.size, bytes_accessed=rows * cols * 10, transcendentals=0
        ),
        name="update",
    )(*args)


def body(amplitudes, amp_mask, integrals, int_mask, group_orbital_numbers, occ_energy, vir_energy):
    tile_total = lax.axis_size("occ")
    vir_count = lax.axis_size("vir")
    row_tile = lax.axis_index("occ")
    vir_place = lax.axis_index("vir")
    span = W // vir_count
    slab_cols = span * W
    chunks = 2 if span >= 16 else 1
    width = span // chunks
    block = width * span
    rows = PAIR_SQ + EXCHANGE_CODE_ROWS

    def exchanged(packed):
        moved = lax.all_to_all(
            packed.reshape(tile_total * vir_count, rows, block), ("occ", "vir"), split_axis=0, concat_axis=0, tiled=True
        )
        return moved.reshape(tile_total, vir_count, rows, block)

    screened = screen_call(chunks, int_mask, integrals)
    first = lax.all_gather(screened[0], "occ", axis=0, tiled=True)
    *screened, first = lax.optimization_barrier((*screened[1:], first))
    rest = [lax.all_gather(part, "occ", axis=0, tiled=True) for part in screened]
    slabs = [[first, rest[0]]] + [[part] for part in rest[1:]]
    ladders, arrived = [], []
    for slab in slabs:
        ladder, packed = ladder_call(
            tile_total, vir_count, chunks, amp_mask[0], group_orbital_numbers, amplitudes, slab
        )
        ladders.append(ladder)
        arrived.append(exchanged(packed))

    place = jnp.arange(vir_count * block)
    owner, there_part = place // block, place // (width * width) % chunks
    here, there = place // width % width, place % width
    mirror_spread = one_hot_of(here * W + owner * span + there_part * width + there, width * W)
    place = jnp.arange(vir_count * width * width)
    owner, b, a = place // (width * width), place // width % width, place % width
    direct_spread = one_hot_of(
        jnp.concatenate([a * W + owner * span + c * width + b for c in range(chunks)]), width * W
    )

    occ_table = occ_energy.reshape(tile_total, ORBITALS_IN_GRP)
    own_energy = lax.dynamic_slice_in_dim(occ_table, row_tile, 1, 0)[0]
    occ_sum = (own_energy[None, :, None] + occ_table[:, None, :]).reshape(tile_total, 1, PAIR_SQ)
    vir_own = lax.dynamic_slice_in_dim(vir_energy, vir_place * span, span, 0)
    vir_sum = (vir_own[:, None] + vir_energy[None, :]).reshape(1, -1)
    update = None
    for chunk in range(chunks):
        direct = direct_call(chunk, direct_spread, ladders)
        update = update_call(chunk, chunks, 4, arrived[chunk], mirror_spread, vir_sum, occ_sum, direct, update)
    return update


def solution(mesh):
    in_specs = (P("occ", None), P("occ", None, None), P("occ", "vir"), P(), P(), P(), P())
    out_specs = P("occ", "vir")
    return jax.shard_map(body, mesh=mesh, in_specs=in_specs, out_specs=out_specs, check_vma=False)
```

```python
import functools

import jax
import jax.numpy as jnp
from jax import lax
from jax.experimental import pallas as pl
from jax.experimental.pallas import tpu as pltpu
from jax.sharding import PartitionSpec as P

VT = 32
NVT = 2
W = 64
ORBITALS_IN_GRP = 16
PAIR_SQ = ORBITALS_IN_GRP * ORBITALS_IN_GRP
CODE_ROWS = 16
EXCHANGE_CODE_ROWS = 8
AT_ONCE = 4
SLAB_BITS = 14.0
TOP = 32700.0
STEPS = 8.0
VMEM_LIMIT = 56 * 1024 * 1024


def one_hot_of(target, amount):
    return (target[:, None] == jnp.arange(amount)[None, :]).astype(jnp.bfloat16)


def split(values):
    high = values.astype(jnp.bfloat16)
    return high, (values - high.astype(jnp.float32)).astype(jnp.bfloat16)


def dot(left, right):
    return jnp.dot(left, right, preferred_element_type=jnp.float32)


def scale_of(code):
    return jnp.exp2(code * (1.0 / STEPS))


def screen_kernel(part, int_mask, slab_ref, coded_ref, plain_ref, *later_refs):
    slab_rows, slab_cols = slab_ref.shape
    coded_cols = coded_ref.shape[1]
    cols = coded_cols + plain_ref.shape[1]
    span = slab_cols // W
    row_label = lax.axis_index("occ") * slab_rows // W // VT * NVT
    col_label = lax.axis_index("vir") * slab_cols // W // VT * NVT
    natural = lax.broadcasted_iota(jnp.int32, (slab_cols, 1), 0)
    a, b = natural // W, natural % W
    target = b // span * (part * span) + (a // part * part + b % part) * part + a % part
    place = lax.broadcasted_iota(jnp.int32, (slab_cols, cols), 1)
    to = lax.broadcasted_iota(jnp.int32, (1, cols), 1)
    second = lax.broadcasted_iota(jnp.int32, (slab_rows, 1), 0) % W >= VT
    for chunk in range(span // part):
        right = to // (part * span) * span + chunk * part + to // part % part >= VT
        kept = [
            jnp.where(right, int_mask[label, col_label + 1], int_mask[label, col_label])
            for label in (row_label, row_label + 1)
        ]
        ones = place == jnp.where(b % span // part == chunk, target, -1)
        moved = dot(slab_ref[...], ones.astype(jnp.float32).astype(jnp.bfloat16))
        moved = jnp.where(jnp.where(second, kept[1], kept[0]) > 0, moved, 0.0)
        if chunk:
            later_refs[chunk - 1][...] = moved.astype(jnp.bfloat16)
        else:
            plain_ref[...] = moved[:, coded_cols:].astype(jnp.bfloat16)
            moved = moved[:, :coded_cols]
            most = jnp.maximum(jnp.max(jnp.abs(moved), axis=0, keepdims=True), 1e-30)
            code = jnp.floor(jnp.log2(most)) + 1.0
            coded_ref[:slab_rows, :] = jnp.round(moved * jnp.exp2(SLAB_BITS - code)).astype(jnp.int32).astype(jnp.int16)
            coded_ref[slab_rows:, :] = jnp.broadcast_to(
                code.astype(jnp.int32), (CODE_ROWS, coded_cols)
            ).astype(jnp.int16)


def screen_call(chunks, int_mask, integrals):
    slab_rows, slab_cols = integrals.shape
    cols = slab_cols // chunks
    coded_cols = cols - cols // 4
    plain_cols = [cols // 4] + [cols] * (chunks - 1)
    vmem = pl.BlockSpec(memory_space=pltpu.VMEM)
    return pl.pallas_call(
        functools.partial(screen_kernel, slab_cols // W // chunks),
        in_specs=[pl.BlockSpec(memory_space=pltpu.SMEM), vmem],
        out_specs=[vmem] * (1 + len(plain_cols)),
        out_shape=[jax.ShapeDtypeStruct((slab_rows + CODE_ROWS, coded_cols), jnp.int16)]
        + [jax.ShapeDtypeStruct((slab_rows, each), integrals.dtype) for each in plain_cols],
        compiler_params=pltpu.CompilerParams(vmem_limit_bytes=VMEM_LIMIT),
        name="screen",
    )(int_mask, integrals)


def ladder_kernel(tile_total, vir_count, chunks, coded, parts, amp_mask, numbers, rows_ref, *refs):
    gathered_refs, refs = refs[:parts], refs[parts:]
    ladder_ref, packed_ref, product = refs[:3]
    slab_refs = gathered_refs
    if coded:
        slab_refs, stage, sems = (refs[3], *gathered_refs[1:]), refs[4], refs[5]
    step = pl.program_id(0)
    cols = product.shape[1]
    slab_rows = slab_refs[0].shape[0] // tile_total
    shard_rows = slab_rows + CODE_ROWS
    block = cols // vir_count
    lanes = block // chunks

    def multiply():
        tile = step
        lane = lax.broadcasted_iota(jnp.int32, (1, W * W), 1)
        left = lane % W < VT
        keep = jnp.where(
            lane < W * VT,
            jnp.where(left, amp_mask[tile, 0], amp_mask[tile, 1]),
            jnp.where(left, amp_mask[tile, 2], amp_mask[tile, 3]),
        )
        keep = keep.astype(jnp.float32).astype(jnp.bfloat16)
        screened = rows_ref[...] * keep
        at = 0
        for slab_ref in slab_refs:
            product[:, at : at + slab_ref.shape[1]] = dot(screened, slab_ref[...])
            at += slab_ref.shape[1]

    def decode():
        def copy_of(shard):
            at = pl.ds(pl.multiple_of(shard * shard_rows, CODE_ROWS), shard_rows)
            return pltpu.make_async_copy(gathered_refs[0].at[at, :], stage.at[at, :], sems.at[shard])

        for shard in range(tile_total):
            copy_of(shard).start()

        def use(shard, carry):
            copy_of(shard).wait()
            at = pl.multiple_of(shard * shard_rows, CODE_ROWS)
            code = stage[pl.ds(pl.multiple_of(at + slab_rows, CODE_ROWS), CODE_ROWS), :]
            values = stage[pl.ds(at, slab_rows), :].astype(jnp.int32).astype(jnp.float32)
            scale = jnp.exp2(code.astype(jnp.int32).astype(jnp.float32)[:1] - SLAB_BITS)
            to = pl.ds(pl.multiple_of(shard * slab_rows, slab_rows), slab_rows)
            slab_refs[0][to, :] = (values * scale).astype(jnp.bfloat16)
            return carry

        lax.fori_loop(0, tile_total, use, 0)

    def finish():
        tile = jnp.maximum(step - 1, 0)
        pair = lax.broadcasted_iota(jnp.int32, (PAIR_SQ, 1), 0)
        own_number = numbers[lax.axis_index("occ")]
        nonzero = (pair // ORBITALS_IN_GRP < own_number) & (pair % ORBITALS_IN_GRP < numbers[tile])
        ladder = jnp.where(nonzero, product[...], 0.0)
        for h in range(chunks):
            ladder_ref[h] = jnp.concatenate(
                [ladder[:, v * block + h * lanes : v * block + (h + 1) * lanes] for v in range(vir_count)], axis=1
            )
        by_place = ladder.reshape(ORBITALS_IN_GRP, ORBITALS_IN_GRP, cols)
        mirror = jnp.swapaxes(by_place, 0, 1).reshape(PAIR_SQ, cols)
        most = jnp.maximum(jnp.max(jnp.abs(ladder), axis=0, keepdims=True), 1e-30)
        code = jnp.ceil(jnp.log2(most) * STEPS)
        coded_rows = jnp.round(mirror * (TOP / scale_of(code))).astype(jnp.int32).astype(jnp.int16)
        code_rows = jnp.broadcast_to(code.astype(jnp.int32), (EXCHANGE_CODE_ROWS, cols)).astype(jnp.int16)
        for v in range(vir_count):
            packed_ref[0, v, :PAIR_SQ] = coded_rows[:, v * block : (v + 1) * block]
            packed_ref[0, v, PAIR_SQ:] = code_rows[:, v * block : (v + 1) * block]

    if coded:

        @pl.when(step == 0)
        def _():
            decode()

    @pl.when(step < tile_total)
    def _():
        finish()
        multiply()

    @pl.when(step == tile_total)
    def _():
        finish()


def ladder_call(tile_total, vir_count, chunks, amp_mask, numbers, amplitudes, slab):
    coded = slab[0].dtype == jnp.int16
    cols = sum(part.shape[1] for part in slab)
    block = cols // vir_count
    smem = pl.BlockSpec(memory_space=pltpu.SMEM)
    rows = tile_total * PAIR_SQ
    before = lambda step: jnp.maximum(step - 1, 0)
    packed_block = (vir_count, PAIR_SQ + EXCHANGE_CODE_ROWS, block)
    return pl.pallas_call(
        functools.partial(ladder_kernel, tile_total, vir_count, chunks, coded, len(slab)),
        grid=(tile_total + 1,),
        in_specs=[
            smem,
            smem,
            pl.BlockSpec((PAIR_SQ, W * W), lambda step: (jnp.minimum(step, tile_total - 1), 0)),
            *[
                pl.BlockSpec(memory_space=pl.ANY)
                if part.dtype == jnp.int16
                else pl.BlockSpec(part.shape, lambda step: (0, 0))
                for part in slab
            ],
        ],
        out_specs=[
            pl.BlockSpec((chunks, PAIR_SQ, cols // chunks), lambda step: (0, before(step), 0)),
            pl.BlockSpec((1,) + packed_block, lambda step: (before(step), 0, 0, 0)),
        ],
        out_shape=[
            jax.ShapeDtypeStruct((chunks, rows, cols // chunks), jnp.float32),
            jax.ShapeDtypeStruct((tile_total,) + packed_block, jnp.int16),
        ],
        scratch_shapes=[pltpu.VMEM((PAIR_SQ, cols), jnp.float32)]
        + [
            pltpu.VMEM((W * W, slab[0].shape[1]), jnp.bfloat16),
            pltpu.VMEM(slab[0].shape, slab[0].dtype),
            pltpu.SemaphoreType.DMA((tile_total,)),
        ]
        * coded,
        compiler_params=pltpu.CompilerParams(vmem_limit_bytes=VMEM_LIMIT),
        cost_estimate=pl.CostEstimate(
            flops=2 * rows * cols * W * W,
            bytes_accessed=rows * (W * W * 2 + cols * 6) + W * W * cols * 2,
            transcendentals=0,
        ),
        name="ladder",
    )(amp_mask, numbers, amplitudes, *slab)


def moved_columns(values, spread_ref):
    both = dot(jnp.concatenate(split(values), axis=0), spread_ref[...])
    return both[: values.shape[0]] + both[values.shape[0] :]


def direct_kernel(spread_ref, *refs):
    refs[-1][...] = moved_columns(jnp.concatenate([ref[0] for ref in refs[:-1]], axis=1), spread_ref)


def direct_call(chunk, spread, ladders):
    rows = ladders[0].shape[1]
    step_rows = AT_ONCE * PAIR_SQ
    return pl.pallas_call(
        direct_kernel,
        grid=(rows // step_rows,),
        in_specs=[pl.BlockSpec(spread.shape, lambda step: (0, 0))]
        + [pl.BlockSpec((1, step_rows, ladder.shape[2]), lambda step: (chunk, step, 0)) for ladder in ladders],
        out_specs=pl.BlockSpec((step_rows, spread.shape[1]), lambda step: (step, 0)),
        out_shape=jax.ShapeDtypeStruct((rows, spread.shape[1]), jnp.float32),
        compiler_params=pltpu.CompilerParams(vmem_limit_bytes=VMEM_LIMIT),
        cost_estimate=pl.CostEstimate(
            flops=4 * rows * spread.size, bytes_accessed=rows * spread.shape[1] * 8, transcendentals=0
        ),
        name="direct",
    )(spread, *ladders)


def update_kernel(vir_count, at_once, spread_ref, vir_ref, occ_ref, *refs):
    arrived_refs, refs = refs[:vir_count], refs[vir_count:]
    direct_refs = refs[:at_once]
    tiles = []
    for n in range(at_once):
        blocks = []
        for v in range(vir_count):
            code = arrived_refs[v][n, 0, PAIR_SQ:].astype(jnp.int32).astype(jnp.float32)[:1]
            values = arrived_refs[v][n, 0, :PAIR_SQ].astype(jnp.int32).astype(jnp.float32)
            blocks.append(values * (scale_of(code) * (1.0 / TOP)))
        tiles.append(jnp.concatenate(blocks, axis=1))
    mirror = moved_columns(jnp.concatenate(tiles, axis=0), spread_ref)
    for n, direct_ref in enumerate(direct_refs):
        at = slice(n * PAIR_SQ, (n + 1) * PAIR_SQ)
        occ = jnp.transpose(jnp.broadcast_to(occ_ref[n], (128, PAIR_SQ)))[:, :1]
        refs[-1][at, :] = (direct_ref[...] + mirror[at]) / (vir_ref[...] - occ)


def update_call(chunk, chunks, at_once, arrived, spread, vir_sum, occ_sum, direct, earlier):
    cols = spread.shape[1]
    rows = direct.shape[0]
    step_rows = at_once * PAIR_SQ
    vir_count = arrived.shape[1]
    args = [spread, vir_sum, occ_sum] + [arrived] * vir_count + [direct] * at_once
    in_specs = [
        pl.BlockSpec(spread.shape, lambda step: (0, 0)),
        pl.BlockSpec((1, cols), lambda step: (0, chunk)),
        pl.BlockSpec((at_once, 1, PAIR_SQ), lambda step: (step, 0, 0)),
    ]
    in_specs += [
        pl.BlockSpec((at_once, 1) + arrived.shape[2:], lambda step, v=v: (step, v, 0, 0)) for v in range(vir_count)
    ]
    in_specs += [pl.BlockSpec((PAIR_SQ, cols), lambda step, n=n: (step * at_once + n, 0)) for n in range(at_once)]
    aliases = {}
    if earlier is not None:
        aliases = {len(args): 0}
        args.append(earlier)
        in_specs.append(pl.BlockSpec(memory_space=pl.ANY))
    return pl.pallas_call(
        functools.partial(update_kernel, vir_count, at_once),
        grid=(rows // step_rows,),
        in_specs=in_specs,
        out_specs=pl.BlockSpec((step_rows, cols), lambda step: (step, chunk)),
        out_shape=jax.ShapeDtypeStruct((rows, chunks * cols), jnp.float32),
        input_output_aliases=aliases,
        compiler_params=pltpu.CompilerParams(vmem_limit_bytes=VMEM_LIMIT),
        cost_estimate=pl.CostEstimate(
            flops=4 * rows * spread.size, bytes_accessed=rows * cols * 10, transcendentals=0
        ),
        name="update",
    )(*args)


def body(amplitudes, amp_mask, integrals, int_mask, group_orbital_numbers, occ_energy, vir_energy):
    tile_total = lax.axis_size("occ")
    vir_count = lax.axis_size("vir")
    row_tile = lax.axis_index("occ")
    vir_place = lax.axis_index("vir")
    span = W // vir_count
    slab_cols = span * W
    chunks = 2 if span >= 16 else 1
    width = span // chunks
    block = width * span
    rows = PAIR_SQ + EXCHANGE_CODE_ROWS

    def exchanged(packed):
        moved = lax.all_to_all(
            packed.reshape(tile_total * vir_count, rows, block), ("occ", "vir"), split_axis=0, concat_axis=0, tiled=True
        )
        return moved.reshape(tile_total, vir_count, rows, block)

    coded, *plain = screen_call(chunks, int_mask, integrals)
    plain = [lax.all_gather(part, "occ", axis=0, tiled=True) for part in plain]
    slabs = [[lax.all_gather(coded, "occ", axis=0, tiled=True), plain[0]]] + [[part] for part in plain[1:]]
    ladders, arrived = [], []
    for slab in slabs:
        ladder, packed = ladder_call(
            tile_total, vir_count, chunks, amp_mask[0], group_orbital_numbers, amplitudes, slab
        )
        ladders.append(ladder)
        arrived.append(exchanged(packed))

    place = jnp.arange(vir_count * block)
    owner, there_part = place // block, place // (width * width) % chunks
    here, there = place // width % width, place % width
    mirror_spread = one_hot_of(here * W + owner * span + there_part * width + there, width * W)
    place = jnp.arange(vir_count * width * width)
    owner, b, a = place // (width * width), place // width % width, place % width
    direct_spread = one_hot_of(
        jnp.concatenate([a * W + owner * span + c * width + b for c in range(chunks)]), width * W
    )

    occ_table = occ_energy.reshape(tile_total, ORBITALS_IN_GRP)
    own_energy = lax.dynamic_slice_in_dim(occ_table, row_tile, 1, 0)[0]
    occ_sum = (own_energy[None, :, None] + occ_table[:, None, :]).reshape(tile_total, 1, PAIR_SQ)
    vir_own = lax.dynamic_slice_in_dim(vir_energy, vir_place * span, span, 0)
    vir_sum = (vir_own[:, None] + vir_energy[None, :]).reshape(1, -1)
    update = None
    for chunk in range(chunks):
        direct = direct_call(chunk, direct_spread, ladders)
        update = update_call(chunk, chunks, 4, arrived[chunk], mirror_spread, vir_sum, occ_sum, direct, update)
    return update


def solution(mesh):
    in_specs = (P("occ", None), P("occ", None, None), P("occ", "vir"), P(), P(), P(), P())
    out_specs = P("occ", "vir")
    return jax.shard_map(body, mesh=mesh, in_specs=in_specs, out_specs=out_specs, check_vma=False)
```

```python
import functools

import jax
import jax.numpy as jnp
from jax import lax
from jax.experimental import pallas as pl
from jax.experimental.pallas import tpu as pltpu
from jax.sharding import PartitionSpec as P

VT = 32
NVT = 2
W = 64
ORBITALS_IN_GRP = 16
PAIR_SQ = ORBITALS_IN_GRP * ORBITALS_IN_GRP
CODE_ROWS = 16
EXCHANGE_CODE_ROWS = 8
AT_ONCE = 4
SLAB_BITS = 14.0
TOP = 32700.0
STEPS = 8.0
VMEM_LIMIT = 56 * 1024 * 1024


def one_hot_of(target, amount):
    return (target[:, None] == jnp.arange(amount)[None, :]).astype(jnp.bfloat16)


def split(values):
    high = values.astype(jnp.bfloat16)
    return high, (values - high.astype(jnp.float32)).astype(jnp.bfloat16)


def dot(left, right):
    return jnp.dot(left, right, preferred_element_type=jnp.float32)


def scale_of(code):
    return jnp.exp2(code * (1.0 / STEPS))


def screen_kernel(part, int_mask, slab_ref, coded_ref, plain_ref, *later_refs):
    slab_rows, slab_cols = slab_ref.shape
    coded_cols = coded_ref.shape[1]
    cols = coded_cols + plain_ref.shape[1]
    span = slab_cols // W
    row_label = lax.axis_index("occ") * slab_rows // W // VT * NVT
    col_label = lax.axis_index("vir") * slab_cols // W // VT * NVT
    natural = lax.broadcasted_iota(jnp.int32, (slab_cols, 1), 0)
    a, b = natural // W, natural % W
    target = b // span * (part * span) + (a // part * part + b % part) * part + a % part
    place = lax.broadcasted_iota(jnp.int32, (slab_cols, cols), 1)
    to = lax.broadcasted_iota(jnp.int32, (1, cols), 1)
    second = lax.broadcasted_iota(jnp.int32, (slab_rows, 1), 0) % W >= VT
    for chunk in range(span // part):
        right = to // (part * span) * span + chunk * part + to // part % part >= VT
        kept = [
            jnp.where(right, int_mask[label, col_label + 1], int_mask[label, col_label])
            for label in (row_label, row_label + 1)
        ]
        ones = place == jnp.where(b % span // part == chunk, target, -1)
        moved = dot(slab_ref[...], ones.astype(jnp.float32).astype(jnp.bfloat16))
        moved = jnp.where(jnp.where(second, kept[1], kept[0]) > 0, moved, 0.0)
        if chunk:
            later_refs[chunk - 1][...] = moved.astype(jnp.bfloat16)
        else:
            plain_ref[...] = moved[:, coded_cols:].astype(jnp.bfloat16)
            moved = moved[:, :coded_cols]
            most = jnp.maximum(jnp.max(jnp.abs(moved), axis=0, keepdims=True), 1e-30)
            code = jnp.floor(jnp.log2(most)) + 1.0
            coded_ref[:slab_rows, :] = jnp.round(moved * jnp.exp2(SLAB_BITS - code)).astype(jnp.int32).astype(jnp.int16)
            coded_ref[slab_rows:, :] = jnp.broadcast_to(
                code.astype(jnp.int32), (CODE_ROWS, coded_cols)
            ).astype(jnp.int16)


def screen_call(chunks, int_mask, integrals):
    slab_rows, slab_cols = integrals.shape
    cols = slab_cols // chunks
    coded_cols = cols - cols // 4
    plain_cols = [cols // 4] + [cols] * (chunks - 1)
    vmem = pl.BlockSpec(memory_space=pltpu.VMEM)
    return pl.pallas_call(
        functools.partial(screen_kernel, slab_cols // W // chunks),
        in_specs=[pl.BlockSpec(memory_space=pltpu.SMEM), vmem],
        out_specs=[vmem] * (1 + len(plain_cols)),
        out_shape=[jax.ShapeDtypeStruct((slab_rows + CODE_ROWS, coded_cols), jnp.int16)]
        + [jax.ShapeDtypeStruct((slab_rows, each), integrals.dtype) for each in plain_cols],
        compiler_params=pltpu.CompilerParams(vmem_limit_bytes=VMEM_LIMIT),
        name="screen",
    )(int_mask, integrals)


def ladder_kernel(tile_total, vir_count, chunks, coded, parts, amp_mask, numbers, rows_ref, *refs):
    gathered_refs, refs = refs[:parts], refs[parts:]
    ladder_ref, packed_ref, product = refs[:3]
    slab_refs = gathered_refs
    if coded:
        slab_refs, stage, sems = refs[3:4], refs[4], refs[5]
    step = pl.program_id(0)
    cols = product.shape[1]
    slab_rows = slab_refs[0].shape[0] // tile_total
    shard_rows = slab_rows + CODE_ROWS
    block = cols // vir_count
    lanes = block // chunks

    def multiply():
        tile = step
        lane = lax.broadcasted_iota(jnp.int32, (1, W * W), 1)
        left = lane % W < VT
        keep = jnp.where(
            lane < W * VT,
            jnp.where(left, amp_mask[tile, 0], amp_mask[tile, 1]),
            jnp.where(left, amp_mask[tile, 2], amp_mask[tile, 3]),
        )
        keep = keep.astype(jnp.float32).astype(jnp.bfloat16)
        screened = rows_ref[...] * keep
        at = 0
        for slab_ref in slab_refs:
            product[:, at : at + slab_ref.shape[1]] = dot(screened, slab_ref[...])
            at += slab_ref.shape[1]

    def decode():
        def copy_of(shard):
            at = pl.ds(pl.multiple_of(shard * shard_rows, CODE_ROWS), shard_rows)
            return pltpu.make_async_copy(gathered_refs[0].at[at, :], stage.at[at, :], sems.at[shard])

        coded_cols = stage.shape[1]
        for shard in range(tile_total):
            copy_of(shard).start()

        def use(shard, carry):
            copy_of(shard).wait()
            at = pl.multiple_of(shard * shard_rows, CODE_ROWS)
            code = stage[pl.ds(pl.multiple_of(at + slab_rows, CODE_ROWS), CODE_ROWS), :]
            values = stage[pl.ds(at, slab_rows), :].astype(jnp.int32).astype(jnp.float32)
            scale = jnp.exp2(code.astype(jnp.int32).astype(jnp.float32)[:1] - SLAB_BITS)
            to = pl.ds(pl.multiple_of(shard * slab_rows, slab_rows), slab_rows)
            slab_refs[0][to, coded_cols:] = gathered_refs[1][to, :]
            slab_refs[0][to, :coded_cols] = (values * scale).astype(jnp.bfloat16)
            return carry

        lax.fori_loop(0, tile_total, use, 0)

    def finish():
        tile = jnp.maximum(step - 1, 0)
        pair = lax.broadcasted_iota(jnp.int32, (PAIR_SQ, 1), 0)
        own_number = numbers[lax.axis_index("occ")]
        nonzero = (pair // ORBITALS_IN_GRP < own_number) & (pair % ORBITALS_IN_GRP < numbers[tile])
        ladder = jnp.where(nonzero, product[...], 0.0)
        for h in range(chunks):
            ladder_ref[h] = jnp.concatenate(
                [ladder[:, v * block + h * lanes : v * block + (h + 1) * lanes] for v in range(vir_count)], axis=1
            )
        by_place = ladder.reshape(ORBITALS_IN_GRP, ORBITALS_IN_GRP, cols)
        mirror = jnp.swapaxes(by_place, 0, 1).reshape(PAIR_SQ, cols)
        most = jnp.maximum(jnp.max(jnp.abs(ladder), axis=0, keepdims=True), 1e-30)
        code = jnp.ceil(jnp.log2(most) * STEPS)
        coded_rows = jnp.round(mirror * (TOP / scale_of(code))).astype(jnp.int32).astype(jnp.int16)
        code_rows = jnp.broadcast_to(code.astype(jnp.int32), (EXCHANGE_CODE_ROWS, cols)).astype(jnp.int16)
        for v in range(vir_count):
            packed_ref[0, v, :PAIR_SQ] = coded_rows[:, v * block : (v + 1) * block]
            packed_ref[0, v, PAIR_SQ:] = code_rows[:, v * block : (v + 1) * block]

    if coded:

        @pl.when(step == 0)
        def _():
            decode()

    @pl.when(step < tile_total)
    def _():
        finish()
        multiply()

    @pl.when(step == tile_total)
    def _():
        finish()


def ladder_call(tile_total, vir_count, chunks, amp_mask, numbers, amplitudes, slab):
    coded = slab[0].dtype == jnp.int16
    cols = sum(part.shape[1] for part in slab)
    block = cols // vir_count
    smem = pl.BlockSpec(memory_space=pltpu.SMEM)
    rows = tile_total * PAIR_SQ
    before = lambda step: jnp.maximum(step - 1, 0)
    packed_block = (vir_count, PAIR_SQ + EXCHANGE_CODE_ROWS, block)
    return pl.pallas_call(
        functools.partial(ladder_kernel, tile_total, vir_count, chunks, coded, len(slab)),
        grid=(tile_total + 1,),
        in_specs=[
            smem,
            smem,
            pl.BlockSpec((PAIR_SQ, W * W), lambda step: (jnp.minimum(step, tile_total - 1), 0)),
            *[
                pl.BlockSpec(memory_space=pl.ANY)
                if part.dtype == jnp.int16
                else pl.BlockSpec(part.shape, lambda step: (0, 0))
                for part in slab
            ],
        ],
        out_specs=[
            pl.BlockSpec((chunks, PAIR_SQ, cols // chunks), lambda step: (0, before(step), 0)),
            pl.BlockSpec((1,) + packed_block, lambda step: (before(step), 0, 0, 0)),
        ],
        out_shape=[
            jax.ShapeDtypeStruct((chunks, rows, cols // chunks), jnp.float32),
            jax.ShapeDtypeStruct((tile_total,) + packed_block, jnp.int16),
        ],
        scratch_shapes=[pltpu.VMEM((PAIR_SQ, cols), jnp.float32)]
        + [
            pltpu.VMEM((W * W, cols), jnp.bfloat16),
            pltpu.VMEM(slab[0].shape, slab[0].dtype),
            pltpu.SemaphoreType.DMA((tile_total,)),
        ]
        * coded,
        compiler_params=pltpu.CompilerParams(vmem_limit_bytes=VMEM_LIMIT),
        cost_estimate=pl.CostEstimate(
            flops=2 * rows * cols * W * W,
            bytes_accessed=rows * (W * W * 2 + cols * 6) + W * W * cols * 2,
            transcendentals=0,
        ),
        name="ladder",
    )(amp_mask, numbers, amplitudes, *slab)


def moved_columns(values, spread_ref):
    both = dot(jnp.concatenate(split(values), axis=0), spread_ref[...])
    return both[: values.shape[0]] + both[values.shape[0] :]


def direct_kernel(spread_ref, *refs):
    refs[-1][...] = moved_columns(jnp.concatenate([ref[0] for ref in refs[:-1]], axis=1), spread_ref)


def direct_call(chunk, spread, ladders):
    rows = ladders[0].shape[1]
    step_rows = AT_ONCE * PAIR_SQ
    return pl.pallas_call(
        direct_kernel,
        grid=(rows // step_rows,),
        in_specs=[pl.BlockSpec(spread.shape, lambda step: (0, 0))]
        + [pl.BlockSpec((1, step_rows, ladder.shape[2]), lambda step: (chunk, step, 0)) for ladder in ladders],
        out_specs=pl.BlockSpec((step_rows, spread.shape[1]), lambda step: (step, 0)),
        out_shape=jax.ShapeDtypeStruct((rows, spread.shape[1]), jnp.float32),
        compiler_params=pltpu.CompilerParams(vmem_limit_bytes=VMEM_LIMIT),
        cost_estimate=pl.CostEstimate(
            flops=4 * rows * spread.size, bytes_accessed=rows * spread.shape[1] * 8, transcendentals=0
        ),
        name="direct",
    )(spread, *ladders)


def update_kernel(vir_count, at_once, spread_ref, vir_ref, occ_ref, *refs):
    arrived_refs, refs = refs[:vir_count], refs[vir_count:]
    direct_refs = refs[:at_once]
    tiles = []
    for n in range(at_once):
        blocks = []
        for v in range(vir_count):
            code = arrived_refs[v][n, 0, PAIR_SQ:].astype(jnp.int32).astype(jnp.float32)[:1]
            values = arrived_refs[v][n, 0, :PAIR_SQ].astype(jnp.int32).astype(jnp.float32)
            blocks.append(values * (scale_of(code) * (1.0 / TOP)))
        tiles.append(jnp.concatenate(blocks, axis=1))
    mirror = moved_columns(jnp.concatenate(tiles, axis=0), spread_ref)
    for n, direct_ref in enumerate(direct_refs):
        at = slice(n * PAIR_SQ, (n + 1) * PAIR_SQ)
        occ = jnp.transpose(jnp.broadcast_to(occ_ref[n], (128, PAIR_SQ)))[:, :1]
        refs[-1][at, :] = (direct_ref[...] + mirror[at]) / (vir_ref[...] - occ)


def update_call(chunk, chunks, at_once, arrived, spread, vir_sum, occ_sum, direct, earlier):
    cols = spread.shape[1]
    rows = direct.shape[0]
    step_rows = at_once * PAIR_SQ
    vir_count = arrived.shape[1]
    args = [spread, vir_sum, occ_sum] + [arrived] * vir_count + [direct] * at_once
    in_specs = [
        pl.BlockSpec(spread.shape, lambda step: (0, 0)),
        pl.BlockSpec((1, cols), lambda step: (0, chunk)),
        pl.BlockSpec((at_once, 1, PAIR_SQ), lambda step: (step, 0, 0)),
    ]
    in_specs += [
        pl.BlockSpec((at_once, 1) + arrived.shape[2:], lambda step, v=v: (step, v, 0, 0)) for v in range(vir_count)
    ]
    in_specs += [pl.BlockSpec((PAIR_SQ, cols), lambda step, n=n: (step * at_once + n, 0)) for n in range(at_once)]
    aliases = {}
    if earlier is not None:
        aliases = {len(args): 0}
        args.append(earlier)
        in_specs.append(pl.BlockSpec(memory_space=pl.ANY))
    return pl.pallas_call(
        functools.partial(update_kernel, vir_count, at_once),
        grid=(rows // step_rows,),
        in_specs=in_specs,
        out_specs=pl.BlockSpec((step_rows, cols), lambda step: (step, chunk)),
        out_shape=jax.ShapeDtypeStruct((rows, chunks * cols), jnp.float32),
        input_output_aliases=aliases,
        compiler_params=pltpu.CompilerParams(vmem_limit_bytes=VMEM_LIMIT),
        cost_estimate=pl.CostEstimate(
            flops=4 * rows * spread.size, bytes_accessed=rows * cols * 10, transcendentals=0
        ),
        name="update",
    )(*args)


def body(amplitudes, amp_mask, integrals, int_mask, group_orbital_numbers, occ_energy, vir_energy):
    tile_total = lax.axis_size("occ")
    vir_count = lax.axis_size("vir")
    row_tile = lax.axis_index("occ")
    vir_place = lax.axis_index("vir")
    span = W // vir_count
    slab_cols = span * W
    chunks = 2 if span >= 16 else 1
    width = span // chunks
    block = width * span
    rows = PAIR_SQ + EXCHANGE_CODE_ROWS

    def exchanged(packed):
        moved = lax.all_to_all(
            packed.reshape(tile_total * vir_count, rows, block), ("occ", "vir"), split_axis=0, concat_axis=0, tiled=True
        )
        return moved.reshape(tile_total, vir_count, rows, block)

    coded, *plain = screen_call(chunks, int_mask, integrals)
    plain = [lax.all_gather(part, "occ", axis=0, tiled=True) for part in plain]
    slabs = [[lax.all_gather(coded, "occ", axis=0, tiled=True), plain[0]]] + [[part] for part in plain[1:]]
    ladders, arrived = [], []
    for slab in slabs:
        ladder, packed = ladder_call(
            tile_total, vir_count, chunks, amp_mask[0], group_orbital_numbers, amplitudes, slab
        )
        ladders.append(ladder)
        arrived.append(exchanged(packed))

    place = jnp.arange(vir_count * block)
    owner, there_part = place // block, place // (width * width) % chunks
    here, there = place // width % width, place % width
    mirror_spread = one_hot_of(here * W + owner * span + there_part * width + there, width * W)
    place = jnp.arange(vir_count * width * width)
    owner, b, a = place // (width * width), place // width % width, place % width
    direct_spread = one_hot_of(
        jnp.concatenate([a * W + owner * span + c * width + b for c in range(chunks)]), width * W
    )

    occ_table = occ_energy.reshape(tile_total, ORBITALS_IN_GRP)
    own_energy = lax.dynamic_slice_in_dim(occ_table, row_tile, 1, 0)[0]
    occ_sum = (own_energy[None, :, None] + occ_table[:, None, :]).reshape(tile_total, 1, PAIR_SQ)
    vir_own = lax.dynamic_slice_in_dim(vir_energy, vir_place * span, span, 0)
    vir_sum = (vir_own[:, None] + vir_energy[None, :]).reshape(1, -1)
    update = None
    for chunk in range(chunks):
        direct = direct_call(chunk, direct_spread, ladders)
        update = update_call(chunk, chunks, 4, arrived[chunk], mirror_spread, vir_sum, occ_sum, direct, update)
    return update


def solution(mesh):
    in_specs = (P("occ", None), P("occ", None, None), P("occ", "vir"), P(), P(), P(), P())
    out_specs = P("occ", "vir")
    return jax.shard_map(body, mesh=mesh, in_specs=in_specs, out_specs=out_specs, check_vma=False)
```

```python
import functools

import jax
import jax.numpy as jnp
from jax import lax
from jax.experimental import pallas as pl
from jax.experimental.pallas import tpu as pltpu
from jax.sharding import PartitionSpec as P

VT = 32
NVT = 2
W = 64
ORBITALS_IN_GRP = 16
PAIR_SQ = ORBITALS_IN_GRP * ORBITALS_IN_GRP
CODE_ROWS = 16
EXCHANGE_CODE_ROWS = 8
AT_ONCE = 4
SLAB_BITS = 14.0
TOP = 32700.0
STEPS = 8.0
VMEM_LIMIT = 56 * 1024 * 1024


def one_hot_of(target, amount):
    return (target[:, None] == jnp.arange(amount)[None, :]).astype(jnp.bfloat16)


def split(values):
    high = values.astype(jnp.bfloat16)
    return high, (values - high.astype(jnp.float32)).astype(jnp.bfloat16)


def dot(left, right):
    return jnp.dot(left, right, preferred_element_type=jnp.float32)


def scale_of(code):
    return jnp.exp2(code * (1.0 / STEPS))


def screen_kernel(part, int_mask, slab_ref, coded_ref, plain_ref, *later_refs):
    slab_rows, slab_cols = slab_ref.shape
    coded_cols = coded_ref.shape[1]
    cols = coded_cols + plain_ref.shape[1]
    span = slab_cols // W
    row_label = lax.axis_index("occ") * slab_rows // W // VT * NVT
    col_label = lax.axis_index("vir") * slab_cols // W // VT * NVT
    natural = lax.broadcasted_iota(jnp.int32, (slab_cols, 1), 0)
    a, b = natural // W, natural % W
    target = b // span * (part * span) + (a // part * part + b % part) * part + a % part
    place = lax.broadcasted_iota(jnp.int32, (slab_cols, cols), 1)
    to = lax.broadcasted_iota(jnp.int32, (1, cols), 1)
    second = lax.broadcasted_iota(jnp.int32, (slab_rows, 1), 0) % W >= VT
    for chunk in range(span // part):
        right = to // (part * span) * span + chunk * part + to // part % part >= VT
        kept = [
            jnp.where(right, int_mask[label, col_label + 1], int_mask[label, col_label])
            for label in (row_label, row_label + 1)
        ]
        ones = place == jnp.where(b % span // part == chunk, target, -1)
        moved = dot(slab_ref[...], ones.astype(jnp.float32).astype(jnp.bfloat16))
        moved = jnp.where(jnp.where(second, kept[1], kept[0]) > 0, moved, 0.0)
        if chunk:
            later_refs[chunk - 1][...] = moved.astype(jnp.bfloat16)
        else:
            plain_ref[...] = moved[:, coded_cols:].astype(jnp.bfloat16)
            moved = moved[:, :coded_cols]
            most = jnp.maximum(jnp.max(jnp.abs(moved), axis=0, keepdims=True), 1e-30)
            code = jnp.floor(jnp.log2(most)) + 1.0
            coded_ref[:slab_rows, :] = jnp.round(moved * jnp.exp2(SLAB_BITS - code)).astype(jnp.int32).astype(jnp.int16)
            coded_ref[slab_rows:, :] = jnp.broadcast_to(
                code.astype(jnp.int32), (CODE_ROWS, coded_cols)
            ).astype(jnp.int16)


def screen_call(chunks, int_mask, integrals):
    slab_rows, slab_cols = integrals.shape
    cols = slab_cols // chunks
    coded_cols = cols - cols // 2
    plain_cols = [cols // 2] + [cols] * (chunks - 1)
    vmem = pl.BlockSpec(memory_space=pltpu.VMEM)
    return pl.pallas_call(
        functools.partial(screen_kernel, slab_cols // W // chunks),
        in_specs=[pl.BlockSpec(memory_space=pltpu.SMEM), vmem],
        out_specs=[vmem] * (1 + len(plain_cols)),
        out_shape=[jax.ShapeDtypeStruct((slab_rows + CODE_ROWS, coded_cols), jnp.int16)]
        + [jax.ShapeDtypeStruct((slab_rows, each), integrals.dtype) for each in plain_cols],
        compiler_params=pltpu.CompilerParams(vmem_limit_bytes=VMEM_LIMIT),
        name="screen",
    )(int_mask, integrals)


def ladder_kernel(tile_total, vir_count, chunks, coded, parts, amp_mask, numbers, rows_ref, *refs):
    gathered_refs, refs = refs[:parts], refs[parts:]
    ladder_ref, packed_ref, product = refs[:3]
    slab_refs = gathered_refs
    if coded:
        slab_refs, stage, sems = refs[3:4], refs[4], refs[5]
    step = pl.program_id(0)
    cols = product.shape[1]
    slab_rows = slab_refs[0].shape[0] // tile_total
    shard_rows = slab_rows + CODE_ROWS
    block = cols // vir_count
    lanes = block // chunks

    def multiply():
        tile = step
        lane = lax.broadcasted_iota(jnp.int32, (1, W * W), 1)
        left = lane % W < VT
        keep = jnp.where(
            lane < W * VT,
            jnp.where(left, amp_mask[tile, 0], amp_mask[tile, 1]),
            jnp.where(left, amp_mask[tile, 2], amp_mask[tile, 3]),
        )
        keep = keep.astype(jnp.float32).astype(jnp.bfloat16)
        screened = rows_ref[...] * keep
        at = 0
        for slab_ref in slab_refs:
            product[:, at : at + slab_ref.shape[1]] = dot(screened, slab_ref[...])
            at += slab_ref.shape[1]

    def decode():
        def copy_of(shard):
            at = pl.ds(pl.multiple_of(shard * shard_rows, CODE_ROWS), shard_rows)
            return pltpu.make_async_copy(gathered_refs[0].at[at, :], stage.at[at, :], sems.at[shard])

        coded_cols = stage.shape[1]
        for shard in range(tile_total):
            copy_of(shard).start()

        def use(shard, carry):
            copy_of(shard).wait()
            at = pl.multiple_of(shard * shard_rows, CODE_ROWS)
            code = stage[pl.ds(pl.multiple_of(at + slab_rows, CODE_ROWS), CODE_ROWS), :]
            values = stage[pl.ds(at, slab_rows), :].astype(jnp.int32).astype(jnp.float32)
            scale = jnp.exp2(code.astype(jnp.int32).astype(jnp.float32)[:1] - SLAB_BITS)
            to = pl.ds(pl.multiple_of(shard * slab_rows, slab_rows), slab_rows)
            slab_refs[0][to, coded_cols:] = gathered_refs[1][to, :]
            slab_refs[0][to, :coded_cols] = (values * scale).astype(jnp.bfloat16)
            return carry

        lax.fori_loop(0, tile_total, use, 0)

    def finish():
        tile = jnp.maximum(step - 1, 0)
        pair = lax.broadcasted_iota(jnp.int32, (PAIR_SQ, 1), 0)
        own_number = numbers[lax.axis_index("occ")]
        nonzero = (pair // ORBITALS_IN_GRP < own_number) & (pair % ORBITALS_IN_GRP < numbers[tile])
        ladder = jnp.where(nonzero, product[...], 0.0)
        for h in range(chunks):
            ladder_ref[h] = jnp.concatenate(
                [ladder[:, v * block + h * lanes : v * block + (h + 1) * lanes] for v in range(vir_count)], axis=1
            )
        by_place = ladder.reshape(ORBITALS_IN_GRP, ORBITALS_IN_GRP, cols)
        mirror = jnp.swapaxes(by_place, 0, 1).reshape(PAIR_SQ, cols)
        most = jnp.maximum(jnp.max(jnp.abs(ladder), axis=0, keepdims=True), 1e-30)
        code = jnp.ceil(jnp.log2(most) * STEPS)
        coded_rows = jnp.round(mirror * (TOP / scale_of(code))).astype(jnp.int32).astype(jnp.int16)
        code_rows = jnp.broadcast_to(code.astype(jnp.int32), (EXCHANGE_CODE_ROWS, cols)).astype(jnp.int16)
        for v in range(vir_count):
            packed_ref[0, v, :PAIR_SQ] = coded_rows[:, v * block : (v + 1) * block]
            packed_ref[0, v, PAIR_SQ:] = code_rows[:, v * block : (v + 1) * block]

    if coded:

        @pl.when(step == 0)
        def _():
            decode()

    @pl.when(step < tile_total)
    def _():
        finish()
        multiply()

    @pl.when(step == tile_total)
    def _():
        finish()


def ladder_call(tile_total, vir_count, chunks, amp_mask, numbers, amplitudes, slab):
    coded = slab[0].dtype == jnp.int16
    cols = sum(part.shape[1] for part in slab)
    block = cols // vir_count
    smem = pl.BlockSpec(memory_space=pltpu.SMEM)
    rows = tile_total * PAIR_SQ
    before = lambda step: jnp.maximum(step - 1, 0)
    packed_block = (vir_count, PAIR_SQ + EXCHANGE_CODE_ROWS, block)
    return pl.pallas_call(
        functools.partial(ladder_kernel, tile_total, vir_count, chunks, coded, len(slab)),
        grid=(tile_total + 1,),
        in_specs=[
            smem,
            smem,
            pl.BlockSpec((PAIR_SQ, W * W), lambda step: (jnp.minimum(step, tile_total - 1), 0)),
            *[
                pl.BlockSpec(memory_space=pl.ANY)
                if part.dtype == jnp.int16
                else pl.BlockSpec(part.shape, lambda step: (0, 0))
                for part in slab
            ],
        ],
        out_specs=[
            pl.BlockSpec((chunks, PAIR_SQ, cols // chunks), lambda step: (0, before(step), 0)),
            pl.BlockSpec((1,) + packed_block, lambda step: (before(step), 0, 0, 0)),
        ],
        out_shape=[
            jax.ShapeDtypeStruct((chunks, rows, cols // chunks), jnp.float32),
            jax.ShapeDtypeStruct((tile_total,) + packed_block, jnp.int16),
        ],
        scratch_shapes=[pltpu.VMEM((PAIR_SQ, cols), jnp.float32)]
        + [
            pltpu.VMEM((W * W, cols), jnp.bfloat16),
            pltpu.VMEM(slab[0].shape, slab[0].dtype),
            pltpu.SemaphoreType.DMA((tile_total,)),
        ]
        * coded,
        compiler_params=pltpu.CompilerParams(vmem_limit_bytes=VMEM_LIMIT),
        cost_estimate=pl.CostEstimate(
            flops=2 * rows * cols * W * W,
            bytes_accessed=rows * (W * W * 2 + cols * 6) + W * W * cols * 2,
            transcendentals=0,
        ),
        name="ladder",
    )(amp_mask, numbers, amplitudes, *slab)


def moved_columns(values, spread_ref):
    both = dot(jnp.concatenate(split(values), axis=0), spread_ref[...])
    return both[: values.shape[0]] + both[values.shape[0] :]


def direct_kernel(spread_ref, *refs):
    refs[-1][...] = moved_columns(jnp.concatenate([ref[0] for ref in refs[:-1]], axis=1), spread_ref)


def direct_call(chunk, spread, ladders):
    rows = ladders[0].shape[1]
    step_rows = AT_ONCE * PAIR_SQ
    return pl.pallas_call(
        direct_kernel,
        grid=(rows // step_rows,),
        in_specs=[pl.BlockSpec(spread.shape, lambda step: (0, 0))]
        + [pl.BlockSpec((1, step_rows, ladder.shape[2]), lambda step: (chunk, step, 0)) for ladder in ladders],
        out_specs=pl.BlockSpec((step_rows, spread.shape[1]), lambda step: (step, 0)),
        out_shape=jax.ShapeDtypeStruct((rows, spread.shape[1]), jnp.float32),
        compiler_params=pltpu.CompilerParams(vmem_limit_bytes=VMEM_LIMIT),
        cost_estimate=pl.CostEstimate(
            flops=4 * rows * spread.size, bytes_accessed=rows * spread.shape[1] * 8, transcendentals=0
        ),
        name="direct",
    )(spread, *ladders)


def update_kernel(vir_count, at_once, spread_ref, vir_ref, occ_ref, *refs):
    arrived_refs, refs = refs[:vir_count], refs[vir_count:]
    direct_refs = refs[:at_once]
    tiles = []
    for n in range(at_once):
        blocks = []
        for v in range(vir_count):
            code = arrived_refs[v][n, 0, PAIR_SQ:].astype(jnp.int32).astype(jnp.float32)[:1]
            values = arrived_refs[v][n, 0, :PAIR_SQ].astype(jnp.int32).astype(jnp.float32)
            blocks.append(values * (scale_of(code) * (1.0 / TOP)))
        tiles.append(jnp.concatenate(blocks, axis=1))
    mirror = moved_columns(jnp.concatenate(tiles, axis=0), spread_ref)
    for n, direct_ref in enumerate(direct_refs):
        at = slice(n * PAIR_SQ, (n + 1) * PAIR_SQ)
        occ = jnp.transpose(jnp.broadcast_to(occ_ref[n], (128, PAIR_SQ)))[:, :1]
        refs[-1][at, :] = (direct_ref[...] + mirror[at]) / (vir_ref[...] - occ)


def update_call(chunk, chunks, at_once, arrived, spread, vir_sum, occ_sum, direct, earlier):
    cols = spread.shape[1]
    rows = direct.shape[0]
    step_rows = at_once * PAIR_SQ
    vir_count = arrived.shape[1]
    args = [spread, vir_sum, occ_sum] + [arrived] * vir_count + [direct] * at_once
    in_specs = [
        pl.BlockSpec(spread.shape, lambda step: (0, 0)),
        pl.BlockSpec((1, cols), lambda step: (0, chunk)),
        pl.BlockSpec((at_once, 1, PAIR_SQ), lambda step: (step, 0, 0)),
    ]
    in_specs += [
        pl.BlockSpec((at_once, 1) + arrived.shape[2:], lambda step, v=v: (step, v, 0, 0)) for v in range(vir_count)
    ]
    in_specs += [pl.BlockSpec((PAIR_SQ, cols), lambda step, n=n: (step * at_once + n, 0)) for n in range(at_once)]
    aliases = {}
    if earlier is not None:
        aliases = {len(args): 0}
        args.append(earlier)
        in_specs.append(pl.BlockSpec(memory_space=pl.ANY))
    return pl.pallas_call(
        functools.partial(update_kernel, vir_count, at_once),
        grid=(rows // step_rows,),
        in_specs=in_specs,
        out_specs=pl.BlockSpec((step_rows, cols), lambda step: (step, chunk)),
        out_shape=jax.ShapeDtypeStruct((rows, chunks * cols), jnp.float32),
        input_output_aliases=aliases,
        compiler_params=pltpu.CompilerParams(vmem_limit_bytes=VMEM_LIMIT),
        cost_estimate=pl.CostEstimate(
            flops=4 * rows * spread.size, bytes_accessed=rows * cols * 10, transcendentals=0
        ),
        name="update",
    )(*args)


def body(amplitudes, amp_mask, integrals, int_mask, group_orbital_numbers, occ_energy, vir_energy):
    tile_total = lax.axis_size("occ")
    vir_count = lax.axis_size("vir")
    row_tile = lax.axis_index("occ")
    vir_place = lax.axis_index("vir")
    span = W // vir_count
    slab_cols = span * W
    chunks = 2 if span >= 16 else 1
    width = span // chunks
    block = width * span
    rows = PAIR_SQ + EXCHANGE_CODE_ROWS

    def exchanged(packed):
        moved = lax.all_to_all(
            packed.reshape(tile_total * vir_count, rows, block), ("occ", "vir"), split_axis=0, concat_axis=0, tiled=True
        )
        return moved.reshape(tile_total, vir_count, rows, block)

    coded, *plain = screen_call(chunks, int_mask, integrals)
    plain = [lax.all_gather(part, "occ", axis=0, tiled=True) for part in plain]
    slabs = [[lax.all_gather(coded, "occ", axis=0, tiled=True), plain[0]]] + [[part] for part in plain[1:]]
    ladders, arrived = [], []
    for slab in slabs:
        ladder, packed = ladder_call(
            tile_total, vir_count, chunks, amp_mask[0], group_orbital_numbers, amplitudes, slab
        )
        ladders.append(ladder)
        arrived.append(exchanged(packed))

    place = jnp.arange(vir_count * block)
    owner, there_part = place // block, place // (width * width) % chunks
    here, there = place // width % width, place % width
    mirror_spread = one_hot_of(here * W + owner * span + there_part * width + there, width * W)
    place = jnp.arange(vir_count * width * width)
    owner, b, a = place // (width * width), place // width % width, place % width
    direct_spread = one_hot_of(
        jnp.concatenate([a * W + owner * span + c * width + b for c in range(chunks)]), width * W
    )

    occ_table = occ_energy.reshape(tile_total, ORBITALS_IN_GRP)
    own_energy = lax.dynamic_slice_in_dim(occ_table, row_tile, 1, 0)[0]
    occ_sum = (own_energy[None, :, None] + occ_table[:, None, :]).reshape(tile_total, 1, PAIR_SQ)
    vir_own = lax.dynamic_slice_in_dim(vir_energy, vir_place * span, span, 0)
    vir_sum = (vir_own[:, None] + vir_energy[None, :]).reshape(1, -1)
    update = None
    for chunk in range(chunks):
        direct = direct_call(chunk, direct_spread, ladders)
        update = update_call(chunk, chunks, 4, arrived[chunk], mirror_spread, vir_sum, occ_sum, direct, update)
    return update


def solution(mesh):
    in_specs = (P("occ", None), P("occ", None, None), P("occ", "vir"), P(), P(), P(), P())
    out_specs = P("occ", "vir")
    return jax.shard_map(body, mesh=mesh, in_specs=in_specs, out_specs=out_specs, check_vma=False)
```

```python
import functools

import jax
import jax.numpy as jnp
from jax import lax
from jax.experimental import pallas as pl
from jax.experimental.pallas import tpu as pltpu
from jax.sharding import PartitionSpec as P

VT = 32
NVT = 2
W = 64
ORBITALS_IN_GRP = 16
PAIR_SQ = ORBITALS_IN_GRP * ORBITALS_IN_GRP
CODE_ROWS = 16
EXCHANGE_CODE_ROWS = 8
AT_ONCE = 4
SLAB_BITS = 14.0
TOP = 32700.0
STEPS = 8.0
VMEM_LIMIT = 56 * 1024 * 1024


def one_hot_of(target, amount):
    return (target[:, None] == jnp.arange(amount)[None, :]).astype(jnp.bfloat16)


def split(values):
    high = values.astype(jnp.bfloat16)
    return high, (values - high.astype(jnp.float32)).astype(jnp.bfloat16)


def dot(left, right):
    return jnp.dot(left, right, preferred_element_type=jnp.float32)


def scale_of(code):
    return jnp.exp2(code * (1.0 / STEPS))


def screen_kernel(part, int_mask, slab_ref, coded_ref, plain_ref, *later_refs):
    slab_rows, slab_cols = slab_ref.shape
    coded_cols = coded_ref.shape[1]
    cols = coded_cols + plain_ref.shape[1]
    span = slab_cols // W
    row_label = lax.axis_index("occ") * slab_rows // W // VT * NVT
    col_label = lax.axis_index("vir") * slab_cols // W // VT * NVT
    natural = lax.broadcasted_iota(jnp.int32, (slab_cols, 1), 0)
    a, b = natural // W, natural % W
    target = b // span * (part * span) + (a // part * part + b % part) * part + a % part
    place = lax.broadcasted_iota(jnp.int32, (slab_cols, cols), 1)
    to = lax.broadcasted_iota(jnp.int32, (1, cols), 1)
    second = lax.broadcasted_iota(jnp.int32, (slab_rows, 1), 0) % W >= VT
    for chunk in range(span // part):
        right = to // (part * span) * span + chunk * part + to // part % part >= VT
        kept = [
            jnp.where(right, int_mask[label, col_label + 1], int_mask[label, col_label])
            for label in (row_label, row_label + 1)
        ]
        ones = place == jnp.where(b % span // part == chunk, target, -1)
        moved = dot(slab_ref[...], ones.astype(jnp.float32).astype(jnp.bfloat16))
        moved = jnp.where(jnp.where(second, kept[1], kept[0]) > 0, moved, 0.0)
        if chunk:
            later_refs[chunk - 1][...] = moved.astype(jnp.bfloat16)
        else:
            plain_ref[...] = moved[:, coded_cols:].astype(jnp.bfloat16)
            moved = moved[:, :coded_cols]
            most = jnp.maximum(jnp.max(jnp.abs(moved), axis=0, keepdims=True), 1e-30)
            code = jnp.floor(jnp.log2(most)) + 1.0
            coded_ref[:slab_rows, :] = jnp.round(moved * jnp.exp2(SLAB_BITS - code)).astype(jnp.int32).astype(jnp.int16)
            coded_ref[slab_rows:, :] = jnp.broadcast_to(
                code.astype(jnp.int32), (CODE_ROWS, coded_cols)
            ).astype(jnp.int16)


def screen_call(chunks, int_mask, integrals):
    slab_rows, slab_cols = integrals.shape
    cols = slab_cols // chunks
    coded_cols = cols - cols // 4
    plain_cols = [cols // 4] + [cols] * (chunks - 1)
    vmem = pl.BlockSpec(memory_space=pltpu.VMEM)
    return pl.pallas_call(
        functools.partial(screen_kernel, slab_cols // W // chunks),
        in_specs=[pl.BlockSpec(memory_space=pltpu.SMEM), vmem],
        out_specs=[vmem] * (1 + len(plain_cols)),
        out_shape=[jax.ShapeDtypeStruct((slab_rows + CODE_ROWS, coded_cols), jnp.int16)]
        + [jax.ShapeDtypeStruct((slab_rows, each), integrals.dtype) for each in plain_cols],
        compiler_params=pltpu.CompilerParams(vmem_limit_bytes=VMEM_LIMIT),
        name="screen",
    )(int_mask, integrals)


def ladder_kernel(tile_total, vir_count, chunks, coded, parts, amp_mask, numbers, rows_ref, *refs):
    gathered_refs, refs = refs[:parts], refs[parts:]
    ladder_ref, packed_ref, product = refs[:3]
    slab_refs = gathered_refs
    if coded:
        slab_refs, stage, sems = refs[3:4], refs[4], refs[5]
    step = pl.program_id(0)
    cols = product.shape[1]
    slab_rows = slab_refs[0].shape[0] // tile_total
    shard_rows = slab_rows + CODE_ROWS
    block = cols // vir_count
    lanes = block // chunks

    def multiply():
        tile = step
        lane = lax.broadcasted_iota(jnp.int32, (1, W * W), 1)
        left = lane % W < VT
        keep = jnp.where(
            lane < W * VT,
            jnp.where(left, amp_mask[tile, 0], amp_mask[tile, 1]),
            jnp.where(left, amp_mask[tile, 2], amp_mask[tile, 3]),
        )
        keep = keep.astype(jnp.float32).astype(jnp.bfloat16)
        screened = rows_ref[...] * keep
        at = 0
        for slab_ref in slab_refs:
            product[:, at : at + slab_ref.shape[1]] = dot(screened, slab_ref[...])
            at += slab_ref.shape[1]

    def decode():
        def copy_of(shard):
            at = pl.ds(pl.multiple_of(shard * shard_rows, CODE_ROWS), shard_rows)
            return pltpu.make_async_copy(gathered_refs[0].at[at, :], stage.at[at, :], sems.at[shard])

        coded_cols = stage.shape[1]
        for shard in range(tile_total):
            copy_of(shard).start()

        def use(shard, carry):
            copy_of(shard).wait()
            at = pl.multiple_of(shard * shard_rows, CODE_ROWS)
            code = stage[pl.ds(pl.multiple_of(at + slab_rows, CODE_ROWS), CODE_ROWS), :]
            values = stage[pl.ds(at, slab_rows), :].astype(jnp.int32).astype(jnp.float32)
            scale = jnp.exp2(code.astype(jnp.int32).astype(jnp.float32)[:1] - SLAB_BITS)
            to = pl.ds(pl.multiple_of(shard * slab_rows, slab_rows), slab_rows)
            slab_refs[0][to, coded_cols:] = gathered_refs[1][to, :]
            slab_refs[0][to, :coded_cols] = (values * scale).astype(jnp.bfloat16)
            return carry

        lax.fori_loop(0, tile_total, use, 0)

    def finish():
        tile = jnp.maximum(step - 1, 0)
        pair = lax.broadcasted_iota(jnp.int32, (PAIR_SQ, 1), 0)
        own_number = numbers[lax.axis_index("occ")]
        nonzero = (pair // ORBITALS_IN_GRP < own_number) & (pair % ORBITALS_IN_GRP < numbers[tile])
        ladder = jnp.where(nonzero, product[...], 0.0)
        for h in range(chunks):
            ladder_ref[h] = jnp.concatenate(
                [ladder[:, v * block + h * lanes : v * block + (h + 1) * lanes] for v in range(vir_count)], axis=1
            )
        by_place = ladder.reshape(ORBITALS_IN_GRP, ORBITALS_IN_GRP, cols)
        mirror = jnp.swapaxes(by_place, 0, 1).reshape(PAIR_SQ, cols)
        most = jnp.maximum(jnp.max(jnp.abs(ladder), axis=0, keepdims=True), 1e-30)
        code = jnp.ceil(jnp.log2(most) * STEPS)
        coded_rows = jnp.round(mirror * (TOP / scale_of(code))).astype(jnp.int32).astype(jnp.int16)
        code_rows = jnp.broadcast_to(code.astype(jnp.int32), (EXCHANGE_CODE_ROWS, cols)).astype(jnp.int16)
        for v in range(vir_count):
            packed_ref[0, v, :PAIR_SQ] = coded_rows[:, v * block : (v + 1) * block]
            packed_ref[0, v, PAIR_SQ:] = code_rows[:, v * block : (v + 1) * block]

    if coded:

        @pl.when(step == 0)
        def _():
            decode()

    @pl.when(step < tile_total)
    def _():
        finish()
        multiply()

    @pl.when(step == tile_total)
    def _():
        finish()


def ladder_call(tile_total, vir_count, chunks, amp_mask, numbers, amplitudes, slab):
    coded = slab[0].dtype == jnp.int16
    cols = sum(part.shape[1] for part in slab)
    block = cols // vir_count
    smem = pl.BlockSpec(memory_space=pltpu.SMEM)
    rows = tile_total * PAIR_SQ
    before = lambda step: jnp.maximum(step - 1, 0)
    packed_block = (vir_count, PAIR_SQ + EXCHANGE_CODE_ROWS, block)
    return pl.pallas_call(
        functools.partial(ladder_kernel, tile_total, vir_count, chunks, coded, len(slab)),
        grid=(tile_total + 1,),
        in_specs=[
            smem,
            smem,
            pl.BlockSpec((PAIR_SQ, W * W), lambda step: (jnp.minimum(step, tile_total - 1), 0)),
            *[
                pl.BlockSpec(memory_space=pl.ANY)
                if part.dtype == jnp.int16
                else pl.BlockSpec(part.shape, lambda step: (0, 0))
                for part in slab
            ],
        ],
        out_specs=[
            pl.BlockSpec((chunks, PAIR_SQ, cols // chunks), lambda step: (0, before(step), 0)),
            pl.BlockSpec((1,) + packed_block, lambda step: (before(step), 0, 0, 0)),
        ],
        out_shape=[
            jax.ShapeDtypeStruct((chunks, rows, cols // chunks), jnp.float32),
            jax.ShapeDtypeStruct((tile_total,) + packed_block, jnp.int16),
        ],
        scratch_shapes=[pltpu.VMEM((PAIR_SQ, cols), jnp.float32)]
        + [
            pltpu.VMEM((W * W, cols), jnp.bfloat16),
            pltpu.VMEM(slab[0].shape, slab[0].dtype),
            pltpu.SemaphoreType.DMA((tile_total,)),
        ]
        * coded,
        compiler_params=pltpu.CompilerParams(vmem_limit_bytes=VMEM_LIMIT),
        cost_estimate=pl.CostEstimate(
            flops=2 * rows * cols * W * W,
            bytes_accessed=rows * (W * W * 2 + cols * 6) + W * W * cols * 2,
            transcendentals=0,
        ),
        name="ladder",
    )(amp_mask, numbers, amplitudes, *slab)


def moved_columns(values, spread_ref):
    both = dot(jnp.concatenate(split(values), axis=0), spread_ref[...])
    return both[: values.shape[0]] + both[values.shape[0] :]


def direct_kernel(spread_ref, *refs):
    refs[-1][...] = moved_columns(jnp.concatenate([ref[0] for ref in refs[:-1]], axis=1), spread_ref)


def direct_call(chunk, spread, ladders):
    rows = ladders[0].shape[1]
    step_rows = AT_ONCE * PAIR_SQ
    return pl.pallas_call(
        direct_kernel,
        grid=(rows // step_rows,),
        in_specs=[pl.BlockSpec(spread.shape, lambda step: (0, 0))]
        + [pl.BlockSpec((1, step_rows, ladder.shape[2]), lambda step: (chunk, step, 0)) for ladder in ladders],
        out_specs=pl.BlockSpec((step_rows, spread.shape[1]), lambda step: (step, 0)),
        out_shape=jax.ShapeDtypeStruct((rows, spread.shape[1]), jnp.float32),
        compiler_params=pltpu.CompilerParams(vmem_limit_bytes=VMEM_LIMIT),
        cost_estimate=pl.CostEstimate(
            flops=4 * rows * spread.size, bytes_accessed=rows * spread.shape[1] * 8, transcendentals=0
        ),
        name="direct",
    )(spread, *ladders)


def update_kernel(vir_count, at_once, spread_ref, vir_ref, occ_ref, *refs):
    arrived_refs, refs = refs[:vir_count], refs[vir_count:]
    direct_refs = refs[:at_once]
    tiles = []
    for n in range(at_once):
        blocks = []
        for v in range(vir_count):
            code = arrived_refs[v][n, 0, PAIR_SQ:].astype(jnp.int32).astype(jnp.float32)[:1]
            values = arrived_refs[v][n, 0, :PAIR_SQ].astype(jnp.int32).astype(jnp.float32)
            blocks.append(values * (scale_of(code) * (1.0 / TOP)))
        tiles.append(jnp.concatenate(blocks, axis=1))
    mirror = moved_columns(jnp.concatenate(tiles, axis=0), spread_ref)
    for n, direct_ref in enumerate(direct_refs):
        at = slice(n * PAIR_SQ, (n + 1) * PAIR_SQ)
        occ = jnp.transpose(jnp.broadcast_to(occ_ref[n], (128, PAIR_SQ)))[:, :1]
        denominator = vir_ref[...] - occ
        inverse = pl.reciprocal(denominator, approx=True)
        for _ in range(2):
            inverse = inverse * (2.0 - denominator * inverse)
        refs[-1][at, :] = (direct_ref[...] + mirror[at]) * inverse


def update_call(chunk, chunks, at_once, arrived, spread, vir_sum, occ_sum, direct, earlier):
    cols = spread.shape[1]
    rows = direct.shape[0]
    step_rows = at_once * PAIR_SQ
    vir_count = arrived.shape[1]
    args = [spread, vir_sum, occ_sum] + [arrived] * vir_count + [direct] * at_once
    in_specs = [
        pl.BlockSpec(spread.shape, lambda step: (0, 0)),
        pl.BlockSpec((1, cols), lambda step: (0, chunk)),
        pl.BlockSpec((at_once, 1, PAIR_SQ), lambda step: (step, 0, 0)),
    ]
    in_specs += [
        pl.BlockSpec((at_once, 1) + arrived.shape[2:], lambda step, v=v: (step, v, 0, 0)) for v in range(vir_count)
    ]
    in_specs += [pl.BlockSpec((PAIR_SQ, cols), lambda step, n=n: (step * at_once + n, 0)) for n in range(at_once)]
    aliases = {}
    if earlier is not None:
        aliases = {len(args): 0}
        args.append(earlier)
        in_specs.append(pl.BlockSpec(memory_space=pl.ANY))
    return pl.pallas_call(
        functools.partial(update_kernel, vir_count, at_once),
        grid=(rows // step_rows,),
        in_specs=in_specs,
        out_specs=pl.BlockSpec((step_rows, cols), lambda step: (step, chunk)),
        out_shape=jax.ShapeDtypeStruct((rows, chunks * cols), jnp.float32),
        input_output_aliases=aliases,
        compiler_params=pltpu.CompilerParams(vmem_limit_bytes=VMEM_LIMIT),
        cost_estimate=pl.CostEstimate(
            flops=4 * rows * spread.size, bytes_accessed=rows * cols * 10, transcendentals=0
        ),
        name="update",
    )(*args)


def body(amplitudes, amp_mask, integrals, int_mask, group_orbital_numbers, occ_energy, vir_energy):
    tile_total = lax.axis_size("occ")
    vir_count = lax.axis_size("vir")
    row_tile = lax.axis_index("occ")
    vir_place = lax.axis_index("vir")
    span = W // vir_count
    slab_cols = span * W
    chunks = 2 if span >= 16 else 1
    width = span // chunks
    block = width * span
    rows = PAIR_SQ + EXCHANGE_CODE_ROWS

    def exchanged(packed):
        moved = lax.all_to_all(
            packed.reshape(tile_total * vir_count, rows, block), ("occ", "vir"), split_axis=0, concat_axis=0, tiled=True
        )
        return moved.reshape(tile_total, vir_count, rows, block)

    coded, *plain = screen_call(chunks, int_mask, integrals)
    plain = [lax.all_gather(part, "occ", axis=0, tiled=True) for part in plain]
    slabs = [[lax.all_gather(coded, "occ", axis=0, tiled=True), plain[0]]] + [[part] for part in plain[1:]]
    ladders, arrived = [], []
    for slab in slabs:
        ladder, packed = ladder_call(
            tile_total, vir_count, chunks, amp_mask[0], group_orbital_numbers, amplitudes, slab
        )
        ladders.append(ladder)
        arrived.append(exchanged(packed))

    place = jnp.arange(vir_count * block)
    owner, there_part = place // block, place // (width * width) % chunks
    here, there = place // width % width, place % width
    mirror_spread = one_hot_of(here * W + owner * span + there_part * width + there, width * W)
    place = jnp.arange(vir_count * width * width)
    owner, b, a = place // (width * width), place // width % width, place % width
    direct_spread = one_hot_of(
        jnp.concatenate([a * W + owner * span + c * width + b for c in range(chunks)]), width * W
    )

    occ_table = occ_energy.reshape(tile_total, ORBITALS_IN_GRP)
    own_energy = lax.dynamic_slice_in_dim(occ_table, row_tile, 1, 0)[0]
    occ_sum = (own_energy[None, :, None] + occ_table[:, None, :]).reshape(tile_total, 1, PAIR_SQ)
    vir_own = lax.dynamic_slice_in_dim(vir_energy, vir_place * span, span, 0)
    vir_sum = (vir_own[:, None] + vir_energy[None, :]).reshape(1, -1)
    update = None
    for chunk in range(chunks):
        direct = direct_call(chunk, direct_spread, ladders)
        update = update_call(chunk, chunks, 4, arrived[chunk], mirror_spread, vir_sum, occ_sum, direct, update)
    return update


def solution(mesh):
    in_specs = (P("occ", None), P("occ", None, None), P("occ", "vir"), P(), P(), P(), P())
    out_specs = P("occ", "vir")
    return jax.shard_map(body, mesh=mesh, in_specs=in_specs, out_specs=out_specs, check_vma=False)
```
